32 devices in a mesh: dom: 32 (over z, y, x, core).
Axes of the slice: x: 2, y: 2, z: 4, core: 2. Of those that a mesh axis runs over, the one named last changes fastest.
Arguments:
- strips: float32 [16384, 256], P('dom')
- columns: int32 [256, 4], P('dom'), may hold values from 0 to 39, as said below
- send_list: int32 [32, 4, 8], P('dom'), may hold values from 0 to 7, each once within a row
- send_count: int32 [32, 4], P('dom'), may hold values from 1 to 8, as said below
- shifts: float32 [4], replicated, may hold values from 0.25 to 1
- prev_basis: float32 [3, 32, 16384], P(None, None, 'dom')
- mix: float32 [3, 32], replicated, may hold values from -1 to 1
Outputs:
- new_basis: float32 [3, 4, 16384], P(None, None, 'dom')
- factors: float32 [3, 36, 4], replicated
The draws below stay inside these ranges and needn't reach their ends.
Inputs may be any that keep to these rules, and one draw needn't show every extreme that they name: `columns`: entry 0 of block row r of a partition is r itself. An entry e below 8 names the partition's own block row e; an entry e of 8 or more names ghost slot (e - 8) % 8 of link (e - 8) // 8. `send_count`: slot j of a link carries data when j is below the sender's count for that link, zeros otherwise. `send_list`: each partition's list for one link names each of its 8 block rows once.
All inputs are finite; a program needn't handle non-finite values.
Results may differ from the reference program's by a relative error of at most 0.013.
Values sent between devices are 32-bit elements; how exact they have to be, the bound alone decides.
No kernel may reach another device: no remote copies, remote signals or barrier semaphores. Data moves between devices by JAX's collectives and lax.ppermute only.
A program may use at most 64 MiB of HBM per device.

```python
import math
import jax
import jax.numpy as jnp
from jax import lax

BLOCK = 64
COMPS = 3
KB = 4
LINKS = 4
S = 4
P_SIZE = 32
RB = 8
NBLK = 256
NROWS = 16384
N_DOM = 32


def draw_strips(key, part):
    key = jax.random.fold_in(key, 11)
    noise_key, diag_key = jax.random.split(key)
    shape = (NROWS, KB * BLOCK)
    noise = jax.random.normal(noise_key, shape, jnp.float32)
    diagonal = jax.random.uniform(diag_key, (NROWS, 1), jnp.float32, 1.0, 2.5)
    row_pos = lax.broadcasted_iota(jnp.int32, shape, 0) % BLOCK
    col_pos = lax.broadcasted_iota(jnp.int32, shape, 1)
    return noise / math.sqrt(KB * BLOCK) + jnp.where(row_pos == col_pos, diagonal, 0.0)


def draw_columns(key, part):
    key = jax.random.fold_in(key, 12)
    local_key, ghost_key = jax.random.split(key)
    own = lax.broadcasted_iota(jnp.int32, (NBLK, 1), 0) % RB
    local = jax.random.randint(local_key, (NBLK, 1), 0, RB, jnp.int32)
    ghost = jax.random.randint(ghost_key, (NBLK, KB - 2), RB, RB + LINKS * RB, jnp.int32)
    table = jnp.concatenate([own, local, ghost], axis=1)
    return table.at[0, KB - 1].set(RB + LINKS * RB - 1)


def draw_send_count(key, part):
    key = jax.random.fold_in(key, 13)
    counts = jax.random.randint(key, (N_DOM, LINKS), 1, RB + 1, jnp.int32)
    return counts.at[0, 0].set(RB).at[0, 1].set(1)


def ramped(shape, top):
    place = lax.broadcasted_iota(jnp.float32, (shape[2],), 0) / float(shape[2])
    return 1.0 + (top - 1.0) * place


def draw_prev_basis(key, part):
    key = jax.random.fold_in(key, 14)
    noise_key, scale_key = jax.random.split(key)
    shape = (COMPS, P_SIZE, NROWS)
    noise = jax.random.normal(noise_key, shape, jnp.float32)
    spread = jax.random.uniform(scale_key, (NROWS,), jnp.float32, -1.15, 1.15)
    rise = ramped(shape, 3.0)
    return noise * (jnp.exp(spread) * rise)[None, None, :]


def bell_draw(stream_key, shape, scale, bound, held_as=jnp.bfloat16):
    array = jax.random.normal(stream_key, shape, jnp.float32) * scale
    return jnp.minimum(jnp.maximum(array, -bound), bound).astype(held_as)


def setup_inputs(seed: int = 0) -> dict:
    arg_keys = jax.random.split(jax.random.key(seed), 8)
    strips = draw_strips(jax.random.fold_in(arg_keys[7], 71), 0)
    columns = draw_columns(jax.random.fold_in(arg_keys[7], 71), 0)
    send_list = jax.vmap(lambda own: jax.random.permutation(own, RB))(jax.random.split(arg_keys[2], N_DOM * LINKS)).reshape((N_DOM, LINKS, RB)).astype(jnp.int32)
    send_count = draw_send_count(jax.random.fold_in(arg_keys[7], 71), 0)
    shifts = jnp.clip(jax.random.uniform(arg_keys[4], (S,), jnp.float32, 0.25, 1.0), 0.25, 1.0)
    prev_basis = draw_prev_basis(jax.random.fold_in(arg_keys[7], 71), 0)
    mix = bell_draw(arg_keys[6], (COMPS, P_SIZE), P_SIZE ** -0.5, 1.0, jnp.float32)
    return dict(strips=strips, columns=columns, send_list=send_list, send_count=send_count, shifts=shifts, prev_basis=prev_basis, mix=mix)


link_steps = (1, -1, 8, -8)

def extend(vec, send_list, send_count):
    pieces = [vec]
    devices = jnp.arange(N_DOM, dtype=jnp.int32)
    slots = jnp.arange(RB, dtype=jnp.int32)
    for link, step in enumerate(link_steps):
        order = send_list[:, link, :]
        packed = jnp.take_along_axis(vec, order[None, :, :, None], axis=2)
        live = slots[None, :] < send_count[:, link][:, None]
        packed = jnp.where(live[None, :, :, None], packed, jnp.zeros_like(packed))
        moved = jnp.roll(packed, step, axis=1)
        source = devices - step
        valid = (source >= 0) & (source < N_DOM)
        pieces.append(jnp.where(valid[None, :, None, None], moved, jnp.zeros_like(moved)))
    return jnp.concatenate(pieces, axis=2)

def apply(ext, matrix, columns):
    picks = columns.reshape(N_DOM, RB * KB)
    picked = jnp.take_along_axis(ext, picks[None, :, :, None], axis=2)
    picked = picked.reshape(COMPS, N_DOM, RB, KB * BLOCK)
    return jnp.einsum('drik,cdrk->cdri', matrix, picked, precision=lax.Precision.HIGHEST)

def reference(strips, columns, send_list, send_count, shifts, prev_basis, mix):
    matrix = strips.reshape(N_DOM, RB, BLOCK, KB * BLOCK)
    start = jnp.einsum('cp,cpn->cn', mix, prev_basis, precision=lax.Precision.HIGHEST)
    vec = start.reshape(COMPS, N_DOM, RB, BLOCK)
    vectors = []
    for step in range(S):
        image = apply(extend(vec, send_list, send_count), matrix, columns)
        vec = image - shifts[step] * vec
        vectors.append(vec.reshape(COMPS, NROWS))
    basis = jnp.stack(vectors, axis=1)
    total = float(NROWS)
    coef = jnp.einsum('cpn,csn->cps', prev_basis, basis, precision=lax.Precision.HIGHEST) / total
    projected = basis - jnp.einsum('cps,cpn->csn', coef, prev_basis, precision=lax.Precision.HIGHEST)
    gram = jnp.einsum('csn,ctn->cst', projected, projected, precision=lax.Precision.HIGHEST) / total
    lower = jnp.linalg.cholesky(gram)
    new_basis = lax.linalg.triangular_solve(lower, projected, left_side=True, lower=True)
    factors = jnp.concatenate([coef, jnp.swapaxes(lower, 1, 2)], axis=1)
    return (new_basis, factors)
```

```python
import jax
import jax.numpy as jnp
from jax import lax
from jax.experimental import pallas as pl
from jax.experimental.pallas import tpu as pltpu
from jax.sharding import PartitionSpec as P

BLOCK = 64
S = 4
FAR = 8
DEAD = 1000.0
HIGHEST = lax.Precision.HIGHEST
NN = (((1,), (0,)), ((), ()))
NT = (((1,), (1,)), ((), ()))


def dot(a, b, dims=NN, precision=None):
    return lax.dot_general(a, b, dims, precision=precision, preferred_element_type=jnp.float32)


def iota(shape, axis):
    return lax.broadcasted_iota(jnp.int32, shape, axis)


def split(x):
    high = x.astype(jnp.bfloat16)
    return high, (x - high.astype(jnp.float32)).astype(jnp.bfloat16)


def own_lanes(blocks):
    shape = (blocks, blocks * BLOCK)
    return iota(shape, 1) // BLOCK == iota(shape, 0)


def fold(masked):
    total = masked[:, :128]
    for t in range(1, masked.shape[1] // 128):
        total = total + masked[:, t * 128 : (t + 1) * 128]
    return total + pltpu.roll(total, BLOCK, 1)


def doubled(tile, comp):
    part = tile[:, (comp // 2) * 128 : (comp // 2 + 1) * 128]
    turned = pltpu.roll(part, BLOCK, 1)
    low = iota(part.shape, 1) < BLOCK
    return jnp.where(low, part, turned) if comp % 2 == 0 else jnp.where(low, turned, part)


def joined(parts, tail):
    low = iota(parts[0].shape, 1) < BLOCK
    return jnp.concatenate([jnp.where(low, parts[0], parts[1]), jnp.where(low, parts[2], tail)], axis=1)


def start_kernel(prev_ref, mix_ref, list_ref, count_ref, out_ref):
    comps, vecs, rows = prev_ref.shape
    blocks = rows // BLOCK
    prev = prev_ref[...].reshape(comps * vecs, rows)
    mix = jnp.concatenate([mix_ref[...]] * comps, axis=1)
    mix = jnp.where(iota(mix.shape, 1) // vecs == iota(mix.shape, 0), mix, 0.0)
    start = dot(mix, prev, precision=HIGHEST)
    own = own_lanes(blocks)
    parts = [
        fold(jnp.where(own, jnp.broadcast_to(start[c : c + 1], own.shape), 0.0)) for c in range(comps)
    ]
    square = (blocks, blocks)
    tail = jnp.zeros((blocks, 128), jnp.float32)
    for link in range(4):
        order = jnp.broadcast_to(list_ref[0, link : link + 1, :], square)
        live = iota(square, 1) < jnp.broadcast_to(count_ref[0:1, link : link + 1], square)
        order = jnp.where(live, order.astype(jnp.float32), DEAD)
        column = jnp.sum(jnp.where(iota(square, 0) == iota(square, 1), order, 0.0), axis=1, keepdims=True)
        tail = jnp.where(iota(tail.shape, 1) == BLOCK + link, column, tail)
    out_ref[...] = joined(parts, tail)


def prepare_kernel(strips_ref, high_ref, low_ref):
    high, low = split(strips_ref[...].T)
    high_ref[...] = high
    low_ref[...] = low


def previous_gram_kernel(prev_ref, out_ref):
    comps, vecs, rows = prev_ref.shape
    prev = prev_ref[...].reshape(comps * vecs, rows)
    full = dot(prev, prev, NT, HIGHEST)
    owner = iota((vecs, comps * vecs), 1) // vecs
    total = jnp.where(owner == 0, full[:vecs], 0.0)
    for c in range(1, comps):
        total = total + jnp.where(owner == c, full[c * vecs : (c + 1) * vecs], 0.0)
    out_ref[...] = jnp.concatenate([total, jnp.zeros((vecs, 128 - comps * vecs), jnp.float32)], axis=1)


def selection(columns, pieces, place):
    blocks, count = columns.shape
    rows = [(iota((blocks, 128), 0) == iota((blocks, 128), 1)).astype(jnp.float32)]
    even, even_far = lax.rem(place, 2) == 0, lax.rem(place // FAR, 2) == 0
    slots = [
        (jnp.where(even, 2, 1), (pieces[2], pieces[1]), even),
        (jnp.where(even, 1, 2), (pieces[1], pieces[2]), even),
        (jnp.where(even_far, 4, 3), (pieces[4], pieces[3]), even_far),
        (jnp.where(even_far, 3, 4), (pieces[3], pieces[4]), even_far),
    ]
    for link, (slot, (when, other), test) in enumerate(slots):
        lane = 192 + link
        order = jnp.where(test, when[:, lane : lane + 1], other[:, lane : lane + 1])
        at = order.astype(jnp.int32) + slot * blocks
        rows.append((iota((blocks, 128), 1) == at).astype(jnp.float32))
    rows.append(jnp.zeros((128 - 5 * blocks, 128), jnp.float32))
    table = jnp.concatenate(rows, axis=0).astype(jnp.bfloat16)
    picks = [
        (iota((blocks, 128), 1) == columns[:, k : k + 1]).astype(jnp.float32) for k in range(count)
    ]
    return dot(jnp.concatenate(picks, axis=0).astype(jnp.bfloat16), table)


def multiply(choose, pieces, shift, high, low):
    blocks = pieces[0].shape[0]
    count = choose.shape[0] // blocks
    comps = 3
    ext = jnp.concatenate(pieces + [jnp.zeros((128 - 5 * blocks, 256), jnp.float32)], axis=0)
    picked = dot(choose.astype(jnp.bfloat16), jnp.concatenate(split(ext), axis=1))
    halves = []
    for half in range(2):
        for c in range(comps):
            lane = half * 256 + c * BLOCK
            halves.append(
                jnp.concatenate(
                    [picked[k * blocks : (k + 1) * blocks, lane : lane + BLOCK] for k in range(count)],
                    axis=1,
                )
            )
    left = jnp.concatenate(halves, axis=0).astype(jnp.bfloat16)
    both = dot(left, high) + dot(left, low)
    image = both[: comps * blocks] + both[comps * blocks :]
    own = own_lanes(blocks)
    parts, lines = [], []
    for c in range(comps):
        part = fold(jnp.where(own, image[c * blocks : (c + 1) * blocks], 0.0))
        part = part - shift * doubled(pieces[0], c)
        parts.append(part)
        wide = jnp.concatenate([part] * (blocks // 2), axis=1)
        lines.append(jnp.sum(jnp.where(own, wide, 0.0), axis=0, keepdims=True))
    return joined(parts, jnp.zeros_like(parts[0])), lines


def spread(lines, old):
    where = iota(old.shape, 0)
    for c, line in enumerate(lines):
        old = jnp.where(where == c, jnp.broadcast_to(line, old.shape), old)
    return old


def first_kernel(own, a, b, c, d, columns, shifts, high, low, tile_ref, lines_ref, choose_ref):
    pieces = [ref[...] for ref in (own, a, b, c, d)]
    choose = selection(columns[...], pieces, lax.axis_index("dom"))
    choose_ref[...] = choose
    tile, lines = multiply(choose, pieces, shifts[0], high[...], low[...])
    tile_ref[...] = tile
    lines_ref[...] = spread(lines, jnp.zeros(lines_ref.shape, jnp.float32))


def middle_kernel(step, own, a, b, c, d, choose, shifts, high, low, tile_ref, lines_ref):
    pieces = [ref[...] for ref in (own, a, b, c, d)]
    tile, lines = multiply(choose[...], pieces, shifts[step], high[...], low[...])
    tile_ref[...] = tile
    lines_ref[...] = spread(lines, jnp.zeros(lines_ref.shape, jnp.float32))


def last_kernel(
    own, a, b, c, d, choose, shifts, high, low, l0, l1, l2, prev_ref, prev_gram, lines_ref, gram_ref
):
    pieces = [ref[...] for ref in (own, a, b, c, d)]
    _, lines = multiply(choose[...], pieces, shifts[S - 1], high[...], low[...])
    comps, vecs, rows = prev_ref.shape
    last = spread(lines, jnp.zeros(lines_ref.shape, jnp.float32))
    lines_ref[...] = last
    basis = jnp.concatenate([l0[...], l1[...], l2[...], last], axis=0)
    prev = prev_ref[...].reshape(comps * vecs, rows)
    with_prev = dot(basis, prev, NT, HIGHEST)
    with_basis = dot(basis, basis, NT, HIGHEST)
    gram = jnp.concatenate([with_prev, with_basis], axis=1)
    lane = iota((8, 128), 1)
    comp = iota((8, 128), 0)
    mine = jnp.where(lane < comps * vecs, lane // vecs, lax.rem(lane, 8)) == comp
    result = jnp.zeros((8, 128), jnp.float32)
    for k in range(S):
        line = jnp.sum(jnp.where(mine, gram[k * 8 : (k + 1) * 8], 0.0), axis=0, keepdims=True)
        result = jnp.where(comp == k, jnp.broadcast_to(line, result.shape), result)
    gram_ref[...] = jnp.concatenate([prev_gram[...], result], axis=0)


def finish_kernel(total, gram_ref, prev_ref, l0, l1, l2, l3, basis_ref, factors_ref):
    comps, vecs, rows = prev_ref.shape
    width = comps * vecs
    gram = gram_ref[...] * (1.0 / total)
    small = gram[vecs:]
    lane, comp = iota((8, 128), 1), iota((8, 128), 0)
    in_prev = (lane < width) & (lane // vecs == comp)
    coef, cross = [], []
    for k in range(S):
        line = jnp.broadcast_to(small[k : k + 1], (8, 128))
        coef.append(jnp.where(in_prev, line, 0.0))
        cross.append([jnp.where(lane == width + 8 * l + comp, line, 0.0) for l in range(k + 1)])
    coefs = jnp.concatenate(coef, axis=0)
    prev = prev_ref[...].reshape(width, rows)
    basis = jnp.concatenate([l0[...], l1[...], l2[...], l3[...]], axis=0)
    projected = basis - dot(coefs[:, :width], prev, precision=HIGHEST)
    square = jnp.concatenate([gram[:vecs]] * comps, axis=0)
    r, q = iota(square.shape, 0), iota(square.shape, 1)
    square = jnp.where(r // vecs == q // vecs, square, 0.0) - jnp.where(r == q, 2.0, 0.0)
    turned = dot(coefs[:, :width], square, precision=HIGHEST)
    entry = {}
    for k in range(S):
        for l in range(k + 1):
            value = turned[k * 8 : (k + 1) * 8] * coef[l] + cross[k][l]
            entry[k, l] = jnp.sum(value, axis=1, keepdims=True)
    lower = {}
    for k in range(S):
        for l in range(k + 1):
            value = entry[k, l]
            for m in range(l):
                value = value - lower[k, m] * lower[l, m]
            lower[k, l] = jnp.sqrt(value) if l == k else value / lower[l, l]
    vectors = []
    for k in range(S):
        value = projected[k * 8 : (k + 1) * 8]
        for l in range(k):
            value = value - lower[k, l] * vectors[l]
        value = value / lower[k, k]
        vectors.append(value)
        for c in range(comps):
            basis_ref[c, k : k + 1, :] = value[c : c + 1]
    across = jnp.concatenate([small] * 16, axis=0).T
    for c in range(comps):
        factors_ref[c, :vecs, :] = across[c * vecs : (c + 1) * vecs, :S]
    for k in range(S):
        line = jnp.zeros((8, 128), jnp.float32)
        for l in range(k, S):
            line = jnp.where(lane == l, lower[l, k], line)
        for c in range(comps):
            factors_ref[c, vecs + k : vecs + k + 1, :] = line[c : c + 1, :S]


VMEM = pl.BlockSpec(memory_space=pltpu.VMEM)
SMEM = pl.BlockSpec(memory_space=pltpu.SMEM)


def call(kernel, outs, specs, flops, moved):
    shapes = [jax.ShapeDtypeStruct(shape, kind) for shape, kind in outs]
    return pl.pallas_call(
        kernel,
        out_shape=shapes if len(shapes) > 1 else shapes[0],
        in_specs=specs,
        out_specs=[VMEM] * len(shapes) if len(shapes) > 1 else VMEM,
        compiler_params=pltpu.CompilerParams(vmem_limit_bytes=24 * 1024 * 1024),
        cost_estimate=pl.CostEstimate(flops=flops, bytes_accessed=moved, transcendentals=0),
    )


def pairs_of(length, step, odd):
    firsts = [d for d in range(length - step) if (d // step) % 2 == odd]
    return [(d, d + step) for d in firsts] + [(d + step, d) for d in firsts]


def ghosts(tile):
    length = lax.axis_size("dom")
    return [
        lax.ppermute(tile, "dom", pairs_of(length, step, odd)) for step in (1, FAR) for odd in (0, 1)
    ]


def summed(value):
    length = lax.axis_size("dom")
    step = 1
    while step < length:
        value = value + lax.ppermute(value, "dom", [(d, d ^ step) for d in range(length)])
        step *= 2
    return value


def local(strips, columns, send_list, send_count, shifts, prev_basis, mix):
    comps, vecs, rows = prev_basis.shape
    blocks = columns.shape[0]
    width = strips.shape[1]
    f32, bf16 = jnp.float32, jnp.bfloat16
    tile_out, lines_out = ((blocks, 256), f32), ((8, rows), f32)
    tile = call(start_kernel, [tile_out], [VMEM] * 4, 600000, 250000)(
        prev_basis, mix, send_list, send_count
    )
    high, low = call(
        prepare_kernel, [((width, rows), bf16), ((width, rows), bf16)], [VMEM], 1000000, 1000000
    )(strips)
    prev_gram = call(previous_gram_kernel, [((vecs, 128), f32)], [VMEM], 60000000, 250000)(prev_basis)
    step_specs = [VMEM] * 6 + [SMEM, VMEM, VMEM]
    tile, l0, choose = call(
        first_kernel,
        [tile_out, lines_out, ((4 * blocks, 128), f32)],
        step_specs,
        50000000,
        600000,
    )(tile, *ghosts(tile), columns, shifts, high, low)
    middle = []
    for step in (1, 2):
        tile, line = call(
            lambda *refs, step=step: middle_kernel(step, *refs),
            [tile_out, lines_out],
            step_specs,
            50000000,
            600000,
        )(tile, *ghosts(tile), choose, shifts, high, low)
        middle.append(line)
    l1, l2 = middle
    l3, gram = call(
        last_kernel,
        [lines_out, ((vecs + 8, 128), f32)],
        step_specs + [VMEM] * 5,
        80000000,
        900000,
    )(tile, *ghosts(tile), choose, shifts, high, low, l0, l1, l2, prev_basis, prev_gram)
    gram = summed(gram)
    total = float(lax.axis_size("dom") * rows)
    return call(
        lambda *refs: finish_kernel(total, *refs),
        [((comps, S, rows), f32), ((comps, vecs + S, S), f32)],
        [VMEM] * 6,
        50000000,
        400000,
    )(gram, prev_basis, l0, l1, l2, l3)


def solution(mesh):
    in_specs = (
        P("dom", None),
        P("dom", None),
        P("dom", None, None),
        P("dom", None),
        P(),
        P(None, None, "dom"),
        P(),
    )
    out_specs = (P(None, None, "dom"), P())
    return jax.shard_map(local, mesh=mesh, in_specs=in_specs, out_specs=out_specs, check_vma=False)
```

```python
import jax
import jax.numpy as jnp
from jax import lax
from jax.experimental import pallas as pl
from jax.experimental.pallas import tpu as pltpu
from jax.sharding import PartitionSpec as P

BLOCK = 64
S = 4
FAR = 8
DEAD = 1000.0
HIGHEST = lax.Precision.HIGHEST
NN = (((1,), (0,)), ((), ()))
NT = (((1,), (1,)), ((), ()))


def dot(a, b, dims=NN, precision=None):
    return lax.dot_general(a, b, dims, precision=precision, preferred_element_type=jnp.float32)


def iota(shape, axis):
    return lax.broadcasted_iota(jnp.int32, shape, axis)


def split(x):
    high = x.astype(jnp.bfloat16)
    return high, (x - high.astype(jnp.float32)).astype(jnp.bfloat16)


def own_lanes(blocks):
    shape = (blocks, blocks * BLOCK)
    return iota(shape, 1) // BLOCK == iota(shape, 0)


def fold(masked):
    total = masked[:, :128]
    for t in range(1, masked.shape[1] // 128):
        total = total + masked[:, t * 128 : (t + 1) * 128]
    return total + pltpu.roll(total, BLOCK, 1)


def doubled(tile, comp):
    part = tile[:, (comp // 2) * 128 : (comp // 2 + 1) * 128]
    turned = pltpu.roll(part, BLOCK, 1)
    low = iota(part.shape, 1) < BLOCK
    return jnp.where(low, part, turned) if comp % 2 == 0 else jnp.where(low, turned, part)


def joined(parts, tail):
    low = iota(parts[0].shape, 1) < BLOCK
    return jnp.concatenate([jnp.where(low, parts[0], parts[1]), jnp.where(low, parts[2], tail)], axis=1)


def start_kernel(prev_ref, mix_ref, list_ref, count_ref, out_ref):
    comps, vecs, rows = prev_ref.shape
    blocks = rows // BLOCK
    prev = prev_ref[...].reshape(comps * vecs, rows)
    mix = jnp.concatenate([mix_ref[...]] * comps, axis=1)
    mix = jnp.where(iota(mix.shape, 1) // vecs == iota(mix.shape, 0), mix, 0.0)
    start = dot(mix, prev, precision=HIGHEST)
    own = own_lanes(blocks)
    parts = [
        fold(jnp.where(own, jnp.broadcast_to(start[c : c + 1], own.shape), 0.0)) for c in range(comps)
    ]
    square = (blocks, blocks)
    tail = jnp.zeros((blocks, 128), jnp.float32)
    for link in range(4):
        order = jnp.broadcast_to(list_ref[0, link : link + 1, :], square)
        live = iota(square, 1) < jnp.broadcast_to(count_ref[0:1, link : link + 1], square)
        order = jnp.where(live, order.astype(jnp.float32), DEAD)
        column = jnp.sum(jnp.where(iota(square, 0) == iota(square, 1), order, 0.0), axis=1, keepdims=True)
        tail = jnp.where(iota(tail.shape, 1) == BLOCK + link, column, tail)
    out_ref[...] = joined(parts, tail)


def prepare_kernel(strips_ref, high_ref, low_ref):
    high, low = split(strips_ref[...].T)
    high_ref[...] = high
    low_ref[...] = low


def previous_gram_kernel(prev_ref, out_ref):
    comps, vecs, rows = prev_ref.shape
    prev = prev_ref[...].reshape(comps * vecs, rows)
    full = dot(prev, prev, NT, HIGHEST)
    owner = iota((vecs, comps * vecs), 1) // vecs
    total = jnp.where(owner == 0, full[:vecs], 0.0)
    for c in range(1, comps):
        total = total + jnp.where(owner == c, full[c * vecs : (c + 1) * vecs], 0.0)
    out_ref[...] = jnp.concatenate([total, jnp.zeros((vecs, 128 - comps * vecs), jnp.float32)], axis=1)


def selection(columns, pieces, place):
    blocks, count = columns.shape
    rows = [(iota((blocks, 128), 0) == iota((blocks, 128), 1)).astype(jnp.float32)]
    even, even_far = lax.rem(place, 2) == 0, lax.rem(place // FAR, 2) == 0
    slots = [
        (jnp.where(even, 2, 1), (pieces[2], pieces[1]), even),
        (jnp.where(even, 1, 2), (pieces[1], pieces[2]), even),
        (jnp.where(even_far, 4, 3), (pieces[4], pieces[3]), even_far),
        (jnp.where(even_far, 3, 4), (pieces[3], pieces[4]), even_far),
    ]
    for link, (slot, (when, other), test) in enumerate(slots):
        lane = 192 + link
        order = jnp.where(test, when[:, lane : lane + 1], other[:, lane : lane + 1])
        at = order.astype(jnp.int32) + slot * blocks
        rows.append((iota((blocks, 128), 1) == at).astype(jnp.float32))
    rows.append(jnp.zeros((128 - 5 * blocks, 128), jnp.float32))
    table = jnp.concatenate(rows, axis=0).astype(jnp.bfloat16)
    picks = [
        (iota((blocks, 128), 1) == columns[:, k : k + 1]).astype(jnp.float32) for k in range(count)
    ]
    return dot(jnp.concatenate(picks, axis=0).astype(jnp.bfloat16), table)


def multiply(choose, pieces, shift, high, low):
    blocks = pieces[0].shape[0]
    count = choose.shape[0] // blocks
    comps = 3
    ext = jnp.concatenate(pieces + [jnp.zeros((128 - 5 * blocks, 256), jnp.float32)], axis=0)
    picked = dot(choose.astype(jnp.bfloat16), jnp.concatenate(split(ext), axis=1))
    halves = []
    for half in range(2):
        for c in range(comps):
            lane = half * 256 + c * BLOCK
            halves.append(
                jnp.concatenate(
                    [picked[k * blocks : (k + 1) * blocks, lane : lane + BLOCK] for k in range(count)],
                    axis=1,
                )
            )
    left = jnp.concatenate(halves, axis=0).astype(jnp.bfloat16)
    both = dot(left, high) + dot(left, low)
    image = both[: comps * blocks] + both[comps * blocks :]
    own = own_lanes(blocks)
    parts, lines = [], []
    for c in range(comps):
        part = fold(jnp.where(own, image[c * blocks : (c + 1) * blocks], 0.0))
        part = part - shift * doubled(pieces[0], c)
        parts.append(part)
        wide = jnp.concatenate([part] * (blocks // 2), axis=1)
        lines.append(jnp.sum(jnp.where(own, wide, 0.0), axis=0, keepdims=True))
    return joined(parts, jnp.zeros_like(parts[0])), lines


def spread(lines, old):
    where = iota(old.shape, 0)
    for c, line in enumerate(lines):
        old = jnp.where(where == c, jnp.broadcast_to(line, old.shape), old)
    return old


def first_kernel(own, a, b, c, d, columns, shifts, high, low, tile_ref, lines_ref, choose_ref):
    pieces = [ref[...] for ref in (own, a, b, c, d)]
    choose = selection(columns[...], pieces, lax.axis_index("dom"))
    choose_ref[...] = choose
    tile, lines = multiply(choose, pieces, shifts[0], high[...], low[...])
    tile_ref[...] = tile
    lines_ref[...] = spread(lines, jnp.zeros(lines_ref.shape, jnp.float32))


def middle_kernel(step, own, a, b, c, d, choose, shifts, high, low, tile_ref, lines_ref):
    pieces = [ref[...] for ref in (own, a, b, c, d)]
    tile, lines = multiply(choose[...], pieces, shifts[step], high[...], low[...])
    tile_ref[...] = tile
    lines_ref[...] = spread(lines, jnp.zeros(lines_ref.shape, jnp.float32))


def last_kernel(
    own, a, b, c, d, choose, shifts, high, low, l0, l1, l2, prev_ref, prev_gram, lines_ref, gram_ref
):
    pieces = [ref[...] for ref in (own, a, b, c, d)]
    _, lines = multiply(choose[...], pieces, shifts[S - 1], high[...], low[...])
    comps, vecs, rows = prev_ref.shape
    last = spread(lines, jnp.zeros(lines_ref.shape, jnp.float32))
    lines_ref[...] = last
    basis = jnp.concatenate([l0[...], l1[...], l2[...], last], axis=0)
    prev = prev_ref[...].reshape(comps * vecs, rows)
    with_prev = dot(basis, prev, NT, HIGHEST)
    with_basis = dot(basis, basis, NT, HIGHEST)
    gram = jnp.concatenate([with_prev, with_basis], axis=1)
    lane = iota((8, 128), 1)
    comp = iota((8, 128), 0)
    mine = jnp.where(lane < comps * vecs, lane // vecs, lax.rem(lane, 8)) == comp
    result = jnp.zeros((8, 128), jnp.float32)
    for k in range(S):
        line = jnp.sum(jnp.where(mine, gram[k * 8 : (k + 1) * 8], 0.0), axis=0, keepdims=True)
        result = jnp.where(comp == k, jnp.broadcast_to(line, result.shape), result)
    gram_ref[...] = jnp.concatenate([prev_gram[...], result], axis=0)


def finish_kernel(total, gram_ref, prev_ref, l0, l1, l2, l3, basis_ref, factors_ref):
    comps, vecs, rows = prev_ref.shape
    width = comps * vecs
    gram = gram_ref[...] * (1.0 / total)
    small = gram[vecs:]
    lane, comp = iota((8, 128), 1), iota((8, 128), 0)
    in_prev = (lane < width) & (lane // vecs == comp)
    coef, cross = [], []
    for k in range(S):
        line = jnp.broadcast_to(small[k : k + 1], (8, 128))
        coef.append(jnp.where(in_prev, line, 0.0))
        cross.append([jnp.where(lane == width + 8 * l + comp, line, 0.0) for l in range(k + 1)])
    coefs = jnp.concatenate(coef, axis=0)
    prev = prev_ref[...].reshape(width, rows)
    basis = jnp.concatenate([l0[...], l1[...], l2[...], l3[...]], axis=0)
    projected = basis - dot(coefs[:, :width], prev, precision=HIGHEST)
    square = jnp.concatenate([gram[:vecs]] * comps, axis=0)
    r, q = iota(square.shape, 0), iota(square.shape, 1)
    square = jnp.where(r // vecs == q // vecs, square, 0.0) - jnp.where(r == q, 2.0, 0.0)
    turned = dot(coefs[:, :width], square, precision=HIGHEST)
    entry = {}
    for k in range(S):
        for l in range(k + 1):
            value = turned[k * 8 : (k + 1) * 8] * coef[l] + cross[k][l]
            entry[k, l] = jnp.sum(value, axis=1, keepdims=True)
    lower = {}
    for k in range(S):
        for l in range(k + 1):
            value = entry[k, l]
            for m in range(l):
                value = value - lower[k, m] * lower[l, m]
            lower[k, l] = jnp.sqrt(value) if l == k else value / lower[l, l]
    vectors = []
    for k in range(S):
        value = projected[k * 8 : (k + 1) * 8]
        for l in range(k):
            value = value - lower[k, l] * vectors[l]
        value = value / lower[k, k]
        vectors.append(value)
        for c in range(comps):
            basis_ref[c, k : k + 1, :] = value[c : c + 1]
    across = jnp.concatenate([small] * 16, axis=0).T
    for c in range(comps):
        factors_ref[c, :vecs, :] = across[c * vecs : (c + 1) * vecs, :S]
    for k in range(S):
        line = jnp.zeros((8, 128), jnp.float32)
        for l in range(k, S):
            line = jnp.where(lane == l, lower[l, k], line)
        for c in range(comps):
            factors_ref[c, vecs + k : vecs + k + 1, :] = line[c : c + 1, :S]


VMEM = pl.BlockSpec(memory_space=pltpu.VMEM)
SMEM = pl.BlockSpec(memory_space=pltpu.SMEM)


def call(kernel, outs, specs, flops, moved):
    shapes = [jax.ShapeDtypeStruct(shape, kind) for shape, kind in outs]
    return pl.pallas_call(
        kernel,
        out_shape=shapes if len(shapes) > 1 else shapes[0],
        in_specs=specs,
        out_specs=[VMEM] * len(shapes) if len(shapes) > 1 else VMEM,
        compiler_params=pltpu.CompilerParams(vmem_limit_bytes=24 * 1024 * 1024),
        cost_estimate=pl.CostEstimate(flops=flops, bytes_accessed=moved, transcendentals=0),
    )


def pairs_of(length, step, odd):
    firsts = [d for d in range(length - step) if (d // step) % 2 == odd]
    return [(d, d + step) for d in firsts] + [(d + step, d) for d in firsts]


def ghosts(tile):
    length = lax.axis_size("dom")
    return [
        lax.ppermute(tile, "dom", pairs_of(length, step, odd)) for step in (1, FAR) for odd in (0, 1)
    ]


def summed(value):
    return jnp.sum(lax.all_gather(value, "dom"), axis=0)


def local(strips, columns, send_list, send_count, shifts, prev_basis, mix):
    comps, vecs, rows = prev_basis.shape
    blocks = columns.shape[0]
    width = strips.shape[1]
    f32, bf16 = jnp.float32, jnp.bfloat16
    tile_out, lines_out = ((blocks, 256), f32), ((8, rows), f32)
    tile = call(start_kernel, [tile_out], [VMEM] * 4, 600000, 250000)(
        prev_basis, mix, send_list, send_count
    )
    high, low = call(
        prepare_kernel, [((width, rows), bf16), ((width, rows), bf16)], [VMEM], 1000000, 1000000
    )(strips)
    prev_gram = call(previous_gram_kernel, [((vecs, 128), f32)], [VMEM], 60000000, 250000)(prev_basis)
    step_specs = [VMEM] * 6 + [SMEM, VMEM, VMEM]
    tile, l0, choose = call(
        first_kernel,
        [tile_out, lines_out, ((4 * blocks, 128), f32)],
        step_specs,
        50000000,
        600000,
    )(tile, *ghosts(tile), columns, shifts, high, low)
    middle = []
    for step in (1, 2):
        tile, line = call(
            lambda *refs, step=step: middle_kernel(step, *refs),
            [tile_out, lines_out],
            step_specs,
            50000000,
            600000,
        )(tile, *ghosts(tile), choose, shifts, high, low)
        middle.append(line)
    l1, l2 = middle
    l3, gram = call(
        last_kernel,
        [lines_out, ((vecs + 8, 128), f32)],
        step_specs + [VMEM] * 5,
        80000000,
        900000,
    )(tile, *ghosts(tile), choose, shifts, high, low, l0, l1, l2, prev_basis, prev_gram)
    gram = summed(gram)
    total = float(lax.axis_size("dom") * rows)
    return call(
        lambda *refs: finish_kernel(total, *refs),
        [((comps, S, rows), f32), ((comps, vecs + S, S), f32)],
        [VMEM] * 6,
        50000000,
        400000,
    )(gram, prev_basis, l0, l1, l2, l3)


def solution(mesh):
    in_specs = (
        P("dom", None),
        P("dom", None),
        P("dom", None, None),
        P("dom", None),
        P(),
        P(None, None, "dom"),
        P(),
    )
    out_specs = (P(None, None, "dom"), P())
    return jax.shard_map(local, mesh=mesh, in_specs=in_specs, out_specs=out_specs, check_vma=False)
```

```python
import jax
import jax.numpy as jnp
from jax import lax
from jax.experimental import pallas as pl
from jax.experimental.pallas import tpu as pltpu
from jax.sharding import PartitionSpec as P

BLOCK = 64
S = 4
FAR = 8
COMPS = 3
DEAD = 1000.0
HIGHEST = lax.Precision.HIGHEST
NN = (((1,), (0,)), ((), ()))
NT = (((1,), (1,)), ((), ()))


def dot(a, b, dims=NN, precision=None):
    return lax.dot_general(a, b, dims, precision=precision, preferred_element_type=jnp.float32)


def iota(shape, axis):
    return lax.broadcasted_iota(jnp.int32, shape, axis)


def own_lanes(rows, width):
    return iota((rows, width), 1) // BLOCK == iota((rows, width), 0) % 8


def fold(masked):
    total = masked[:, :128]
    for t in range(1, masked.shape[1] // 128):
        total = total + masked[:, t * 128 : (t + 1) * 128]
    return total + pltpu.roll(total, BLOCK, 1)


def lines_of(tile, width):
    wide = jnp.concatenate([tile] * (width // 128), axis=1)
    wide = jnp.where(own_lanes(wide.shape[0], width), wide, 0.0)
    where = iota((8, width), 0)
    result = jnp.zeros((8, width), jnp.float32)
    for c in range(COMPS):
        line = jnp.sum(wide[c * 8 : (c + 1) * 8], axis=0, keepdims=True)
        result = jnp.where(where == c, jnp.broadcast_to(line, result.shape), result)
    return result


def fetch(pairs, sems):
    copies = [pltpu.make_async_copy(src, dst, sems.at[i]) for i, (src, dst) in enumerate(pairs)]
    for copy in copies:
        copy.start()
    return copies


def start_kernel(prev_in, mix_in, list_in, count_in, out_ref, prev_ref, mix_ref, list_ref, count_ref, sems):
    copies = fetch(
        [(prev_in, prev_ref), (mix_in, mix_ref), (list_in, list_ref), (count_in, count_ref)], sems
    )
    for copy in copies[1:]:
        copy.wait()
    comps, vecs, rows = prev_ref.shape
    mix = jnp.concatenate([mix_ref[...]] * comps, axis=1)
    mix = jnp.where(iota(mix.shape, 1) // vecs == iota(mix.shape, 0), mix, 0.0)
    order = list_ref[0].astype(jnp.float32)
    order = jnp.concatenate([order, jnp.zeros((4, 120), jnp.float32)], axis=1)
    meta = jnp.zeros((8, 128), jnp.float32)
    slot = iota((1, 128), 1)
    for link in range(4):
        live = slot < jnp.broadcast_to(count_ref[0:1, link : link + 1], slot.shape)
        line = jnp.where(live, order[link : link + 1], DEAD)
        line = pltpu.roll(jnp.broadcast_to(line, (8, 128)), 8 + 8 * link, 1)
        meta = jnp.where(iota((8, 128), 1) // 8 == link + 1, line, meta)
    out_ref[8 * comps :, :] = meta
    copies[0].wait()
    start = dot(mix, prev_ref[...].reshape(comps * vecs, rows), precision=HIGHEST)
    own = own_lanes(8, rows)
    for c in range(comps):
        line = jnp.broadcast_to(start[c : c + 1], own.shape)
        out_ref[c * 8 : (c + 1) * 8, :] = fold(jnp.where(own, line, 0.0))


def prepare_kernel(strips_in, columns_in, shifts_in, high_ref, low_ref, aux_ref, strips, columns, shifts, sems):
    parts = strips.shape[0]
    depth = strips.shape[1]
    pairs = [(columns_in, columns), (shifts_in, shifts)]
    pairs += [(strips_in.at[pl.ds(p * depth, depth)], strips.at[p]) for p in range(parts)]
    copies = fetch(pairs, sems)
    copies[0].wait()
    copies[1].wait()
    where = iota((8, 128), 1)
    table = jnp.zeros((8, 128), jnp.float32)
    eye = iota((8, 8), 0) == iota((8, 8), 1)
    for k in range(columns.shape[0]):
        line = jnp.broadcast_to(columns[k : k + 1, :].astype(jnp.float32), (8, 8))
        column = jnp.sum(jnp.where(eye, line, 0.0), axis=1, keepdims=True)
        table = jnp.where(where == k, column, table)
    for k in range(S):
        aux_ref[8 * k : 8 * k + 8, :] = jnp.full((8, 128), shifts[k], jnp.float32)
    aux_ref[8 * S :, :] = table
    for p in range(parts):
        copies[2 + p].wait()
        turned = strips[p].T
        high = turned.astype(jnp.bfloat16)
        high_ref[:, p * depth : (p + 1) * depth] = high
        low_ref[:, p * depth : (p + 1) * depth] = (turned - high.astype(jnp.float32)).astype(jnp.bfloat16)


def selection(table, metas, place):
    even, even_far = lax.rem(place, 2) == 0, lax.rem(place // FAR, 2) == 0
    slots = [
        (jnp.where(even, 48.0, 24.0), metas[1], metas[0], even),
        (jnp.where(even, 24.0, 48.0), metas[0], metas[1], even),
        (jnp.where(even_far, 96.0, 72.0), metas[3], metas[2], even_far),
        (jnp.where(even_far, 72.0, 96.0), metas[2], metas[3], even_far),
    ]
    lane = iota((1, 128), 1)
    target = lane.astype(jnp.float32)
    for link, (base, when, other, test) in enumerate(slots):
        target = jnp.where(lane // 8 == link + 1, jnp.where(test, when, other) + base, target)
    target = jnp.broadcast_to(target, (8, 128))
    lane = iota((8, 128), 1).astype(jnp.float32)
    at = [
        jnp.sum(jnp.where(lane == table[:, k : k + 1], target, 0.0), axis=1, keepdims=True)
        for k in range(4)
    ]
    lane = iota((8, 256), 1).astype(jnp.float32)
    groups = []
    for pair in range(2):
        for c in range(COMPS):
            first = lane == at[2 * pair] + float(8 * c)
            second = lane == at[2 * pair + 1] + float(8 * c + 120)
            groups.append((first | second).astype(jnp.float32))
    return jnp.concatenate(groups, axis=0)


def multiply(choose, pieces, shift, high, low):
    rows = 8 * COMPS
    ext = jnp.concatenate(pieces, axis=0)
    front = iota(ext.shape, 1) < BLOCK
    top = ext.astype(jnp.bfloat16).astype(jnp.float32)
    rest = ext - top
    zero = jnp.zeros_like(ext)
    picked = jnp.concatenate(
        [
            jnp.concatenate([jnp.where(front, top, zero), jnp.where(front, rest, zero)], axis=1),
            jnp.concatenate([jnp.where(front, zero, top), jnp.where(front, zero, rest)], axis=1),
            jnp.zeros((256 - 2 * ext.shape[0], 256), jnp.float32),
        ],
        axis=0,
    ).astype(jnp.bfloat16)
    x = dot(choose.astype(jnp.bfloat16), picked)
    left = jnp.concatenate(
        [
            jnp.concatenate([x[:rows, :128], x[rows:, :128]], axis=1),
            jnp.concatenate([x[:rows, 128:], x[rows:, 128:]], axis=1),
        ],
        axis=0,
    ).astype(jnp.bfloat16)
    both = dot(left, high) + dot(left, low)
    image = both[:rows] + both[rows:]
    image = fold(jnp.where(own_lanes(rows, image.shape[1]), image, 0.0))
    return image - jnp.concatenate([shift] * COMPS, axis=0) * pieces[0]


def first_kernel(own, a, b, c, d, aux, high, low, tile_ref, choose_ref):
    rows = 8 * COMPS
    refs = (own, a, b, c, d)
    pieces = [ref[:rows, :] for ref in refs]
    metas = [ref[rows : rows + 1, :] for ref in refs[1:]]
    choose = selection(aux[8 * S :, :], metas, lax.axis_index("dom"))
    choose_ref[...] = choose
    tile_ref[...] = multiply(choose, pieces, aux[:8, :], high[...], low[...])


def middle_kernel(step, own, a, b, c, d, choose, aux, high, low, tile_ref):
    pieces = [ref[...] for ref in (own, a, b, c, d)]
    tile_ref[...] = multiply(choose[...], pieces, aux[8 * step : 8 * step + 8, :], high[...], low[...])


def collect(gram, width, vecs):
    lane, comp = iota(gram.shape, 1), iota(gram.shape, 0)
    mine = jnp.where(lane < width, lane // vecs, lane % 8) == comp
    return jnp.sum(jnp.where(mine, gram, 0.0), axis=0, keepdims=True)


def early_kernel(prev_ref, t0, t1, t2, lines_ref, gram_ref):
    comps, vecs, rows = prev_ref.shape
    width = comps * vecs
    lines = jnp.concatenate([lines_of(t[...], rows) for t in (t0, t1, t2)], axis=0)
    lines_ref[...] = lines
    prev = prev_ref[...].reshape(width, rows)
    full = dot(prev, prev, NT, HIGHEST)
    owner = iota((vecs, width), 1) // vecs
    total = jnp.where(owner == 0, full[:vecs], 0.0)
    for c in range(1, comps):
        total = total + jnp.where(owner == c, full[c * vecs : (c + 1) * vecs], 0.0)
    gram_ref[:vecs, :] = jnp.concatenate([total, jnp.zeros((vecs, 128 - width), jnp.float32)], axis=1)
    against = jnp.concatenate([prev, lines, jnp.zeros((8, rows), jnp.float32)], axis=0)
    gram = dot(lines, against, NT, HIGHEST)
    result = jnp.zeros((8, 128), jnp.float32)
    for k in range(S - 1):
        line = collect(gram[k * 8 : (k + 1) * 8], width, vecs)
        result = jnp.where(iota((8, 128), 0) == k, jnp.broadcast_to(line, result.shape), result)
    gram_ref[vecs:, :] = result


def last_kernel(own, a, b, c, d, choose, aux, high, low, lines, prev_ref, early, line_ref, gram_ref):
    pieces = [ref[...] for ref in (own, a, b, c, d)]
    tile = multiply(choose[...], pieces, aux[8 * S - 8 : 8 * S, :], high[...], low[...])
    comps, vecs, rows = prev_ref.shape
    width = comps * vecs
    last = lines_of(tile, rows)
    line_ref[...] = last
    against = jnp.concatenate([prev_ref[...].reshape(width, rows), lines[...], last], axis=0)
    line = collect(dot(last, against, NT, HIGHEST), width, vecs)
    gram_ref[:vecs, :] = early[:vecs, :]
    gram_ref[vecs:, :] = jnp.where(
        iota((8, 128), 0) == S - 1, jnp.broadcast_to(line, (8, 128)), early[vecs:, :]
    )


def finish_kernel(total, mine_ref, other_ref, prev_ref, lines, last, basis_ref, factors_ref):
    comps, vecs, rows = prev_ref.shape
    width = comps * vecs
    odd = lax.rem(lax.axis_index("dom"), 2) == 1
    gram = jnp.where(odd, mine_ref[...], other_ref[...]) * (1.0 / total)
    small = gram[vecs:]
    lane, comp = iota((8, 128), 1), iota((8, 128), 0)
    in_prev = (lane < width) & (lane // vecs == comp)
    coef, cross = [], []
    for k in range(S):
        line = jnp.broadcast_to(small[k : k + 1], (8, 128))
        coef.append(jnp.where(in_prev, line, 0.0))
        cross.append([jnp.where(lane == width + 8 * l + comp, line, 0.0) for l in range(k + 1)])
    coefs = jnp.concatenate(coef, axis=0)
    prev = prev_ref[...].reshape(width, rows)
    basis = jnp.concatenate([lines[...], last[...]], axis=0)
    projected = basis - dot(coefs[:, :width], prev, precision=HIGHEST)
    square = jnp.concatenate([gram[:vecs]] * comps, axis=0)
    r, q = iota(square.shape, 0), iota(square.shape, 1)
    square = jnp.where(r // vecs == q // vecs, square, 0.0) - jnp.where(r == q, 2.0, 0.0)
    turned = dot(coefs[:, :width], square, precision=HIGHEST)
    entry = {}
    for k in range(S):
        for l in range(k + 1):
            value = turned[k * 8 : (k + 1) * 8] * coef[l] + cross[k][l]
            entry[k, l] = jnp.sum(value, axis=1, keepdims=True)
    lower = {}
    for k in range(S):
        for l in range(k + 1):
            value = entry[k, l]
            for m in range(l):
                value = value - lower[k, m] * lower[l, m]
            lower[k, l] = jnp.sqrt(value) if l == k else value / lower[l, l]
    vectors = []
    for k in range(S):
        value = projected[k * 8 : (k + 1) * 8]
        for l in range(k):
            value = value - lower[k, l] * vectors[l]
        value = value / lower[k, k]
        vectors.append(value)
        for c in range(comps):
            basis_ref[c, k : k + 1, :] = value[c : c + 1]
    for c in range(comps):
        factors_ref[c, :, :vecs] = small[:S, c * vecs : (c + 1) * vecs]
    for k in range(S):
        line = jnp.zeros((8, 128), jnp.float32)
        for l in range(k + 1):
            line = jnp.where(lane == l, lower[k, l], line)
        for c in range(comps):
            factors_ref[c, k : k + 1, vecs:] = line[c : c + 1, :S]


VMEM = pl.BlockSpec(memory_space=pltpu.VMEM)
HBM = pl.BlockSpec(memory_space=pltpu.HBM)


def in_hbm(*arrays):
    return [pltpu.with_memory_space_constraint(x, pltpu.HBM) for x in arrays]


def call(kernel, outs, specs, flops, moved, scratch=()):
    shapes = [jax.ShapeDtypeStruct(shape, kind) for shape, kind in outs]
    return pl.pallas_call(
        kernel,
        out_shape=shapes if len(shapes) > 1 else shapes[0],
        in_specs=specs,
        out_specs=[VMEM] * len(shapes) if len(shapes) > 1 else VMEM,
        scratch_shapes=list(scratch),
        compiler_params=pltpu.CompilerParams(vmem_limit_bytes=24 * 1024 * 1024),
        cost_estimate=pl.CostEstimate(flops=flops, bytes_accessed=moved, transcendentals=0),
    )


def pairs_of(length, step, odd):
    firsts = [d for d in range(length - step) if (d // step) % 2 == odd]
    return [(d, d + step) for d in firsts] + [(d + step, d) for d in firsts]


def ghosts(tile):
    length = lax.axis_size("dom")
    near = lax.ppermute(tile, "dom", pairs_of(length, 1, 0))
    far_odd = lax.ppermute(tile, "dom", pairs_of(length, FAR, 1))
    far_even = lax.ppermute(tile, "dom", pairs_of(length, FAR, 0))
    across = lax.ppermute(tile, "dom", pairs_of(length, 1, 1))
    return near, across, far_even, far_odd


def summed(value):
    length = lax.axis_size("dom")
    value = value + lax.ppermute(value, "dom", [(d, d ^ 1) for d in range(length)])
    step = 2
    while step < length:
        value = value + lax.ppermute(value, "dom", [(d, d ^ step) for d in range(1, length, 2)])
        step *= 2
    return value, lax.ppermute(value, "dom", [(d, d ^ 1) for d in range(length)])


def local(strips, columns, send_list, send_count, shifts, prev_basis, mix):
    comps, vecs, rows = prev_basis.shape
    blocks = columns.shape[0]
    width = strips.shape[1]
    f32, bf16, dma = jnp.float32, jnp.bfloat16, pltpu.SemaphoreType.DMA
    tile_out = ((comps * blocks, 128), f32)
    tile = call(
        start_kernel,
        [((comps * blocks + 8, 128), f32)],
        [HBM] * 4,
        600000,
        250000,
        [
            pltpu.VMEM(prev_basis.shape, f32),
            pltpu.VMEM(mix.shape, f32),
            pltpu.VMEM(send_list.shape, jnp.int32),
            pltpu.VMEM(send_count.shape, jnp.int32),
            dma((4,)),
        ],
    )(*in_hbm(prev_basis, mix, send_list, send_count))
    high, low, aux = call(
        prepare_kernel,
        [((width, rows), bf16), ((width, rows), bf16), ((8 * S + 8, 128), f32)],
        [HBM] * 3,
        1000000,
        1000000,
        [
            pltpu.VMEM((4, rows // 4, width), f32),
            pltpu.VMEM(columns.shape[::-1], jnp.int32),
            pltpu.SMEM(shifts.shape, f32),
            dma((6,)),
        ],
    )(*in_hbm(strips, columns.T, shifts))
    tiles = []
    tile, choose = call(
        first_kernel, [tile_out, ((2 * comps * blocks, 256), f32)], [VMEM] * 8, 50000000, 600000
    )(tile, *ghosts(tile), aux, high, low)
    tiles.append(tile)
    for step in (1, 2):
        tile = call(
            lambda *refs, step=step: middle_kernel(step, *refs), [tile_out], [VMEM] * 9, 50000000, 600000
        )(tile, *ghosts(tile), choose, aux, high, low)
        tiles.append(tile)
    received = ghosts(tile)
    gram_out = ((vecs + 8, 128), f32)
    lines, early = call(
        early_kernel, [((8 * S - 8, rows), f32), gram_out], [VMEM] * 4, 60000000, 250000
    )(prev_basis, *tiles)
    last, gram = call(
        last_kernel, [((8, rows), f32), gram_out], [VMEM] * 12, 80000000, 900000
    )(tile, *received, choose, aux, high, low, lines, prev_basis, early)
    total = float(lax.axis_size("dom") * rows)
    basis, factors = call(
        lambda *refs: finish_kernel(total, *refs),
        [((comps, S, rows), f32), ((comps, S, vecs + S), f32)],
        [VMEM] * 5,
        50000000,
        400000,
    )(*summed(gram), prev_basis, lines, last)
    return basis, jnp.swapaxes(factors, 1, 2)


def solution(mesh):
    in_specs = (
        P("dom", None),
        P("dom", None),
        P("dom", None, None),
        P("dom", None),
        P(),
        P(None, None, "dom"),
        P(),
    )
    out_specs = (P(None, None, "dom"), P())
    return jax.shard_map(local, mesh=mesh, in_specs=in_specs, out_specs=out_specs, check_vma=False)
```

```python
import jax
import jax.numpy as jnp
from jax import lax
from jax.experimental import pallas as pl
from jax.experimental.pallas import tpu as pltpu
from jax.sharding import PartitionSpec as P

BLOCK = 64
S = 4
FAR = 8
COMPS = 3
DEAD = 1000.0
HIGHEST = lax.Precision.HIGHEST
NN = (((1,), (0,)), ((), ()))
NT = (((1,), (1,)), ((), ()))


def dot(a, b, dims=NN, precision=None):
    return lax.dot_general(a, b, dims, precision=precision, preferred_element_type=jnp.float32)


def iota(shape, axis):
    return lax.broadcasted_iota(jnp.int32, shape, axis)


def own_lanes(rows, width):
    return iota((rows, width), 1) // BLOCK == iota((rows, width), 0) % 8


def fold(masked):
    total = masked[:, :128]
    for t in range(1, masked.shape[1] // 128):
        total = total + masked[:, t * 128 : (t + 1) * 128]
    return total + pltpu.roll(total, BLOCK, 1)


def lines_of(tile, width):
    wide = jnp.concatenate([tile] * (width // 128), axis=1)
    wide = jnp.where(own_lanes(wide.shape[0], width), wide, 0.0)
    where = iota((8, width), 0)
    result = jnp.zeros((8, width), jnp.float32)
    for c in range(COMPS):
        line = jnp.sum(wide[c * 8 : (c + 1) * 8], axis=0, keepdims=True)
        result = jnp.where(where == c, jnp.broadcast_to(line, result.shape), result)
    return result


def fetch(pairs, sems):
    copies = [pltpu.make_async_copy(src, dst, sems.at[i]) for i, (src, dst) in enumerate(pairs)]
    for copy in copies:
        copy.start()
    return copies


def start_kernel(prev_in, mix_in, list_in, count_in, out_ref, prev_ref, mix_ref, list_ref, count_ref, sems):
    copies = fetch(
        [(prev_in, prev_ref), (mix_in, mix_ref), (list_in, list_ref), (count_in, count_ref)], sems
    )
    for copy in copies[1:]:
        copy.wait()
    comps, vecs, rows = prev_ref.shape
    mix = jnp.concatenate([mix_ref[...]] * comps, axis=1)
    mix = jnp.where(iota(mix.shape, 1) // vecs == iota(mix.shape, 0), mix, 0.0)
    order = list_ref[0].astype(jnp.float32)
    order = jnp.concatenate([order, jnp.zeros((4, 120), jnp.float32)], axis=1)
    meta = jnp.zeros((8, 128), jnp.float32)
    slot = iota((1, 128), 1)
    for link in range(4):
        live = slot < jnp.broadcast_to(count_ref[0:1, link : link + 1], slot.shape)
        line = jnp.where(live, order[link : link + 1], DEAD)
        line = pltpu.roll(jnp.broadcast_to(line, (8, 128)), 8 + 8 * link, 1)
        meta = jnp.where(iota((8, 128), 1) // 8 == link + 1, line, meta)
    out_ref[8 * comps :, :] = meta
    copies[0].wait()
    start = dot(mix, prev_ref[...].reshape(comps * vecs, rows), precision=HIGHEST)
    own = own_lanes(8, rows)
    for c in range(comps):
        line = jnp.broadcast_to(start[c : c + 1], own.shape)
        out_ref[c * 8 : (c + 1) * 8, :] = fold(jnp.where(own, line, 0.0))


def prepare_kernel(strips_in, columns_in, shifts_in, high_ref, low_ref, aux_ref, strips, columns, shifts, sems):
    parts = strips.shape[0]
    depth = strips.shape[1]
    pairs = [(columns_in, columns), (shifts_in, shifts)]
    pairs += [(strips_in.at[pl.ds(p * depth, depth)], strips.at[p]) for p in range(parts)]
    copies = fetch(pairs, sems)
    copies[0].wait()
    copies[1].wait()
    where = iota((8, 128), 1)
    table = jnp.zeros((8, 128), jnp.float32)
    eye = iota((8, 8), 0) == iota((8, 8), 1)
    for k in range(columns.shape[0]):
        line = jnp.broadcast_to(columns[k : k + 1, :].astype(jnp.float32), (8, 8))
        column = jnp.sum(jnp.where(eye, line, 0.0), axis=1, keepdims=True)
        table = jnp.where(where == k, column, table)
    for k in range(S):
        aux_ref[8 * k : 8 * k + 8, :] = jnp.full((8, 128), shifts[k], jnp.float32)
    aux_ref[8 * S :, :] = table
    for p in range(parts):
        copies[2 + p].wait()
        turned = strips[p].T
        high = turned.astype(jnp.bfloat16)
        high_ref[:, p * depth : (p + 1) * depth] = high
        low_ref[:, p * depth : (p + 1) * depth] = (turned - high.astype(jnp.float32)).astype(jnp.bfloat16)


def selection(table, metas, place, length):
    even, even_far = lax.rem(place, 2) == 0, lax.rem(place // FAR, 2) == 0
    near, far_odd, far_even, across = metas
    slots = [
        (place >= 1, jnp.where(even, 96.0, 24.0), jnp.where(even, across, near)),
        (place < length - 1, jnp.where(even, 24.0, 96.0), jnp.where(even, near, across)),
        (place >= FAR, jnp.where(even_far, 48.0, 72.0), jnp.where(even_far, far_odd, far_even)),
        (place < length - FAR, jnp.where(even_far, 72.0, 48.0), jnp.where(even_far, far_even, far_odd)),
    ]
    lane = iota((1, 128), 1)
    target = lane.astype(jnp.float32)
    for link, (valid, base, order) in enumerate(slots):
        order = order + jnp.where(valid, base, DEAD)
        target = jnp.where(lane // 8 == link + 1, order, target)
    target = jnp.broadcast_to(target, (8, 128))
    lane = iota((8, 128), 1).astype(jnp.float32)
    at = [
        jnp.sum(jnp.where(lane == table[:, k : k + 1], target, 0.0), axis=1, keepdims=True)
        for k in range(4)
    ]
    lane = iota((8, 256), 1).astype(jnp.float32)
    groups = []
    for pair in range(2):
        for c in range(COMPS):
            first = lane == at[2 * pair] + float(8 * c)
            second = lane == at[2 * pair + 1] + float(8 * c + 120)
            groups.append((first | second).astype(jnp.float32))
    return jnp.concatenate(groups, axis=0)


def multiply(choose, pieces, shift, high, low):
    rows = 8 * COMPS
    ext = jnp.concatenate(pieces, axis=0)
    front = iota(ext.shape, 1) < BLOCK
    top = ext.astype(jnp.bfloat16).astype(jnp.float32)
    rest = ext - top
    zero = jnp.zeros_like(ext)
    picked = jnp.concatenate(
        [
            jnp.concatenate([jnp.where(front, top, zero), jnp.where(front, rest, zero)], axis=1),
            jnp.concatenate([jnp.where(front, zero, top), jnp.where(front, zero, rest)], axis=1),
            jnp.zeros((256 - 2 * ext.shape[0], 256), jnp.float32),
        ],
        axis=0,
    ).astype(jnp.bfloat16)
    x = dot(choose.astype(jnp.bfloat16), picked)
    left = jnp.concatenate(
        [
            jnp.concatenate([x[:rows, :128], x[rows:, :128]], axis=1),
            jnp.concatenate([x[:rows, 128:], x[rows:, 128:]], axis=1),
        ],
        axis=0,
    ).astype(jnp.bfloat16)
    both = dot(left, high) + dot(left, low)
    image = both[:rows] + both[rows:]
    image = fold(jnp.where(own_lanes(rows, image.shape[1]), image, 0.0))
    return image - jnp.concatenate([shift] * COMPS, axis=0) * pieces[0]


def first_kernel(length, own, a, b, c, d, aux, high, low, tile_ref, choose_ref):
    rows = 8 * COMPS
    refs = (own, a, b, c, d)
    pieces = [ref[:rows, :] for ref in refs]
    metas = [ref[rows : rows + 1, :] for ref in refs[1:]]
    choose = selection(aux[8 * S :, :], metas, lax.axis_index("dom"), length)
    choose_ref[...] = choose
    tile_ref[...] = multiply(choose, pieces, aux[:8, :], high[...], low[...])


def middle_kernel(step, own, a, b, c, d, choose, aux, high, low, tile_ref):
    pieces = [ref[...] for ref in (own, a, b, c, d)]
    tile_ref[...] = multiply(choose[...], pieces, aux[8 * step : 8 * step + 8, :], high[...], low[...])


def collect(gram, width, vecs):
    lane, comp = iota(gram.shape, 1), iota(gram.shape, 0)
    mine = jnp.where(lane < width, lane // vecs, lane % 8) == comp
    return jnp.sum(jnp.where(mine, gram, 0.0), axis=0, keepdims=True)


def early_kernel(prev_ref, t0, t1, t2, lines_ref, gram_ref):
    comps, vecs, rows = prev_ref.shape
    width = comps * vecs
    lines = jnp.concatenate([lines_of(t[...], rows) for t in (t0, t1, t2)], axis=0)
    lines_ref[...] = lines
    prev = prev_ref[...].reshape(width, rows)
    full = dot(prev, prev, NT, HIGHEST)
    owner = iota((vecs, width), 1) // vecs
    total = jnp.where(owner == 0, full[:vecs], 0.0)
    for c in range(1, comps):
        total = total + jnp.where(owner == c, full[c * vecs : (c + 1) * vecs], 0.0)
    gram_ref[:vecs, :] = jnp.concatenate([total, jnp.zeros((vecs, 128 - width), jnp.float32)], axis=1)
    against = jnp.concatenate([prev, lines, jnp.zeros((8, rows), jnp.float32)], axis=0)
    gram = dot(lines, against, NT, HIGHEST)
    result = jnp.zeros((8, 128), jnp.float32)
    for k in range(S - 1):
        line = collect(gram[k * 8 : (k + 1) * 8], width, vecs)
        result = jnp.where(iota((8, 128), 0) == k, jnp.broadcast_to(line, result.shape), result)
    gram_ref[vecs:, :] = result


def last_kernel(own, a, b, c, d, choose, aux, high, low, lines, prev_ref, early, line_ref, gram_ref):
    pieces = [ref[...] for ref in (own, a, b, c, d)]
    tile = multiply(choose[...], pieces, aux[8 * S - 8 : 8 * S, :], high[...], low[...])
    comps, vecs, rows = prev_ref.shape
    width = comps * vecs
    last = lines_of(tile, rows)
    line_ref[...] = last
    against = jnp.concatenate([prev_ref[...].reshape(width, rows), lines[...], last], axis=0)
    line = collect(dot(last, against, NT, HIGHEST), width, vecs)
    gram_ref[:vecs, :] = early[:vecs, :]
    gram_ref[vecs:, :] = jnp.where(
        iota((8, 128), 0) == S - 1, jnp.broadcast_to(line, (8, 128)), early[vecs:, :]
    )


def finish_kernel(total, mine_ref, other_ref, prev_ref, lines, last, basis_ref, factors_ref):
    comps, vecs, rows = prev_ref.shape
    width = comps * vecs
    odd = lax.rem(lax.axis_index("dom"), 2) == 1
    gram = jnp.where(odd, mine_ref[...], other_ref[...]) * (1.0 / total)
    small = gram[vecs:]
    lane, comp = iota((8, 128), 1), iota((8, 128), 0)
    in_prev = (lane < width) & (lane // vecs == comp)
    coef, cross = [], []
    for k in range(S):
        line = jnp.broadcast_to(small[k : k + 1], (8, 128))
        coef.append(jnp.where(in_prev, line, 0.0))
        cross.append([jnp.where(lane == width + 8 * l + comp, line, 0.0) for l in range(k + 1)])
    coefs = jnp.concatenate(coef, axis=0)
    prev = prev_ref[...].reshape(width, rows)
    basis = jnp.concatenate([lines[...], last[...]], axis=0)
    projected = basis - dot(coefs[:, :width], prev, precision=HIGHEST)
    square = jnp.concatenate([gram[:vecs]] * comps, axis=0)
    r, q = iota(square.shape, 0), iota(square.shape, 1)
    square = jnp.where(r // vecs == q // vecs, square, 0.0) - jnp.where(r == q, 2.0, 0.0)
    turned = dot(coefs[:, :width], square, precision=HIGHEST)
    entry = {}
    for k in range(S):
        for l in range(k + 1):
            value = turned[k * 8 : (k + 1) * 8] * coef[l] + cross[k][l]
            entry[k, l] = jnp.sum(value, axis=1, keepdims=True)
    lower = {}
    for k in range(S):
        for l in range(k + 1):
            value = entry[k, l]
            for m in range(l):
                value = value - lower[k, m] * lower[l, m]
            lower[k, l] = jnp.sqrt(value) if l == k else value / lower[l, l]
    vectors = []
    for k in range(S):
        value = projected[k * 8 : (k + 1) * 8]
        for l in range(k):
            value = value - lower[k, l] * vectors[l]
        value = value / lower[k, k]
        vectors.append(value)
        for c in range(comps):
            basis_ref[c, k : k + 1, :] = value[c : c + 1]
    for c in range(comps):
        factors_ref[c, :, :vecs] = small[:S, c * vecs : (c + 1) * vecs]
    for k in range(S):
        line = jnp.zeros((8, 128), jnp.float32)
        for l in range(k + 1):
            line = jnp.where(lane == l, lower[k, l], line)
        for c in range(comps):
            factors_ref[c, k : k + 1, vecs:] = line[c : c + 1, :S]


VMEM = pl.BlockSpec(memory_space=pltpu.VMEM)
HBM = pl.BlockSpec(memory_space=pltpu.HBM)


def in_hbm(*arrays):
    return [pltpu.with_memory_space_constraint(x, pltpu.HBM) for x in arrays]


def call(kernel, outs, specs, flops, moved, scratch=()):
    shapes = [jax.ShapeDtypeStruct(shape, kind) for shape, kind in outs]
    return pl.pallas_call(
        kernel,
        out_shape=shapes if len(shapes) > 1 else shapes[0],
        in_specs=specs,
        out_specs=[VMEM] * len(shapes) if len(shapes) > 1 else VMEM,
        scratch_shapes=list(scratch),
        compiler_params=pltpu.CompilerParams(vmem_limit_bytes=24 * 1024 * 1024),
        cost_estimate=pl.CostEstimate(flops=flops, bytes_accessed=moved, transcendentals=0),
    )


def swap(value, partner):
    return lax.ppermute(value, "dom", [(d, partner(d)) for d in range(lax.axis_size("dom"))])


def linked(step, odd):
    length = lax.axis_size("dom")

    def partner(d):
        other = d + step if (d // step) % 2 == odd else d - step
        return other if 0 <= other < length else d

    return partner


def ghosts(tile):
    return [swap(tile, linked(step, odd)) for step, odd in ((1, 0), (FAR, 1), (FAR, 0), (1, 1))]


def summed(value):
    value = value + swap(value, lambda d: d ^ 1)
    step = 2
    while step < lax.axis_size("dom"):
        value = value + swap(value, lambda d: d ^ step if d % 2 else d)
        step *= 2
    return value, swap(value, lambda d: d ^ 1)


def local(strips, columns, send_list, send_count, shifts, prev_basis, mix):
    comps, vecs, rows = prev_basis.shape
    blocks = columns.shape[0]
    width = strips.shape[1]
    f32, bf16, dma = jnp.float32, jnp.bfloat16, pltpu.SemaphoreType.DMA
    tile_out = ((comps * blocks, 128), f32)
    tile = call(
        start_kernel,
        [((comps * blocks + 8, 128), f32)],
        [HBM] * 4,
        600000,
        250000,
        [
            pltpu.VMEM(prev_basis.shape, f32),
            pltpu.VMEM(mix.shape, f32),
            pltpu.VMEM(send_list.shape, jnp.int32),
            pltpu.VMEM(send_count.shape, jnp.int32),
            dma((4,)),
        ],
    )(*in_hbm(prev_basis, mix, send_list, send_count))
    high, low, aux = call(
        prepare_kernel,
        [((width, rows), bf16), ((width, rows), bf16), ((8 * S + 8, 128), f32)],
        [HBM] * 3,
        1000000,
        1000000,
        [
            pltpu.VMEM((4, rows // 4, width), f32),
            pltpu.VMEM(columns.shape[::-1], jnp.int32),
            pltpu.SMEM(shifts.shape, f32),
            dma((6,)),
        ],
    )(*in_hbm(strips, columns.T, shifts))
    tiles = []
    length = lax.axis_size("dom")
    tile, choose = call(
        lambda *refs: first_kernel(length, *refs),
        [tile_out, ((2 * comps * blocks, 256), f32)],
        [VMEM] * 8,
        50000000,
        600000,
    )(tile, *ghosts(tile), aux, high, low)
    tiles.append(tile)
    for step in (1, 2):
        tile = call(
            lambda *refs, step=step: middle_kernel(step, *refs), [tile_out], [VMEM] * 9, 50000000, 600000
        )(tile, *ghosts(tile), choose, aux, high, low)
        tiles.append(tile)
    received = ghosts(tile)
    gram_out = ((vecs + 8, 128), f32)
    lines, early = call(
        early_kernel, [((8 * S - 8, rows), f32), gram_out], [VMEM] * 4, 60000000, 250000
    )(prev_basis, *tiles)
    last, gram = call(
        last_kernel, [((8, rows), f32), gram_out], [VMEM] * 12, 80000000, 900000
    )(tile, *received, choose, aux, high, low, lines, prev_basis, early)
    total = float(length * rows)
    basis, factors = call(
        lambda *refs: finish_kernel(total, *refs),
        [((comps, S, rows), f32), ((comps, S, vecs + S), f32)],
        [VMEM] * 5,
        50000000,
        400000,
    )(*summed(gram), prev_basis, lines, last)
    return basis, jnp.swapaxes(factors, 1, 2)


def solution(mesh):
    in_specs = (
        P("dom", None),
        P("dom", None),
        P("dom", None, None),
        P("dom", None),
        P(),
        P(None, None, "dom"),
        P(),
    )
    out_specs = (P(None, None, "dom"), P())
    return jax.shard_map(local, mesh=mesh, in_specs=in_specs, out_specs=out_specs, check_vma=False)
```

```python
import jax
import jax.numpy as jnp
from jax import lax
from jax.experimental import pallas as pl
from jax.experimental.pallas import tpu as pltpu
from jax.sharding import PartitionSpec as P

BLOCK = 64
S = 4
FAR = 8
COMPS = 3
DEAD = 1000.0
HIGHEST = lax.Precision.HIGHEST
NN = (((1,), (0,)), ((), ()))
NT = (((1,), (1,)), ((), ()))


def dot(a, b, dims=NN, precision=None):
    return lax.dot_general(a, b, dims, precision=precision, preferred_element_type=jnp.float32)


def iota(shape, axis):
    return lax.broadcasted_iota(jnp.int32, shape, axis)


def own_lanes(rows, width):
    return iota((rows, width), 1) // BLOCK == iota((rows, width), 0) % 8


def fold(masked):
    total = masked[:, :128]
    for t in range(1, masked.shape[1] // 128):
        total = total + masked[:, t * 128 : (t + 1) * 128]
    return total + pltpu.roll(total, BLOCK, 1)


def lines_of(tile, width):
    wide = jnp.concatenate([tile] * (width // 128), axis=1)
    wide = jnp.where(own_lanes(wide.shape[0], width), wide, 0.0)
    where = iota((8, width), 0)
    result = jnp.zeros((8, width), jnp.float32)
    for c in range(COMPS):
        line = jnp.sum(wide[c * 8 : (c + 1) * 8], axis=0, keepdims=True)
        result = jnp.where(where == c, jnp.broadcast_to(line, result.shape), result)
    return result


def fetch(pairs, sems):
    copies = [pltpu.make_async_copy(src, dst, sems.at[i]) for i, (src, dst) in enumerate(pairs)]
    for copy in copies:
        copy.start()
    return copies


def start_kernel(prev_in, mix_in, list_in, count_in, out_ref, prev_ref, mix_ref, list_ref, count_ref, sems):
    copies = fetch(
        [(prev_in, prev_ref), (mix_in, mix_ref), (list_in, list_ref), (count_in, count_ref)], sems
    )
    for copy in copies[1:]:
        copy.wait()
    comps, vecs, rows = prev_ref.shape
    mix = jnp.concatenate([mix_ref[...]] * comps, axis=1)
    mix = jnp.where(iota(mix.shape, 1) // vecs == iota(mix.shape, 0), mix, 0.0)
    order = list_ref[0].astype(jnp.float32)
    order = jnp.concatenate([order, jnp.zeros((4, 120), jnp.float32)], axis=1)
    meta = jnp.zeros((8, 128), jnp.float32)
    slot = iota((1, 128), 1)
    for link in range(4):
        live = slot < jnp.broadcast_to(count_ref[0:1, link : link + 1], slot.shape)
        line = jnp.where(live, order[link : link + 1], DEAD)
        line = pltpu.roll(jnp.broadcast_to(line, (8, 128)), 8 + 8 * link, 1)
        meta = jnp.where(iota((8, 128), 1) // 8 == link + 1, line, meta)
    out_ref[8 * comps :, :] = meta
    copies[0].wait()
    start = dot(mix, prev_ref[...].reshape(comps * vecs, rows), precision=HIGHEST)
    own = own_lanes(8, rows)
    for c in range(comps):
        line = jnp.broadcast_to(start[c : c + 1], own.shape)
        out_ref[c * 8 : (c + 1) * 8, :] = fold(jnp.where(own, line, 0.0))


def prepare_kernel(strips_in, columns_in, shifts_in, high_ref, low_ref, aux_ref, strips, columns, shifts, sems):
    parts = strips.shape[0]
    depth = strips.shape[1]
    pairs = [(columns_in, columns), (shifts_in, shifts)]
    pairs += [(strips_in.at[pl.ds(p * depth, depth)], strips.at[p]) for p in range(parts)]
    copies = fetch(pairs, sems)
    copies[0].wait()
    copies[1].wait()
    where = iota((8, 128), 1)
    table = jnp.zeros((8, 128), jnp.float32)
    eye = iota((8, 8), 0) == iota((8, 8), 1)
    for k in range(columns.shape[0]):
        line = jnp.broadcast_to(columns[k : k + 1, :].astype(jnp.float32), (8, 8))
        column = jnp.sum(jnp.where(eye, line, 0.0), axis=1, keepdims=True)
        table = jnp.where(where == k, column, table)
    for k in range(S):
        aux_ref[8 * k : 8 * k + 8, :] = jnp.full((8, 128), shifts[k], jnp.float32)
    aux_ref[8 * S :, :] = table
    for p in range(parts):
        copies[2 + p].wait()
        turned = strips[p].T
        high = turned.astype(jnp.bfloat16)
        high_ref[:, p * depth : (p + 1) * depth] = high
        low_ref[:, p * depth : (p + 1) * depth] = (turned - high.astype(jnp.float32)).astype(jnp.bfloat16)


def selection(table, metas, place, length):
    even, even_far = lax.rem(place, 2) == 0, lax.rem(place // FAR, 2) == 0
    near, far_odd, far_even, across = metas
    moved = (place == 1) | (place == length - 2)
    across = jnp.where(moved, far_odd, across)
    circle = jnp.where(moved, 48.0, 96.0)
    slots = [
        (place >= 1, jnp.where(even, circle, 24.0), jnp.where(even, across, near)),
        (place < length - 1, jnp.where(even, 24.0, circle), jnp.where(even, near, across)),
        (place >= FAR, jnp.where(even_far, 48.0, 72.0), jnp.where(even_far, far_odd, far_even)),
        (place < length - FAR, jnp.where(even_far, 72.0, 48.0), jnp.where(even_far, far_even, far_odd)),
    ]
    lane = iota((1, 128), 1)
    target = lane.astype(jnp.float32)
    for link, (valid, base, order) in enumerate(slots):
        order = order + jnp.where(valid, base, DEAD)
        target = jnp.where(lane // 8 == link + 1, order, target)
    target = jnp.broadcast_to(target, (8, 128))
    lane = iota((8, 128), 1).astype(jnp.float32)
    at = [
        jnp.sum(jnp.where(lane == table[:, k : k + 1], target, 0.0), axis=1, keepdims=True)
        for k in range(4)
    ]
    lane = iota((8, 256), 1).astype(jnp.float32)
    groups = []
    for pair in range(2):
        for c in range(COMPS):
            first = lane == at[2 * pair] + float(8 * c)
            second = lane == at[2 * pair + 1] + float(8 * c + 120)
            groups.append((first | second).astype(jnp.float32))
    return jnp.concatenate(groups, axis=0)


def multiply(choose, pieces, shift, high, low):
    rows = 8 * COMPS
    ext = jnp.concatenate(pieces, axis=0)
    front = iota(ext.shape, 1) < BLOCK
    top = ext.astype(jnp.bfloat16).astype(jnp.float32)
    rest = ext - top
    zero = jnp.zeros_like(ext)
    picked = jnp.concatenate(
        [
            jnp.concatenate([jnp.where(front, top, zero), jnp.where(front, rest, zero)], axis=1),
            jnp.concatenate([jnp.where(front, zero, top), jnp.where(front, zero, rest)], axis=1),
            jnp.zeros((256 - 2 * ext.shape[0], 256), jnp.float32),
        ],
        axis=0,
    ).astype(jnp.bfloat16)
    x = dot(choose.astype(jnp.bfloat16), picked)
    left = jnp.concatenate(
        [
            jnp.concatenate([x[:rows, :128], x[rows:, :128]], axis=1),
            jnp.concatenate([x[:rows, 128:], x[rows:, 128:]], axis=1),
        ],
        axis=0,
    ).astype(jnp.bfloat16)
    both = dot(left, high) + dot(left, low)
    image = both[:rows] + both[rows:]
    image = fold(jnp.where(own_lanes(rows, image.shape[1]), image, 0.0))
    return image - jnp.concatenate([shift] * COMPS, axis=0) * pieces[0]


def first_kernel(length, own, a, b, c, d, aux, high, low, tile_ref, choose_ref):
    rows = 8 * COMPS
    refs = (own, a, b, c, d)
    pieces = [ref[:rows, :] for ref in refs]
    metas = [ref[rows : rows + 1, :] for ref in refs[1:]]
    choose = selection(aux[8 * S :, :], metas, lax.axis_index("dom"), length)
    choose_ref[...] = choose
    tile_ref[...] = multiply(choose, pieces, aux[:8, :], high[...], low[...])


def middle_kernel(step, own, a, b, c, d, choose, aux, high, low, tile_ref):
    pieces = [ref[...] for ref in (own, a, b, c, d)]
    tile_ref[...] = multiply(choose[...], pieces, aux[8 * step : 8 * step + 8, :], high[...], low[...])


def collect(gram, width, vecs):
    lane, comp = iota(gram.shape, 1), iota(gram.shape, 0)
    mine = jnp.where(lane < width, lane // vecs, lane % 8) == comp
    return jnp.sum(jnp.where(mine, gram, 0.0), axis=0, keepdims=True)


def early_kernel(prev_ref, t0, t1, t2, lines_ref, gram_ref):
    comps, vecs, rows = prev_ref.shape
    width = comps * vecs
    lines = jnp.concatenate([lines_of(t[...], rows) for t in (t0, t1, t2)], axis=0)
    lines_ref[...] = lines
    prev = prev_ref[...].reshape(width, rows)
    full = dot(prev, prev, NT, HIGHEST)
    owner = iota((vecs, width), 1) // vecs
    total = jnp.where(owner == 0, full[:vecs], 0.0)
    for c in range(1, comps):
        total = total + jnp.where(owner == c, full[c * vecs : (c + 1) * vecs], 0.0)
    gram_ref[:vecs, :] = jnp.concatenate([total, jnp.zeros((vecs, 128 - width), jnp.float32)], axis=1)
    against = jnp.concatenate([prev, lines, jnp.zeros((8, rows), jnp.float32)], axis=0)
    gram = dot(lines, against, NT, HIGHEST)
    result = jnp.zeros((8, 128), jnp.float32)
    for k in range(S - 1):
        line = collect(gram[k * 8 : (k + 1) * 8], width, vecs)
        result = jnp.where(iota((8, 128), 0) == k, jnp.broadcast_to(line, result.shape), result)
    gram_ref[vecs:, :] = result


def last_kernel(own, a, b, c, d, choose, aux, high, low, lines, prev_ref, early, line_ref, gram_ref):
    pieces = [ref[...] for ref in (own, a, b, c, d)]
    tile = multiply(choose[...], pieces, aux[8 * S - 8 : 8 * S, :], high[...], low[...])
    comps, vecs, rows = prev_ref.shape
    width = comps * vecs
    last = lines_of(tile, rows)
    line_ref[...] = last
    against = jnp.concatenate([prev_ref[...].reshape(width, rows), lines[...], last], axis=0)
    line = collect(dot(last, against, NT, HIGHEST), width, vecs)
    gram_ref[:vecs, :] = early[:vecs, :]
    gram_ref[vecs:, :] = jnp.where(
        iota((8, 128), 0) == S - 1, jnp.broadcast_to(line, (8, 128)), early[vecs:, :]
    )


def finish_kernel(total, gram_in, prev_ref, lines, last, basis_ref, factors_ref):
    comps, vecs, rows = prev_ref.shape
    width = comps * vecs
    gram = gram_in[...] * (1.0 / total)
    small = gram[vecs:]
    lane, comp = iota((8, 128), 1), iota((8, 128), 0)
    in_prev = (lane < width) & (lane // vecs == comp)
    coef, cross = [], []
    for k in range(S):
        line = jnp.broadcast_to(small[k : k + 1], (8, 128))
        coef.append(jnp.where(in_prev, line, 0.0))
        cross.append([jnp.where(lane == width + 8 * l + comp, line, 0.0) for l in range(k + 1)])
    coefs = jnp.concatenate(coef, axis=0)
    prev = prev_ref[...].reshape(width, rows)
    basis = jnp.concatenate([lines[...], last[...]], axis=0)
    projected = basis - dot(coefs[:, :width], prev, precision=HIGHEST)
    square = jnp.concatenate([gram[:vecs]] * comps, axis=0)
    r, q = iota(square.shape, 0), iota(square.shape, 1)
    square = jnp.where(r // vecs == q // vecs, square, 0.0) - jnp.where(r == q, 2.0, 0.0)
    turned = dot(coefs[:, :width], square, precision=HIGHEST)
    entry = {}
    for k in range(S):
        for l in range(k + 1):
            value = turned[k * 8 : (k + 1) * 8] * coef[l] + cross[k][l]
            entry[k, l] = jnp.sum(value, axis=1, keepdims=True)
    lower = {}
    for k in range(S):
        for l in range(k + 1):
            value = entry[k, l]
            for m in range(l):
                value = value - lower[k, m] * lower[l, m]
            lower[k, l] = jnp.sqrt(value) if l == k else value / lower[l, l]
    vectors = []
    for k in range(S):
        value = projected[k * 8 : (k + 1) * 8]
        for l in range(k):
            value = value - lower[k, l] * vectors[l]
        value = value / lower[k, k]
        vectors.append(value)
        for c in range(comps):
            basis_ref[c, k : k + 1, :] = value[c : c + 1]
    for c in range(comps):
        factors_ref[c, :, :vecs] = small[:S, c * vecs : (c + 1) * vecs]
    for k in range(S):
        line = jnp.zeros((8, 128), jnp.float32)
        for l in range(k + 1):
            line = jnp.where(lane == l, lower[k, l], line)
        for c in range(comps):
            factors_ref[c, k : k + 1, vecs:] = line[c : c + 1, :S]


VMEM = pl.BlockSpec(memory_space=pltpu.VMEM)
HBM = pl.BlockSpec(memory_space=pltpu.HBM)


def in_hbm(*arrays):
    return [pltpu.with_memory_space_constraint(x, pltpu.HBM) for x in arrays]


def call(kernel, outs, specs, flops, moved, scratch=()):
    shapes = [jax.ShapeDtypeStruct(shape, kind) for shape, kind in outs]
    return pl.pallas_call(
        kernel,
        out_shape=shapes if len(shapes) > 1 else shapes[0],
        in_specs=specs,
        out_specs=[VMEM] * len(shapes) if len(shapes) > 1 else VMEM,
        scratch_shapes=list(scratch),
        compiler_params=pltpu.CompilerParams(vmem_limit_bytes=24 * 1024 * 1024),
        cost_estimate=pl.CostEstimate(flops=flops, bytes_accessed=moved, transcendentals=0),
    )


def send(value, target):
    return lax.ppermute(value, "dom", [(d, target[d]) for d in range(lax.axis_size("dom"))])


def neighbours(length, step, odd):
    target = {}
    for d in range(length):
        other = d + step if (d // step) % 2 == odd else d - step
        target[d] = other if 0 <= other < length else None
    return target


def ghosts(tile):
    length = lax.axis_size("dom")
    last = length - 1
    near, across = neighbours(length, 1, 0), neighbours(length, 1, 1)
    far_even, far_odd = neighbours(length, FAR, 0), neighbours(length, FAR, 1)
    across.update({0: 1, 1: 2, 2: 0, last: last - 1, last - 1: last - 2, last - 2: last})
    for d in range(length):
        if far_odd[d] is None:
            far_odd[d] = d ^ 1
    far_odd.update({0: 3, 3: 0, 1: 2, 2: 1})
    far_odd.update({last: last - 3, last - 3: last, last - 1: last - 2, last - 2: last - 1})
    return [send(tile, target) for target in (near, far_odd, far_even, across)]


def summed(value):
    step = 1
    while step < lax.axis_size("dom"):
        value = value + send(value, {d: d ^ (step | 1) for d in range(lax.axis_size("dom"))})
        step *= 2
    return value


def local(strips, columns, send_list, send_count, shifts, prev_basis, mix):
    comps, vecs, rows = prev_basis.shape
    blocks = columns.shape[0]
    width = strips.shape[1]
    f32, bf16, dma = jnp.float32, jnp.bfloat16, pltpu.SemaphoreType.DMA
    tile_out = ((comps * blocks, 128), f32)
    tile = call(
        start_kernel,
        [((comps * blocks + 8, 128), f32)],
        [HBM] * 4,
        600000,
        250000,
        [
            pltpu.VMEM(prev_basis.shape, f32),
            pltpu.VMEM(mix.shape, f32),
            pltpu.VMEM(send_list.shape, jnp.int32),
            pltpu.VMEM(send_count.shape, jnp.int32),
            dma((4,)),
        ],
    )(*in_hbm(prev_basis, mix, send_list, send_count))
    high, low, aux = call(
        prepare_kernel,
        [((width, rows), bf16), ((width, rows), bf16), ((8 * S + 8, 128), f32)],
        [HBM] * 3,
        1000000,
        1000000,
        [
            pltpu.VMEM((4, rows // 4, width), f32),
            pltpu.VMEM(columns.shape[::-1], jnp.int32),
            pltpu.SMEM(shifts.shape, f32),
            dma((6,)),
        ],
    )(*in_hbm(strips, columns.T, shifts))
    tiles = []
    length = lax.axis_size("dom")
    tile, choose = call(
        lambda *refs: first_kernel(length, *refs),
        [tile_out, ((2 * comps * blocks, 256), f32)],
        [VMEM] * 8,
        50000000,
        600000,
    )(tile, *ghosts(tile), aux, high, low)
    tiles.append(tile)
    for step in (1, 2):
        tile = call(
            lambda *refs, step=step: middle_kernel(step, *refs), [tile_out], [VMEM] * 9, 50000000, 600000
        )(tile, *ghosts(tile), choose, aux, high, low)
        tiles.append(tile)
    received = ghosts(tile)
    gram_out = ((vecs + 8, 128), f32)
    lines, early = call(
        early_kernel, [((8 * S - 8, rows), f32), gram_out], [VMEM] * 4, 60000000, 250000
    )(prev_basis, *tiles)
    last, gram = call(
        last_kernel, [((8, rows), f32), gram_out], [VMEM] * 12, 80000000, 900000
    )(tile, *received, choose, aux, high, low, lines, prev_basis, early)
    total = float(length * rows)
    basis, factors = call(
        lambda *refs: finish_kernel(total, *refs),
        [((comps, S, rows), f32), ((comps, S, vecs + S), f32)],
        [VMEM] * 4,
        50000000,
        400000,
    )(summed(gram), prev_basis, lines, last)
    return basis, jnp.swapaxes(factors, 1, 2)


def solution(mesh):
    in_specs = (
        P("dom", None),
        P("dom", None),
        P("dom", None, None),
        P("dom", None),
        P(),
        P(None, None, "dom"),
        P(),
    )
    out_specs = (P(None, None, "dom"), P())
    return jax.shard_map(local, mesh=mesh, in_specs=in_specs, out_specs=out_specs, check_vma=False)
```

```python
import jax
import jax.numpy as jnp
from jax import lax
from jax.experimental import pallas as pl
from jax.experimental.pallas import tpu as pltpu
from jax.sharding import PartitionSpec as P

BLOCK = 64
S = 4
FAR = 8
COMPS = 3
DEAD = 1000.0
HIGHEST = lax.Precision.HIGHEST
NN = (((1,), (0,)), ((), ()))
NT = (((1,), (1,)), ((), ()))


def dot(a, b, dims=NN, precision=None):
    return lax.dot_general(a, b, dims, precision=precision, preferred_element_type=jnp.float32)


def iota(shape, axis):
    return lax.broadcasted_iota(jnp.int32, shape, axis)


def own_lanes(rows, width):
    return iota((rows, width), 1) // BLOCK == iota((rows, width), 0) % 8


def fold(masked):
    total = masked[:, :128]
    for t in range(1, masked.shape[1] // 128):
        total = total + masked[:, t * 128 : (t + 1) * 128]
    return total + pltpu.roll(total, BLOCK, 1)


def lines_of(tile, width):
    wide = jnp.concatenate([tile] * (width // 128), axis=1)
    wide = jnp.where(own_lanes(wide.shape[0], width), wide, 0.0)
    where = iota((8, width), 0)
    result = jnp.zeros((8, width), jnp.float32)
    for c in range(COMPS):
        line = jnp.sum(wide[c * 8 : (c + 1) * 8], axis=0, keepdims=True)
        result = jnp.where(where == c, jnp.broadcast_to(line, result.shape), result)
    return result


def split(x):
    parts = []
    for _ in range(3):
        parts.append(x.astype(jnp.bfloat16))
        x = x - parts[-1].astype(jnp.float32)
    return parts


def fetch(pairs, sems):
    copies = [pltpu.make_async_copy(src, dst, sems.at[i]) for i, (src, dst) in enumerate(pairs)]
    for copy in copies:
        copy.start()
    return copies


def start_kernel(prev_in, mix_in, list_in, count_in, out_ref, prev_ref, mix_ref, list_ref, count_ref, sems):
    copies = fetch(
        [(prev_in, prev_ref), (mix_in, mix_ref), (list_in, list_ref), (count_in, count_ref)], sems
    )
    for copy in copies[1:]:
        copy.wait()
    comps, vecs, rows = prev_ref.shape
    mix = jnp.concatenate([mix_ref[...]] * comps, axis=1)
    mix = jnp.where(iota(mix.shape, 1) // vecs == iota(mix.shape, 0), mix, 0.0)
    order = list_ref[0].astype(jnp.float32)
    order = jnp.concatenate([order, jnp.zeros((4, 120), jnp.float32)], axis=1)
    meta = jnp.zeros((8, 128), jnp.float32)
    slot = iota((1, 128), 1)
    for link in range(4):
        live = slot < jnp.broadcast_to(count_ref[0:1, link : link + 1], slot.shape)
        line = jnp.where(live, order[link : link + 1], DEAD)
        line = pltpu.roll(jnp.broadcast_to(line, (8, 128)), 8 + 8 * link, 1)
        meta = jnp.where(iota((8, 128), 1) // 8 == link + 1, line, meta)
    out_ref[8 * comps :, :] = meta
    copies[0].wait()
    start = dot(mix, prev_ref[...].reshape(comps * vecs, rows), precision=HIGHEST)
    own = own_lanes(8, rows)
    for c in range(comps):
        line = jnp.broadcast_to(start[c : c + 1], own.shape)
        out_ref[c * 8 : (c + 1) * 8, :] = fold(jnp.where(own, line, 0.0))


def prepare_kernel(strips_in, columns_in, shifts_in, high_ref, low_ref, aux_ref, strips, columns, shifts, sems):
    parts = strips.shape[0]
    depth = strips.shape[1]
    pairs = [(columns_in, columns), (shifts_in, shifts)]
    pairs += [(strips_in.at[pl.ds(p * depth, depth)], strips.at[p]) for p in range(parts)]
    copies = fetch(pairs, sems)
    copies[0].wait()
    copies[1].wait()
    where = iota((8, 128), 1)
    table = jnp.zeros((8, 128), jnp.float32)
    eye = iota((8, 8), 0) == iota((8, 8), 1)
    for k in range(columns.shape[0]):
        line = jnp.broadcast_to(columns[k : k + 1, :].astype(jnp.float32), (8, 8))
        column = jnp.sum(jnp.where(eye, line, 0.0), axis=1, keepdims=True)
        table = jnp.where(where == k, column, table)
    for k in range(S):
        aux_ref[8 * k : 8 * k + 8, :] = jnp.full((8, 128), shifts[k], jnp.float32)
    aux_ref[8 * S :, :] = table
    for p in range(parts):
        copies[2 + p].wait()
        turned = strips[p].T
        high = turned.astype(jnp.bfloat16)
        high_ref[:, p * depth : (p + 1) * depth] = high
        low_ref[:, p * depth : (p + 1) * depth] = (turned - high.astype(jnp.float32)).astype(jnp.bfloat16)


def selection(table, metas, place, length):
    even, even_far = lax.rem(place, 2) == 0, lax.rem(place // FAR, 2) == 0
    near, far_odd, far_even, across = metas
    moved = (place == 1) | (place == length - 2)
    across = jnp.where(moved, far_odd, across)
    circle = jnp.where(moved, 48.0, 96.0)
    slots = [
        (place >= 1, jnp.where(even, circle, 24.0), jnp.where(even, across, near)),
        (place < length - 1, jnp.where(even, 24.0, circle), jnp.where(even, near, across)),
        (place >= FAR, jnp.where(even_far, 48.0, 72.0), jnp.where(even_far, far_odd, far_even)),
        (place < length - FAR, jnp.where(even_far, 72.0, 48.0), jnp.where(even_far, far_even, far_odd)),
    ]
    lane = iota((1, 128), 1)
    target = lane.astype(jnp.float32)
    for link, (valid, base, order) in enumerate(slots):
        order = order + jnp.where(valid, base, DEAD)
        target = jnp.where(lane // 8 == link + 1, order, target)
    target = jnp.broadcast_to(target, (8, 128))
    lane = iota((8, 128), 1).astype(jnp.float32)
    at = [
        jnp.sum(jnp.where(lane == table[:, k : k + 1], target, 0.0), axis=1, keepdims=True)
        for k in range(4)
    ]
    lane = iota((8, 256), 1).astype(jnp.float32)
    groups = []
    for pair in range(2):
        for c in range(COMPS):
            first = lane == at[2 * pair] + float(8 * c)
            second = lane == at[2 * pair + 1] + float(8 * c + 120)
            groups.append((first | second).astype(jnp.float32))
    return jnp.concatenate(groups, axis=0)


def multiply(choose, pieces, shift, high, low):
    rows = 8 * COMPS
    ext = jnp.concatenate(pieces, axis=0)
    front = iota(ext.shape, 1) < BLOCK
    top = ext.astype(jnp.bfloat16).astype(jnp.float32)
    rest = ext - top
    zero = jnp.zeros_like(ext)
    picked = jnp.concatenate(
        [
            jnp.concatenate([jnp.where(front, top, zero), jnp.where(front, rest, zero)], axis=1),
            jnp.concatenate([jnp.where(front, zero, top), jnp.where(front, zero, rest)], axis=1),
            jnp.zeros((256 - 2 * ext.shape[0], 256), jnp.float32),
        ],
        axis=0,
    ).astype(jnp.bfloat16)
    x = dot(choose.astype(jnp.bfloat16), picked)
    left = jnp.concatenate(
        [
            jnp.concatenate([x[:rows, :128], x[rows:, :128]], axis=1),
            jnp.concatenate([x[:rows, 128:], x[rows:, 128:]], axis=1),
        ],
        axis=0,
    ).astype(jnp.bfloat16)
    both = dot(left, high) + dot(left, low)
    image = both[:rows] + both[rows:]
    image = fold(jnp.where(own_lanes(rows, image.shape[1]), image, 0.0))
    return image - jnp.concatenate([shift] * COMPS, axis=0) * pieces[0]


def first_kernel(length, own, a, b, c, d, aux, high, low, tile_ref, choose_ref):
    rows = 8 * COMPS
    refs = (own, a, b, c, d)
    pieces = [ref[:rows, :] for ref in refs]
    metas = [ref[rows : rows + 1, :] for ref in refs[1:]]
    choose = selection(aux[8 * S :, :], metas, lax.axis_index("dom"), length)
    choose_ref[...] = choose
    tile_ref[...] = multiply(choose, pieces, aux[:8, :], high[...], low[...])


def middle_kernel(step, own, a, b, c, d, choose, aux, high, low, tile_ref):
    pieces = [ref[...] for ref in (own, a, b, c, d)]
    tile_ref[...] = multiply(choose[...], pieces, aux[8 * step : 8 * step + 8, :], high[...], low[...])


def collect(gram, width, vecs):
    lane, comp = iota(gram.shape, 1), iota(gram.shape, 0)
    mine = jnp.where(lane < width, lane // vecs, lane % 8) == comp
    return jnp.sum(jnp.where(mine, gram, 0.0), axis=0, keepdims=True)


def early_kernel(prev_ref, t0, t1, t2, lines_ref, gram_ref, *turned_refs):
    comps, vecs, rows = prev_ref.shape
    width = comps * vecs
    lines = jnp.concatenate([lines_of(t[...], rows) for t in (t0, t1, t2)], axis=0)
    lines_ref[...] = lines
    prev = prev_ref[...].reshape(width, rows)
    full = dot(prev, prev, NT, HIGHEST)
    owner = iota((vecs, width), 1) // vecs
    total = jnp.where(owner == 0, full[:vecs], 0.0)
    for c in range(1, comps):
        total = total + jnp.where(owner == c, full[c * vecs : (c + 1) * vecs], 0.0)
    gram_ref[:vecs, :] = jnp.concatenate([total, jnp.zeros((vecs, 128 - width), jnp.float32)], axis=1)
    against = jnp.concatenate([prev, lines, jnp.zeros((8, rows), jnp.float32)], axis=0)
    for ref, part in zip(turned_refs, split(against.T)):
        ref[...] = part
    gram = dot(lines, against, NT, HIGHEST)
    result = jnp.zeros((8, 128), jnp.float32)
    for k in range(S - 1):
        line = collect(gram[k * 8 : (k + 1) * 8], width, vecs)
        result = jnp.where(iota((8, 128), 0) == k, jnp.broadcast_to(line, result.shape), result)
    gram_ref[vecs:, :] = result


def last_kernel(own, a, b, c, d, choose, aux, high, low, early, t0, t1, t2, line_ref, gram_ref):
    pieces = [ref[...] for ref in (own, a, b, c, d)]
    tile = multiply(choose[...], pieces, aux[8 * S - 8 : 8 * S, :], high[...], low[...])
    rows = line_ref.shape[1]
    vecs = early.shape[0] - 8
    width = COMPS * vecs
    last = lines_of(tile, rows)
    line_ref[...] = last
    parts = [part.astype(jnp.float32) for part in split(last)]
    left = jnp.concatenate(parts + [jnp.zeros_like(last)], axis=0).astype(jnp.bfloat16)
    products = dot(left, t0[...]) + dot(left, t1[...]) + dot(left, t2[...])
    gram = products[:8] + (products[8:16] + products[16:24])
    square = jnp.sum(last * last, axis=1, keepdims=True)
    gram = jnp.where(iota(gram.shape, 1) == width + 8 * (S - 1) + iota(gram.shape, 0), square, gram)
    line = collect(gram, width, vecs)
    gram_ref[:vecs, :] = early[:vecs, :]
    gram_ref[vecs:, :] = jnp.where(
        iota((8, 128), 0) == S - 1, jnp.broadcast_to(line, (8, 128)), early[vecs:, :]
    )


def finish_kernel(total, gram_in, prev_ref, lines, last, basis_ref, factors_ref):
    comps, vecs, rows = prev_ref.shape
    width = comps * vecs
    gram = gram_in[...] * (1.0 / total)
    small = gram[vecs:]
    lane, comp = iota((8, 128), 1), iota((8, 128), 0)
    in_prev = (lane < width) & (lane // vecs == comp)
    coef, cross = [], []
    for k in range(S):
        line = jnp.broadcast_to(small[k : k + 1], (8, 128))
        coef.append(jnp.where(in_prev, line, 0.0))
        cross.append([jnp.where(lane == width + 8 * l + comp, line, 0.0) for l in range(k + 1)])
    coefs = jnp.concatenate(coef, axis=0)
    square = jnp.concatenate([gram[:vecs]] * comps, axis=0)
    r, q = iota(square.shape, 0), iota(square.shape, 1)
    square = jnp.where(r // vecs == q // vecs, square, 0.0) - jnp.where(r == q, 2.0, 0.0)
    turned = dot(coefs[:, :width], square, precision=HIGHEST)
    prev = prev_ref[...].reshape(width, rows)
    basis = jnp.concatenate([lines[...], last[...]], axis=0)
    projected = basis - dot(coefs[:, :width], prev, precision=HIGHEST)
    unit, scale = {}, {}
    for l in range(S):
        for k in range(l, S):
            value = turned[k * 8 : (k + 1) * 8] * coef[l] + cross[k][l]
            value = jnp.sum(value, axis=1, keepdims=True)
            for m in range(l):
                value = value - (unit[k, m] * scale[m]) * unit[l, m]
            if k == l:
                scale[l] = value
            else:
                unit[k, l] = value / scale[l]
    roots = [jnp.sqrt(scale[k]) for k in range(S)]
    lower = {(k, l): unit[k, l] * roots[l] if l < k else roots[k] for k in range(S) for l in range(k + 1)}
    vectors = []
    for k in range(S):
        value = projected[k * 8 : (k + 1) * 8]
        for l in range(k):
            value = value - unit[k, l] * vectors[l]
        vectors.append(value)
        value = value / roots[k]
        for c in range(comps):
            basis_ref[c, k : k + 1, :] = value[c : c + 1]
    for c in range(comps):
        factors_ref[c, :, :vecs] = small[:S, c * vecs : (c + 1) * vecs]
    for k in range(S):
        line = jnp.zeros((8, 128), jnp.float32)
        for l in range(k + 1):
            line = jnp.where(lane == l, lower[k, l], line)
        for c in range(comps):
            factors_ref[c, k : k + 1, vecs:] = line[c : c + 1, :S]


VMEM = pl.BlockSpec(memory_space=pltpu.VMEM)
HBM = pl.BlockSpec(memory_space=pltpu.HBM)


def in_hbm(*arrays):
    return [pltpu.with_memory_space_constraint(x, pltpu.HBM) for x in arrays]


def call(kernel, outs, specs, flops, moved, scratch=()):
    shapes = [jax.ShapeDtypeStruct(shape, kind) for shape, kind in outs]
    return pl.pallas_call(
        kernel,
        out_shape=shapes if len(shapes) > 1 else shapes[0],
        in_specs=specs,
        out_specs=[VMEM] * len(shapes) if len(shapes) > 1 else VMEM,
        scratch_shapes=list(scratch),
        compiler_params=pltpu.CompilerParams(vmem_limit_bytes=24 * 1024 * 1024),
        cost_estimate=pl.CostEstimate(flops=flops, bytes_accessed=moved, transcendentals=0),
    )


def send(value, target):
    return lax.ppermute(value, "dom", [(d, target[d]) for d in range(lax.axis_size("dom"))])


def neighbours(length, step, odd):
    target = {}
    for d in range(length):
        other = d + step if (d // step) % 2 == odd else d - step
        target[d] = other if 0 <= other < length else None
    return target


def ghosts(tile):
    length = lax.axis_size("dom")
    last = length - 1
    near, across = neighbours(length, 1, 0), neighbours(length, 1, 1)
    far_even, far_odd = neighbours(length, FAR, 0), neighbours(length, FAR, 1)
    across.update({0: 1, 1: 2, 2: 0, last: last - 1, last - 1: last - 2, last - 2: last})
    for d in range(length):
        if far_odd[d] is None:
            far_odd[d] = d ^ 1
    far_odd.update({0: 3, 3: 0, 1: 2, 2: 1})
    far_odd.update({last: last - 3, last - 3: last, last - 1: last - 2, last - 2: last - 1})
    return [send(tile, target) for target in (near, far_odd, far_even, across)]


def summed(value):
    length = lax.axis_size("dom")

    def fetched(step):
        return send(value, {d: d ^ (step | 1) for d in range(length)})

    value = value + fetched(1)
    step = 2
    while step < length:
        if 2 * step < length:
            farthest = fetched(3 * step)
            first, second = fetched(step), fetched(2 * step)
            value = (value + first) + (second + farthest)
        else:
            value = value + fetched(step)
        step *= 4
    return value


def local(strips, columns, send_list, send_count, shifts, prev_basis, mix):
    comps, vecs, rows = prev_basis.shape
    blocks = columns.shape[0]
    width = strips.shape[1]
    f32, bf16, dma = jnp.float32, jnp.bfloat16, pltpu.SemaphoreType.DMA
    tile_out = ((comps * blocks, 128), f32)
    tile = call(
        start_kernel,
        [((comps * blocks + 8, 128), f32)],
        [HBM] * 4,
        600000,
        250000,
        [
            pltpu.VMEM(prev_basis.shape, f32),
            pltpu.VMEM(mix.shape, f32),
            pltpu.VMEM(send_list.shape, jnp.int32),
            pltpu.VMEM(send_count.shape, jnp.int32),
            dma((4,)),
        ],
    )(*in_hbm(prev_basis, mix, send_list, send_count))
    high, low, aux = call(
        prepare_kernel,
        [((width, rows), bf16), ((width, rows), bf16), ((8 * S + 8, 128), f32)],
        [HBM] * 3,
        1000000,
        1000000,
        [
            pltpu.VMEM((4, rows // 4, width), f32),
            pltpu.VMEM(columns.shape[::-1], jnp.int32),
            pltpu.SMEM(shifts.shape, f32),
            dma((6,)),
        ],
    )(*in_hbm(strips, columns.T, shifts))
    tiles = []
    length = lax.axis_size("dom")
    tile, choose = call(
        lambda *refs: first_kernel(length, *refs),
        [tile_out, ((2 * comps * blocks, 256), f32)],
        [VMEM] * 8,
        50000000,
        600000,
    )(tile, *ghosts(tile), aux, high, low)
    tiles.append(tile)
    for step in (1, 2):
        tile = call(
            lambda *refs, step=step: middle_kernel(step, *refs), [tile_out], [VMEM] * 9, 50000000, 600000
        )(tile, *ghosts(tile), choose, aux, high, low)
        tiles.append(tile)
    received = ghosts(tile)
    gram_out = ((vecs + 8, 128), f32)
    lines, early, *turned = call(
        early_kernel,
        [((8 * S - 8, rows), f32), gram_out] + [((rows, 128), bf16)] * 3,
        [VMEM] * 4,
        60000000,
        250000,
    )(prev_basis, *tiles)
    last, gram = call(
        last_kernel, [((8, rows), f32), gram_out], [VMEM] * 13, 80000000, 900000
    )(tile, *received, choose, aux, high, low, early, *turned)
    total = float(length * rows)
    basis, factors = call(
        lambda *refs: finish_kernel(total, *refs),
        [((comps, S, rows), f32), ((comps, S, vecs + S), f32)],
        [VMEM] * 4,
        50000000,
        400000,
    )(summed(gram), prev_basis, lines, last)
    return basis, jnp.swapaxes(factors, 1, 2)


def solution(mesh):
    in_specs = (
        P("dom", None),
        P("dom", None),
        P("dom", None, None),
        P("dom", None),
        P(),
        P(None, None, "dom"),
        P(),
    )
    out_specs = (P(None, None, "dom"), P())
    return jax.shard_map(local, mesh=mesh, in_specs=in_specs, out_specs=out_specs, check_vma=False)
```

```python
import jax
import jax.numpy as jnp
from jax import lax
from jax.experimental import pallas as pl
from jax.experimental.pallas import tpu as pltpu
from jax.sharding import PartitionSpec as P

BLOCK = 64
S = 4
FAR = 8
COMPS = 3
DEAD = 1000.0
HIGHEST = lax.Precision.HIGHEST
NN = (((1,), (0,)), ((), ()))
NT = (((1,), (1,)), ((), ()))


def dot(a, b, dims=NN, precision=None):
    return lax.dot_general(a, b, dims, precision=precision, preferred_element_type=jnp.float32)


def iota(shape, axis):
    return lax.broadcasted_iota(jnp.int32, shape, axis)


def own_lanes(rows, width):
    return iota((rows, width), 1) // BLOCK == iota((rows, width), 0) % 8


def fold(masked):
    total = masked[:, :128]
    for t in range(1, masked.shape[1] // 128):
        total = total + masked[:, t * 128 : (t + 1) * 128]
    return total + pltpu.roll(total, BLOCK, 1)


def lines_of(tile, width):
    wide = jnp.concatenate([tile] * (width // 128), axis=1)
    wide = jnp.where(own_lanes(wide.shape[0], width), wide, 0.0)
    where = iota((8, width), 0)
    result = jnp.zeros((8, width), jnp.float32)
    for c in range(COMPS):
        line = jnp.sum(wide[c * 8 : (c + 1) * 8], axis=0, keepdims=True)
        result = jnp.where(where == c, jnp.broadcast_to(line, result.shape), result)
    return result


def split(x):
    parts = []
    for _ in range(3):
        parts.append(x.astype(jnp.bfloat16))
        x = x - parts[-1].astype(jnp.float32)
    return parts


def fetch(pairs, sems):
    copies = [pltpu.make_async_copy(src, dst, sems.at[i]) for i, (src, dst) in enumerate(pairs)]
    for copy in copies:
        copy.start()
    return copies


def start_kernel(prev_in, mix_in, list_in, count_in, out_ref, prev_ref, mix_ref, list_ref, count_ref, sems):
    copies = fetch(
        [(prev_in, prev_ref), (mix_in, mix_ref), (list_in, list_ref), (count_in, count_ref)], sems
    )
    for copy in copies[1:]:
        copy.wait()
    comps, vecs, rows = prev_ref.shape
    eye = iota((vecs, vecs), 0) == iota((vecs, vecs), 1)
    weights = []
    for c in range(comps):
        line = jnp.broadcast_to(mix_ref[c : c + 1, :], eye.shape)
        weights.append(jnp.sum(jnp.where(eye, line, 0.0), axis=1, keepdims=True))
    order = list_ref[0].astype(jnp.float32)
    order = jnp.concatenate([order, jnp.zeros((4, 120), jnp.float32)], axis=1)
    meta = jnp.zeros((8, 128), jnp.float32)
    slot = iota((1, 128), 1)
    for link in range(4):
        live = slot < jnp.broadcast_to(count_ref[0:1, link : link + 1], slot.shape)
        line = jnp.where(live, order[link : link + 1], DEAD)
        line = pltpu.roll(jnp.broadcast_to(line, (8, 128)), 8 + 8 * link, 1)
        meta = jnp.where(iota((8, 128), 1) // 8 == link + 1, line, meta)
    out_ref[8 * comps :, :] = meta
    copies[0].wait()
    own = own_lanes(8, rows)
    for c in range(comps):
        start = jnp.sum(weights[c] * prev_ref[c], axis=0, keepdims=True)
        line = jnp.broadcast_to(start, own.shape)
        out_ref[c * 8 : (c + 1) * 8, :] = fold(jnp.where(own, line, 0.0))


def prepare_kernel(strips_in, columns_in, shifts_in, high_ref, low_ref, aux_ref, strips, columns, shifts, sems):
    parts = strips.shape[0]
    depth = strips.shape[1]
    pairs = [(columns_in, columns), (shifts_in, shifts)]
    pairs += [(strips_in.at[pl.ds(p * depth, depth)], strips.at[p]) for p in range(parts)]
    copies = fetch(pairs, sems)
    copies[0].wait()
    copies[1].wait()
    where = iota((8, 128), 1)
    table = jnp.zeros((8, 128), jnp.float32)
    eye = iota((8, 8), 0) == iota((8, 8), 1)
    for k in range(columns.shape[0]):
        line = jnp.broadcast_to(columns[k : k + 1, :].astype(jnp.float32), (8, 8))
        column = jnp.sum(jnp.where(eye, line, 0.0), axis=1, keepdims=True)
        table = jnp.where(where == k, column, table)
    for k in range(S):
        aux_ref[8 * k : 8 * k + 8, :] = jnp.full((8, 128), shifts[k], jnp.float32)
    aux_ref[8 * S :, :] = table
    for p in range(parts):
        copies[2 + p].wait()
        turned = strips[p].T
        high = turned.astype(jnp.bfloat16)
        high_ref[:, p * depth : (p + 1) * depth] = high
        low_ref[:, p * depth : (p + 1) * depth] = (turned - high.astype(jnp.float32)).astype(jnp.bfloat16)


def selection(table, metas, place, length):
    even, even_far = lax.rem(place, 2) == 0, lax.rem(place // FAR, 2) == 0
    near, far_odd, far_even, across = metas
    moved = (place == 1) | (place == length - 2)
    across = jnp.where(moved, far_odd, across)
    circle = jnp.where(moved, 48.0, 96.0)
    slots = [
        (place >= 1, jnp.where(even, circle, 24.0), jnp.where(even, across, near)),
        (place < length - 1, jnp.where(even, 24.0, circle), jnp.where(even, near, across)),
        (place >= FAR, jnp.where(even_far, 48.0, 72.0), jnp.where(even_far, far_odd, far_even)),
        (place < length - FAR, jnp.where(even_far, 72.0, 48.0), jnp.where(even_far, far_even, far_odd)),
    ]
    lane = iota((1, 128), 1)
    target = lane.astype(jnp.float32)
    for link, (valid, base, order) in enumerate(slots):
        order = order + jnp.where(valid, base, DEAD)
        target = jnp.where(lane // 8 == link + 1, order, target)
    target = jnp.broadcast_to(target, (8, 128))
    lane = iota((8, 128), 1).astype(jnp.float32)
    at = [
        jnp.sum(jnp.where(lane == table[:, k : k + 1], target, 0.0), axis=1, keepdims=True)
        for k in range(4)
    ]
    groups = [(lane == at[k] + float(8 * c)).astype(jnp.float32) for k in range(4) for c in range(COMPS)]
    return jnp.concatenate(groups, axis=0).astype(jnp.bfloat16)


def multiply(choose, pieces, shift, high, low):
    rows = 8 * COMPS
    ext = jnp.concatenate(pieces + [jnp.zeros((128 - 5 * rows, 128), jnp.float32)], axis=0)
    top = ext.astype(jnp.bfloat16).astype(jnp.float32)
    x = dot(choose, jnp.concatenate([top, ext - top], axis=1).astype(jnp.bfloat16))
    front = iota((rows, 256), 1) % 128 < BLOCK
    pairs = [
        jnp.where(front, x[2 * t * rows : (2 * t + 1) * rows], x[(2 * t + 1) * rows : (2 * t + 2) * rows])
        for t in range(2)
    ]
    left = jnp.concatenate(
        [
            jnp.concatenate([pair[:, half * 128 : (half + 1) * 128] for pair in pairs], axis=1)
            for half in range(2)
        ],
        axis=0,
    ).astype(jnp.bfloat16)
    both = dot(left, high) + dot(left, low)
    image = both[:rows] + both[rows:]
    image = fold(jnp.where(own_lanes(rows, image.shape[1]), image, 0.0))
    return image - jnp.concatenate([shift] * COMPS, axis=0) * pieces[0]


def first_kernel(length, own, a, b, c, d, aux, high, low, tile_ref, choose_ref):
    rows = 8 * COMPS
    refs = (own, a, b, c, d)
    pieces = [ref[:rows, :] for ref in refs]
    metas = [ref[rows : rows + 1, :] for ref in refs[1:]]
    choose = selection(aux[8 * S :, :], metas, lax.axis_index("dom"), length)
    choose_ref[...] = choose
    tile_ref[...] = multiply(choose, pieces, aux[:8, :], high[...], low[...])


def middle_kernel(step, own, a, b, c, d, choose, aux, high, low, tile_ref):
    pieces = [ref[...] for ref in (own, a, b, c, d)]
    tile_ref[...] = multiply(choose[...], pieces, aux[8 * step : 8 * step + 8, :], high[...], low[...])


def collect(gram, width, vecs):
    lane, comp = iota(gram.shape, 1), iota(gram.shape, 0)
    mine = jnp.where(lane < width, lane // vecs, lane % 8) == comp
    return jnp.sum(jnp.where(mine, gram, 0.0), axis=0, keepdims=True)


def early_kernel(prev_ref, t0, t1, t2, lines_ref, gram_ref, *turned_refs):
    comps, vecs, rows = prev_ref.shape
    width = comps * vecs
    lines = jnp.concatenate([lines_of(t[...], rows) for t in (t0, t1, t2)], axis=0)
    lines_ref[...] = lines
    prev = prev_ref[...].reshape(width, rows)
    full = dot(prev, prev, NT, HIGHEST)
    owner = iota((vecs, width), 1) // vecs
    total = jnp.where(owner == 0, full[:vecs], 0.0)
    for c in range(1, comps):
        total = total + jnp.where(owner == c, full[c * vecs : (c + 1) * vecs], 0.0)
    gram_ref[:vecs, :] = jnp.concatenate([total, jnp.zeros((vecs, 128 - width), jnp.float32)], axis=1)
    against = jnp.concatenate([prev, lines, jnp.zeros((8, rows), jnp.float32)], axis=0)
    for ref, part in zip(turned_refs, split(against.T)):
        ref[...] = part
    gram = dot(lines, against, NT, HIGHEST)
    result = jnp.zeros((8, 128), jnp.float32)
    for k in range(S - 1):
        line = collect(gram[k * 8 : (k + 1) * 8], width, vecs)
        result = jnp.where(iota((8, 128), 0) == k, jnp.broadcast_to(line, result.shape), result)
    gram_ref[vecs:, :] = result


def last_kernel(own, a, b, c, d, choose, aux, high, low, early, t0, t1, t2, line_ref, gram_ref):
    pieces = [ref[...] for ref in (own, a, b, c, d)]
    tile = multiply(choose[...], pieces, aux[8 * S - 8 : 8 * S, :], high[...], low[...])
    rows = line_ref.shape[1]
    vecs = early.shape[0] - 8
    width = COMPS * vecs
    last = lines_of(tile, rows)
    line_ref[...] = last
    parts = [part.astype(jnp.float32) for part in split(last)]
    left = jnp.concatenate(parts + [jnp.zeros_like(last)], axis=0).astype(jnp.bfloat16)
    products = dot(left, t0[...]) + dot(left, t1[...]) + dot(left, t2[...])
    gram = products[:8] + (products[8:16] + products[16:24])
    square = jnp.sum(last * last, axis=1, keepdims=True)
    gram = jnp.where(iota(gram.shape, 1) == width + 8 * (S - 1) + iota(gram.shape, 0), square, gram)
    line = collect(gram, width, vecs)
    gram_ref[:vecs, :] = early[:vecs, :]
    gram_ref[vecs:, :] = jnp.where(
        iota((8, 128), 0) == S - 1, jnp.broadcast_to(line, (8, 128)), early[vecs:, :]
    )


def finish_kernel(total, gram_in, prev_ref, lines, last, basis_ref, factors_ref):
    comps, vecs, rows = prev_ref.shape
    width = comps * vecs
    gram = gram_in[...] * (1.0 / total)
    small = gram[vecs:]
    lane, comp = iota((8, 128), 1), iota((8, 128), 0)
    in_prev = (lane < width) & (lane // vecs == comp)
    coef, cross = [], []
    for k in range(S):
        line = jnp.broadcast_to(small[k : k + 1], (8, 128))
        coef.append(jnp.where(in_prev, line, 0.0))
        cross.append([jnp.where(lane == width + 8 * l + comp, line, 0.0) for l in range(k + 1)])
    coefs = jnp.concatenate(coef, axis=0)
    square = jnp.concatenate([gram[:vecs]] * comps, axis=0)
    r, q = iota(square.shape, 0), iota(square.shape, 1)
    square = jnp.where(r // vecs == q // vecs, square, 0.0) - jnp.where(r == q, 2.0, 0.0)
    turned = dot(coefs[:, :width], square, precision=HIGHEST)
    prev = prev_ref[...].reshape(width, rows)
    basis = jnp.concatenate([lines[...], last[...]], axis=0)
    projected = basis - dot(coefs[:, :width], prev, precision=HIGHEST)
    unit, scale = {}, {}
    for l in range(S):
        for k in range(l, S):
            value = turned[k * 8 : (k + 1) * 8] * coef[l] + cross[k][l]
            value = jnp.sum(value, axis=1, keepdims=True)
            for m in range(l):
                value = value - (unit[k, m] * scale[m]) * unit[l, m]
            if k == l:
                scale[l] = value
            else:
                unit[k, l] = value / scale[l]
    roots = [jnp.sqrt(scale[k]) for k in range(S)]
    lower = {(k, l): unit[k, l] * roots[l] if l < k else roots[k] for k in range(S) for l in range(k + 1)}
    vectors = []
    for k in range(S):
        value = projected[k * 8 : (k + 1) * 8]
        for l in range(k):
            value = value - unit[k, l] * vectors[l]
        vectors.append(value)
        value = value / roots[k]
        for c in range(comps):
            basis_ref[c, k : k + 1, :] = value[c : c + 1]
    for c in range(comps):
        factors_ref[c, :, :vecs] = small[:S, c * vecs : (c + 1) * vecs]
    for k in range(S):
        line = jnp.zeros((8, 128), jnp.float32)
        for l in range(k + 1):
            line = jnp.where(lane == l, lower[k, l], line)
        for c in range(comps):
            factors_ref[c, k : k + 1, vecs:] = line[c : c + 1, :S]


VMEM = pl.BlockSpec(memory_space=pltpu.VMEM)
HBM = pl.BlockSpec(memory_space=pltpu.HBM)


def in_hbm(*arrays):
    return [pltpu.with_memory_space_constraint(x, pltpu.HBM) for x in arrays]


def call(kernel, outs, specs, flops, moved, scratch=()):
    shapes = [jax.ShapeDtypeStruct(shape, kind) for shape, kind in outs]
    return pl.pallas_call(
        kernel,
        out_shape=shapes if len(shapes) > 1 else shapes[0],
        in_specs=specs,
        out_specs=[VMEM] * len(shapes) if len(shapes) > 1 else VMEM,
        scratch_shapes=list(scratch),
        compiler_params=pltpu.CompilerParams(vmem_limit_bytes=24 * 1024 * 1024),
        cost_estimate=pl.CostEstimate(flops=flops, bytes_accessed=moved, transcendentals=0),
    )


def send(value, target):
    return lax.ppermute(value, "dom", [(d, target[d]) for d in range(lax.axis_size("dom"))])


def neighbours(length, step, odd):
    target = {}
    for d in range(length):
        other = d + step if (d // step) % 2 == odd else d - step
        target[d] = other if 0 <= other < length else None
    return target


def ghosts(tile):
    length = lax.axis_size("dom")
    last = length - 1
    near, across = neighbours(length, 1, 0), neighbours(length, 1, 1)
    far_even, far_odd = neighbours(length, FAR, 0), neighbours(length, FAR, 1)
    across.update({0: 1, 1: 2, 2: 0, last: last - 1, last - 1: last - 2, last - 2: last})
    for d in range(length):
        if far_odd[d] is None:
            far_odd[d] = d ^ 1
    far_odd.update({0: 3, 3: 0, 1: 2, 2: 1})
    far_odd.update({last: last - 3, last - 3: last, last - 1: last - 2, last - 2: last - 1})
    return [send(tile, target) for target in (near, far_odd, far_even, across)]


def summed(value):
    length = lax.axis_size("dom")

    def fetched(step):
        return send(value, {d: d ^ (step | 1) for d in range(length)})

    value = value + fetched(1)
    step = 2
    while step < length:
        if 2 * step < length:
            farthest = fetched(3 * step)
            first, second = fetched(step), fetched(2 * step)
            value = (value + first) + (second + farthest)
        else:
            value = value + fetched(step)
        step *= 4
    return value


def local(strips, columns, send_list, send_count, shifts, prev_basis, mix):
    comps, vecs, rows = prev_basis.shape
    blocks = columns.shape[0]
    width = strips.shape[1]
    f32, bf16, dma = jnp.float32, jnp.bfloat16, pltpu.SemaphoreType.DMA
    tile_out = ((comps * blocks, 128), f32)
    tile = call(
        start_kernel,
        [((comps * blocks + 8, 128), f32)],
        [HBM] * 4,
        600000,
        250000,
        [
            pltpu.VMEM(prev_basis.shape, f32),
            pltpu.VMEM(mix.shape, f32),
            pltpu.VMEM(send_list.shape, jnp.int32),
            pltpu.VMEM(send_count.shape, jnp.int32),
            dma((4,)),
        ],
    )(*in_hbm(prev_basis, mix, send_list, send_count))
    high, low, aux = call(
        prepare_kernel,
        [((width, rows), bf16), ((width, rows), bf16), ((8 * S + 8, 128), f32)],
        [HBM] * 3,
        1000000,
        1000000,
        [
            pltpu.VMEM((4, rows // 4, width), f32),
            pltpu.VMEM(columns.shape[::-1], jnp.int32),
            pltpu.SMEM(shifts.shape, f32),
            dma((6,)),
        ],
    )(*in_hbm(strips, columns.T, shifts))
    tiles = []
    length = lax.axis_size("dom")
    tile, choose = call(
        lambda *refs: first_kernel(length, *refs),
        [tile_out, ((4 * comps * blocks, 128), bf16)],
        [VMEM] * 8,
        50000000,
        600000,
    )(tile, *ghosts(tile), aux, high, low)
    tiles.append(tile)
    for step in (1, 2):
        tile = call(
            lambda *refs, step=step: middle_kernel(step, *refs), [tile_out], [VMEM] * 9, 50000000, 600000
        )(tile, *ghosts(tile), choose, aux, high, low)
        tiles.append(tile)
    received = ghosts(tile)
    gram_out = ((vecs + 8, 128), f32)
    lines, early, *turned = call(
        early_kernel,
        [((8 * S - 8, rows), f32), gram_out] + [((rows, 128), bf16)] * 3,
        [VMEM] * 4,
        60000000,
        250000,
    )(prev_basis, *tiles)
    last, gram = call(
        last_kernel, [((8, rows), f32), gram_out], [VMEM] * 13, 80000000, 900000
    )(tile, *received, choose, aux, high, low, early, *turned)
    total = float(length * rows)
    basis, factors = call(
        lambda *refs: finish_kernel(total, *refs),
        [((comps, S, rows), f32), ((comps, S, vecs + S), f32)],
        [VMEM] * 4,
        50000000,
        400000,
    )(summed(gram), prev_basis, lines, last)
    return basis, jnp.swapaxes(factors, 1, 2)


def solution(mesh):
    in_specs = (
        P("dom", None),
        P("dom", None),
        P("dom", None, None),
        P("dom", None),
        P(),
        P(None, None, "dom"),
        P(),
    )
    out_specs = (P(None, None, "dom"), P())
    return jax.shard_map(local, mesh=mesh, in_specs=in_specs, out_specs=out_specs, check_vma=False)
```

```python
import jax
import jax.numpy as jnp
from jax import lax
from jax.experimental import pallas as pl
from jax.experimental.pallas import tpu as pltpu
from jax.sharding import PartitionSpec as P

BLOCK = 64
S = 4
FAR = 8
COMPS = 3
DEAD = 1000.0
HIGHEST = lax.Precision.HIGHEST
NN = (((1,), (0,)), ((), ()))
NT = (((1,), (1,)), ((), ()))


def dot(a, b, dims=NN, precision=None):
    return lax.dot_general(a, b, dims, precision=precision, preferred_element_type=jnp.float32)


def iota(shape, axis):
    return lax.broadcasted_iota(jnp.int32, shape, axis)


def own_lanes(rows, width):
    return iota((rows, width), 1) // BLOCK == iota((rows, width), 0) % 8


def fold(masked):
    total = masked[:, :128]
    for t in range(1, masked.shape[1] // 128):
        total = total + masked[:, t * 128 : (t + 1) * 128]
    return total + pltpu.roll(total, BLOCK, 1)


def lines_of(tile, width):
    wide = jnp.concatenate([tile] * (width // 128), axis=1)
    wide = jnp.where(own_lanes(wide.shape[0], width), wide, 0.0)
    where = iota((8, width), 0)
    result = jnp.zeros((8, width), jnp.float32)
    for c in range(COMPS):
        line = jnp.sum(wide[c * 8 : (c + 1) * 8], axis=0, keepdims=True)
        result = jnp.where(where == c, jnp.broadcast_to(line, result.shape), result)
    return result


def split(x):
    parts = []
    for _ in range(3):
        parts.append(x.astype(jnp.bfloat16))
        x = x - parts[-1].astype(jnp.float32)
    return parts


def fetch(pairs, sems):
    copies = [pltpu.make_async_copy(src, dst, sems.at[i]) for i, (src, dst) in enumerate(pairs)]
    for copy in copies:
        copy.start()
    return copies


def start_kernel(prev_in, mix_in, list_in, count_in, out_ref, prev_ref, mix_ref, list_ref, count_ref, sems):
    copies = fetch(
        [(prev_in, prev_ref), (mix_in, mix_ref), (list_in, list_ref), (count_in, count_ref)], sems
    )
    for copy in copies[1:]:
        copy.wait()
    comps, vecs, rows = prev_ref.shape
    eye = iota((vecs, vecs), 0) == iota((vecs, vecs), 1)
    weights = []
    for c in range(comps):
        line = jnp.broadcast_to(mix_ref[c : c + 1, :], eye.shape)
        weights.append(jnp.sum(jnp.where(eye, line, 0.0), axis=1, keepdims=True))
    order = list_ref[0].astype(jnp.float32)
    order = jnp.concatenate([order, jnp.zeros((4, 120), jnp.float32)], axis=1)
    meta = jnp.zeros((8, 128), jnp.float32)
    slot = iota((1, 128), 1)
    for link in range(4):
        live = slot < jnp.broadcast_to(count_ref[0:1, link : link + 1], slot.shape)
        line = jnp.where(live, order[link : link + 1], DEAD)
        line = pltpu.roll(jnp.broadcast_to(line, (8, 128)), 8 + 8 * link, 1)
        meta = jnp.where(iota((8, 128), 1) // 8 == link + 1, line, meta)
    out_ref[8 * comps :, :] = meta
    copies[0].wait()
    own = own_lanes(8, rows)
    for c in range(comps):
        start = jnp.sum(weights[c] * prev_ref[c], axis=0, keepdims=True)
        line = jnp.broadcast_to(start, own.shape)
        out_ref[c * 8 : (c + 1) * 8, :] = fold(jnp.where(own, line, 0.0))


def prepare_kernel(strips_in, columns_in, shifts_in, high_ref, low_ref, aux_ref, strips, columns, shifts, sems):
    parts = strips.shape[0]
    depth = strips.shape[1]
    pairs = [(columns_in, columns), (shifts_in, shifts)]
    pairs += [(strips_in.at[pl.ds(p * depth, depth)], strips.at[p]) for p in range(parts)]
    copies = fetch(pairs, sems)
    copies[0].wait()
    copies[1].wait()
    where = iota((8, 128), 1)
    table = jnp.zeros((8, 128), jnp.float32)
    eye = iota((8, 8), 0) == iota((8, 8), 1)
    for k in range(columns.shape[0]):
        line = jnp.broadcast_to(columns[k : k + 1, :].astype(jnp.float32), (8, 8))
        column = jnp.sum(jnp.where(eye, line, 0.0), axis=1, keepdims=True)
        table = jnp.where(where == k, column, table)
    for k in range(S):
        aux_ref[8 * k : 8 * k + 8, :] = jnp.full((8, 128), shifts[k], jnp.float32)
    aux_ref[8 * S :, :] = table
    for p in range(parts):
        copies[2 + p].wait()
        turned = strips[p].T
        high = turned.astype(jnp.bfloat16)
        high_ref[:, p * depth : (p + 1) * depth] = high
        low_ref[:, p * depth : (p + 1) * depth] = (turned - high.astype(jnp.float32)).astype(jnp.bfloat16)


def selection(table, metas, place, length):
    even, even_far = lax.rem(place, 2) == 0, lax.rem(place // FAR, 2) == 0
    near, far_odd, far_even, across = metas
    moved = (place == 1) | (place == length - 2)
    across = jnp.where(moved, far_odd, across)
    circle = jnp.where(moved, 48.0, 96.0)
    slots = [
        (place >= 1, jnp.where(even, circle, 24.0), jnp.where(even, across, near)),
        (place < length - 1, jnp.where(even, 24.0, circle), jnp.where(even, near, across)),
        (place >= FAR, jnp.where(even_far, 48.0, 72.0), jnp.where(even_far, far_odd, far_even)),
        (place < length - FAR, jnp.where(even_far, 72.0, 48.0), jnp.where(even_far, far_even, far_odd)),
    ]
    lane = iota((1, 128), 1)
    target = lane.astype(jnp.float32)
    for link, (valid, base, order) in enumerate(slots):
        order = order + jnp.where(valid, base, DEAD)
        target = jnp.where(lane // 8 == link + 1, order, target)
    target = jnp.broadcast_to(target, (8, 128))
    lane = iota((8, 128), 1).astype(jnp.float32)
    at = [
        jnp.sum(jnp.where(lane == table[:, k : k + 1], target, 0.0), axis=1, keepdims=True)
        for k in range(4)
    ]
    groups = [(lane == at[k] + float(8 * c)).astype(jnp.float32) for k in range(4) for c in range(COMPS)]
    return jnp.concatenate(groups, axis=0).astype(jnp.bfloat16)


def multiply(choose, pieces, shift, high, low):
    rows = 8 * COMPS
    ext = jnp.concatenate(pieces + [jnp.zeros((128 - 5 * rows, 128), jnp.float32)], axis=0)
    top = ext.astype(jnp.bfloat16).astype(jnp.float32)
    x = dot(choose, jnp.concatenate([top, ext - top], axis=1).astype(jnp.bfloat16))
    front = iota((rows, 256), 1) % 128 < BLOCK
    pairs = [
        jnp.where(front, x[2 * t * rows : (2 * t + 1) * rows], x[(2 * t + 1) * rows : (2 * t + 2) * rows])
        for t in range(2)
    ]
    left = jnp.concatenate(
        [
            jnp.concatenate([pair[:, half * 128 : (half + 1) * 128] for pair in pairs], axis=1)
            for half in range(2)
        ],
        axis=0,
    ).astype(jnp.bfloat16)
    both = dot(left, high) + dot(left, low)
    image = both[:rows] + both[rows:]
    image = fold(jnp.where(own_lanes(rows, image.shape[1]), image, 0.0))
    return image - jnp.concatenate([shift] * COMPS, axis=0) * pieces[0]


def first_kernel(length, own, a, b, c, d, aux, high, low, tile_ref, choose_ref):
    rows = 8 * COMPS
    refs = (own, a, b, c, d)
    pieces = [ref[:rows, :] for ref in refs]
    metas = [ref[rows : rows + 1, :] for ref in refs[1:]]
    choose = selection(aux[8 * S :, :], metas, lax.axis_index("dom"), length)
    choose_ref[...] = choose
    tile_ref[...] = multiply(choose, pieces, aux[:8, :], high[...], low[...])


def middle_kernel(step, own, a, b, c, d, choose, aux, high, low, tile_ref):
    pieces = [ref[...] for ref in (own, a, b, c, d)]
    tile_ref[...] = multiply(choose[...], pieces, aux[8 * step : 8 * step + 8, :], high[...], low[...])


def collect(gram, width, vecs):
    lane, comp = iota(gram.shape, 1), iota(gram.shape, 0)
    mine = jnp.where(lane < width, lane // vecs, lane % 8) == comp
    return jnp.sum(jnp.where(mine, gram, 0.0), axis=0, keepdims=True)


def early_kernel(prev_ref, t0, t1, t2, lines_ref, gram_ref, *turned_refs):
    comps, vecs, rows = prev_ref.shape
    width = comps * vecs
    lines = jnp.concatenate([lines_of(t[...], rows) for t in (t0, t1, t2)], axis=0)
    lines_ref[...] = lines
    prev = prev_ref[...].reshape(width, rows)
    full = dot(prev, prev, NT, HIGHEST)
    owner = iota((vecs, width), 1) // vecs
    total = jnp.where(owner == 0, full[:vecs], 0.0)
    for c in range(1, comps):
        total = total + jnp.where(owner == c, full[c * vecs : (c + 1) * vecs], 0.0)
    gram_ref[:vecs, :] = jnp.concatenate([total, jnp.zeros((vecs, 128 - width), jnp.float32)], axis=1)
    against = jnp.concatenate([prev, lines, jnp.zeros((8, rows), jnp.float32)], axis=0)
    for ref, part in zip(turned_refs, split(against.T)):
        ref[...] = part
    gram = dot(lines, against, NT, HIGHEST)
    result = jnp.zeros((8, 128), jnp.float32)
    for k in range(S - 1):
        line = collect(gram[k * 8 : (k + 1) * 8], width, vecs)
        result = jnp.where(iota((8, 128), 0) == k, jnp.broadcast_to(line, result.shape), result)
    gram_ref[vecs:, :] = result


def last_kernel(own, a, b, c, d, choose, aux, high, low, early, t0, t1, t2, line_ref, gram_ref):
    pieces = [ref[...] for ref in (own, a, b, c, d)]
    tile = multiply(choose[...], pieces, aux[8 * S - 8 : 8 * S, :], high[...], low[...])
    rows = line_ref.shape[1]
    vecs = early.shape[0] - 8
    width = COMPS * vecs
    last = lines_of(tile, rows)
    line_ref[...] = last
    parts = [part.astype(jnp.float32) for part in split(last)]
    left = jnp.concatenate(parts + [jnp.zeros_like(last)], axis=0).astype(jnp.bfloat16)
    products = dot(left, t0[...]) + dot(left, t1[...]) + dot(left, t2[...])
    gram = products[:8] + (products[8:16] + products[16:24])
    square = jnp.sum(last * last, axis=1, keepdims=True)
    gram = jnp.where(iota(gram.shape, 1) == width + 8 * (S - 1) + iota(gram.shape, 0), square, gram)
    line = collect(gram, width, vecs)
    gram_ref[:vecs, :] = early[:vecs, :]
    gram_ref[vecs:, :] = jnp.where(
        iota((8, 128), 0) == S - 1, jnp.broadcast_to(line, (8, 128)), early[vecs:, :]
    )


def finish_kernel(total, gram_in, prev_ref, lines, last, basis_ref, factors_ref):
    comps, vecs, rows = prev_ref.shape
    width = comps * vecs
    gram = gram_in[...] * (1.0 / total)
    small = gram[vecs:]
    lane, comp = iota((8, 128), 1), iota((8, 128), 0)
    in_prev = (lane < width) & (lane // vecs == comp)
    coef, cross = [], []
    for k in range(S):
        line = jnp.broadcast_to(small[k : k + 1], (8, 128))
        coef.append(jnp.where(in_prev, line, 0.0))
        cross.append([jnp.where(lane == width + 8 * l + comp, line, 0.0) for l in range(k + 1)])
    coefs = jnp.concatenate(coef, axis=0)
    square = jnp.concatenate([gram[:vecs]] * comps, axis=0)
    r, q = iota(square.shape, 0), iota(square.shape, 1)
    square = jnp.where(r // vecs == q // vecs, square, 0.0) - jnp.where(r == q, 2.0, 0.0)
    turned = dot(coefs[:, :width], square, precision=HIGHEST)
    prev = prev_ref[...].reshape(width, rows)
    basis = jnp.concatenate([lines[...], last[...]], axis=0)
    projected = basis - dot(coefs[:, :width], prev, precision=HIGHEST)
    unit, scale = {}, {}
    for l in range(S):
        for k in range(l, S):
            value = turned[k * 8 : (k + 1) * 8] * coef[l] + cross[k][l]
            value = jnp.sum(value, axis=1, keepdims=True)
            for m in range(l):
                value = value - (unit[k, m] * scale[m]) * unit[l, m]
            if k == l:
                scale[l] = value
            else:
                unit[k, l] = value / scale[l]
    roots = [jnp.sqrt(scale[k]) for k in range(S)]
    lower = {(k, l): unit[k, l] * roots[l] if l < k else roots[k] for k in range(S) for l in range(k + 1)}
    vectors = []
    for k in range(S):
        value = projected[k * 8 : (k + 1) * 8]
        for l in range(k):
            value = value - unit[k, l] * vectors[l]
        vectors.append(value)
        value = value / roots[k]
        for c in range(comps):
            basis_ref[c, k : k + 1, :] = value[c : c + 1]
    for c in range(comps):
        factors_ref[c, :, :vecs] = small[:S, c * vecs : (c + 1) * vecs]
    for k in range(S):
        line = jnp.zeros((8, 128), jnp.float32)
        for l in range(k + 1):
            line = jnp.where(lane == l, lower[k, l], line)
        for c in range(comps):
            factors_ref[c, k : k + 1, vecs:] = line[c : c + 1, :S]


VMEM = pl.BlockSpec(memory_space=pltpu.VMEM)
HBM = pl.BlockSpec(memory_space=pltpu.HBM)


def in_hbm(*arrays):
    return [pltpu.with_memory_space_constraint(x, pltpu.HBM) for x in arrays]


def call(kernel, outs, specs, flops, moved, scratch=()):
    shapes = [jax.ShapeDtypeStruct(shape, kind) for shape, kind in outs]
    return pl.pallas_call(
        kernel,
        out_shape=shapes if len(shapes) > 1 else shapes[0],
        in_specs=specs,
        out_specs=[VMEM] * len(shapes) if len(shapes) > 1 else VMEM,
        scratch_shapes=list(scratch),
        compiler_params=pltpu.CompilerParams(vmem_limit_bytes=24 * 1024 * 1024),
        cost_estimate=pl.CostEstimate(flops=flops, bytes_accessed=moved, transcendentals=0),
    )


def send(value, target):
    return lax.ppermute(value, "dom", [(d, target[d]) for d in range(lax.axis_size("dom"))])


def neighbours(length, step, odd):
    target = {}
    for d in range(length):
        other = d + step if (d // step) % 2 == odd else d - step
        target[d] = other if 0 <= other < length else None
    return target


def ghosts(tile):
    length = lax.axis_size("dom")
    last = length - 1
    near, across = neighbours(length, 1, 0), neighbours(length, 1, 1)
    far_even, far_odd = neighbours(length, FAR, 0), neighbours(length, FAR, 1)
    across.update({0: 1, 1: 2, 2: 0, last: last - 1, last - 1: last - 2, last - 2: last})
    for d in range(length):
        if far_odd[d] is None:
            far_odd[d] = d ^ 1
    far_odd.update({0: 3, 3: 0, 1: 2, 2: 1})
    far_odd.update({last: last - 3, last - 3: last, last - 1: last - 2, last - 2: last - 1})
    return [send(tile, target) for target in (near, far_odd, far_even, across)]


def summed(value):
    length = lax.axis_size("dom")
    value = value + send(value, {d: d ^ 1 for d in range(length)})
    step = 2
    while step < length:
        size = min(4, length // step)
        groups = [
            [low + step * k for k in range(size)]
            for low in range(length)
            if low // step % size == 0
        ]
        parts = jnp.broadcast_to(value, (size,) + value.shape)
        parts = lax.all_to_all(parts, "dom", 0, 0, axis_index_groups=groups)
        value = parts[0] + parts[1]
        if size == 4:
            value = value + (parts[2] + parts[3])
        step *= size
    return value


def local(strips, columns, send_list, send_count, shifts, prev_basis, mix):
    comps, vecs, rows = prev_basis.shape
    blocks = columns.shape[0]
    width = strips.shape[1]
    f32, bf16, dma = jnp.float32, jnp.bfloat16, pltpu.SemaphoreType.DMA
    tile_out = ((comps * blocks, 128), f32)
    tile = call(
        start_kernel,
        [((comps * blocks + 8, 128), f32)],
        [HBM] * 4,
        600000,
        250000,
        [
            pltpu.VMEM(prev_basis.shape, f32),
            pltpu.VMEM(mix.shape, f32),
            pltpu.VMEM(send_list.shape, jnp.int32),
            pltpu.VMEM(send_count.shape, jnp.int32),
            dma((4,)),
        ],
    )(*in_hbm(prev_basis, mix, send_list, send_count))
    high, low, aux = call(
        prepare_kernel,
        [((width, rows), bf16), ((width, rows), bf16), ((8 * S + 8, 128), f32)],
        [HBM] * 3,
        1000000,
        1000000,
        [
            pltpu.VMEM((4, rows // 4, width), f32),
            pltpu.VMEM(columns.shape[::-1], jnp.int32),
            pltpu.SMEM(shifts.shape, f32),
            dma((6,)),
        ],
    )(*in_hbm(strips, columns.T, shifts))
    tiles = []
    length = lax.axis_size("dom")
    tile, choose = call(
        lambda *refs: first_kernel(length, *refs),
        [tile_out, ((4 * comps * blocks, 128), bf16)],
        [VMEM] * 8,
        50000000,
        600000,
    )(tile, *ghosts(tile), aux, high, low)
    tiles.append(tile)
    for step in (1, 2):
        tile = call(
            lambda *refs, step=step: middle_kernel(step, *refs), [tile_out], [VMEM] * 9, 50000000, 600000
        )(tile, *ghosts(tile), choose, aux, high, low)
        tiles.append(tile)
    received = ghosts(tile)
    gram_out = ((vecs + 8, 128), f32)
    lines, early, *turned = call(
        early_kernel,
        [((8 * S - 8, rows), f32), gram_out] + [((rows, 128), bf16)] * 3,
        [VMEM] * 4,
        60000000,
        250000,
    )(prev_basis, *tiles)
    last, gram = call(
        last_kernel, [((8, rows), f32), gram_out], [VMEM] * 13, 80000000, 900000
    )(tile, *received, choose, aux, high, low, early, *turned)
    total = float(length * rows)
    basis, factors = call(
        lambda *refs: finish_kernel(total, *refs),
        [((comps, S, rows), f32), ((comps, S, vecs + S), f32)],
        [VMEM] * 4,
        50000000,
        400000,
    )(summed(gram), prev_basis, lines, last)
    return basis, jnp.swapaxes(factors, 1, 2)


def solution(mesh):
    in_specs = (
        P("dom", None),
        P("dom", None),
        P("dom", None, None),
        P("dom", None),
        P(),
        P(None, None, "dom"),
        P(),
    )
    out_specs = (P(None, None, "dom"), P())
    return jax.shard_map(local, mesh=mesh, in_specs=in_specs, out_specs=out_specs, check_vma=False)
```

```python
import jax
import jax.numpy as jnp
from jax import lax
from jax.experimental import pallas as pl
from jax.experimental.pallas import tpu as pltpu
from jax.sharding import PartitionSpec as P

BLOCK = 64
S = 4
FAR = 8
COMPS = 3
DEAD = 1000.0
HIGHEST = lax.Precision.HIGHEST
NN = (((1,), (0,)), ((), ()))
NT = (((1,), (1,)), ((), ()))


def dot(a, b, dims=NN, precision=None):
    return lax.dot_general(a, b, dims, precision=precision, preferred_element_type=jnp.float32)


def iota(shape, axis):
    return lax.broadcasted_iota(jnp.int32, shape, axis)


def packed(tile, tail=None):
    low = iota((8, 128), 1) < BLOCK
    last = tile[16:] if tail is None else jnp.where(low, tile[16:], tail)
    return jnp.concatenate([jnp.where(low, tile[:8], tile[8:16]), last], axis=0)


def unpacked(sent):
    low = iota((8, 128), 1) < BLOCK
    pair, last = sent[:8], sent[8:]
    turned, rest = pltpu.roll(pair, BLOCK, 1), pltpu.roll(last, BLOCK, 1)
    parts = [jnp.where(low, pair, turned), jnp.where(low, turned, pair), jnp.where(low, last, rest)]
    return jnp.concatenate(parts, axis=0), rest


PLACES = {
    (0, 0): (0, 0),
    (0, 1): (0, 32),
    (0, 2): (0, 56),
    (0, 3): (0, 72),
    (1, 0): (0, 80),
    (1, 2): (0, 112),
    (1, 1): (1, 0),
    (1, 3): (1, 24),
    (2, 0): (1, 32),
    (2, 1): (1, 64),
    (2, 2): (1, 88),
    (2, 3): (1, 104),
}


def own_lanes(rows, width):
    return iota((rows, width), 1) // BLOCK == iota((rows, width), 0) % 8


def fold(masked):
    total = masked[:, :128]
    for t in range(1, masked.shape[1] // 128):
        total = total + masked[:, t * 128 : (t + 1) * 128]
    return total + pltpu.roll(total, BLOCK, 1)


def lines_of(tile, width):
    wide = jnp.concatenate([tile] * (width // 128), axis=1)
    wide = jnp.where(own_lanes(wide.shape[0], width), wide, 0.0)
    where = iota((8, width), 0)
    result = jnp.zeros((8, width), jnp.float32)
    for c in range(COMPS):
        line = jnp.sum(wide[c * 8 : (c + 1) * 8], axis=0, keepdims=True)
        result = jnp.where(where == c, jnp.broadcast_to(line, result.shape), result)
    return result


def split(x):
    parts = []
    for _ in range(3):
        parts.append(x.astype(jnp.bfloat16))
        x = x - parts[-1].astype(jnp.float32)
    return parts


def fetch(pairs, sems):
    copies = [pltpu.make_async_copy(src, dst, sems.at[i]) for i, (src, dst) in enumerate(pairs)]
    for copy in copies:
        copy.start()
    return copies


def start_kernel(prev_in, mix_in, list_in, count_in, sent_ref, tile_ref, prev_ref, mix_ref, list_ref, count_ref, sems):
    copies = fetch(
        [(prev_in, prev_ref), (mix_in, mix_ref), (list_in, list_ref), (count_in, count_ref)], sems
    )
    for copy in copies[1:]:
        copy.wait()
    comps, vecs, rows = prev_ref.shape
    eye = iota((vecs, vecs), 0) == iota((vecs, vecs), 1)
    weights = []
    for c in range(comps):
        line = jnp.broadcast_to(mix_ref[c : c + 1, :], eye.shape)
        weights.append(jnp.sum(jnp.where(eye, line, 0.0), axis=1, keepdims=True))
    order = list_ref[0].astype(jnp.float32)
    order = jnp.concatenate([order, jnp.zeros((4, 120), jnp.float32)], axis=1)
    meta = jnp.zeros((8, 128), jnp.float32)
    slot = iota((1, 128), 1)
    for link in range(4):
        live = slot < jnp.broadcast_to(count_ref[0:1, link : link + 1], slot.shape)
        line = jnp.where(live, order[link : link + 1], DEAD)
        line = pltpu.roll(jnp.broadcast_to(line, (8, 128)), BLOCK + 8 + 8 * link, 1)
        meta = jnp.where(iota((8, 128), 1) // 8 == BLOCK // 8 + link + 1, line, meta)
    copies[0].wait()
    own = own_lanes(8, rows)
    parts = []
    for c in range(comps):
        start = jnp.sum(weights[c] * prev_ref[c], axis=0, keepdims=True)
        line = jnp.broadcast_to(start, own.shape)
        parts.append(fold(jnp.where(own, line, 0.0)))
    tile = jnp.concatenate(parts, axis=0)
    tile_ref[...] = tile
    sent_ref[...] = packed(tile, meta)


def prepare_kernel(strips_in, columns_in, shifts_in, high_ref, low_ref, aux_ref, strips, columns, shifts, sems):
    parts = strips.shape[0]
    depth = strips.shape[1]
    pairs = [(columns_in, columns), (shifts_in, shifts)]
    pairs += [(strips_in.at[pl.ds(p * depth, depth)], strips.at[p]) for p in range(parts)]
    copies = fetch(pairs, sems)
    copies[0].wait()
    copies[1].wait()
    where = iota((8, 128), 1)
    table = jnp.zeros((8, 128), jnp.float32)
    eye = iota((8, 8), 0) == iota((8, 8), 1)
    for k in range(columns.shape[0]):
        line = jnp.broadcast_to(columns[k : k + 1, :].astype(jnp.float32), (8, 8))
        column = jnp.sum(jnp.where(eye, line, 0.0), axis=1, keepdims=True)
        table = jnp.where(where == k, column, table)
    for k in range(S):
        aux_ref[8 * k : 8 * k + 8, :] = jnp.full((8, 128), shifts[k], jnp.float32)
    aux_ref[8 * S :, :] = table
    for p in range(parts):
        copies[2 + p].wait()
        turned = strips[p].T
        high = turned.astype(jnp.bfloat16)
        high_ref[:, p * depth : (p + 1) * depth] = high
        low_ref[:, p * depth : (p + 1) * depth] = (turned - high.astype(jnp.float32)).astype(jnp.bfloat16)


def selection(table, metas, place, length):
    even, even_far = lax.rem(place, 2) == 0, lax.rem(place // FAR, 2) == 0
    near, far_odd, far_even, across = metas
    moved = (place == 1) | (place == length - 2)
    across = jnp.where(moved, far_odd, across)
    circle = jnp.where(moved, 48.0, 96.0)
    slots = [
        (place >= 1, jnp.where(even, circle, 24.0), jnp.where(even, across, near)),
        (place < length - 1, jnp.where(even, 24.0, circle), jnp.where(even, near, across)),
        (place >= FAR, jnp.where(even_far, 48.0, 72.0), jnp.where(even_far, far_odd, far_even)),
        (place < length - FAR, jnp.where(even_far, 72.0, 48.0), jnp.where(even_far, far_even, far_odd)),
    ]
    lane = iota((1, 128), 1)
    target = lane.astype(jnp.float32)
    for link, (valid, base, order) in enumerate(slots):
        order = order + jnp.where(valid, base, DEAD)
        target = jnp.where(lane // 8 == link + 1, order, target)
    target = jnp.broadcast_to(target, (8, 128))
    lane = iota((8, 128), 1).astype(jnp.float32)
    at = [
        jnp.sum(jnp.where(lane == table[:, k : k + 1], target, 0.0), axis=1, keepdims=True)
        for k in range(4)
    ]
    groups = [(lane == at[k] + float(8 * c)).astype(jnp.float32) for k in range(4) for c in range(COMPS)]
    return jnp.concatenate(groups, axis=0).astype(jnp.bfloat16)


def multiply(choose, pieces, shift, high, low):
    rows = 8 * COMPS
    ext = jnp.concatenate(pieces + [jnp.zeros((128 - 5 * rows, 128), jnp.float32)], axis=0)
    top = ext.astype(jnp.bfloat16).astype(jnp.float32)
    x = dot(choose, jnp.concatenate([top, ext - top], axis=1).astype(jnp.bfloat16))
    front = iota((rows, 256), 1) % 128 < BLOCK
    pairs = [
        jnp.where(front, x[2 * t * rows : (2 * t + 1) * rows], x[(2 * t + 1) * rows : (2 * t + 2) * rows])
        for t in range(2)
    ]
    left = jnp.concatenate(
        [
            jnp.concatenate([pair[:, half * 128 : (half + 1) * 128] for pair in pairs], axis=1)
            for half in range(2)
        ],
        axis=0,
    ).astype(jnp.bfloat16)
    both = dot(left, high) + dot(left, low)
    image = both[:rows] + both[rows:]
    image = fold(jnp.where(own_lanes(rows, image.shape[1]), image, 0.0))
    return image - jnp.concatenate([shift] * COMPS, axis=0) * pieces[0]


def first_kernel(length, own, a, b, c, d, aux, high, low, sent_ref, tile_ref, choose_ref):
    received = [unpacked(ref[...]) for ref in (a, b, c, d)]
    metas = [rest[:1] for _, rest in received]
    choose = selection(aux[8 * S :, :], metas, lax.axis_index("dom"), length)
    choose_ref[...] = choose
    pieces = [own[...]] + [tile for tile, _ in received]
    tile = multiply(choose, pieces, aux[:8, :], high[...], low[...])
    tile_ref[...] = tile
    sent_ref[...] = packed(tile)


def middle_kernel(step, own, a, b, c, d, choose, aux, high, low, sent_ref, tile_ref):
    pieces = [own[...]] + [unpacked(ref[...])[0] for ref in (a, b, c, d)]
    tile = multiply(choose[...], pieces, aux[8 * step : 8 * step + 8, :], high[...], low[...])
    tile_ref[...] = tile
    sent_ref[...] = packed(tile)


def collect(gram, width, vecs):
    lane, comp = iota(gram.shape, 1), iota(gram.shape, 0)
    mine = jnp.where(lane < width, lane // vecs, lane % 8) == comp
    return jnp.sum(jnp.where(mine, gram, 0.0), axis=0, keepdims=True)


def early_kernel(prev_ref, t0, t1, t2, lines_ref, gram_ref, *turned_refs):
    comps, vecs, rows = prev_ref.shape
    width = comps * vecs
    lines = jnp.concatenate([lines_of(t[...], rows) for t in (t0, t1, t2)], axis=0)
    lines_ref[...] = lines
    prev = prev_ref[...].reshape(width, rows)
    full = dot(prev, prev, NT, HIGHEST)
    full = jnp.concatenate([full, jnp.zeros((width, 128 - width), jnp.float32)], axis=1)
    lane = iota((8, 128), 1)
    tiles = [jnp.zeros((8, 128), jnp.float32)] * 2
    for (c, g), (t, first) in PLACES.items():
        at = c * vecs + 8 * g
        piece = pltpu.roll(full[at : at + 8], (first - at) % 128, 1)
        tiles[t] = jnp.where((lane >= first) & (lane < first + vecs - 8 * g), piece, tiles[t])
    gram_ref[:16, :] = jnp.concatenate(tiles, axis=0)
    against = jnp.concatenate([prev, lines, jnp.zeros((8, rows), jnp.float32)], axis=0)
    for ref, part in zip(turned_refs, split(against.T)):
        ref[...] = part
    gram = dot(lines, against, NT, HIGHEST)
    result = jnp.zeros((8, 128), jnp.float32)
    for k in range(S - 1):
        line = collect(gram[k * 8 : (k + 1) * 8], width, vecs)
        result = jnp.where(iota((8, 128), 0) == k, jnp.broadcast_to(line, result.shape), result)
    gram_ref[16:, :] = result


def last_kernel(vecs, own, a, b, c, d, choose, aux, high, low, early, t0, t1, t2, line_ref, gram_ref):
    pieces = [own[...]] + [unpacked(ref[...])[0] for ref in (a, b, c, d)]
    tile = multiply(choose[...], pieces, aux[8 * S - 8 : 8 * S, :], high[...], low[...])
    rows = line_ref.shape[1]
    width = COMPS * vecs
    last = lines_of(tile, rows)
    line_ref[...] = last
    parts = [part.astype(jnp.float32) for part in split(last)]
    left = jnp.concatenate(parts + [jnp.zeros_like(last)], axis=0).astype(jnp.bfloat16)
    products = dot(left, t0[...]) + dot(left, t1[...]) + dot(left, t2[...])
    gram = products[:8] + (products[8:16] + products[16:24])
    square = jnp.sum(last * last, axis=1, keepdims=True)
    gram = jnp.where(iota(gram.shape, 1) == width + 8 * (S - 1) + iota(gram.shape, 0), square, gram)
    line = collect(gram, width, vecs)
    gram_ref[:16, :] = early[:16, :]
    gram_ref[16:, :] = jnp.where(
        iota((8, 128), 0) == S - 1, jnp.broadcast_to(line, (8, 128)), early[16:, :]
    )


def finish_kernel(total, gram_in, prev_ref, lines, last, basis_ref, factors_ref):
    comps, vecs, rows = prev_ref.shape
    width = comps * vecs
    gram = gram_in[...] * (1.0 / total)
    small = gram[16:]
    lane, comp = iota((8, 128), 1), iota((8, 128), 0)
    in_prev = (lane < width) & (lane // vecs == comp)
    coef, cross = [], []
    for k in range(S):
        line = jnp.broadcast_to(small[k : k + 1], (8, 128))
        coef.append(jnp.where(in_prev, line, 0.0))
        cross.append([jnp.where(lane == width + 8 * l + comp, line, 0.0) for l in range(k + 1)])
    coefs = jnp.concatenate(coef, axis=0)
    pieces = []
    for c in range(comps):
        for g in range(vecs // 8):
            t, first = PLACES[c, g]
            at = c * vecs + 8 * g
            piece = pltpu.roll(gram[8 * t : 8 * t + 8], (at - first) % 128, 1)
            piece = jnp.where(lane < at + 8, 0.5 * piece, piece)
            piece = jnp.where((lane >= at) & (lane < (c + 1) * vecs), piece, 0.0)
            pieces.append(piece - jnp.where(lane == at + comp, 1.0, 0.0))
    half = jnp.concatenate(pieces, axis=0)
    turned = dot(coefs[:, :width], half, precision=HIGHEST)
    prev = prev_ref[...].reshape(width, rows)
    basis = jnp.concatenate([lines[...], last[...]], axis=0)
    projected = basis - dot(coefs[:, :width], prev, precision=HIGHEST)
    unit, scale = {}, {}
    for l in range(S):
        for k in range(l, S):
            value = turned[k * 8 : (k + 1) * 8] * coef[l] + turned[l * 8 : (l + 1) * 8] * coef[k] + cross[k][l]
            value = jnp.sum(value, axis=1, keepdims=True)
            for m in range(l):
                value = value - (unit[k, m] * scale[m]) * unit[l, m]
            if k == l:
                scale[l] = value
            else:
                unit[k, l] = value / scale[l]
    roots = [jnp.sqrt(scale[k]) for k in range(S)]
    lower = {(k, l): unit[k, l] * roots[l] if l < k else roots[k] for k in range(S) for l in range(k + 1)}
    vectors = []
    for k in range(S):
        value = projected[k * 8 : (k + 1) * 8]
        for l in range(k):
            value = value - unit[k, l] * vectors[l]
        vectors.append(value)
        value = value / roots[k]
        for c in range(comps):
            basis_ref[c, k : k + 1, :] = value[c : c + 1]
    for c in range(comps):
        factors_ref[c, :, :vecs] = small[:S, c * vecs : (c + 1) * vecs]
    for k in range(S):
        line = jnp.zeros((8, 128), jnp.float32)
        for l in range(k + 1):
            line = jnp.where(lane == l, lower[k, l], line)
        for c in range(comps):
            factors_ref[c, k : k + 1, vecs:] = line[c : c + 1, :S]


VMEM = pl.BlockSpec(memory_space=pltpu.VMEM)
HBM = pl.BlockSpec(memory_space=pltpu.HBM)


def in_hbm(*arrays):
    return [pltpu.with_memory_space_constraint(x, pltpu.HBM) for x in arrays]


def call(kernel, outs, specs, flops, moved, scratch=()):
    shapes = [jax.ShapeDtypeStruct(shape, kind) for shape, kind in outs]
    return pl.pallas_call(
        kernel,
        out_shape=shapes if len(shapes) > 1 else shapes[0],
        in_specs=specs,
        out_specs=[VMEM] * len(shapes) if len(shapes) > 1 else VMEM,
        scratch_shapes=list(scratch),
        compiler_params=pltpu.CompilerParams(vmem_limit_bytes=24 * 1024 * 1024),
        cost_estimate=pl.CostEstimate(flops=flops, bytes_accessed=moved, transcendentals=0),
    )


def send(value, target):
    return lax.ppermute(value, "dom", [(d, target[d]) for d in range(lax.axis_size("dom"))])


def neighbours(length, step, odd):
    target = {}
    for d in range(length):
        other = d + step if (d // step) % 2 == odd else d - step
        target[d] = other if 0 <= other < length else None
    return target


def ghosts(tile):
    length = lax.axis_size("dom")
    last = length - 1
    near, across = neighbours(length, 1, 0), neighbours(length, 1, 1)
    far_even, far_odd = neighbours(length, FAR, 0), neighbours(length, FAR, 1)
    across.update({0: 1, 1: 2, 2: 0, last: last - 1, last - 1: last - 2, last - 2: last})
    for d in range(length):
        if far_odd[d] is None:
            far_odd[d] = d ^ 1
    far_odd.update({0: 3, 3: 0, 1: 2, 2: 1})
    far_odd.update({last: last - 3, last - 3: last, last - 1: last - 2, last - 2: last - 1})
    return [send(tile, target) for target in (near, far_odd, far_even, across)]


def summed(value):
    length = lax.axis_size("dom")

    def fetched(step):
        return send(value, {d: d ^ (step | 1) for d in range(length)})

    value = value + fetched(1)
    step = 2
    while step < length:
        if 2 * step < length:
            farthest = fetched(3 * step)
            first, second = fetched(step), fetched(2 * step)
            value = (value + first) + (second + farthest)
        else:
            value = value + fetched(step)
        step *= 4
    return value


def local(strips, columns, send_list, send_count, shifts, prev_basis, mix):
    comps, vecs, rows = prev_basis.shape
    blocks = columns.shape[0]
    width = strips.shape[1]
    f32, bf16, dma = jnp.float32, jnp.bfloat16, pltpu.SemaphoreType.DMA
    tile_out = ((comps * blocks, 128), f32)
    sent_out = ((16, 128), f32)
    sent, tile = call(
        start_kernel,
        [sent_out, tile_out],
        [HBM] * 4,
        600000,
        250000,
        [
            pltpu.VMEM(prev_basis.shape, f32),
            pltpu.VMEM(mix.shape, f32),
            pltpu.VMEM(send_list.shape, jnp.int32),
            pltpu.VMEM(send_count.shape, jnp.int32),
            dma((4,)),
        ],
    )(*in_hbm(prev_basis, mix, send_list, send_count))
    high, low, aux = call(
        prepare_kernel,
        [((width, rows), bf16), ((width, rows), bf16), ((8 * S + 8, 128), f32)],
        [HBM] * 3,
        1000000,
        1000000,
        [
            pltpu.VMEM((4, rows // 4, width), f32),
            pltpu.VMEM(columns.shape[::-1], jnp.int32),
            pltpu.SMEM(shifts.shape, f32),
            dma((6,)),
        ],
    )(*in_hbm(strips, columns.T, shifts))
    tiles = []
    length = lax.axis_size("dom")
    sent, tile, choose = call(
        lambda *refs: first_kernel(length, *refs),
        [sent_out, tile_out, ((4 * comps * blocks, 128), bf16)],
        [VMEM] * 8,
        50000000,
        600000,
    )(tile, *ghosts(sent), aux, high, low)
    tiles.append(tile)
    for step in (1, 2):
        sent, tile = call(
            lambda *refs, step=step: middle_kernel(step, *refs),
            [sent_out, tile_out],
            [VMEM] * 9,
            50000000,
            600000,
        )(tile, *ghosts(sent), choose, aux, high, low)
        tiles.append(tile)
    received = ghosts(sent)
    gram_out = ((24, 128), f32)
    lines, early, *turned = call(
        early_kernel,
        [((8 * S - 8, rows), f32), gram_out] + [((rows, 128), bf16)] * 3,
        [VMEM] * 4,
        60000000,
        250000,
    )(prev_basis, *tiles)
    last, gram = call(
        lambda *refs: last_kernel(vecs, *refs),
        [((8, rows), f32), gram_out],
        [VMEM] * 13,
        80000000,
        900000,
    )(tile, *received, choose, aux, high, low, early, *turned)
    total = float(length * rows)
    basis, factors = call(
        lambda *refs: finish_kernel(total, *refs),
        [((comps, S, rows), f32), ((comps, S, vecs + S), f32)],
        [VMEM] * 4,
        50000000,
        400000,
    )(summed(gram), prev_basis, lines, last)
    return basis, jnp.swapaxes(factors, 1, 2)


def solution(mesh):
    in_specs = (
        P("dom", None),
        P("dom", None),
        P("dom", None, None),
        P("dom", None),
        P(),
        P(None, None, "dom"),
        P(),
    )
    out_specs = (P(None, None, "dom"), P())
    return jax.shard_map(local, mesh=mesh, in_specs=in_specs, out_specs=out_specs, check_vma=False)
```

```python
import jax
import jax.numpy as jnp
from jax import lax
from jax.experimental import pallas as pl
from jax.experimental.pallas import tpu as pltpu
from jax.sharding import PartitionSpec as P

BLOCK = 64
S = 4
FAR = 8
COMPS = 3
DEAD = 1000.0
HIGHEST = lax.Precision.HIGHEST
NN = (((1,), (0,)), ((), ()))
NT = (((1,), (1,)), ((), ()))


def dot(a, b, dims=NN, precision=None):
    return lax.dot_general(a, b, dims, precision=precision, preferred_element_type=jnp.float32)


def iota(shape, axis):
    return lax.broadcasted_iota(jnp.int32, shape, axis)


PLACES = {
    (0, 0): (0, 0),
    (0, 1): (0, 32),
    (0, 2): (0, 56),
    (0, 3): (0, 72),
    (1, 0): (0, 80),
    (1, 2): (0, 112),
    (1, 1): (1, 0),
    (1, 3): (1, 24),
    (2, 0): (1, 32),
    (2, 1): (1, 64),
    (2, 2): (1, 88),
    (2, 3): (1, 104),
}


def own_lanes(rows, width):
    return iota((rows, width), 1) // BLOCK == iota((rows, width), 0) % 8


def fold(masked):
    total = masked[:, :128]
    for t in range(1, masked.shape[1] // 128):
        total = total + masked[:, t * 128 : (t + 1) * 128]
    return total + pltpu.roll(total, BLOCK, 1)


def lines_of(tile, width):
    wide = jnp.concatenate([tile] * (width // 128), axis=1)
    wide = jnp.where(own_lanes(wide.shape[0], width), wide, 0.0)
    where = iota((8, width), 0)
    result = jnp.zeros((8, width), jnp.float32)
    for c in range(COMPS):
        line = jnp.sum(wide[c * 8 : (c + 1) * 8], axis=0, keepdims=True)
        result = jnp.where(where == c, jnp.broadcast_to(line, result.shape), result)
    return result


def split(x):
    parts = []
    for _ in range(3):
        parts.append(x.astype(jnp.bfloat16))
        x = x - parts[-1].astype(jnp.float32)
    return parts


def split_dot(x, parts):
    left = [part.astype(jnp.float32) for part in split(x)]
    left.append(jnp.zeros((-3 * x.shape[0] % 16, x.shape[1]), jnp.float32))
    left = jnp.concatenate([part for part in left if part.shape[0]], axis=0).astype(jnp.bfloat16)
    products = dot(left, parts[0]) + dot(left, parts[1]) + dot(left, parts[2])
    rows = x.shape[0]
    return products[:rows] + (products[rows : 2 * rows] + products[2 * rows : 3 * rows])


def fetch(pairs, sems):
    copies = [pltpu.make_async_copy(src, dst, sems.at[i]) for i, (src, dst) in enumerate(pairs)]
    for copy in copies:
        copy.start()
    return copies


def start_kernel(prev_in, mix_in, list_in, count_in, out_ref, prev_ref, mix_ref, list_ref, count_ref, sems):
    copies = fetch(
        [(prev_in, prev_ref), (mix_in, mix_ref), (list_in, list_ref), (count_in, count_ref)], sems
    )
    for copy in copies[1:]:
        copy.wait()
    comps, vecs, rows = prev_ref.shape
    eye = iota((vecs, vecs), 0) == iota((vecs, vecs), 1)
    weights = []
    for c in range(comps):
        line = jnp.broadcast_to(mix_ref[c : c + 1, :], eye.shape)
        weights.append(jnp.sum(jnp.where(eye, line, 0.0), axis=1, keepdims=True))
    order = list_ref[0].astype(jnp.float32)
    order = jnp.concatenate([order, jnp.zeros((4, 120), jnp.float32)], axis=1)
    meta = jnp.zeros((8, 128), jnp.float32)
    slot = iota((1, 128), 1)
    for link in range(4):
        live = slot < jnp.broadcast_to(count_ref[0:1, link : link + 1], slot.shape)
        line = jnp.where(live, order[link : link + 1], DEAD)
        line = pltpu.roll(jnp.broadcast_to(line, (8, 128)), 8 + 8 * link, 1)
        meta = jnp.where(iota((8, 128), 1) // 8 == link + 1, line, meta)
    out_ref[8 * comps :, :] = meta
    copies[0].wait()
    own = own_lanes(8, rows)
    for c in range(comps):
        start = jnp.sum(weights[c] * prev_ref[c], axis=0, keepdims=True)
        line = jnp.broadcast_to(start, own.shape)
        out_ref[c * 8 : (c + 1) * 8, :] = fold(jnp.where(own, line, 0.0))


def prepare_kernel(strips_in, columns_in, shifts_in, high_ref, low_ref, aux_ref, strips, columns, shifts, sems):
    parts = strips.shape[0]
    depth = strips.shape[1]
    pairs = [(columns_in, columns), (shifts_in, shifts)]
    pairs += [(strips_in.at[pl.ds(p * depth, depth)], strips.at[p]) for p in range(parts)]
    copies = fetch(pairs, sems)
    copies[0].wait()
    copies[1].wait()
    where = iota((8, 128), 1)
    table = jnp.zeros((8, 128), jnp.float32)
    eye = iota((8, 8), 0) == iota((8, 8), 1)
    for k in range(columns.shape[0]):
        line = jnp.broadcast_to(columns[k : k + 1, :].astype(jnp.float32), (8, 8))
        column = jnp.sum(jnp.where(eye, line, 0.0), axis=1, keepdims=True)
        table = jnp.where(where == k, column, table)
    for k in range(S):
        aux_ref[8 * k : 8 * k + 8, :] = jnp.full((8, 128), shifts[k], jnp.float32)
    aux_ref[8 * S :, :] = table
    for p in range(parts):
        copies[2 + p].wait()
        turned = strips[p].T
        high = turned.astype(jnp.bfloat16)
        high_ref[:, p * depth : (p + 1) * depth] = high
        low_ref[:, p * depth : (p + 1) * depth] = (turned - high.astype(jnp.float32)).astype(jnp.bfloat16)


def selection(table, metas, place, length):
    even, even_far = lax.rem(place, 2) == 0, lax.rem(place // FAR, 2) == 0
    near, far_odd, far_even, across = metas
    moved = (place == 2) | (place == length - 3)
    across = jnp.where(moved, far_odd, across)
    circle = jnp.where(moved, 48.0, 96.0)
    slots = [
        (place >= 1, jnp.where(even, circle, 24.0), jnp.where(even, across, near)),
        (place < length - 1, jnp.where(even, 24.0, circle), jnp.where(even, near, across)),
        (place >= FAR, jnp.where(even_far, 48.0, 72.0), jnp.where(even_far, far_odd, far_even)),
        (place < length - FAR, jnp.where(even_far, 72.0, 48.0), jnp.where(even_far, far_even, far_odd)),
    ]
    lane = iota((1, 128), 1)
    target = lane.astype(jnp.float32)
    for link, (valid, base, order) in enumerate(slots):
        order = order + jnp.where(valid, base, DEAD)
        target = jnp.where(lane // 8 == link + 1, order, target)
    target = jnp.broadcast_to(target, (8, 128))
    lane = iota((8, 128), 1).astype(jnp.float32)
    at = [
        jnp.sum(jnp.where(lane == table[:, k : k + 1], target, 0.0), axis=1, keepdims=True)
        for k in range(4)
    ]
    groups = [(lane == at[k] + float(8 * c)).astype(jnp.float32) for k in range(4) for c in range(COMPS)]
    return jnp.concatenate(groups, axis=0).astype(jnp.bfloat16)


def multiply(choose, pieces, shift, high, low):
    rows = 8 * COMPS
    ext = jnp.concatenate(pieces + [jnp.zeros((128 - 5 * rows, 128), jnp.float32)], axis=0)
    top = ext.astype(jnp.bfloat16).astype(jnp.float32)
    x = dot(choose, jnp.concatenate([top, ext - top], axis=1).astype(jnp.bfloat16))
    front = iota((rows, 256), 1) % 128 < BLOCK
    pairs = [
        jnp.where(front, x[2 * t * rows : (2 * t + 1) * rows], x[(2 * t + 1) * rows : (2 * t + 2) * rows])
        for t in range(2)
    ]
    left = jnp.concatenate(
        [
            jnp.concatenate([pair[:, half * 128 : (half + 1) * 128] for pair in pairs], axis=1)
            for half in range(2)
        ],
        axis=0,
    ).astype(jnp.bfloat16)
    both = dot(left, high) + dot(left, low)
    image = both[:rows] + both[rows:]
    image = fold(jnp.where(own_lanes(rows, image.shape[1]), image, 0.0))
    return image - jnp.concatenate([shift] * COMPS, axis=0) * pieces[0]


def first_kernel(length, own, a, b, c, d, aux, high, low, tile_ref, choose_ref):
    rows = 8 * COMPS
    refs = (own, a, b, c, d)
    pieces = [ref[:rows, :] for ref in refs]
    metas = [ref[rows : rows + 1, :] for ref in refs[1:]]
    choose = selection(aux[8 * S :, :], metas, lax.axis_index("dom"), length)
    choose_ref[...] = choose
    tile_ref[...] = multiply(choose, pieces, aux[:8, :], high[...], low[...])


def middle_kernel(step, own, a, b, c, d, choose, aux, high, low, tile_ref):
    pieces = [ref[...] for ref in (own, a, b, c, d)]
    tile_ref[...] = multiply(choose[...], pieces, aux[8 * step : 8 * step + 8, :], high[...], low[...])


def collect(gram, width, vecs):
    lane, comp = iota(gram.shape, 1), iota(gram.shape, 0)
    mine = jnp.where(lane < width, lane // vecs, lane % 8) == comp
    return jnp.sum(jnp.where(mine, gram, 0.0), axis=0, keepdims=True)


def early_kernel(prev_ref, t0, t1, t2, lines_ref, gram_ref, *split_refs):
    comps, vecs, rows = prev_ref.shape
    width = comps * vecs
    lines = jnp.concatenate([lines_of(t[...], rows) for t in (t0, t1, t2)], axis=0)
    lines_ref[...] = lines
    prev = prev_ref[...].reshape(width, rows)
    full = dot(prev, prev, NT, HIGHEST)
    full = jnp.concatenate([full, jnp.zeros((width, 128 - width), jnp.float32)], axis=1)
    lane = iota((8, 128), 1)
    tiles = [jnp.zeros((8, 128), jnp.float32)] * 2
    for (c, g), (t, first) in PLACES.items():
        at = c * vecs + 8 * g
        piece = pltpu.roll(full[at : at + 8], (first - at) % 128, 1)
        tiles[t] = jnp.where((lane >= first) & (lane < first + vecs - 8 * g), piece, tiles[t])
    gram_ref[:16, :] = jnp.concatenate(tiles, axis=0)
    against = jnp.concatenate([prev, lines, jnp.zeros((8, rows), jnp.float32)], axis=0)
    for ref, part in zip(split_refs, split(against.T) + split(prev)):
        ref[...] = part
    gram = dot(lines, against, NT, HIGHEST)
    result = jnp.zeros((8, 128), jnp.float32)
    for k in range(S - 1):
        line = collect(gram[k * 8 : (k + 1) * 8], width, vecs)
        result = jnp.where(iota((8, 128), 0) == k, jnp.broadcast_to(line, result.shape), result)
    gram_ref[16:, :] = result


def last_kernel(vecs, own, a, b, c, d, choose, aux, high, low, early, t0, t1, t2, line_ref, gram_ref):
    pieces = [ref[...] for ref in (own, a, b, c, d)]
    tile = multiply(choose[...], pieces, aux[8 * S - 8 : 8 * S, :], high[...], low[...])
    rows = line_ref.shape[1]
    width = COMPS * vecs
    last = lines_of(tile, rows)
    line_ref[...] = last
    gram = split_dot(last, (t0[...], t1[...], t2[...]))
    square = jnp.sum(last * last, axis=1, keepdims=True)
    gram = jnp.where(iota(gram.shape, 1) == width + 8 * (S - 1) + iota(gram.shape, 0), square, gram)
    line = collect(gram, width, vecs)
    gram_ref[:16, :] = early[:16, :]
    gram_ref[16:, :] = jnp.where(
        iota((8, 128), 0) == S - 1, jnp.broadcast_to(line, (8, 128)), early[16:, :]
    )


def finish_kernel(total, vecs, gram_in, p0, p1, p2, lines, last, basis_ref, factors_ref):
    comps = COMPS
    width = comps * vecs
    gram = gram_in[...] * (1.0 / total)
    small = gram[16:]
    lane, comp = iota((8, 128), 1), iota((8, 128), 0)
    in_prev = (lane < width) & (lane // vecs == comp)
    coef, cross = [], []
    for k in range(S):
        line = jnp.broadcast_to(small[k : k + 1], (8, 128))
        coef.append(jnp.where(in_prev, line, 0.0))
        cross.append([jnp.where(lane == width + 8 * l + comp, line, 0.0) for l in range(k + 1)])
    coefs = jnp.concatenate(coef, axis=0)
    pieces = []
    for c in range(comps):
        for g in range(vecs // 8):
            t, first = PLACES[c, g]
            at = c * vecs + 8 * g
            piece = pltpu.roll(gram[8 * t : 8 * t + 8], (at - first) % 128, 1)
            piece = jnp.where(lane < at + 8, 0.5 * piece, piece)
            piece = jnp.where((lane >= at) & (lane < (c + 1) * vecs), piece, 0.0)
            pieces.append(piece - jnp.where(lane == at + comp, 1.0, 0.0))
    half = split(jnp.concatenate(pieces, axis=0))
    turned = split_dot(coefs[:, :width], half)
    basis = jnp.concatenate([lines[...], last[...]], axis=0)
    projected = basis - split_dot(coefs[:, :width], (p0[...], p1[...], p2[...]))
    unit, scale = {}, {}
    for l in range(S):
        for k in range(l, S):
            value = turned[k * 8 : (k + 1) * 8] * coef[l] + turned[l * 8 : (l + 1) * 8] * coef[k] + cross[k][l]
            value = jnp.sum(value, axis=1, keepdims=True)
            for m in range(l):
                value = value - (unit[k, m] * scale[m]) * unit[l, m]
            if k == l:
                scale[l] = value
            else:
                unit[k, l] = value / scale[l]
    roots = [jnp.sqrt(scale[k]) for k in range(S)]
    lower = {(k, l): unit[k, l] * roots[l] if l < k else roots[k] for k in range(S) for l in range(k + 1)}
    vectors = []
    for k in range(S):
        value = projected[k * 8 : (k + 1) * 8]
        for l in range(k):
            value = value - unit[k, l] * vectors[l]
        vectors.append(value)
        value = value / roots[k]
        for c in range(comps):
            basis_ref[c, k : k + 1, :] = value[c : c + 1]
    for c in range(comps):
        factors_ref[c, :, :vecs] = small[:S, c * vecs : (c + 1) * vecs]
    for k in range(S):
        line = jnp.zeros((8, 128), jnp.float32)
        for l in range(k + 1):
            line = jnp.where(lane == l, lower[k, l], line)
        for c in range(comps):
            factors_ref[c, k : k + 1, vecs:] = line[c : c + 1, :S]


VMEM = pl.BlockSpec(memory_space=pltpu.VMEM)
HBM = pl.BlockSpec(memory_space=pltpu.HBM)


def in_hbm(*arrays):
    return [pltpu.with_memory_space_constraint(x, pltpu.HBM) for x in arrays]


def call(kernel, outs, specs, flops, moved, scratch=()):
    shapes = [jax.ShapeDtypeStruct(shape, kind) for shape, kind in outs]
    return pl.pallas_call(
        kernel,
        out_shape=shapes if len(shapes) > 1 else shapes[0],
        in_specs=specs,
        out_specs=[VMEM] * len(shapes) if len(shapes) > 1 else VMEM,
        scratch_shapes=list(scratch),
        compiler_params=pltpu.CompilerParams(vmem_limit_bytes=24 * 1024 * 1024),
        cost_estimate=pl.CostEstimate(flops=flops, bytes_accessed=moved, transcendentals=0),
    )


def send(value, target):
    return lax.ppermute(value, "dom", [(d, target[d]) for d in range(lax.axis_size("dom"))])


def neighbours(length, step, odd):
    target = {}
    for d in range(length):
        other = d + step if (d // step) % 2 == odd else d - step
        target[d] = other if 0 <= other < length else None
    return target


def ghosts(tile):
    length = lax.axis_size("dom")
    last = length - 1
    near, across = neighbours(length, 1, 0), neighbours(length, 1, 1)
    far_even, far_odd = neighbours(length, FAR, 0), neighbours(length, FAR, 1)
    across.update({0: 2, 2: 1, 1: 0, last: last - 2, last - 2: last - 1, last - 1: last})
    for d in range(length):
        if far_odd[d] is None:
            far_odd[d] = d ^ 1
    far_odd.update({1: 2, 2: 3, 3: 0, 0: 1})
    far_odd.update({last - 1: last - 2, last - 2: last - 3, last - 3: last, last: last - 1})
    return [send(tile, target) for target in (near, far_odd, far_even, across)]


def summed(value):
    length = lax.axis_size("dom")

    def fetched(step):
        return send(value, {d: d ^ (step | 1) for d in range(length)})

    value = value + fetched(1)
    step = 2
    while step < length:
        if 2 * step < length:
            farthest = fetched(3 * step)
            first, second = fetched(step), fetched(2 * step)
            value = (value + first) + (second + farthest)
        else:
            value = value + fetched(step)
        step *= 4
    return value


def local(strips, columns, send_list, send_count, shifts, prev_basis, mix):
    comps, vecs, rows = prev_basis.shape
    blocks = columns.shape[0]
    width = strips.shape[1]
    f32, bf16, dma = jnp.float32, jnp.bfloat16, pltpu.SemaphoreType.DMA
    tile_out = ((comps * blocks, 128), f32)
    tile = call(
        start_kernel,
        [((comps * blocks + 8, 128), f32)],
        [HBM] * 4,
        600000,
        250000,
        [
            pltpu.VMEM(prev_basis.shape, f32),
            pltpu.VMEM(mix.shape, f32),
            pltpu.VMEM(send_list.shape, jnp.int32),
            pltpu.VMEM(send_count.shape, jnp.int32),
            dma((4,)),
        ],
    )(*in_hbm(prev_basis, mix, send_list, send_count))
    high, low, aux = call(
        prepare_kernel,
        [((width, rows), bf16), ((width, rows), bf16), ((8 * S + 8, 128), f32)],
        [HBM] * 3,
        1000000,
        1000000,
        [
            pltpu.VMEM((4, rows // 4, width), f32),
            pltpu.VMEM(columns.shape[::-1], jnp.int32),
            pltpu.SMEM(shifts.shape, f32),
            dma((6,)),
        ],
    )(*in_hbm(strips, columns.T, shifts))
    tiles = []
    length = lax.axis_size("dom")
    tile, choose = call(
        lambda *refs: first_kernel(length, *refs),
        [tile_out, ((4 * comps * blocks, 128), bf16)],
        [VMEM] * 8,
        50000000,
        600000,
    )(tile, *ghosts(tile), aux, high, low)
    tiles.append(tile)
    for step in (1, 2):
        tile = call(
            lambda *refs, step=step: middle_kernel(step, *refs), [tile_out], [VMEM] * 9, 50000000, 600000
        )(tile, *ghosts(tile), choose, aux, high, low)
        tiles.append(tile)
    received = ghosts(tile)
    gram_out = ((24, 128), f32)
    lines, early, *parts = call(
        early_kernel,
        [((8 * S - 8, rows), f32), gram_out] + [((rows, 128), bf16)] * 3 + [((comps * vecs, rows), bf16)] * 3,
        [VMEM] * 4,
        60000000,
        250000,
    )(prev_basis, *tiles)
    last, gram = call(
        lambda *refs: last_kernel(vecs, *refs),
        [((8, rows), f32), gram_out],
        [VMEM] * 13,
        80000000,
        900000,
    )(tile, *received, choose, aux, high, low, early, *parts[:3])
    total = float(length * rows)
    basis, factors = call(
        lambda *refs: finish_kernel(total, vecs, *refs),
        [((comps, S, rows), f32), ((comps, S, vecs + S), f32)],
        [VMEM] * 6,
        50000000,
        400000,
    )(summed(gram), *parts[3:], lines, last)
    return basis, jnp.swapaxes(factors, 1, 2)


def solution(mesh):
    in_specs = (
        P("dom", None),
        P("dom", None),
        P("dom", None, None),
        P("dom", None),
        P(),
        P(None, None, "dom"),
        P(),
    )
    out_specs = (P(None, None, "dom"), P())
    return jax.shard_map(local, mesh=mesh, in_specs=in_specs, out_specs=out_specs, check_vma=False)
```

```python
import jax
import jax.numpy as jnp
from jax import lax
from jax.experimental import pallas as pl
from jax.experimental.pallas import tpu as pltpu
from jax.sharding import PartitionSpec as P

BLOCK = 64
S = 4
FAR = 8
COMPS = 3
DEAD = 1000.0
HIGHEST = lax.Precision.HIGHEST
NN = (((1,), (0,)), ((), ()))
NT = (((1,), (1,)), ((), ()))


def dot(a, b, dims=NN, precision=None):
    return lax.dot_general(a, b, dims, precision=precision, preferred_element_type=jnp.float32)


def iota(shape, axis):
    return lax.broadcasted_iota(jnp.int32, shape, axis)


def packed(parts, tail=None):
    low = iota((8, 128), 1) < BLOCK
    last = parts[2] if tail is None else jnp.where(low, parts[2], tail)
    return jnp.concatenate([jnp.where(low, parts[0], parts[1]), last], axis=0)


def parts_of(tile):
    low = iota((8, 128), 1) < BLOCK
    turned = pltpu.roll(tile[:8], BLOCK, 1)
    return [jnp.where(low, tile[:8], turned), jnp.where(low, turned, tile[:8]), tile[8:]]


def opened(tile):
    low = iota((8, 128), 1) < BLOCK
    turned = pltpu.roll(tile[8:], BLOCK, 1)
    return jnp.concatenate([tile[:8], jnp.where(low, tile[8:], turned)], axis=0), turned[:1]


PLACES = {(c, g): (g % 2, (0, 8, 0, 0)[g] + 32 * c) for c in range(COMPS) for g in range(4)}
PLACES.update({(0, 2): (0, 96), (1, 2): (0, 112), (2, 2): (1, 96)})


def own_lanes(rows, width):
    return iota((rows, width), 1) // BLOCK == iota((rows, width), 0) % 8


def fold(masked):
    total = masked[:, :128]
    for t in range(1, masked.shape[1] // 128):
        total = total + masked[:, t * 128 : (t + 1) * 128]
    return total + pltpu.roll(total, BLOCK, 1)


def lines_of(tile, width):
    wide = jnp.concatenate([jnp.concatenate(parts_of(tile), axis=0)] * (width // 128), axis=1)
    wide = jnp.where(own_lanes(wide.shape[0], width), wide, 0.0)
    where = iota((8, width), 0)
    result = jnp.zeros((8, width), jnp.float32)
    for c in range(COMPS):
        line = jnp.sum(wide[c * 8 : (c + 1) * 8], axis=0, keepdims=True)
        result = jnp.where(where == c, jnp.broadcast_to(line, result.shape), result)
    return result


def split(x):
    parts = []
    for _ in range(3):
        parts.append(x.astype(jnp.bfloat16))
        x = x - parts[-1].astype(jnp.float32)
    return parts


def fetch(pairs, sems):
    copies = [pltpu.make_async_copy(src, dst, sems.at[i]) for i, (src, dst) in enumerate(pairs)]
    for copy in copies:
        copy.start()
    return copies


def start_kernel(prev_in, mix_in, list_in, count_in, tile_ref, prev_ref, mix_ref, list_ref, count_ref, sems):
    comps, vecs, rows = prev_ref.shape
    pairs = [(mix_in, mix_ref), (list_in, list_ref), (count_in, count_ref)]
    halves = [(c, pl.ds(h * (vecs // 2), vecs // 2)) for c in range(comps) for h in range(2)]
    pairs += [(prev_in.at[c, part], prev_ref.at[c, part]) for c, part in halves]
    copies = fetch(pairs, sems)
    for copy in copies[:3]:
        copy.wait()
    eye = iota((vecs, vecs), 0) == iota((vecs, vecs), 1)
    weights = []
    for c in range(comps):
        line = jnp.broadcast_to(mix_ref[c : c + 1, :], eye.shape)
        weights.append(jnp.sum(jnp.where(eye, line, 0.0), axis=1, keepdims=True))
    order = list_ref[0].astype(jnp.float32)
    order = jnp.concatenate([order, jnp.zeros((4, 120), jnp.float32)], axis=1)
    meta = jnp.zeros((8, 128), jnp.float32)
    slot = iota((1, 128), 1)
    for link in range(4):
        live = slot < jnp.broadcast_to(count_ref[0:1, link : link + 1], slot.shape)
        line = jnp.where(live, order[link : link + 1], DEAD)
        line = pltpu.roll(jnp.broadcast_to(line, (8, 128)), BLOCK + 8 + 8 * link, 1)
        meta = jnp.where(iota((8, 128), 1) // 8 == BLOCK // 8 + link + 1, line, meta)
    own = own_lanes(8, rows)
    parts = []
    for c in range(comps):
        copies[3 + 2 * c].wait()
        copies[4 + 2 * c].wait()
        start = jnp.sum(weights[c] * prev_ref[c], axis=0, keepdims=True)
        line = jnp.broadcast_to(start, own.shape)
        parts.append(fold(jnp.where(own, line, 0.0)))
    tile_ref[...] = packed(parts, meta)


def prepare_kernel(strips_in, columns_in, shifts_in, high_ref, low_ref, aux_ref, strips, columns, shifts, sems):
    parts = strips.shape[0]
    depth = strips.shape[1]
    pairs = [(columns_in, columns), (shifts_in, shifts)]
    pairs += [(strips_in.at[pl.ds(p * depth, depth)], strips.at[p]) for p in range(parts)]
    copies = fetch(pairs, sems)
    copies[0].wait()
    copies[1].wait()
    where = iota((8, 128), 1)
    table = jnp.zeros((8, 128), jnp.float32)
    eye = iota((8, 8), 0) == iota((8, 8), 1)
    for k in range(columns.shape[0]):
        line = jnp.broadcast_to(columns[k : k + 1, :].astype(jnp.float32), (8, 8))
        column = jnp.sum(jnp.where(eye, line, 0.0), axis=1, keepdims=True)
        table = jnp.where(where == k, column, table)
    for k in range(S):
        aux_ref[8 * k : 8 * k + 8, :] = jnp.full((8, 128), shifts[k], jnp.float32)
    aux_ref[8 * S :, :] = table
    for p in range(parts):
        copies[2 + p].wait()
        turned = strips[p].T
        high = turned.astype(jnp.bfloat16)
        high_ref[:, p * depth : (p + 1) * depth] = high
        low_ref[:, p * depth : (p + 1) * depth] = (turned - high.astype(jnp.float32)).astype(jnp.bfloat16)


def selection(table, metas, place, length):
    even, even_far = lax.rem(place, 2) == 0, lax.rem(place // FAR, 2) == 0
    near, far_odd, far_even, across = metas
    moved = (place == 2) | (place == length - 3)
    across = jnp.where(moved, far_odd, across)
    circle = jnp.where(moved, 32.0, 64.0)
    slots = [
        (place >= 1, jnp.where(even, circle, 16.0), jnp.where(even, across, near)),
        (place < length - 1, jnp.where(even, 16.0, circle), jnp.where(even, near, across)),
        (place >= FAR, jnp.where(even_far, 32.0, 48.0), jnp.where(even_far, far_odd, far_even)),
        (place < length - FAR, jnp.where(even_far, 48.0, 32.0), jnp.where(even_far, far_even, far_odd)),
    ]
    lane = iota((1, 128), 1)
    target = lane.astype(jnp.float32)
    for link, (valid, base, order) in enumerate(slots):
        order = order + jnp.where(valid, base, DEAD)
        target = jnp.where(lane // 8 == link + 1, order, target)
    target = jnp.broadcast_to(target, (8, 128))
    lane = iota((8, 128), 1).astype(jnp.float32)
    at = [
        jnp.sum(jnp.where(lane == table[:, k : k + 1], target, 0.0), axis=1, keepdims=True)
        for k in range(4)
    ]
    groups = [(lane == at[k] + float(8 * c)).astype(jnp.float32) for k in range(4) for c in range(2)]
    return jnp.concatenate(groups, axis=0).astype(jnp.bfloat16)


def multiply(choose, pieces, shift, high, low):
    ext = jnp.concatenate(pieces + [jnp.zeros((48, 128), jnp.float32)], axis=0)
    top = ext.astype(jnp.bfloat16).astype(jnp.float32)
    x = dot(choose, jnp.concatenate([top, ext - top], axis=1).astype(jnp.bfloat16))
    front = iota((8, 128), 1) < BLOCK
    halves = []
    for half in range(2):
        columns = []
        for t in range(2):
            a, b = [x[k * 16 : (k + 1) * 16, half * 128 : (half + 1) * 128] for k in (2 * t, 2 * t + 1)]
            one = jnp.where(front, a[:8], pltpu.roll(b[:8], BLOCK, 1))
            two = jnp.where(front, pltpu.roll(a[:8], BLOCK, 1), b[:8])
            columns.append(jnp.concatenate([one, two, jnp.where(front, a[8:], b[8:])], axis=0))
        halves.append(jnp.concatenate(columns, axis=1))
    left = jnp.concatenate(halves, axis=0).astype(jnp.bfloat16)
    both = dot(left, high) + dot(left, low)
    rows = 8 * COMPS
    image = both[:rows] + both[rows:]
    image = fold(jnp.where(own_lanes(rows, image.shape[1]), image, 0.0))
    image = packed([image[c * 8 : (c + 1) * 8] for c in range(COMPS)])
    return image - jnp.concatenate([shift] * 2, axis=0) * pieces[0]


def first_kernel(length, own, a, b, c, d, aux, high, low, tile_ref, choose_ref):
    tiles = [opened(ref[...]) for ref in (own, a, b, c, d)]
    metas = [meta for _, meta in tiles[1:]]
    choose = selection(aux[8 * S :, :], metas, lax.axis_index("dom"), length)
    choose_ref[...] = choose
    pieces = [tile for tile, _ in tiles]
    tile_ref[...] = multiply(choose, pieces, aux[:8, :], high[...], low[...])


def middle_kernel(step, own, a, b, c, d, choose, aux, high, low, tile_ref):
    pieces = [ref[...] for ref in (own, a, b, c, d)]
    tile_ref[...] = multiply(choose[...], pieces, aux[8 * step : 8 * step + 8, :], high[...], low[...])


def collect(gram, width, vecs):
    lane, comp = iota(gram.shape, 1), iota(gram.shape, 0)
    mine = jnp.where(lane < width, lane // vecs, lane % 8) == comp
    return jnp.sum(jnp.where(mine, gram, 0.0), axis=0, keepdims=True)


def early_kernel(prev_ref, t0, t1, t2, lines_ref, gram_ref, *turned_refs):
    comps, vecs, rows = prev_ref.shape
    width = comps * vecs
    lines = jnp.concatenate([lines_of(t[...], rows) for t in (t0, t1, t2)], axis=0)
    lines_ref[...] = lines
    prev = prev_ref[...].reshape(width, rows)
    full = dot(prev, prev, NT, HIGHEST)
    full = jnp.concatenate([full, jnp.zeros((width, 128 - width), jnp.float32)], axis=1)
    lane = iota((8, 128), 1)
    tiles = [jnp.zeros((8, 128), jnp.float32)] * 2
    for (c, g), (t, first) in PLACES.items():
        at = c * vecs + 8 * g
        piece = pltpu.roll(full[at : at + 8], (first - at) % 128, 1)
        tiles[t] = jnp.where((lane >= first) & (lane < first + vecs - 8 * g), piece, tiles[t])
    gram_ref[:16, :] = jnp.concatenate(tiles, axis=0)
    against = jnp.concatenate([prev, lines, jnp.zeros((8, rows), jnp.float32)], axis=0)
    for ref, part in zip(turned_refs, split(against.T)):
        ref[...] = part
    gram = dot(lines, against, NT, HIGHEST)
    result = jnp.zeros((8, 128), jnp.float32)
    for k in range(S - 1):
        line = collect(gram[k * 8 : (k + 1) * 8], width, vecs)
        result = jnp.where(iota((8, 128), 0) == k, jnp.broadcast_to(line, result.shape), result)
    gram_ref[16:, :] = result


def last_kernel(vecs, own, a, b, c, d, choose, aux, high, low, early, t0, t1, t2, line_ref, gram_ref):
    pieces = [ref[...] for ref in (own, a, b, c, d)]
    tile = multiply(choose[...], pieces, aux[8 * S - 8 : 8 * S, :], high[...], low[...])
    rows = line_ref.shape[1]
    width = COMPS * vecs
    last = lines_of(tile, rows)
    line_ref[...] = last
    parts = [part.astype(jnp.float32) for part in split(last)]
    left = jnp.concatenate(parts + [jnp.zeros_like(last)], axis=0).astype(jnp.bfloat16)
    products = dot(left, t0[...]) + dot(left, t1[...]) + dot(left, t2[...])
    gram = products[:8] + (products[8:16] + products[16:24])
    square = jnp.sum(last * last, axis=1, keepdims=True)
    gram = jnp.where(iota(gram.shape, 1) == width + 8 * (S - 1) + iota(gram.shape, 0), square, gram)
    line = collect(gram, width, vecs)
    gram_ref[:16, :] = early[:16, :]
    gram_ref[16:, :] = jnp.where(
        iota((8, 128), 0) == S - 1, jnp.broadcast_to(line, (8, 128)), early[16:, :]
    )


def finish_kernel(total, gram_in, prev_ref, lines, last, basis_ref, factors_ref):
    comps, vecs, rows = prev_ref.shape
    width = comps * vecs
    gram = gram_in[...] * (1.0 / total)
    small = gram[16:]
    lane, comp = iota((8, 128), 1), iota((8, 128), 0)
    in_prev = (lane < width) & (lane // vecs == comp)
    coef, cross = [], []
    for k in range(S):
        line = jnp.broadcast_to(small[k : k + 1], (8, 128))
        coef.append(jnp.where(in_prev, line, 0.0))
        cross.append([jnp.where(lane == width + 8 * l + comp, line, 0.0) for l in range(k + 1)])
    coefs = jnp.concatenate(coef, axis=0)
    pieces, turns = [], {}
    for c in range(comps):
        for g in range(vecs // 8):
            t, first = PLACES[c, g]
            at = c * vecs + 8 * g
            turn = t, (at - first) % 128
            if turn not in turns:
                piece = gram[8 * t : 8 * t + 8]
                turns[turn] = pltpu.roll(piece, turn[1], 1) if turn[1] else piece
            piece = turns[turn]
            piece = jnp.where(lane < at + 8, 0.5 * piece, piece)
            piece = jnp.where((lane >= at) & (lane < (c + 1) * vecs), piece, 0.0)
            pieces.append(piece - jnp.where(lane == at + comp, 1.0, 0.0))
    half = jnp.concatenate(pieces, axis=0)
    turned = dot(coefs[:, :width], half, precision=HIGHEST)
    prev = prev_ref[...].reshape(width, rows)
    basis = jnp.concatenate([lines[...], last[...]], axis=0)
    projected = basis - dot(coefs[:, :width], prev, precision=HIGHEST)
    unit, scale = {}, {}
    for l in range(S):
        for k in range(l, S):
            value = turned[k * 8 : (k + 1) * 8] * coef[l] + turned[l * 8 : (l + 1) * 8] * coef[k] + cross[k][l]
            value = jnp.sum(value, axis=1, keepdims=True)
            for m in range(l):
                value = value - (unit[k, m] * scale[m]) * unit[l, m]
            if k == l:
                scale[l] = value
            else:
                unit[k, l] = value / scale[l]
    roots = [jnp.sqrt(scale[k]) for k in range(S)]
    lower = {(k, l): unit[k, l] * roots[l] if l < k else roots[k] for k in range(S) for l in range(k + 1)}
    vectors = []
    for k in range(S):
        value = projected[k * 8 : (k + 1) * 8]
        for l in range(k):
            value = value - unit[k, l] * vectors[l]
        vectors.append(value)
        value = value / roots[k]
        for c in range(comps):
            basis_ref[c, k : k + 1, :] = value[c : c + 1]
    for c in range(comps):
        factors_ref[c, :, :vecs] = small[:S, c * vecs : (c + 1) * vecs]
    for k in range(S):
        line = jnp.zeros((8, 128), jnp.float32)
        for l in range(k + 1):
            line = jnp.where(lane == l, lower[k, l], line)
        for c in range(comps):
            factors_ref[c, k : k + 1, vecs:] = line[c : c + 1, :S]


VMEM = pl.BlockSpec(memory_space=pltpu.VMEM)
HBM = pl.BlockSpec(memory_space=pltpu.HBM)


def in_hbm(*arrays):
    return [pltpu.with_memory_space_constraint(x, pltpu.HBM) for x in arrays]


def call(kernel, outs, specs, flops, moved, scratch=()):
    shapes = [jax.ShapeDtypeStruct(shape, kind) for shape, kind in outs]
    return pl.pallas_call(
        kernel,
        out_shape=shapes if len(shapes) > 1 else shapes[0],
        in_specs=specs,
        out_specs=[VMEM] * len(shapes) if len(shapes) > 1 else VMEM,
        scratch_shapes=list(scratch),
        compiler_params=pltpu.CompilerParams(vmem_limit_bytes=24 * 1024 * 1024),
        cost_estimate=pl.CostEstimate(flops=flops, bytes_accessed=moved, transcendentals=0),
    )


def send(value, target):
    return lax.ppermute(value, "dom", [(d, target[d]) for d in range(lax.axis_size("dom"))])


def neighbours(length, step, odd):
    target = {}
    for d in range(length):
        other = d + step if (d // step) % 2 == odd else d - step
        target[d] = other if 0 <= other < length else None
    return target


def ghosts(tile):
    length = lax.axis_size("dom")
    last = length - 1
    near, across = neighbours(length, 1, 0), neighbours(length, 1, 1)
    far_even, far_odd = neighbours(length, FAR, 0), neighbours(length, FAR, 1)
    across.update({0: 2, 2: 1, 1: 0, last: last - 2, last - 2: last - 1, last - 1: last})
    for d in range(length):
        if far_odd[d] is None:
            far_odd[d] = d ^ 1
    far_odd.update({1: 2, 2: 3, 3: 0, 0: 1})
    far_odd.update({last - 1: last - 2, last - 2: last - 3, last - 3: last, last: last - 1})
    return [send(tile, target) for target in (near, far_odd, far_even, across)]


def summed(value):
    length = lax.axis_size("dom")

    def fetched(step):
        return send(value, {d: d ^ (step | 1) for d in range(length)})

    value = value + fetched(1)
    step = 2
    while step < length:
        if 2 * step < length:
            farthest = fetched(3 * step)
            first, second = fetched(step), fetched(2 * step)
            value = (value + first) + (second + farthest)
        else:
            value = value + fetched(step)
        step *= 4
    return value


def local(strips, columns, send_list, send_count, shifts, prev_basis, mix):
    comps, vecs, rows = prev_basis.shape
    blocks = columns.shape[0]
    width = strips.shape[1]
    f32, bf16, dma = jnp.float32, jnp.bfloat16, pltpu.SemaphoreType.DMA
    tile_out = ((2 * blocks, 128), f32)
    tile = call(
        start_kernel,
        [tile_out],
        [HBM] * 4,
        600000,
        250000,
        [
            pltpu.VMEM(prev_basis.shape, f32),
            pltpu.VMEM(mix.shape, f32),
            pltpu.VMEM(send_list.shape, jnp.int32),
            pltpu.VMEM(send_count.shape, jnp.int32),
            dma((9,)),
        ],
    )(*in_hbm(prev_basis, mix, send_list, send_count))
    high, low, aux = call(
        prepare_kernel,
        [((width, rows), bf16), ((width, rows), bf16), ((8 * S + 8, 128), f32)],
        [HBM] * 3,
        1000000,
        1000000,
        [
            pltpu.VMEM((4, rows // 4, width), f32),
            pltpu.VMEM(columns.shape[::-1], jnp.int32),
            pltpu.SMEM(shifts.shape, f32),
            dma((6,)),
        ],
    )(*in_hbm(strips, columns.T, shifts))
    tiles = []
    length = lax.axis_size("dom")
    tile, choose = call(
        lambda *refs: first_kernel(length, *refs),
        [tile_out, ((8 * blocks, 128), bf16)],
        [VMEM] * 8,
        50000000,
        600000,
    )(tile, *ghosts(tile), aux, high, low)
    tiles.append(tile)
    for step in (1, 2):
        tile = call(
            lambda *refs, step=step: middle_kernel(step, *refs), [tile_out], [VMEM] * 9, 50000000, 600000
        )(tile, *ghosts(tile), choose, aux, high, low)
        tiles.append(tile)
    received = ghosts(tile)
    gram_out = ((24, 128), f32)
    lines, early, *turned = call(
        early_kernel,
        [((8 * S - 8, rows), f32), gram_out] + [((rows, 128), bf16)] * 3,
        [VMEM] * 4,
        60000000,
        250000,
    )(prev_basis, *tiles)
    last, gram = call(
        lambda *refs: last_kernel(vecs, *refs),
        [((8, rows), f32), gram_out],
        [VMEM] * 13,
        80000000,
        900000,
    )(tile, *received, choose, aux, high, low, early, *turned)
    total = float(length * rows)
    basis, factors = call(
        lambda *refs: finish_kernel(total, *refs),
        [((comps, S, rows), f32), ((comps, S, vecs + S), f32)],
        [VMEM] * 4,
        50000000,
        400000,
    )(summed(gram), prev_basis, lines, last)
    return basis, jnp.swapaxes(factors, 1, 2)


def solution(mesh):
    in_specs = (
        P("dom", None),
        P("dom", None),
        P("dom", None, None),
        P("dom", None),
        P(),
        P(None, None, "dom"),
        P(),
    )
    out_specs = (P(None, None, "dom"), P())
    return jax.shard_map(local, mesh=mesh, in_specs=in_specs, out_specs=out_specs, check_vma=False)
```

```python
import jax
import jax.numpy as jnp
from jax import lax
from jax.experimental import pallas as pl
from jax.experimental.pallas import tpu as pltpu
from jax.sharding import PartitionSpec as P

BLOCK = 64
S = 4
FAR = 8
COMPS = 3
DEAD = 1000.0
HIGHEST = lax.Precision.HIGHEST
NN = (((1,), (0,)), ((), ()))
NT = (((1,), (1,)), ((), ()))


def dot(a, b, dims=NN, precision=None):
    return lax.dot_general(a, b, dims, precision=precision, preferred_element_type=jnp.float32)


def iota(shape, axis):
    return lax.broadcasted_iota(jnp.int32, shape, axis)


PLACES = {(c, g): (g % 2, (0, 8, 0, 0)[g] + 32 * c) for c in range(COMPS) for g in range(4)}
PLACES.update({(0, 2): (0, 96), (1, 2): (0, 112), (2, 2): (1, 96)})


def own_lanes(rows, width):
    return iota((rows, width), 1) // BLOCK == iota((rows, width), 0) % 8


def fold(masked):
    total = masked[:, :128]
    for t in range(1, masked.shape[1] // 128):
        total = total + masked[:, t * 128 : (t + 1) * 128]
    return total + pltpu.roll(total, BLOCK, 1)


def lines_of(tile, width):
    wide = jnp.concatenate([tile] * (width // 128), axis=1)
    wide = jnp.where(own_lanes(wide.shape[0], width), wide, 0.0)
    where = iota((8, width), 0)
    result = jnp.zeros((8, width), jnp.float32)
    for c in range(COMPS):
        line = jnp.sum(wide[c * 8 : (c + 1) * 8], axis=0, keepdims=True)
        result = jnp.where(where == c, jnp.broadcast_to(line, result.shape), result)
    return result


def split(x):
    parts = []
    for _ in range(3):
        parts.append(x.astype(jnp.bfloat16))
        x = x - parts[-1].astype(jnp.float32)
    return parts


def split_dot(x, parts):
    left = [part.astype(jnp.float32) for part in split(x)]
    left.append(jnp.zeros((-3 * x.shape[0] % 16, x.shape[1]), jnp.float32))
    left = jnp.concatenate([part for part in left if part.shape[0]], axis=0).astype(jnp.bfloat16)
    products = dot(left, parts[0]) + dot(left, parts[1]) + dot(left, parts[2])
    rows = x.shape[0]
    return products[:rows] + (products[rows : 2 * rows] + products[2 * rows : 3 * rows])


def fetch(pairs, sems):
    copies = [pltpu.make_async_copy(src, dst, sems.at[i]) for i, (src, dst) in enumerate(pairs)]
    for copy in copies:
        copy.start()
    return copies


def start_kernel(prev_in, mix_in, list_in, count_in, out_ref, prev_ref, mix_ref, list_ref, count_ref, sems):
    copies = fetch(
        [(prev_in, prev_ref), (mix_in, mix_ref), (list_in, list_ref), (count_in, count_ref)], sems
    )
    for copy in copies[1:]:
        copy.wait()
    comps, vecs, rows = prev_ref.shape
    eye = iota((vecs, vecs), 0) == iota((vecs, vecs), 1)
    weights = []
    for c in range(comps):
        line = jnp.broadcast_to(mix_ref[c : c + 1, :], eye.shape)
        weights.append(jnp.sum(jnp.where(eye, line, 0.0), axis=1, keepdims=True))
    order = list_ref[0].astype(jnp.float32)
    order = jnp.concatenate([order, jnp.zeros((4, 120), jnp.float32)], axis=1)
    meta = jnp.zeros((8, 128), jnp.float32)
    slot = iota((1, 128), 1)
    for link in range(4):
        live = slot < jnp.broadcast_to(count_ref[0:1, link : link + 1], slot.shape)
        line = jnp.where(live, order[link : link + 1], DEAD)
        line = pltpu.roll(jnp.broadcast_to(line, (8, 128)), 8 + 8 * link, 1)
        meta = jnp.where(iota((8, 128), 1) // 8 == link + 1, line, meta)
    out_ref[8 * comps :, :] = meta
    copies[0].wait()
    own = own_lanes(8, rows)
    for c in range(comps):
        start = jnp.sum(weights[c] * prev_ref[c], axis=0, keepdims=True)
        line = jnp.broadcast_to(start, own.shape)
        out_ref[c * 8 : (c + 1) * 8, :] = fold(jnp.where(own, line, 0.0))


def prepare_kernel(strips_in, columns_in, shifts_in, high_ref, low_ref, aux_ref, strips, columns, shifts, sems):
    parts = strips.shape[0]
    depth = strips.shape[1]
    pairs = [(columns_in, columns), (shifts_in, shifts)]
    pairs += [(strips_in.at[pl.ds(p * depth, depth)], strips.at[p]) for p in range(parts)]
    copies = fetch(pairs, sems)
    copies[0].wait()
    copies[1].wait()
    where = iota((8, 128), 1)
    table = jnp.zeros((8, 128), jnp.float32)
    eye = iota((8, 8), 0) == iota((8, 8), 1)
    for k in range(columns.shape[0]):
        line = jnp.broadcast_to(columns[k : k + 1, :].astype(jnp.float32), (8, 8))
        column = jnp.sum(jnp.where(eye, line, 0.0), axis=1, keepdims=True)
        table = jnp.where(where == k, column, table)
    for k in range(S):
        aux_ref[8 * k : 8 * k + 8, :] = jnp.full((8, 128), shifts[k], jnp.float32)
    aux_ref[8 * S :, :] = table
    for p in range(parts):
        copies[2 + p].wait()
        turned = strips[p].T
        high = turned.astype(jnp.bfloat16)
        high_ref[:, p * depth : (p + 1) * depth] = high
        low_ref[:, p * depth : (p + 1) * depth] = (turned - high.astype(jnp.float32)).astype(jnp.bfloat16)


def selection(table, metas, place, length):
    even, even_far = lax.rem(place, 2) == 0, lax.rem(place // FAR, 2) == 0
    near, far_odd, far_even, across = metas
    moved = (place == 2) | (place == length - 3)
    across = jnp.where(moved, far_odd, across)
    circle = jnp.where(moved, 16.0, 32.0)
    slots = [
        (place >= 1, jnp.where(even, circle, 8.0), jnp.where(even, across, near)),
        (place < length - 1, jnp.where(even, 8.0, circle), jnp.where(even, near, across)),
        (place >= FAR, jnp.where(even_far, 16.0, 24.0), jnp.where(even_far, far_odd, far_even)),
        (place < length - FAR, jnp.where(even_far, 24.0, 16.0), jnp.where(even_far, far_even, far_odd)),
    ]
    lane = iota((1, 128), 1)
    target = lane.astype(jnp.float32)
    for link, (valid, base, order) in enumerate(slots):
        order = order + jnp.where(valid, base, DEAD)
        target = jnp.where(lane // 8 == link + 1, order, target)
    target = jnp.broadcast_to(target, (8, 128))
    lane = iota((8, 128), 1).astype(jnp.float32)
    at = [
        jnp.sum(jnp.where(lane == table[:, k : k + 1], target, 0.0), axis=1, keepdims=True)
        for k in range(4)
    ]
    return jnp.concatenate([jnp.broadcast_to(x, (8, 128)) for x in at], axis=0).astype(jnp.int32)


def multiply(choose, pieces, shift, high, low):
    rows = 8 * COMPS
    front = iota((8, 128), 1) < BLOCK
    picked = []
    for k in range(4):
        code = choose[8 * k : 8 * k + 8]
        index, place = code & 7, code >> 3
        blocks = []
        for c in range(COMPS):
            block = jnp.zeros((8, 128), jnp.float32)
            for p, piece in enumerate(pieces):
                found = jnp.take_along_axis(piece[8 * c : 8 * c + 8], index, axis=0)
                block = jnp.where(place == p, found, block)
            blocks.append(block)
        picked.append(blocks)
    x = [
        jnp.concatenate(
            [jnp.where(front, picked[2 * t][c], picked[2 * t + 1][c]) for t in range(2)], axis=1
        )
        for c in range(COMPS)
    ]
    x = jnp.concatenate(x, axis=0)
    top = x.astype(jnp.bfloat16).astype(jnp.float32)
    left = jnp.concatenate([top, x - top], axis=0).astype(jnp.bfloat16)
    both = dot(left, high) + dot(left, low)
    image = both[:rows] + both[rows:]
    image = fold(jnp.where(own_lanes(rows, image.shape[1]), image, 0.0))
    return image - jnp.concatenate([shift] * COMPS, axis=0) * pieces[0]


def first_kernel(length, own, a, b, c, d, aux, high, low, tile_ref, choose_ref):
    rows = 8 * COMPS
    refs = (own, a, b, c, d)
    pieces = [ref[:rows, :] for ref in refs]
    metas = [ref[rows : rows + 1, :] for ref in refs[1:]]
    choose = selection(aux[8 * S :, :], metas, lax.axis_index("dom"), length)
    choose_ref[...] = choose
    tile_ref[...] = multiply(choose, pieces, aux[:8, :], high[...], low[...])


def middle_kernel(step, own, a, b, c, d, choose, aux, high, low, tile_ref):
    pieces = [ref[...] for ref in (own, a, b, c, d)]
    tile_ref[...] = multiply(choose[...], pieces, aux[8 * step : 8 * step + 8, :], high[...], low[...])


def collect(gram, width, vecs):
    lane, comp = iota(gram.shape, 1), iota(gram.shape, 0)
    mine = jnp.where(lane < width, lane // vecs, lane % 8) == comp
    return jnp.sum(jnp.where(mine, gram, 0.0), axis=0, keepdims=True)


def early_kernel(prev_ref, t0, t1, t2, lines_ref, gram_ref, *split_refs):
    comps, vecs, rows = prev_ref.shape
    width = comps * vecs
    lines = jnp.concatenate([lines_of(t[...], rows) for t in (t0, t1, t2)], axis=0)
    lines_ref[...] = lines
    prev = prev_ref[...].reshape(width, rows)
    full = dot(prev, prev, NT, HIGHEST)
    full = jnp.concatenate([full, jnp.zeros((width, 128 - width), jnp.float32)], axis=1)
    lane = iota((8, 128), 1)
    tiles = [jnp.zeros((8, 128), jnp.float32)] * 2
    for (c, g), (t, first) in PLACES.items():
        at = c * vecs + 8 * g
        piece = pltpu.roll(full[at : at + 8], (first - at) % 128, 1)
        tiles[t] = jnp.where((lane >= first) & (lane < first + vecs - 8 * g), piece, tiles[t])
    gram_ref[:16, :] = jnp.concatenate(tiles, axis=0)
    against = jnp.concatenate([prev, lines, jnp.zeros((8, rows), jnp.float32)], axis=0)
    for ref, part in zip(split_refs, split(against.T)):
        ref[...] = part
    gram = dot(lines, against, NT, HIGHEST)
    result = jnp.zeros((8, 128), jnp.float32)
    for k in range(S - 1):
        line = collect(gram[k * 8 : (k + 1) * 8], width, vecs)
        result = jnp.where(iota((8, 128), 0) == k, jnp.broadcast_to(line, result.shape), result)
    gram_ref[16:, :] = result


def last_kernel(vecs, own, a, b, c, d, choose, aux, high, low, early, t0, t1, t2, line_ref, gram_ref):
    pieces = [ref[...] for ref in (own, a, b, c, d)]
    tile = multiply(choose[...], pieces, aux[8 * S - 8 : 8 * S, :], high[...], low[...])
    rows = line_ref.shape[1]
    width = COMPS * vecs
    last = lines_of(tile, rows)
    line_ref[...] = last
    gram = split_dot(last, (t0[...], t1[...], t2[...]))
    square = jnp.sum(last * last, axis=1, keepdims=True)
    gram = jnp.where(iota(gram.shape, 1) == width + 8 * (S - 1) + iota(gram.shape, 0), square, gram)
    line = collect(gram, width, vecs)
    gram_ref[:16, :] = early[:16, :]
    gram_ref[16:, :] = jnp.where(
        iota((8, 128), 0) == S - 1, jnp.broadcast_to(line, (8, 128)), early[16:, :]
    )


def finish_kernel(total, gram_in, prev_ref, lines, last, basis_ref, factors_ref):
    comps, vecs, rows = prev_ref.shape
    width = comps * vecs
    gram = gram_in[...] * (1.0 / total)
    small = gram[16:]
    lane, comp = iota((8, 128), 1), iota((8, 128), 0)
    in_prev = (lane < width) & (lane // vecs == comp)
    coef, cross = [], []
    for k in range(S):
        line = jnp.broadcast_to(small[k : k + 1], (8, 128))
        coef.append(jnp.where(in_prev, line, 0.0))
        cross.append([jnp.where(lane == width + 8 * l + comp, line, 0.0) for l in range(k + 1)])
    coefs = jnp.concatenate(coef, axis=0)
    pieces, turns = [], {}
    for c in range(comps):
        for g in range(vecs // 8):
            t, first = PLACES[c, g]
            at = c * vecs + 8 * g
            turn = t, (at - first) % 128
            if turn not in turns:
                piece = gram[8 * t : 8 * t + 8]
                turns[turn] = pltpu.roll(piece, turn[1], 1) if turn[1] else piece
            piece = turns[turn]
            piece = jnp.where(lane < at + 8, 0.5 * piece, piece)
            piece = jnp.where((lane >= at) & (lane < (c + 1) * vecs), piece, 0.0)
            pieces.append(piece - jnp.where(lane == at + comp, 1.0, 0.0))
    half = jnp.concatenate(pieces, axis=0)
    turned = dot(coefs[:, :width], half, precision=HIGHEST)
    prev = prev_ref[...].reshape(width, rows)
    basis = jnp.concatenate([lines[...], last[...]], axis=0)
    projected = basis - dot(coefs[:, :width], prev, precision=HIGHEST)
    unit, scale = {}, {}
    for l in range(S):
        for k in range(l, S):
            value = turned[k * 8 : (k + 1) * 8] * coef[l] + turned[l * 8 : (l + 1) * 8] * coef[k] + cross[k][l]
            value = jnp.sum(value, axis=1, keepdims=True)
            for m in range(l):
                value = value - (unit[k, m] * scale[m]) * unit[l, m]
            if k == l:
                scale[l] = value
            else:
                unit[k, l] = value / scale[l]
    roots = [jnp.sqrt(scale[k]) for k in range(S)]
    lower = {(k, l): unit[k, l] * roots[l] if l < k else roots[k] for k in range(S) for l in range(k + 1)}
    vectors = []
    for k in range(S):
        value = projected[k * 8 : (k + 1) * 8]
        for l in range(k):
            value = value - unit[k, l] * vectors[l]
        vectors.append(value)
        value = value / roots[k]
        for c in range(comps):
            basis_ref[c, k : k + 1, :] = value[c : c + 1]
    for c in range(comps):
        factors_ref[c, :, :vecs] = small[:S, c * vecs : (c + 1) * vecs]
    for k in range(S):
        line = jnp.zeros((8, 128), jnp.float32)
        for l in range(k + 1):
            line = jnp.where(lane == l, lower[k, l], line)
        for c in range(comps):
            factors_ref[c, k : k + 1, vecs:] = line[c : c + 1, :S]


VMEM = pl.BlockSpec(memory_space=pltpu.VMEM)
HBM = pl.BlockSpec(memory_space=pltpu.HBM)


def in_hbm(*arrays):
    return [pltpu.with_memory_space_constraint(x, pltpu.HBM) for x in arrays]


def call(kernel, outs, specs, flops, moved, scratch=()):
    shapes = [jax.ShapeDtypeStruct(shape, kind) for shape, kind in outs]
    return pl.pallas_call(
        kernel,
        out_shape=shapes if len(shapes) > 1 else shapes[0],
        in_specs=specs,
        out_specs=[VMEM] * len(shapes) if len(shapes) > 1 else VMEM,
        scratch_shapes=list(scratch),
        compiler_params=pltpu.CompilerParams(vmem_limit_bytes=24 * 1024 * 1024),
        cost_estimate=pl.CostEstimate(flops=flops, bytes_accessed=moved, transcendentals=0),
    )


def send(value, target):
    return lax.ppermute(value, "dom", [(d, target[d]) for d in range(lax.axis_size("dom"))])


def neighbours(length, step, odd):
    target = {}
    for d in range(length):
        other = d + step if (d // step) % 2 == odd else d - step
        target[d] = other if 0 <= other < length else None
    return target


def ghosts(tile):
    length = lax.axis_size("dom")
    last = length - 1
    near, across = neighbours(length, 1, 0), neighbours(length, 1, 1)
    far_even, far_odd = neighbours(length, FAR, 0), neighbours(length, FAR, 1)
    across.update({0: 2, 2: 1, 1: 0, last: last - 2, last - 2: last - 1, last - 1: last})
    for d in range(length):
        if far_odd[d] is None:
            far_odd[d] = d ^ 1
    far_odd.update({1: 2, 2: 3, 3: 0, 0: 1})
    far_odd.update({last - 1: last - 2, last - 2: last - 3, last - 3: last, last: last - 1})
    return [send(tile, target) for target in (near, far_odd, far_even, across)]


def summed(value):
    length = lax.axis_size("dom")

    def fetched(step):
        return send(value, {d: d ^ (step | 1) for d in range(length)})

    value = value + fetched(1)
    step = 2
    while step < length:
        if 2 * step < length:
            farthest = fetched(3 * step)
            first, second = fetched(step), fetched(2 * step)
            value = (value + first) + (second + farthest)
        else:
            value = value + fetched(step)
        step *= 4
    return value


def local(strips, columns, send_list, send_count, shifts, prev_basis, mix):
    comps, vecs, rows = prev_basis.shape
    blocks = columns.shape[0]
    width = strips.shape[1]
    f32, bf16, dma = jnp.float32, jnp.bfloat16, pltpu.SemaphoreType.DMA
    tile_out = ((comps * blocks, 128), f32)
    tile = call(
        start_kernel,
        [((comps * blocks + 8, 128), f32)],
        [HBM] * 4,
        600000,
        250000,
        [
            pltpu.VMEM(prev_basis.shape, f32),
            pltpu.VMEM(mix.shape, f32),
            pltpu.VMEM(send_list.shape, jnp.int32),
            pltpu.VMEM(send_count.shape, jnp.int32),
            dma((4,)),
        ],
    )(*in_hbm(prev_basis, mix, send_list, send_count))
    high, low, aux = call(
        prepare_kernel,
        [((width, rows), bf16), ((width, rows), bf16), ((8 * S + 8, 128), f32)],
        [HBM] * 3,
        1000000,
        1000000,
        [
            pltpu.VMEM((4, rows // 4, width), f32),
            pltpu.VMEM(columns.shape[::-1], jnp.int32),
            pltpu.SMEM(shifts.shape, f32),
            dma((6,)),
        ],
    )(*in_hbm(strips, columns.T, shifts))
    tiles = []
    length = lax.axis_size("dom")
    tile, choose = call(
        lambda *refs: first_kernel(length, *refs),
        [tile_out, ((4 * blocks, 128), jnp.int32)],
        [VMEM] * 8,
        50000000,
        600000,
    )(tile, *ghosts(tile), aux, high, low)
    tiles.append(tile)
    for step in (1, 2):
        tile = call(
            lambda *refs, step=step: middle_kernel(step, *refs), [tile_out], [VMEM] * 9, 50000000, 600000
        )(tile, *ghosts(tile), choose, aux, high, low)
        tiles.append(tile)
    received = ghosts(tile)
    gram_out = ((24, 128), f32)
    lines, early, *parts = call(
        early_kernel,
        [((8 * S - 8, rows), f32), gram_out] + [((rows, 128), bf16)] * 3,
        [VMEM] * 4,
        60000000,
        250000,
    )(prev_basis, *tiles)
    last, gram = call(
        lambda *refs: last_kernel(vecs, *refs),
        [((8, rows), f32), gram_out],
        [VMEM] * 13,
        80000000,
        900000,
    )(tile, *received, choose, aux, high, low, early, *parts)
    total = float(length * rows)
    basis, factors = call(
        lambda *refs: finish_kernel(total, *refs),
        [((comps, S, rows), f32), ((comps, S, vecs + S), f32)],
        [VMEM] * 4,
        50000000,
        400000,
    )(summed(gram), prev_basis, lines, last)
    return basis, jnp.swapaxes(factors, 1, 2)


def solution(mesh):
    in_specs = (
        P("dom", None),
        P("dom", None),
        P("dom", None, None),
        P("dom", None),
        P(),
        P(None, None, "dom"),
        P(),
    )
    out_specs = (P(None, None, "dom"), P())
    return jax.shard_map(local, mesh=mesh, in_specs=in_specs, out_specs=out_specs, check_vma=False)
```

```python
import jax
import jax.numpy as jnp
from jax import lax
from jax.experimental import pallas as pl
from jax.experimental.pallas import tpu as pltpu
from jax.sharding import PartitionSpec as P

BLOCK = 64
S = 4
FAR = 8
COMPS = 3
DEAD = 1000.0
HIGHEST = lax.Precision.HIGHEST
NN = (((1,), (0,)), ((), ()))
NT = (((1,), (1,)), ((), ()))


def dot(a, b, dims=NN, precision=None):
    return lax.dot_general(a, b, dims, precision=precision, preferred_element_type=jnp.float32)


def iota(shape, axis):
    return lax.broadcasted_iota(jnp.int32, shape, axis)


PLACES = {(c, g): (g % 2, (0, 8, 0, 0)[g] + 32 * c) for c in range(COMPS) for g in range(4)}
PLACES.update({(0, 2): (0, 96), (1, 2): (0, 112), (2, 2): (1, 96)})


def own_lanes(rows, width):
    return iota((rows, width), 1) // BLOCK == iota((rows, width), 0) % 8


def fold(masked):
    total = masked[:, :128]
    for t in range(1, masked.shape[1] // 128):
        total = total + masked[:, t * 128 : (t + 1) * 128]
    return total + pltpu.roll(total, BLOCK, 1)


def lines_of(tile, width):
    wide = jnp.concatenate([tile] * (width // 128), axis=1)
    wide = jnp.where(own_lanes(wide.shape[0], width), wide, 0.0)
    where = iota((8, width), 0)
    result = jnp.zeros((8, width), jnp.float32)
    for c in range(COMPS):
        line = jnp.sum(wide[c * 8 : (c + 1) * 8], axis=0, keepdims=True)
        result = jnp.where(where == c, jnp.broadcast_to(line, result.shape), result)
    return result


def split(x):
    parts = []
    for _ in range(3):
        parts.append(x.astype(jnp.bfloat16))
        x = x - parts[-1].astype(jnp.float32)
    return parts


def split_dot(x, parts):
    left = [part.astype(jnp.float32) for part in split(x)]
    left.append(jnp.zeros((-3 * x.shape[0] % 16, x.shape[1]), jnp.float32))
    left = jnp.concatenate([part for part in left if part.shape[0]], axis=0).astype(jnp.bfloat16)
    products = dot(left, parts[0]) + dot(left, parts[1]) + dot(left, parts[2])
    rows = x.shape[0]
    return products[:rows] + (products[rows : 2 * rows] + products[2 * rows : 3 * rows])


def fetch(pairs, sems):
    copies = [pltpu.make_async_copy(src, dst, sems.at[i]) for i, (src, dst) in enumerate(pairs)]
    for copy in copies:
        copy.start()
    return copies


def start_kernel(prev_in, mix_in, list_in, count_in, out_ref, prev_ref, mix_ref, list_ref, count_ref, sems):
    copies = fetch(
        [(prev_in, prev_ref), (mix_in, mix_ref), (list_in, list_ref), (count_in, count_ref)], sems
    )
    for copy in copies[1:]:
        copy.wait()
    comps, vecs, rows = prev_ref.shape
    eye = iota((vecs, vecs), 0) == iota((vecs, vecs), 1)
    weights = []
    for c in range(comps):
        line = jnp.broadcast_to(mix_ref[c : c + 1, :], eye.shape)
        weights.append(jnp.sum(jnp.where(eye, line, 0.0), axis=1, keepdims=True))
    order = list_ref[0].astype(jnp.float32)
    order = jnp.concatenate([order, jnp.zeros((4, 120), jnp.float32)], axis=1)
    meta = jnp.zeros((8, 128), jnp.float32)
    slot = iota((1, 128), 1)
    for link in range(4):
        live = slot < jnp.broadcast_to(count_ref[0:1, link : link + 1], slot.shape)
        line = jnp.where(live, order[link : link + 1], DEAD)
        line = pltpu.roll(jnp.broadcast_to(line, (8, 128)), 8 + 8 * link, 1)
        meta = jnp.where(iota((8, 128), 1) // 8 == link + 1, line, meta)
    out_ref[8 * comps :, :] = meta
    copies[0].wait()
    own = own_lanes(8, rows)
    for c in range(comps):
        start = jnp.sum(weights[c] * prev_ref[c], axis=0, keepdims=True)
        line = jnp.broadcast_to(start, own.shape)
        out_ref[c * 8 : (c + 1) * 8, :] = fold(jnp.where(own, line, 0.0))


def prepare_kernel(strips_in, columns_in, shifts_in, high_ref, low_ref, aux_ref, strips, columns, shifts, sems):
    parts = strips.shape[0]
    depth = strips.shape[1]
    pairs = [(columns_in, columns), (shifts_in, shifts)]
    pairs += [(strips_in.at[pl.ds(p * depth, depth)], strips.at[p]) for p in range(parts)]
    copies = fetch(pairs, sems)
    copies[0].wait()
    copies[1].wait()
    where = iota((8, 128), 1)
    table = jnp.zeros((8, 128), jnp.float32)
    eye = iota((8, 8), 0) == iota((8, 8), 1)
    for k in range(columns.shape[0]):
        line = jnp.broadcast_to(columns[k : k + 1, :].astype(jnp.float32), (8, 8))
        column = jnp.sum(jnp.where(eye, line, 0.0), axis=1, keepdims=True)
        table = jnp.where(where == k, column, table)
    for k in range(S):
        aux_ref[8 * k : 8 * k + 8, :] = jnp.full((8, 128), shifts[k], jnp.float32)
    aux_ref[8 * S :, :] = table
    for p in range(parts):
        copies[2 + p].wait()
        turned = strips[p].T
        high = turned.astype(jnp.bfloat16)
        high_ref[:, p * depth : (p + 1) * depth] = high
        low_ref[:, p * depth : (p + 1) * depth] = (turned - high.astype(jnp.float32)).astype(jnp.bfloat16)


def selection(table, metas, place, length):
    even, even_far = lax.rem(place, 2) == 0, lax.rem(place // FAR, 2) == 0
    near, far_odd, far_even, across = metas
    moved = (place == 2) | (place == length - 3)
    across = jnp.where(moved, far_odd, across)
    circle = jnp.where(moved, 16.0, 32.0)
    slots = [
        (place >= 1, jnp.where(even, circle, 8.0), jnp.where(even, across, near)),
        (place < length - 1, jnp.where(even, 8.0, circle), jnp.where(even, near, across)),
        (place >= FAR, jnp.where(even_far, 16.0, 24.0), jnp.where(even_far, far_odd, far_even)),
        (place < length - FAR, jnp.where(even_far, 24.0, 16.0), jnp.where(even_far, far_even, far_odd)),
    ]
    lane = iota((1, 128), 1)
    target = lane.astype(jnp.float32)
    for link, (valid, base, order) in enumerate(slots):
        order = order + jnp.where(valid, base, DEAD)
        target = jnp.where(lane // 8 == link + 1, order, target)
    target = jnp.broadcast_to(target, (8, 128))
    lane = iota((8, 128), 1).astype(jnp.float32)
    at = [
        jnp.sum(jnp.where(lane == table[:, k : k + 1], target, 0.0), axis=1, keepdims=True)
        for k in range(4)
    ]
    return jnp.concatenate([jnp.broadcast_to(x, (8, 128)) for x in at], axis=0).astype(jnp.int32)


def multiply(choose, pieces, shift, high, low):
    rows = 8 * COMPS
    front = iota((8, 128), 1) < BLOCK
    picked = []
    for k in range(4):
        code = choose[8 * k : 8 * k + 8]
        index, place = code & 7, code >> 3
        blocks = []
        for c in range(COMPS):
            block = jnp.zeros((8, 128), jnp.float32)
            for p, piece in enumerate(pieces):
                found = jnp.take_along_axis(piece[8 * c : 8 * c + 8], index, axis=0)
                block = jnp.where(place == p, found, block)
            blocks.append(block)
        picked.append(blocks)
    x = [
        jnp.concatenate(
            [jnp.where(front, picked[2 * t][c], picked[2 * t + 1][c]) for t in range(2)], axis=1
        )
        for c in range(COMPS)
    ]
    x = jnp.concatenate(x, axis=0)
    top = x.astype(jnp.bfloat16).astype(jnp.float32)
    left = jnp.concatenate([top, x - top], axis=0).astype(jnp.bfloat16)
    both = dot(left, high) + dot(left, low)
    image = both[:rows] + both[rows:]
    image = fold(jnp.where(own_lanes(rows, image.shape[1]), image, 0.0))
    return image - jnp.concatenate([shift] * COMPS, axis=0) * pieces[0]


def first_kernel(length, own, a, b, c, d, aux, high, low, tile_ref, choose_ref):
    rows = 8 * COMPS
    refs = (own, a, b, c, d)
    pieces = [ref[:rows, :] for ref in refs]
    metas = [ref[rows : rows + 1, :] for ref in refs[1:]]
    choose = selection(aux[8 * S :, :], metas, lax.axis_index("dom"), length)
    choose_ref[...] = choose
    tile_ref[...] = multiply(choose, pieces, aux[:8, :], high[...], low[...])


def middle_kernel(step, own, a, b, c, d, choose, aux, high, low, tile_ref):
    pieces = [ref[...] for ref in (own, a, b, c, d)]
    tile_ref[...] = multiply(choose[...], pieces, aux[8 * step : 8 * step + 8, :], high[...], low[...])


def collect(gram, width, vecs):
    lane, comp = iota(gram.shape, 1), iota(gram.shape, 0)
    mine = jnp.where(lane < width, lane // vecs, lane % 8) == comp
    return jnp.sum(jnp.where(mine, gram, 0.0), axis=0, keepdims=True)


def early_kernel(prev_ref, t0, t1, t2, lines_ref, gram_ref, *split_refs):
    comps, vecs, rows = prev_ref.shape
    width = comps * vecs
    lines = jnp.concatenate([lines_of(t[...], rows) for t in (t0, t1, t2)], axis=0)
    lines_ref[...] = lines
    prev = prev_ref[...].reshape(width, rows)
    full = dot(prev, prev, NT, HIGHEST)
    full = jnp.concatenate([full, jnp.zeros((width, 128 - width), jnp.float32)], axis=1)
    lane = iota((8, 128), 1)
    tiles = [jnp.zeros((8, 128), jnp.float32)] * 2
    for (c, g), (t, first) in PLACES.items():
        at = c * vecs + 8 * g
        piece = pltpu.roll(full[at : at + 8], (first - at) % 128, 1)
        tiles[t] = jnp.where((lane >= first) & (lane < first + vecs - 8 * g), piece, tiles[t])
    gram_ref[:16, :] = jnp.concatenate(tiles, axis=0)
    against = jnp.concatenate([prev, lines, jnp.zeros((8, rows), jnp.float32)], axis=0)
    for ref, part in zip(split_refs, split(against.T)):
        ref[...] = part
    gram = dot(lines, against, NT, HIGHEST)
    result = jnp.zeros((8, 128), jnp.float32)
    for k in range(S - 1):
        line = collect(gram[k * 8 : (k + 1) * 8], width, vecs)
        result = jnp.where(iota((8, 128), 0) == k, jnp.broadcast_to(line, result.shape), result)
    gram_ref[16:, :] = result


def last_kernel(vecs, own, a, b, c, d, choose, aux, high, low, early, t0, t1, t2, line_ref, gram_ref):
    pieces = [ref[...] for ref in (own, a, b, c, d)]
    tile = multiply(choose[...], pieces, aux[8 * S - 8 : 8 * S, :], high[...], low[...])
    rows = line_ref.shape[1]
    width = COMPS * vecs
    last = lines_of(tile, rows)
    line_ref[...] = last
    gram = split_dot(last, (t0[...], t1[...], t2[...]))
    square = jnp.sum(last * last, axis=1, keepdims=True)
    gram = jnp.where(iota(gram.shape, 1) == width + 8 * (S - 1) + iota(gram.shape, 0), square, gram)
    line = collect(gram, width, vecs)
    gram_ref[:16, :] = early[:16, :]
    gram_ref[16:, :] = jnp.where(
        iota((8, 128), 0) == S - 1, jnp.broadcast_to(line, (8, 128)), early[16:, :]
    )


def finish_kernel(total, gram_in, prev_ref, lines, last, basis_out, factors_out, basis_ref, factors_ref, sems):
    comps, vecs, rows = prev_ref.shape
    width = comps * vecs
    gram = gram_in[...] * (1.0 / total)
    small = gram[16:]
    lane, comp = iota((8, 128), 1), iota((8, 128), 0)
    in_prev = (lane < width) & (lane // vecs == comp)
    coef, cross = [], []
    for k in range(S):
        line = jnp.broadcast_to(small[k : k + 1], (8, 128))
        coef.append(jnp.where(in_prev, line, 0.0))
        cross.append([jnp.where(lane == width + 8 * l + comp, line, 0.0) for l in range(k + 1)])
    coefs = jnp.concatenate(coef, axis=0)
    pieces, turns = [], {}
    for c in range(comps):
        for g in range(vecs // 8):
            t, first = PLACES[c, g]
            at = c * vecs + 8 * g
            turn = t, (at - first) % 128
            if turn not in turns:
                piece = gram[8 * t : 8 * t + 8]
                turns[turn] = pltpu.roll(piece, turn[1], 1) if turn[1] else piece
            piece = turns[turn]
            piece = jnp.where(lane < at + 8, 0.5 * piece, piece)
            piece = jnp.where((lane >= at) & (lane < (c + 1) * vecs), piece, 0.0)
            pieces.append(piece - jnp.where(lane == at + comp, 1.0, 0.0))
    half = jnp.concatenate(pieces, axis=0)
    turned = dot(coefs[:, :width], half, precision=HIGHEST)
    prev = prev_ref[...].reshape(width, rows)
    basis = jnp.concatenate([lines[...], last[...]], axis=0)
    projected = basis - dot(coefs[:, :width], prev, precision=HIGHEST)
    unit, scale = {}, {}
    for l in range(S):
        for k in range(l, S):
            value = turned[k * 8 : (k + 1) * 8] * coef[l] + turned[l * 8 : (l + 1) * 8] * coef[k] + cross[k][l]
            value = jnp.sum(value, axis=1, keepdims=True)
            for m in range(l):
                value = value - (unit[k, m] * scale[m]) * unit[l, m]
            if k == l:
                scale[l] = value
            else:
                unit[k, l] = value / scale[l]
    roots = [jnp.sqrt(scale[k]) for k in range(S)]
    lower = {(k, l): unit[k, l] * roots[l] if l < k else roots[k] for k in range(S) for l in range(k + 1)}
    for c in range(comps):
        factors_ref[c, :, :vecs] = small[:S, c * vecs : (c + 1) * vecs]
    for k in range(S):
        line = jnp.zeros((8, 128), jnp.float32)
        for l in range(k + 1):
            line = jnp.where(lane == l, lower[k, l], line)
        for c in range(comps):
            factors_ref[c, k : k + 1, vecs:] = line[c : c + 1, :S]
    factors_copy = pltpu.make_async_copy(factors_ref, factors_out, sems.at[0])
    factors_copy.start()
    vectors = []
    for k in range(S):
        value = projected[k * 8 : (k + 1) * 8]
        for l in range(k):
            value = value - unit[k, l] * vectors[l]
        vectors.append(value)
        value = value * (1.0 / roots[k])
        for c in range(comps):
            basis_ref[c, k : k + 1, :] = value[c : c + 1]
    basis_copy = pltpu.make_async_copy(basis_ref, basis_out, sems.at[1])
    basis_copy.start()
    factors_copy.wait()
    basis_copy.wait()


VMEM = pl.BlockSpec(memory_space=pltpu.VMEM)
HBM = pl.BlockSpec(memory_space=pltpu.HBM)


def in_hbm(*arrays):
    return [pltpu.with_memory_space_constraint(x, pltpu.HBM) for x in arrays]


def call(kernel, outs, specs, flops, moved, scratch=(), home=None):
    shapes = [jax.ShapeDtypeStruct(shape, kind) for shape, kind in outs]
    return pl.pallas_call(
        kernel,
        out_shape=shapes if len(shapes) > 1 else shapes[0],
        in_specs=specs,
        out_specs=[home or VMEM] * len(shapes) if len(shapes) > 1 else VMEM,
        scratch_shapes=list(scratch),
        compiler_params=pltpu.CompilerParams(vmem_limit_bytes=24 * 1024 * 1024),
        cost_estimate=pl.CostEstimate(flops=flops, bytes_accessed=moved, transcendentals=0),
    )


def send(value, target):
    return lax.ppermute(value, "dom", [(d, target[d]) for d in range(lax.axis_size("dom"))])


def neighbours(length, step, odd):
    target = {}
    for d in range(length):
        other = d + step if (d // step) % 2 == odd else d - step
        target[d] = other if 0 <= other < length else None
    return target


def ghosts(tile):
    length = lax.axis_size("dom")
    last = length - 1
    near, across = neighbours(length, 1, 0), neighbours(length, 1, 1)
    far_even, far_odd = neighbours(length, FAR, 0), neighbours(length, FAR, 1)
    across.update({0: 2, 2: 1, 1: 0, last: last - 2, last - 2: last - 1, last - 1: last})
    for d in range(length):
        if far_odd[d] is None:
            far_odd[d] = d ^ 1
    far_odd.update({1: 2, 2: 3, 3: 0, 0: 1})
    far_odd.update({last - 1: last - 2, last - 2: last - 3, last - 3: last, last: last - 1})
    return [send(tile, target) for target in (near, far_odd, far_even, across)]


def summed(value):
    length = lax.axis_size("dom")

    def fetched(step):
        return send(value, {d: d ^ (step | 1) for d in range(length)})

    value = value + fetched(1)
    step = 2
    while step < length:
        if 2 * step < length:
            farthest = fetched(3 * step)
            first, second = fetched(step), fetched(2 * step)
            value = (value + first) + (second + farthest)
        else:
            value = value + fetched(step)
        step *= 4
    return value


def local(strips, columns, send_list, send_count, shifts, prev_basis, mix):
    comps, vecs, rows = prev_basis.shape
    blocks = columns.shape[0]
    width = strips.shape[1]
    f32, bf16, dma = jnp.float32, jnp.bfloat16, pltpu.SemaphoreType.DMA
    tile_out = ((comps * blocks, 128), f32)
    tile = call(
        start_kernel,
        [((comps * blocks + 8, 128), f32)],
        [HBM] * 4,
        600000,
        250000,
        [
            pltpu.VMEM(prev_basis.shape, f32),
            pltpu.VMEM(mix.shape, f32),
            pltpu.VMEM(send_list.shape, jnp.int32),
            pltpu.VMEM(send_count.shape, jnp.int32),
            dma((4,)),
        ],
    )(*in_hbm(prev_basis, mix, send_list, send_count))
    high, low, aux = call(
        prepare_kernel,
        [((width, rows), bf16), ((width, rows), bf16), ((8 * S + 8, 128), f32)],
        [HBM] * 3,
        1000000,
        1000000,
        [
            pltpu.VMEM((4, rows // 4, width), f32),
            pltpu.VMEM(columns.shape[::-1], jnp.int32),
            pltpu.SMEM(shifts.shape, f32),
            dma((6,)),
        ],
    )(*in_hbm(strips, columns.T, shifts))
    tiles = []
    length = lax.axis_size("dom")
    tile, choose = call(
        lambda *refs: first_kernel(length, *refs),
        [tile_out, ((4 * blocks, 128), jnp.int32)],
        [VMEM] * 8,
        50000000,
        600000,
    )(tile, *ghosts(tile), aux, high, low)
    tiles.append(tile)
    for step in (1, 2):
        tile = call(
            lambda *refs, step=step: middle_kernel(step, *refs), [tile_out], [VMEM] * 9, 50000000, 600000
        )(tile, *ghosts(tile), choose, aux, high, low)
        tiles.append(tile)
    received = ghosts(tile)
    gram_out = ((24, 128), f32)
    lines, early, *parts = call(
        early_kernel,
        [((8 * S - 8, rows), f32), gram_out] + [((rows, 128), bf16)] * 3,
        [VMEM] * 4,
        60000000,
        250000,
    )(prev_basis, *tiles)
    last, gram = call(
        lambda *refs: last_kernel(vecs, *refs),
        [((8, rows), f32), gram_out],
        [VMEM] * 13,
        80000000,
        900000,
    )(tile, *received, choose, aux, high, low, early, *parts)
    total = float(length * rows)
    basis, factors = call(
        lambda *refs: finish_kernel(total, *refs),
        [((comps, S, rows), f32), ((comps, S, vecs + S), f32)],
        [VMEM] * 4,
        50000000,
        400000,
        [
            pltpu.VMEM((comps, S, rows), f32),
            pltpu.VMEM((comps, S, vecs + S), f32),
            dma((2,)),
        ],
        HBM,
    )(summed(gram), prev_basis, lines, last)
    return basis, jnp.swapaxes(factors, 1, 2)


def solution(mesh):
    in_specs = (
        P("dom", None),
        P("dom", None),
        P("dom", None, None),
        P("dom", None),
        P(),
        P(None, None, "dom"),
        P(),
    )
    out_specs = (P(None, None, "dom"), P())
    return jax.shard_map(local, mesh=mesh, in_specs=in_specs, out_specs=out_specs, check_vma=False)
```

```python
import jax
import jax.numpy as jnp
from jax import lax
from jax.experimental import pallas as pl
from jax.experimental.pallas import tpu as pltpu
from jax.sharding import PartitionSpec as P

BLOCK = 64
S = 4
FAR = 8
COMPS = 3
DEAD = 1000.0
HIGHEST = lax.Precision.HIGHEST
NN = (((1,), (0,)), ((), ()))
NT = (((1,), (1,)), ((), ()))


def dot(a, b, dims=NN, precision=None):
    return lax.dot_general(a, b, dims, precision=precision, preferred_element_type=jnp.float32)


def iota(shape, axis):
    return lax.broadcasted_iota(jnp.int32, shape, axis)


PLACES = {(c, g): (g % 2, (0, 8, 0, 0)[g] + 32 * c) for c in range(COMPS) for g in range(4)}
PLACES.update({(0, 2): (0, 96), (1, 2): (0, 112), (2, 2): (1, 96)})


def own_lanes(rows, width):
    return iota((rows, width), 1) // BLOCK == iota((rows, width), 0) % 8


def fold(masked):
    total = masked[:, :128]
    for t in range(1, masked.shape[1] // 128):
        total = total + masked[:, t * 128 : (t + 1) * 128]
    return total + pltpu.roll(total, BLOCK, 1)


def lines_of(tile, width):
    wide = jnp.concatenate([tile] * (width // 128), axis=1)
    return joined(jnp.where(own_lanes(wide.shape[0], width), wide, 0.0))


def joined(wide):
    width = wide.shape[1]
    where = iota((8, width), 0)
    result = jnp.zeros((8, width), jnp.float32)
    for c in range(COMPS):
        line = jnp.sum(wide[c * 8 : (c + 1) * 8], axis=0, keepdims=True)
        result = jnp.where(where == c, jnp.broadcast_to(line, result.shape), result)
    return result


def split(x):
    parts = []
    for _ in range(3):
        parts.append(x.astype(jnp.bfloat16))
        x = x - parts[-1].astype(jnp.float32)
    return parts


def split_dot(x, parts):
    left = [part.astype(jnp.float32) for part in split(x)]
    left.append(jnp.zeros((-3 * x.shape[0] % 16, x.shape[1]), jnp.float32))
    left = jnp.concatenate([part for part in left if part.shape[0]], axis=0).astype(jnp.bfloat16)
    products = dot(left, parts[0]) + dot(left, parts[1]) + dot(left, parts[2])
    rows = x.shape[0]
    return products[:rows] + (products[rows : 2 * rows] + products[2 * rows : 3 * rows])


def fetch(pairs, sems):
    copies = [pltpu.make_async_copy(src, dst, sems.at[i]) for i, (src, dst) in enumerate(pairs)]
    for copy in copies:
        copy.start()
    return copies


def start_kernel(prev_in, mix_in, list_in, count_in, out_ref, prev_ref, mix_ref, list_ref, count_ref, sems):
    copies = fetch(
        [(prev_in, prev_ref), (mix_in, mix_ref), (list_in, list_ref), (count_in, count_ref)], sems
    )
    for copy in copies[1:]:
        copy.wait()
    comps, vecs, rows = prev_ref.shape
    eye = iota((vecs, vecs), 0) == iota((vecs, vecs), 1)
    weights = []
    for c in range(comps):
        line = jnp.broadcast_to(mix_ref[c : c + 1, :], eye.shape)
        weights.append(jnp.sum(jnp.where(eye, line, 0.0), axis=1, keepdims=True))
    order = list_ref[0].astype(jnp.float32)
    order = jnp.concatenate([order, jnp.zeros((4, 120), jnp.float32)], axis=1)
    meta = jnp.zeros((8, 128), jnp.float32)
    slot = iota((1, 128), 1)
    for link in range(4):
        live = slot < jnp.broadcast_to(count_ref[0:1, link : link + 1], slot.shape)
        line = jnp.where(live, order[link : link + 1], DEAD)
        line = pltpu.roll(jnp.broadcast_to(line, (8, 128)), 8 + 8 * link, 1)
        meta = jnp.where(iota((8, 128), 1) // 8 == link + 1, line, meta)
    out_ref[8 * comps :, :] = meta
    copies[0].wait()
    own = own_lanes(8, rows)
    for c in range(comps):
        start = jnp.sum(weights[c] * prev_ref[c], axis=0, keepdims=True)
        line = jnp.broadcast_to(start, own.shape)
        out_ref[c * 8 : (c + 1) * 8, :] = fold(jnp.where(own, line, 0.0))


def prepare_kernel(strips_in, columns_in, shifts_in, high_ref, low_ref, aux_ref, strips, columns, shifts, sems):
    parts = strips.shape[0]
    depth = strips.shape[1]
    pairs = [(columns_in, columns), (shifts_in, shifts)]
    pairs += [(strips_in.at[pl.ds(p * depth, depth)], strips.at[p]) for p in range(parts)]
    copies = fetch(pairs, sems)
    copies[0].wait()
    copies[1].wait()
    where = iota((8, 128), 1)
    table = jnp.zeros((8, 128), jnp.float32)
    eye = iota((8, 8), 0) == iota((8, 8), 1)
    for k in range(columns.shape[0]):
        line = jnp.broadcast_to(columns[k : k + 1, :].astype(jnp.float32), (8, 8))
        column = jnp.sum(jnp.where(eye, line, 0.0), axis=1, keepdims=True)
        table = jnp.where(where == k, column, table)
    for k in range(S):
        aux_ref[8 * k : 8 * k + 8, :] = jnp.full((8, 128), shifts[k], jnp.float32)
    aux_ref[8 * S :, :] = table
    for p in range(parts):
        copies[2 + p].wait()
        turned = strips[p].T
        high = turned.astype(jnp.bfloat16)
        high_ref[:, p * depth : (p + 1) * depth] = high
        low_ref[:, p * depth : (p + 1) * depth] = (turned - high.astype(jnp.float32)).astype(jnp.bfloat16)


def selection(table, metas, place, length):
    even, even_far = lax.rem(place, 2) == 0, lax.rem(place // FAR, 2) == 0
    near, far_odd, far_even, across = metas
    moved = (place == 2) | (place == length - 3)
    across = jnp.where(moved, far_odd, across)
    circle = jnp.where(moved, 16.0, 32.0)
    slots = [
        (place >= 1, jnp.where(even, circle, 8.0), jnp.where(even, across, near)),
        (place < length - 1, jnp.where(even, 8.0, circle), jnp.where(even, near, across)),
        (place >= FAR, jnp.where(even_far, 16.0, 24.0), jnp.where(even_far, far_odd, far_even)),
        (place < length - FAR, jnp.where(even_far, 24.0, 16.0), jnp.where(even_far, far_even, far_odd)),
    ]
    lane = iota((1, 128), 1)
    target = lane.astype(jnp.float32)
    for link, (valid, base, order) in enumerate(slots):
        order = order + jnp.where(valid, base, DEAD)
        target = jnp.where(lane // 8 == link + 1, order, target)
    target = jnp.broadcast_to(target, (8, 128))
    lane = iota((8, 128), 1).astype(jnp.float32)
    at = [
        jnp.sum(jnp.where(lane == table[:, k : k + 1], target, 0.0), axis=1, keepdims=True)
        for k in range(4)
    ]
    return jnp.concatenate([jnp.broadcast_to(x, (8, 128)) for x in at], axis=0).astype(jnp.int32)


def product(choose, pieces, high, low):
    rows = 8 * COMPS
    front = iota((8, 128), 1) < BLOCK
    picked = []
    for k in range(4):
        code = choose[8 * k : 8 * k + 8]
        index, place = code & 7, code >> 3
        blocks = []
        for c in range(COMPS):
            block = jnp.zeros((8, 128), jnp.float32)
            for p, piece in enumerate(pieces):
                found = jnp.take_along_axis(piece[8 * c : 8 * c + 8], index, axis=0)
                block = jnp.where(place == p, found, block)
            blocks.append(block)
        picked.append(blocks)
    x = [
        jnp.concatenate(
            [jnp.where(front, picked[2 * t][c], picked[2 * t + 1][c]) for t in range(2)], axis=1
        )
        for c in range(COMPS)
    ]
    x = jnp.concatenate(x, axis=0)
    top = x.astype(jnp.bfloat16).astype(jnp.float32)
    left = jnp.concatenate([top, x - top], axis=0).astype(jnp.bfloat16)
    both = dot(left, high) + dot(left, low)
    image = both[:rows] + both[rows:]
    return jnp.where(own_lanes(rows, image.shape[1]), image, 0.0)


def multiply(choose, pieces, shift, high, low):
    image = fold(product(choose, pieces, high, low))
    return image - jnp.concatenate([shift] * COMPS, axis=0) * pieces[0]


def first_kernel(length, own, a, b, c, d, aux, high, low, tile_ref, choose_ref):
    rows = 8 * COMPS
    refs = (own, a, b, c, d)
    pieces = [ref[:rows, :] for ref in refs]
    metas = [ref[rows : rows + 1, :] for ref in refs[1:]]
    choose = selection(aux[8 * S :, :], metas, lax.axis_index("dom"), length)
    choose_ref[...] = choose
    tile_ref[...] = multiply(choose, pieces, aux[:8, :], high[...], low[...])


def middle_kernel(step, own, a, b, c, d, choose, aux, high, low, tile_ref):
    pieces = [ref[...] for ref in (own, a, b, c, d)]
    tile_ref[...] = multiply(choose[...], pieces, aux[8 * step : 8 * step + 8, :], high[...], low[...])


def collect(gram, width, vecs):
    lane, comp = iota(gram.shape, 1), iota(gram.shape, 0)
    mine = jnp.where(lane < width, lane // vecs, lane % 8) == comp
    return jnp.sum(jnp.where(mine, gram, 0.0), axis=0, keepdims=True)


def early_kernel(prev_ref, t0, t1, t2, lines_ref, gram_ref, *split_refs):
    comps, vecs, rows = prev_ref.shape
    width = comps * vecs
    lines = jnp.concatenate([lines_of(t[...], rows) for t in (t0, t1, t2)], axis=0)
    lines_ref[...] = lines
    prev = prev_ref[...].reshape(width, rows)
    full = dot(prev, prev, NT, HIGHEST)
    full = jnp.concatenate([full, jnp.zeros((width, 128 - width), jnp.float32)], axis=1)
    lane = iota((8, 128), 1)
    tiles = [jnp.zeros((8, 128), jnp.float32)] * 2
    for (c, g), (t, first) in PLACES.items():
        at = c * vecs + 8 * g
        piece = pltpu.roll(full[at : at + 8], (first - at) % 128, 1)
        tiles[t] = jnp.where((lane >= first) & (lane < first + vecs - 8 * g), piece, tiles[t])
    gram_ref[:16, :] = jnp.concatenate(tiles, axis=0)
    against = jnp.concatenate([prev, lines, jnp.zeros((8, rows), jnp.float32)], axis=0)
    for ref, part in zip(split_refs, split(against.T)):
        ref[...] = part
    gram = dot(lines, against, NT, HIGHEST)
    result = jnp.zeros((8, 128), jnp.float32)
    for k in range(S - 1):
        line = collect(gram[k * 8 : (k + 1) * 8], width, vecs)
        result = jnp.where(iota((8, 128), 0) == k, jnp.broadcast_to(line, result.shape), result)
    gram_ref[16:, :] = result


def last_kernel(
    vecs, own, a, b, c, d, choose, aux, high, low, early, t0, t1, t2, lines, line_ref, gram_ref
):
    pieces = [ref[...] for ref in (own, a, b, c, d)]
    image = joined(product(choose[...], pieces, high[...], low[...]))
    width = COMPS * vecs
    shift = aux[8 * S - 8 : 8 * S, :1]
    last = image - shift * lines[8 * S - 16 :, :]
    line_ref[...] = last
    gram = split_dot(last, (t0[...], t1[...], t2[...]))
    square = jnp.sum(last * last, axis=1, keepdims=True)
    gram = jnp.where(iota(gram.shape, 1) == width + 8 * (S - 1) + iota(gram.shape, 0), square, gram)
    line = collect(gram, width, vecs)
    gram_ref[:16, :] = early[:16, :]
    gram_ref[16:, :] = jnp.where(
        iota((8, 128), 0) == S - 1, jnp.broadcast_to(line, (8, 128)), early[16:, :]
    )


def finish_kernel(total, gram_in, prev_ref, lines, last, basis_ref, factors_ref):
    comps, vecs, rows = prev_ref.shape
    width = comps * vecs
    gram = gram_in[...] * (1.0 / total)
    small = gram[16:]
    lane, comp = iota((8, 128), 1), iota((8, 128), 0)
    in_prev = (lane < width) & (lane // vecs == comp)
    coef, cross = [], []
    for k in range(S):
        line = jnp.broadcast_to(small[k : k + 1], (8, 128))
        coef.append(jnp.where(in_prev, line, 0.0))
        cross.append([jnp.where(lane == width + 8 * l + comp, line, 0.0) for l in range(k + 1)])
    coefs = jnp.concatenate(coef, axis=0)
    pieces, turns = [], {}
    for c in range(comps):
        for g in range(vecs // 8):
            t, first = PLACES[c, g]
            at = c * vecs + 8 * g
            turn = t, (at - first) % 128
            if turn not in turns:
                piece = gram[8 * t : 8 * t + 8]
                turns[turn] = pltpu.roll(piece, turn[1], 1) if turn[1] else piece
            piece = turns[turn]
            piece = jnp.where(lane < at + 8, 0.5 * piece, piece)
            piece = jnp.where((lane >= at) & (lane < (c + 1) * vecs), piece, 0.0)
            pieces.append(piece - jnp.where(lane == at + comp, 1.0, 0.0))
    half = jnp.concatenate(pieces, axis=0)
    turned = dot(coefs[:, :width], half, precision=HIGHEST)
    prev = prev_ref[...].reshape(width, rows)
    basis = jnp.concatenate([lines[...], last[...]], axis=0)
    projected = basis - dot(coefs[:, :width], prev, precision=HIGHEST)
    unit, scale = {}, {}
    for l in range(S):
        for k in range(l, S):
            value = turned[k * 8 : (k + 1) * 8] * coef[l] + turned[l * 8 : (l + 1) * 8] * coef[k] + cross[k][l]
            value = jnp.sum(value, axis=1, keepdims=True)
            for m in range(l):
                value = value - (unit[k, m] * scale[m]) * unit[l, m]
            if k == l:
                scale[l] = value
            else:
                unit[k, l] = value / scale[l]
    roots = [jnp.sqrt(scale[k]) for k in range(S)]
    lower = {(k, l): unit[k, l] * roots[l] if l < k else roots[k] for k in range(S) for l in range(k + 1)}
    vectors = []
    for k in range(S):
        value = projected[k * 8 : (k + 1) * 8]
        for l in range(k):
            value = value - unit[k, l] * vectors[l]
        vectors.append(value)
        value = value * (1.0 / roots[k])
        for c in range(comps):
            basis_ref[c, k : k + 1, :] = value[c : c + 1]
    for c in range(comps):
        factors_ref[c, :, :vecs] = small[:S, c * vecs : (c + 1) * vecs]
    for k in range(S):
        line = jnp.zeros((8, 128), jnp.float32)
        for l in range(k + 1):
            line = jnp.where(lane == l, lower[k, l], line)
        for c in range(comps):
            factors_ref[c, k : k + 1, vecs:] = line[c : c + 1, :S]


VMEM = pl.BlockSpec(memory_space=pltpu.VMEM)
HBM = pl.BlockSpec(memory_space=pltpu.HBM)


def in_hbm(*arrays):
    return [pltpu.with_memory_space_constraint(x, pltpu.HBM) for x in arrays]


def call(kernel, outs, specs, flops, moved, scratch=()):
    shapes = [jax.ShapeDtypeStruct(shape, kind) for shape, kind in outs]
    return pl.pallas_call(
        kernel,
        out_shape=shapes if len(shapes) > 1 else shapes[0],
        in_specs=specs,
        out_specs=[VMEM] * len(shapes) if len(shapes) > 1 else VMEM,
        scratch_shapes=list(scratch),
        compiler_params=pltpu.CompilerParams(vmem_limit_bytes=24 * 1024 * 1024),
        cost_estimate=pl.CostEstimate(flops=flops, bytes_accessed=moved, transcendentals=0),
    )


def send(value, target):
    return lax.ppermute(value, "dom", [(d, target[d]) for d in range(lax.axis_size("dom"))])


def neighbours(length, step, odd):
    target = {}
    for d in range(length):
        other = d + step if (d // step) % 2 == odd else d - step
        target[d] = other if 0 <= other < length else None
    return target


def ghosts(tile):
    length = lax.axis_size("dom")
    last = length - 1
    near, across = neighbours(length, 1, 0), neighbours(length, 1, 1)
    far_even, far_odd = neighbours(length, FAR, 0), neighbours(length, FAR, 1)
    across.update({0: 2, 2: 1, 1: 0, last: last - 2, last - 2: last - 1, last - 1: last})
    for d in range(length):
        if far_odd[d] is None:
            far_odd[d] = d ^ 1
    far_odd.update({1: 2, 2: 3, 3: 0, 0: 1})
    far_odd.update({last - 1: last - 2, last - 2: last - 3, last - 3: last, last: last - 1})
    return [send(tile, target) for target in (near, far_odd, far_even, across)]


def summed(value):
    length = lax.axis_size("dom")

    def fetched(step):
        return send(value, {d: d ^ (step | 1) for d in range(length)})

    value = value + fetched(1)
    step = 2
    while step < length:
        if 2 * step < length:
            farthest = fetched(3 * step)
            first, second = fetched(step), fetched(2 * step)
            value = (value + first) + (second + farthest)
        else:
            value = value + fetched(step)
        step *= 4
    return value


def local(strips, columns, send_list, send_count, shifts, prev_basis, mix):
    comps, vecs, rows = prev_basis.shape
    blocks = columns.shape[0]
    width = strips.shape[1]
    f32, bf16, dma = jnp.float32, jnp.bfloat16, pltpu.SemaphoreType.DMA
    tile_out = ((comps * blocks, 128), f32)
    tile = call(
        start_kernel,
        [((comps * blocks + 8, 128), f32)],
        [HBM] * 4,
        600000,
        250000,
        [
            pltpu.VMEM(prev_basis.shape, f32),
            pltpu.VMEM(mix.shape, f32),
            pltpu.VMEM(send_list.shape, jnp.int32),
            pltpu.VMEM(send_count.shape, jnp.int32),
            dma((4,)),
        ],
    )(*in_hbm(prev_basis, mix, send_list, send_count))
    high, low, aux = call(
        prepare_kernel,
        [((width, rows), bf16), ((width, rows), bf16), ((8 * S + 8, 128), f32)],
        [HBM] * 3,
        1000000,
        1000000,
        [
            pltpu.VMEM((4, rows // 4, width), f32),
            pltpu.VMEM(columns.shape[::-1], jnp.int32),
            pltpu.SMEM(shifts.shape, f32),
            dma((6,)),
        ],
    )(*in_hbm(strips, columns.T, shifts))
    tiles = []
    length = lax.axis_size("dom")
    tile, choose = call(
        lambda *refs: first_kernel(length, *refs),
        [tile_out, ((4 * blocks, 128), jnp.int32)],
        [VMEM] * 8,
        50000000,
        600000,
    )(tile, *ghosts(tile), aux, high, low)
    tiles.append(tile)
    for step in (1, 2):
        tile = call(
            lambda *refs, step=step: middle_kernel(step, *refs), [tile_out], [VMEM] * 9, 50000000, 600000
        )(tile, *ghosts(tile), choose, aux, high, low)
        tiles.append(tile)
    received = ghosts(tile)
    gram_out = ((24, 128), f32)
    lines, early, *parts = call(
        early_kernel,
        [((8 * S - 8, rows), f32), gram_out] + [((rows, 128), bf16)] * 3,
        [VMEM] * 4,
        60000000,
        250000,
    )(prev_basis, *tiles)
    last, gram = call(
        lambda *refs: last_kernel(vecs, *refs),
        [((8, rows), f32), gram_out],
        [VMEM] * 14,
        80000000,
        900000,
    )(tile, *received, choose, aux, high, low, early, *parts, lines)
    total = float(length * rows)
    basis, factors = call(
        lambda *refs: finish_kernel(total, *refs),
        [((comps, S, rows), f32), ((comps, S, vecs + S), f32)],
        [VMEM] * 4,
        50000000,
        400000,
    )(summed(gram), prev_basis, lines, last)
    return basis, jnp.swapaxes(factors, 1, 2)


def solution(mesh):
    in_specs = (
        P("dom", None),
        P("dom", None),
        P("dom", None, None),
        P("dom", None),
        P(),
        P(None, None, "dom"),
        P(),
    )
    out_specs = (P(None, None, "dom"), P())
    return jax.shard_map(local, mesh=mesh, in_specs=in_specs, out_specs=out_specs, check_vma=False)
```

```python
import jax
import jax.numpy as jnp
from jax import lax
from jax.experimental import pallas as pl
from jax.experimental.pallas import tpu as pltpu
from jax.sharding import PartitionSpec as P

BLOCK = 64
S = 4
FAR = 8
COMPS = 3
DEAD = 1000.0
HIGHEST = lax.Precision.HIGHEST
NN = (((1,), (0,)), ((), ()))
NT = (((1,), (1,)), ((), ()))


def dot(a, b, dims=NN, precision=None):
    return lax.dot_general(a, b, dims, precision=precision, preferred_element_type=jnp.float32)


def iota(shape, axis):
    return lax.broadcasted_iota(jnp.int32, shape, axis)


PLACES = {(c, g): (g % 2, (0, 8, 0, 0)[g] + 32 * c) for c in range(COMPS) for g in range(4)}
PLACES.update({(0, 2): (0, 96), (1, 2): (0, 112), (2, 2): (1, 96)})


def own_lanes(rows, width):
    return iota((rows, width), 1) // BLOCK == iota((rows, width), 0) % 8


def fold(masked):
    total = masked[:, :128]
    for t in range(1, masked.shape[1] // 128):
        total = total + masked[:, t * 128 : (t + 1) * 128]
    return total + pltpu.roll(total, BLOCK, 1)


def lines_of(tile, width):
    wide = jnp.concatenate([tile] * (width // 128), axis=1)
    return joined(jnp.where(own_lanes(wide.shape[0], width), wide, 0.0))


def joined(wide):
    width = wide.shape[1]
    where = iota((8, width), 0)
    result = jnp.zeros((8, width), jnp.float32)
    for c in range(COMPS):
        line = jnp.sum(wide[c * 8 : (c + 1) * 8], axis=0, keepdims=True)
        result = jnp.where(where == c, jnp.broadcast_to(line, result.shape), result)
    return result


def split(x):
    parts = []
    for _ in range(3):
        parts.append(x.astype(jnp.bfloat16))
        x = x - parts[-1].astype(jnp.float32)
    return parts


def split_dot(x, parts):
    left = [part.astype(jnp.float32) for part in split(x)]
    left.append(jnp.zeros((-3 * x.shape[0] % 16, x.shape[1]), jnp.float32))
    left = jnp.concatenate([part for part in left if part.shape[0]], axis=0).astype(jnp.bfloat16)
    products = dot(left, parts[0]) + dot(left, parts[1]) + dot(left, parts[2])
    rows = x.shape[0]
    return products[:rows] + (products[rows : 2 * rows] + products[2 * rows : 3 * rows])


def fetch(pairs, sems):
    copies = [pltpu.make_async_copy(src, dst, sems.at[i]) for i, (src, dst) in enumerate(pairs)]
    for copy in copies:
        copy.start()
    return copies


def start_kernel(prev_in, mix_in, list_in, count_in, out_ref, prev_ref, mix_ref, list_ref, count_ref, sems):
    copies = fetch(
        [(prev_in, prev_ref), (mix_in, mix_ref), (list_in, list_ref), (count_in, count_ref)], sems
    )
    for copy in copies[1:]:
        copy.wait()
    comps, vecs, rows = prev_ref.shape
    eye = iota((vecs, vecs), 0) == iota((vecs, vecs), 1)
    weights = []
    for c in range(comps):
        line = jnp.broadcast_to(mix_ref[c : c + 1, :], eye.shape)
        weights.append(jnp.sum(jnp.where(eye, line, 0.0), axis=1, keepdims=True))
    order = list_ref[0].astype(jnp.float32)
    order = jnp.concatenate([order, jnp.zeros((4, 120), jnp.float32)], axis=1)
    meta = jnp.zeros((8, 128), jnp.float32)
    slot = iota((1, 128), 1)
    for link in range(4):
        live = slot < jnp.broadcast_to(count_ref[0:1, link : link + 1], slot.shape)
        line = jnp.where(live, order[link : link + 1], DEAD)
        line = pltpu.roll(jnp.broadcast_to(line, (8, 128)), 8 + 8 * link, 1)
        meta = jnp.where(iota((8, 128), 1) // 8 == link + 1, line, meta)
    out_ref[8 * comps :, :] = meta
    copies[0].wait()
    own = own_lanes(8, rows)
    for c in range(comps):
        start = jnp.sum(weights[c] * prev_ref[c], axis=0, keepdims=True)
        line = jnp.broadcast_to(start, own.shape)
        out_ref[c * 8 : (c + 1) * 8, :] = fold(jnp.where(own, line, 0.0))


def prepare_kernel(strips_in, columns_in, shifts_in, high_ref, low_ref, aux_ref, strips, columns, shifts, sems):
    parts = strips.shape[0]
    depth = strips.shape[1]
    pairs = [(columns_in, columns), (shifts_in, shifts)]
    pairs += [(strips_in.at[pl.ds(p * depth, depth)], strips.at[p]) for p in range(parts)]
    copies = fetch(pairs, sems)
    copies[0].wait()
    copies[1].wait()
    where = iota((8, 128), 1)
    table = jnp.zeros((8, 128), jnp.float32)
    eye = iota((8, 8), 0) == iota((8, 8), 1)
    for k in range(columns.shape[0]):
        line = jnp.broadcast_to(columns[k : k + 1, :].astype(jnp.float32), (8, 8))
        column = jnp.sum(jnp.where(eye, line, 0.0), axis=1, keepdims=True)
        table = jnp.where(where == k, column, table)
    for k in range(S):
        aux_ref[8 * k : 8 * k + 8, :] = jnp.full((8, 128), shifts[k], jnp.float32)
    aux_ref[8 * S :, :] = table
    for p in range(parts):
        copies[2 + p].wait()
        turned = strips[p].T
        high = turned.astype(jnp.bfloat16)
        high_ref[:, p * depth : (p + 1) * depth] = high
        low_ref[:, p * depth : (p + 1) * depth] = (turned - high.astype(jnp.float32)).astype(jnp.bfloat16)


def selection(table, metas, place, length):
    even, even_far = lax.rem(place, 2) == 0, lax.rem(place // FAR, 2) == 0
    near, far_odd, far_even, across = metas
    moved = (place == 2) | (place == length - 3)
    across = jnp.where(moved, far_odd, across)
    circle = jnp.where(moved, 16.0, 32.0)
    slots = [
        (place >= 1, jnp.where(even, circle, 8.0), jnp.where(even, across, near)),
        (place < length - 1, jnp.where(even, 8.0, circle), jnp.where(even, near, across)),
        (place >= FAR, jnp.where(even_far, 16.0, 24.0), jnp.where(even_far, far_odd, far_even)),
        (place < length - FAR, jnp.where(even_far, 24.0, 16.0), jnp.where(even_far, far_even, far_odd)),
    ]
    lane = iota((1, 128), 1)
    target = lane.astype(jnp.float32)
    for link, (valid, base, order) in enumerate(slots):
        order = order + jnp.where(valid, base, DEAD)
        target = jnp.where(lane // 8 == link + 1, order, target)
    target = jnp.broadcast_to(target, (8, 128))
    lane = iota((8, 128), 1).astype(jnp.float32)
    at = [
        jnp.sum(jnp.where(lane == table[:, k : k + 1], target, 0.0), axis=1, keepdims=True)
        for k in range(4)
    ]
    return jnp.concatenate([jnp.broadcast_to(x, (8, 128)) for x in at], axis=0).astype(jnp.int32)


def product(choose, pieces, high, low):
    rows = 8 * COMPS
    front = iota((8, 128), 1) < BLOCK
    picked = []
    for k in range(4):
        code = choose[8 * k : 8 * k + 8]
        index, place = code & 7, code >> 3
        blocks = []
        for c in range(COMPS):
            block = jnp.zeros((8, 128), jnp.float32)
            for p, piece in enumerate(pieces):
                found = jnp.take_along_axis(piece[8 * c : 8 * c + 8], index, axis=0)
                block = jnp.where(place == p, found, block)
            blocks.append(block)
        picked.append(blocks)
    x = [
        jnp.concatenate(
            [jnp.where(front, picked[2 * t][c], picked[2 * t + 1][c]) for t in range(2)], axis=1
        )
        for c in range(COMPS)
    ]
    x = jnp.concatenate(x, axis=0)
    top = x.astype(jnp.bfloat16).astype(jnp.float32)
    left = jnp.concatenate([top, x - top], axis=0).astype(jnp.bfloat16)
    both = dot(left, high) + dot(left, low)
    image = both[:rows] + both[rows:]
    return jnp.where(own_lanes(rows, image.shape[1]), image, 0.0)


def multiply(choose, pieces, shift, high, low):
    image = fold(product(choose, pieces, high, low))
    return image - jnp.concatenate([shift] * COMPS, axis=0) * pieces[0]


def first_kernel(length, own, a, b, c, d, aux, high, low, tile_ref, choose_ref):
    rows = 8 * COMPS
    refs = (own, a, b, c, d)
    pieces = [ref[:rows, :] for ref in refs]
    metas = [ref[rows : rows + 1, :] for ref in refs[1:]]
    choose = selection(aux[8 * S :, :], metas, lax.axis_index("dom"), length)
    choose_ref[...] = choose
    tile_ref[...] = multiply(choose, pieces, aux[:8, :], high[...], low[...])


def middle_kernel(step, own, a, b, c, d, choose, aux, high, low, tile_ref):
    pieces = [ref[...] for ref in (own, a, b, c, d)]
    tile_ref[...] = multiply(choose[...], pieces, aux[8 * step : 8 * step + 8, :], high[...], low[...])


def collect(gram, width, vecs):
    lane, comp = iota(gram.shape, 1), iota(gram.shape, 0)
    mine = jnp.where(lane < width, lane // vecs, lane % 8) == comp
    return jnp.sum(jnp.where(mine, gram, 0.0), axis=0, keepdims=True)


def early_kernel(prev_ref, t0, t1, t2, lines_ref, gram_ref, *split_refs):
    comps, vecs, rows = prev_ref.shape
    width = comps * vecs
    lines = jnp.concatenate([lines_of(t[...], rows) for t in (t0, t1, t2)], axis=0)
    lines_ref[...] = lines
    prev = prev_ref[...].reshape(width, rows)
    full = dot(prev, prev, NT, HIGHEST)
    full = jnp.concatenate([full, jnp.zeros((width, 128 - width), jnp.float32)], axis=1)
    lane = iota((8, 128), 1)
    tiles = [jnp.zeros((8, 128), jnp.float32)] * 2
    for (c, g), (t, first) in PLACES.items():
        at = c * vecs + 8 * g
        piece = pltpu.roll(full[at : at + 8], (first - at) % 128, 1)
        tiles[t] = jnp.where((lane >= first) & (lane < first + vecs - 8 * g), piece, tiles[t])
    gram_ref[:16, :] = jnp.concatenate(tiles, axis=0)
    against = jnp.concatenate([prev, lines, jnp.zeros((8, rows), jnp.float32)], axis=0)
    for ref, part in zip(split_refs, split(against.T)):
        ref[...] = part
    gram = dot(lines, against, NT, HIGHEST)
    result = jnp.zeros((8, 128), jnp.float32)
    for k in range(S - 1):
        line = collect(gram[k * 8 : (k + 1) * 8], width, vecs)
        result = jnp.where(iota((8, 128), 0) == k, jnp.broadcast_to(line, result.shape), result)
    gram_ref[16:, :] = result


def last_kernel(
    vecs, own, a, b, c, d, choose, aux, high, low, early, t0, t1, t2, lines, line_ref, gram_ref
):
    pieces = [ref[...] for ref in (own, a, b, c, d)]
    image = joined(product(choose[...], pieces, high[...], low[...]))
    width = COMPS * vecs
    shift = aux[8 * S - 8 : 8 * S, :1]
    last = image - shift * lines[8 * S - 16 :, :]
    line_ref[...] = last
    gram = split_dot(last, (t0[...], t1[...], t2[...]))
    square = jnp.sum(last * last, axis=1, keepdims=True)
    gram = jnp.where(iota(gram.shape, 1) == width + 8 * (S - 1) + iota(gram.shape, 0), square, gram)
    line = collect(gram, width, vecs)
    gram_ref[:16, :] = early[:16, :]
    gram_ref[16:, :] = jnp.where(
        iota((8, 128), 0) == S - 1, jnp.broadcast_to(line, (8, 128)), early[16:, :]
    )


def finish_kernel(total, gram_in, prev_ref, lines, last, basis_ref, factors_ref):
    comps, vecs, rows = prev_ref.shape
    width = comps * vecs
    gram = gram_in[...] * (1.0 / total)
    small = gram[16:]
    lane, comp = iota((8, 128), 1), iota((8, 128), 0)
    in_prev = (lane < width) & (lane // vecs == comp)
    coef, cross = [], []
    for k in range(S):
        line = jnp.broadcast_to(small[k : k + 1], (8, 128))
        coef.append(jnp.where(in_prev, line, 0.0))
        cross.append([jnp.where(lane == width + 8 * l + comp, line, 0.0) for l in range(k + 1)])
    coefs = jnp.concatenate(coef, axis=0)
    pieces, turns = [], {}
    for c in range(comps):
        for g in range(vecs // 8):
            t, first = PLACES[c, g]
            at = c * vecs + 8 * g
            turn = t, (at - first) % 128
            if turn not in turns:
                piece = gram[8 * t : 8 * t + 8]
                turns[turn] = pltpu.roll(piece, turn[1], 1) if turn[1] else piece
            piece = turns[turn]
            piece = jnp.where(lane < at + 8, 0.5 * piece, piece)
            piece = jnp.where((lane >= at) & (lane < (c + 1) * vecs), piece, 0.0)
            pieces.append(piece - jnp.where(lane == at + comp, 1.0, 0.0))
    half = jnp.concatenate(pieces, axis=0)
    turned = dot(coefs[:, :width], half, precision=HIGHEST)
    prev = prev_ref[...].reshape(width, rows)
    basis = jnp.concatenate([lines[...], last[...]], axis=0)
    projected = basis - dot(coefs[:, :width], prev, precision=HIGHEST)
    unit, scale = {}, {}
    for l in range(S):
        for k in range(l, S):
            value = turned[k * 8 : (k + 1) * 8] * coef[l] + turned[l * 8 : (l + 1) * 8] * coef[k] + cross[k][l]
            value = jnp.sum(value, axis=1, keepdims=True)
            for m in range(l):
                value = value - (unit[k, m] * scale[m]) * unit[l, m]
            if k == l:
                scale[l] = value
            else:
                unit[k, l] = value / scale[l]
    roots = [jnp.sqrt(scale[k]) for k in range(S)]
    lower = {(k, l): unit[k, l] * roots[l] if l < k else roots[k] for k in range(S) for l in range(k + 1)}
    vectors = []
    for k in range(S):
        value = projected[k * 8 : (k + 1) * 8]
        for l in range(k):
            value = value - unit[k, l] * vectors[l]
        vectors.append(value)
        value = value * (1.0 / roots[k])
        for c in range(comps):
            basis_ref[c, k : k + 1, :] = value[c : c + 1]
    for c in range(comps):
        factors_ref[c, :, :vecs] = small[:S, c * vecs : (c + 1) * vecs]
    for k in range(S):
        line = jnp.zeros((8, 128), jnp.float32)
        for l in range(k + 1):
            line = jnp.where(lane == l, lower[k, l], line)
        for c in range(comps):
            factors_ref[c, k : k + 1, vecs:] = line[c : c + 1, :S]


VMEM = pl.BlockSpec(memory_space=pltpu.VMEM)
HBM = pl.BlockSpec(memory_space=pltpu.HBM)


def in_hbm(*arrays):
    return [pltpu.with_memory_space_constraint(x, pltpu.HBM) for x in arrays]


def call(kernel, outs, specs, flops, moved, scratch=()):
    shapes = [jax.ShapeDtypeStruct(shape, kind) for shape, kind in outs]
    return pl.pallas_call(
        kernel,
        out_shape=shapes if len(shapes) > 1 else shapes[0],
        in_specs=specs,
        out_specs=[VMEM] * len(shapes) if len(shapes) > 1 else VMEM,
        scratch_shapes=list(scratch),
        compiler_params=pltpu.CompilerParams(vmem_limit_bytes=24 * 1024 * 1024),
        cost_estimate=pl.CostEstimate(flops=flops, bytes_accessed=moved, transcendentals=0),
    )


def send(value, target):
    return lax.ppermute(value, "dom", [(d, target[d]) for d in range(lax.axis_size("dom"))])


def neighbours(length, step, odd):
    target = {}
    for d in range(length):
        other = d + step if (d // step) % 2 == odd else d - step
        target[d] = other if 0 <= other < length else None
    return target


def ghosts(tile):
    length = lax.axis_size("dom")
    last = length - 1
    near, across = neighbours(length, 1, 0), neighbours(length, 1, 1)
    far_even, far_odd = neighbours(length, FAR, 0), neighbours(length, FAR, 1)
    across.update({0: 2, 2: 1, 1: 0, last: last - 2, last - 2: last - 1, last - 1: last})
    for d in range(length):
        if far_odd[d] is None:
            far_odd[d] = d ^ 1
    far_odd.update({1: 2, 2: 3, 3: 0, 0: 1})
    far_odd.update({last - 1: last - 2, last - 2: last - 3, last - 3: last, last: last - 1})
    return [send(tile, target) for target in (near, far_odd, far_even, across)]


def summed(value):
    length = lax.axis_size("dom")

    def fetched(step):
        return send(value, {d: d ^ (step | 1) for d in range(length)})

    value = value + fetched(1)
    step = length // 2
    while step > 1:
        if step > 2:
            farthest = fetched(step | step // 2)
            first, second = fetched(step // 2), fetched(step)
            value = (value + first) + (second + farthest)
        else:
            value = value + fetched(step)
        step //= 4
    return value


def local(strips, columns, send_list, send_count, shifts, prev_basis, mix):
    comps, vecs, rows = prev_basis.shape
    blocks = columns.shape[0]
    width = strips.shape[1]
    f32, bf16, dma = jnp.float32, jnp.bfloat16, pltpu.SemaphoreType.DMA
    tile_out = ((comps * blocks, 128), f32)
    tile = call(
        start_kernel,
        [((comps * blocks + 8, 128), f32)],
        [HBM] * 4,
        600000,
        250000,
        [
            pltpu.VMEM(prev_basis.shape, f32),
            pltpu.VMEM(mix.shape, f32),
            pltpu.VMEM(send_list.shape, jnp.int32),
            pltpu.VMEM(send_count.shape, jnp.int32),
            dma((4,)),
        ],
    )(*in_hbm(prev_basis, mix, send_list, send_count))
    high, low, aux = call(
        prepare_kernel,
        [((width, rows), bf16), ((width, rows), bf16), ((8 * S + 8, 128), f32)],
        [HBM] * 3,
        1000000,
        1000000,
        [
            pltpu.VMEM((4, rows // 4, width), f32),
            pltpu.VMEM(columns.shape[::-1], jnp.int32),
            pltpu.SMEM(shifts.shape, f32),
            dma((6,)),
        ],
    )(*in_hbm(strips, columns.T, shifts))
    tiles = []
    length = lax.axis_size("dom")
    tile, choose = call(
        lambda *refs: first_kernel(length, *refs),
        [tile_out, ((4 * blocks, 128), jnp.int32)],
        [VMEM] * 8,
        50000000,
        600000,
    )(tile, *ghosts(tile), aux, high, low)
    tiles.append(tile)
    for step in (1, 2):
        tile = call(
            lambda *refs, step=step: middle_kernel(step, *refs), [tile_out], [VMEM] * 9, 50000000, 600000
        )(tile, *ghosts(tile), choose, aux, high, low)
        tiles.append(tile)
    received = ghosts(tile)
    gram_out = ((24, 128), f32)
    lines, early, *parts = call(
        early_kernel,
        [((8 * S - 8, rows), f32), gram_out] + [((rows, 128), bf16)] * 3,
        [VMEM] * 4,
        60000000,
        250000,
    )(prev_basis, *tiles)
    last, gram = call(
        lambda *refs: last_kernel(vecs, *refs),
        [((8, rows), f32), gram_out],
        [VMEM] * 14,
        80000000,
        900000,
    )(tile, *received, choose, aux, high, low, early, *parts, lines)
    total = float(length * rows)
    basis, factors = call(
        lambda *refs: finish_kernel(total, *refs),
        [((comps, S, rows), f32), ((comps, S, vecs + S), f32)],
        [VMEM] * 4,
        50000000,
        400000,
    )(summed(gram), prev_basis, lines, last)
    return basis, jnp.swapaxes(factors, 1, 2)


def solution(mesh):
    in_specs = (
        P("dom", None),
        P("dom", None),
        P("dom", None, None),
        P("dom", None),
        P(),
        P(None, None, "dom"),
        P(),
    )
    out_specs = (P(None, None, "dom"), P())
    return jax.shard_map(local, mesh=mesh, in_specs=in_specs, out_specs=out_specs, check_vma=False)
```

```python
import jax
import jax.numpy as jnp
from jax import lax
from jax.experimental import pallas as pl
from jax.experimental.pallas import tpu as pltpu
from jax.sharding import PartitionSpec as P

BLOCK = 64
S = 4
FAR = 8
COMPS = 3
DEAD = 1000.0
HIGHEST = lax.Precision.HIGHEST
NN = (((1,), (0,)), ((), ()))
NT = (((1,), (1,)), ((), ()))


def dot(a, b, dims=NN, precision=None):
    return lax.dot_general(a, b, dims, precision=precision, preferred_element_type=jnp.float32)


def iota(shape, axis):
    return lax.broadcasted_iota(jnp.int32, shape, axis)


PLACES = {(c, g): (g % 2, (0, 8, 0, 0)[g] + 32 * c) for c in range(COMPS) for g in range(4)}
PLACES.update({(0, 2): (0, 96), (1, 2): (0, 112), (2, 2): (1, 96)})


def own_lanes(rows, width):
    return iota((rows, width), 1) // BLOCK == iota((rows, width), 0) % 8


def fold(masked):
    total = masked[:, :128]
    for t in range(1, masked.shape[1] // 128):
        total = total + masked[:, t * 128 : (t + 1) * 128]
    return total + pltpu.roll(total, BLOCK, 1)


def lines_of(tile, width):
    wide = jnp.concatenate([tile] * (width // 128), axis=1)
    return joined(jnp.where(own_lanes(wide.shape[0], width), wide, 0.0))


def joined(wide):
    width = wide.shape[1]
    where = iota((8, width), 0)
    result = jnp.zeros((8, width), jnp.float32)
    for c in range(COMPS):
        line = jnp.sum(wide[c * 8 : (c + 1) * 8], axis=0, keepdims=True)
        result = jnp.where(where == c, jnp.broadcast_to(line, result.shape), result)
    return result


def split(x):
    parts = []
    for _ in range(3):
        parts.append(x.astype(jnp.bfloat16))
        x = x - parts[-1].astype(jnp.float32)
    return parts


def split_dot(x, parts):
    left = [part.astype(jnp.float32) for part in split(x)]
    left.append(jnp.zeros((-3 * x.shape[0] % 16, x.shape[1]), jnp.float32))
    left = jnp.concatenate([part for part in left if part.shape[0]], axis=0).astype(jnp.bfloat16)
    products = dot(left, parts[0]) + dot(left, parts[1]) + dot(left, parts[2])
    rows = x.shape[0]
    return products[:rows] + (products[rows : 2 * rows] + products[2 * rows : 3 * rows])


def fetch(pairs, sems):
    copies = [pltpu.make_async_copy(src, dst, sems.at[i]) for i, (src, dst) in enumerate(pairs)]
    for copy in copies:
        copy.start()
    return copies


def start_kernel(prev_in, mix_in, list_in, count_in, out_ref, prev_ref, mix_ref, list_ref, count_ref, sems):
    copies = fetch(
        [(prev_in, prev_ref), (mix_in, mix_ref), (list_in, list_ref), (count_in, count_ref)], sems
    )
    for copy in copies[1:]:
        copy.wait()
    comps, vecs, rows = prev_ref.shape
    eye = iota((vecs, vecs), 0) == iota((vecs, vecs), 1)
    weights = []
    for c in range(comps):
        line = jnp.broadcast_to(mix_ref[c : c + 1, :], eye.shape)
        weights.append(jnp.sum(jnp.where(eye, line, 0.0), axis=1, keepdims=True))
    order = list_ref[0].astype(jnp.float32)
    order = jnp.concatenate([order, jnp.zeros((4, 120), jnp.float32)], axis=1)
    meta = jnp.zeros((8, 128), jnp.float32)
    slot = iota((1, 128), 1)
    for link in range(4):
        live = slot < jnp.broadcast_to(count_ref[0:1, link : link + 1], slot.shape)
        line = jnp.where(live, order[link : link + 1], DEAD)
        line = pltpu.roll(jnp.broadcast_to(line, (8, 128)), 8 + 8 * link, 1)
        meta = jnp.where(iota((8, 128), 1) // 8 == link + 1, line, meta)
    out_ref[8 * comps :, :] = meta
    copies[0].wait()
    own = own_lanes(8, rows)
    for c in range(comps):
        start = jnp.sum(weights[c] * prev_ref[c], axis=0, keepdims=True)
        line = jnp.broadcast_to(start, own.shape)
        out_ref[c * 8 : (c + 1) * 8, :] = fold(jnp.where(own, line, 0.0))


def prepare_kernel(strips_in, columns_in, shifts_in, high_ref, low_ref, aux_ref, strips, columns, shifts, sems):
    parts = strips.shape[0]
    depth = strips.shape[1]
    pairs = [(columns_in, columns), (shifts_in, shifts)]
    pairs += [(strips_in.at[pl.ds(p * depth, depth)], strips.at[p]) for p in range(parts)]
    copies = fetch(pairs, sems)
    copies[0].wait()
    copies[1].wait()
    where = iota((8, 128), 1)
    table = jnp.zeros((8, 128), jnp.float32)
    eye = iota((8, 8), 0) == iota((8, 8), 1)
    for k in range(columns.shape[0]):
        line = jnp.broadcast_to(columns[k : k + 1, :].astype(jnp.float32), (8, 8))
        column = jnp.sum(jnp.where(eye, line, 0.0), axis=1, keepdims=True)
        table = jnp.where(where == k, column, table)
    for k in range(S):
        aux_ref[8 * k : 8 * k + 8, :] = jnp.full((8, 128), shifts[k], jnp.float32)
    aux_ref[8 * S :, :] = table
    for p in range(parts):
        copies[2 + p].wait()
        turned = strips[p].T
        high = turned.astype(jnp.bfloat16)
        high_ref[:, p * depth : (p + 1) * depth] = high
        low_ref[:, p * depth : (p + 1) * depth] = (turned - high.astype(jnp.float32)).astype(jnp.bfloat16)


def selection(table, metas, place, length):
    even, even_far = lax.rem(place, 2) == 0, lax.rem(place // FAR, 2) == 0
    near, far_odd, far_even, across = metas
    moved = (place == 2) | (place == length - 3)
    across = jnp.where(moved, far_odd, across)
    circle = jnp.where(moved, 16.0, 32.0)
    slots = [
        (place >= 1, jnp.where(even, circle, 8.0), jnp.where(even, across, near)),
        (place < length - 1, jnp.where(even, 8.0, circle), jnp.where(even, near, across)),
        (place >= FAR, jnp.where(even_far, 16.0, 24.0), jnp.where(even_far, far_odd, far_even)),
        (place < length - FAR, jnp.where(even_far, 24.0, 16.0), jnp.where(even_far, far_even, far_odd)),
    ]
    lane = iota((1, 128), 1)
    target = lane.astype(jnp.float32)
    for link, (valid, base, order) in enumerate(slots):
        order = order + jnp.where(valid, base, DEAD)
        target = jnp.where(lane // 8 == link + 1, order, target)
    target = jnp.broadcast_to(target, (8, 128))
    lane = iota((8, 128), 1).astype(jnp.float32)
    at = [
        jnp.sum(jnp.where(lane == table[:, k : k + 1], target, 0.0), axis=1, keepdims=True)
        for k in range(1, 4)
    ]
    return jnp.concatenate([jnp.broadcast_to(x, (8, 128)) for x in at], axis=0).astype(jnp.int32)


def product(choose, pieces, high, low):
    rows = 8 * COMPS
    front = iota((8, 128), 1) < BLOCK
    picked = [[pieces[0][8 * c : 8 * c + 8] for c in range(COMPS)]]
    for k in range(3):
        code = choose[8 * k : 8 * k + 8]
        index, place = code & 7, code >> 3
        blocks = []
        for c in range(COMPS):
            block = jnp.zeros((8, 128), jnp.float32)
            for p, piece in enumerate(pieces):
                found = jnp.take_along_axis(piece[8 * c : 8 * c + 8], index, axis=0)
                block = jnp.where(place == p, found, block)
            blocks.append(block)
        picked.append(blocks)
    x = [
        jnp.concatenate(
            [jnp.where(front, picked[2 * t][c], picked[2 * t + 1][c]) for t in range(2)], axis=1
        )
        for c in range(COMPS)
    ]
    x = jnp.concatenate(x, axis=0)
    top = x.astype(jnp.bfloat16).astype(jnp.float32)
    left = jnp.concatenate([top, x - top], axis=0).astype(jnp.bfloat16)
    both = dot(left, high) + dot(left, low)
    image = both[:rows] + both[rows:]
    return jnp.where(own_lanes(rows, image.shape[1]), image, 0.0)


def multiply(choose, pieces, shift, high, low):
    image = fold(product(choose, pieces, high, low))
    return image - jnp.concatenate([shift] * COMPS, axis=0) * pieces[0]


def first_kernel(length, own, a, b, c, d, aux, high, low, tile_ref, choose_ref):
    rows = 8 * COMPS
    refs = (own, a, b, c, d)
    pieces = [ref[:rows, :] for ref in refs]
    metas = [ref[rows : rows + 1, :] for ref in refs[1:]]
    choose = selection(aux[8 * S :, :], metas, lax.axis_index("dom"), length)
    choose_ref[...] = choose
    tile_ref[...] = multiply(choose, pieces, aux[:8, :], high[...], low[...])


def middle_kernel(step, own, a, b, c, d, choose, aux, high, low, tile_ref):
    pieces = [ref[...] for ref in (own, a, b, c, d)]
    tile_ref[...] = multiply(choose[...], pieces, aux[8 * step : 8 * step + 8, :], high[...], low[...])


def collect(gram, width, vecs):
    lane, comp = iota(gram.shape, 1), iota(gram.shape, 0)
    mine = jnp.where(lane < width, lane // vecs, lane % 8) == comp
    return jnp.sum(jnp.where(mine, gram, 0.0), axis=0, keepdims=True)


def early_kernel(prev_ref, t0, t1, t2, lines_ref, gram_ref, *split_refs):
    comps, vecs, rows = prev_ref.shape
    width = comps * vecs
    lines = jnp.concatenate([lines_of(t[...], rows) for t in (t0, t1, t2)], axis=0)
    lines_ref[...] = lines
    prev = prev_ref[...].reshape(width, rows)
    full = dot(prev, prev, NT, HIGHEST)
    full = jnp.concatenate([full, jnp.zeros((width, 128 - width), jnp.float32)], axis=1)
    lane = iota((8, 128), 1)
    tiles = [jnp.zeros((8, 128), jnp.float32)] * 2
    for (c, g), (t, first) in PLACES.items():
        at = c * vecs + 8 * g
        piece = pltpu.roll(full[at : at + 8], (first - at) % 128, 1)
        tiles[t] = jnp.where((lane >= first) & (lane < first + vecs - 8 * g), piece, tiles[t])
    gram_ref[:16, :] = jnp.concatenate(tiles, axis=0)
    against = jnp.concatenate([prev, lines, jnp.zeros((8, rows), jnp.float32)], axis=0)
    for ref, part in zip(split_refs, split(against.T)):
        ref[...] = part
    gram = dot(lines, against, NT, HIGHEST)
    result = jnp.zeros((8, 128), jnp.float32)
    for k in range(S - 1):
        line = collect(gram[k * 8 : (k + 1) * 8], width, vecs)
        result = jnp.where(iota((8, 128), 0) == k, jnp.broadcast_to(line, result.shape), result)
    gram_ref[16:, :] = result


def last_kernel(
    vecs, own, a, b, c, d, choose, aux, high, low, early, t0, t1, t2, lines, line_ref, gram_ref
):
    pieces = [ref[...] for ref in (own, a, b, c, d)]
    image = joined(product(choose[...], pieces, high[...], low[...]))
    width = COMPS * vecs
    shift = aux[8 * S - 8 : 8 * S, :1]
    last = image - shift * lines[8 * S - 16 :, :]
    line_ref[...] = last
    gram = split_dot(last, (t0[...], t1[...], t2[...]))
    square = jnp.sum(last * last, axis=1, keepdims=True)
    gram = jnp.where(iota(gram.shape, 1) == width + 8 * (S - 1) + iota(gram.shape, 0), square, gram)
    line = collect(gram, width, vecs)
    gram_ref[:16, :] = early[:16, :]
    gram_ref[16:, :] = jnp.where(
        iota((8, 128), 0) == S - 1, jnp.broadcast_to(line, (8, 128)), early[16:, :]
    )


def finish_kernel(total, gram_in, prev_ref, lines, last, basis_ref, factors_ref):
    comps, vecs, rows = prev_ref.shape
    width = comps * vecs
    gram = gram_in[...] * (1.0 / total)
    small = gram[16:]
    lane, comp = iota((8, 128), 1), iota((8, 128), 0)
    in_prev = (lane < width) & (lane // vecs == comp)
    coef, cross = [], []
    for k in range(S):
        line = jnp.broadcast_to(small[k : k + 1], (8, 128))
        coef.append(jnp.where(in_prev, line, 0.0))
        cross.append([jnp.where(lane == width + 8 * l + comp, line, 0.0) for l in range(k + 1)])
    coefs = jnp.concatenate(coef, axis=0)
    pieces, turns = [], {}
    for c in range(comps):
        for g in range(vecs // 8):
            t, first = PLACES[c, g]
            at = c * vecs + 8 * g
            turn = t, (at - first) % 128
            if turn not in turns:
                piece = gram[8 * t : 8 * t + 8]
                turns[turn] = pltpu.roll(piece, turn[1], 1) if turn[1] else piece
            piece = turns[turn]
            piece = jnp.where(lane < at + 8, 0.5 * piece, piece)
            piece = jnp.where((lane >= at) & (lane < (c + 1) * vecs), piece, 0.0)
            pieces.append(piece - jnp.where(lane == at + comp, 1.0, 0.0))
    half = jnp.concatenate(pieces, axis=0)
    turned = dot(coefs[:, :width], half, precision=HIGHEST)
    prev = prev_ref[...].reshape(width, rows)
    basis = jnp.concatenate([lines[...], last[...]], axis=0)
    projected = basis - dot(coefs[:, :width], prev, precision=HIGHEST)
    unit, scale = {}, {}
    for l in range(S):
        for k in range(l, S):
            value = turned[k * 8 : (k + 1) * 8] * coef[l] + turned[l * 8 : (l + 1) * 8] * coef[k] + cross[k][l]
            value = jnp.sum(value, axis=1, keepdims=True)
            for m in range(l):
                value = value - (unit[k, m] * scale[m]) * unit[l, m]
            if k == l:
                scale[l] = value
            else:
                unit[k, l] = value / scale[l]
    roots = [jnp.sqrt(scale[k]) for k in range(S)]
    lower = {(k, l): unit[k, l] * roots[l] if l < k else roots[k] for k in range(S) for l in range(k + 1)}
    vectors = []
    for k in range(S):
        value = projected[k * 8 : (k + 1) * 8]
        for l in range(k):
            value = value - unit[k, l] * vectors[l]
        vectors.append(value)
        value = value * (1.0 / roots[k])
        for c in range(comps):
            basis_ref[c, k : k + 1, :] = value[c : c + 1]
    for c in range(comps):
        factors_ref[c, :, :vecs] = small[:S, c * vecs : (c + 1) * vecs]
    for k in range(S):
        line = jnp.zeros((8, 128), jnp.float32)
        for l in range(k + 1):
            line = jnp.where(lane == l, lower[k, l], line)
        for c in range(comps):
            factors_ref[c, k : k + 1, vecs:] = line[c : c + 1, :S]


VMEM = pl.BlockSpec(memory_space=pltpu.VMEM)
HBM = pl.BlockSpec(memory_space=pltpu.HBM)


def in_hbm(*arrays):
    return [pltpu.with_memory_space_constraint(x, pltpu.HBM) for x in arrays]


def call(kernel, outs, specs, flops, moved, scratch=()):
    shapes = [jax.ShapeDtypeStruct(shape, kind) for shape, kind in outs]
    return pl.pallas_call(
        kernel,
        out_shape=shapes if len(shapes) > 1 else shapes[0],
        in_specs=specs,
        out_specs=[VMEM] * len(shapes) if len(shapes) > 1 else VMEM,
        scratch_shapes=list(scratch),
        compiler_params=pltpu.CompilerParams(vmem_limit_bytes=24 * 1024 * 1024),
        cost_estimate=pl.CostEstimate(flops=flops, bytes_accessed=moved, transcendentals=0),
    )


def send(value, target):
    return lax.ppermute(value, "dom", [(d, target[d]) for d in range(lax.axis_size("dom"))])


def neighbours(length, step, odd):
    target = {}
    for d in range(length):
        other = d + step if (d // step) % 2 == odd else d - step
        target[d] = other if 0 <= other < length else None
    return target


def ghosts(tile):
    length = lax.axis_size("dom")
    last = length - 1
    near, across = neighbours(length, 1, 0), neighbours(length, 1, 1)
    far_even, far_odd = neighbours(length, FAR, 0), neighbours(length, FAR, 1)
    across.update({0: 2, 2: 1, 1: 0, last: last - 2, last - 2: last - 1, last - 1: last})
    for d in range(length):
        if far_odd[d] is None:
            far_odd[d] = d ^ 1
    far_odd.update({1: 2, 2: 3, 3: 0, 0: 1})
    far_odd.update({last - 1: last - 2, last - 2: last - 3, last - 3: last, last: last - 1})
    return [send(tile, target) for target in (near, far_odd, far_even, across)]


def summed(value):
    length = lax.axis_size("dom")

    def fetched(step):
        return send(value, {d: d ^ (step | 1) for d in range(length)})

    value = value + fetched(1)
    step = 2
    while step < length:
        if 2 * step < length:
            farthest = fetched(3 * step)
            first, second = fetched(step), fetched(2 * step)
            value = (value + first) + (second + farthest)
        else:
            value = value + fetched(step)
        step *= 4
    return value


def local(strips, columns, send_list, send_count, shifts, prev_basis, mix):
    comps, vecs, rows = prev_basis.shape
    blocks = columns.shape[0]
    width = strips.shape[1]
    f32, bf16, dma = jnp.float32, jnp.bfloat16, pltpu.SemaphoreType.DMA
    tile_out = ((comps * blocks, 128), f32)
    tile = call(
        start_kernel,
        [((comps * blocks + 8, 128), f32)],
        [HBM] * 4,
        600000,
        250000,
        [
            pltpu.VMEM(prev_basis.shape, f32),
            pltpu.VMEM(mix.shape, f32),
            pltpu.VMEM(send_list.shape, jnp.int32),
            pltpu.VMEM(send_count.shape, jnp.int32),
            dma((4,)),
        ],
    )(*in_hbm(prev_basis, mix, send_list, send_count))
    high, low, aux = call(
        prepare_kernel,
        [((width, rows), bf16), ((width, rows), bf16), ((8 * S + 8, 128), f32)],
        [HBM] * 3,
        1000000,
        1000000,
        [
            pltpu.VMEM((4, rows // 4, width), f32),
            pltpu.VMEM(columns.shape[::-1], jnp.int32),
            pltpu.SMEM(shifts.shape, f32),
            dma((6,)),
        ],
    )(*in_hbm(strips, columns.T, shifts))
    tiles = []
    length = lax.axis_size("dom")
    tile, choose = call(
        lambda *refs: first_kernel(length, *refs),
        [tile_out, ((3 * blocks, 128), jnp.int32)],
        [VMEM] * 8,
        50000000,
        600000,
    )(tile, *ghosts(tile), aux, high, low)
    tiles.append(tile)
    for step in (1, 2):
        tile = call(
            lambda *refs, step=step: middle_kernel(step, *refs), [tile_out], [VMEM] * 9, 50000000, 600000
        )(tile, *ghosts(tile), choose, aux, high, low)
        tiles.append(tile)
    received = ghosts(tile)
    gram_out = ((24, 128), f32)
    lines, early, *parts = call(
        early_kernel,
        [((8 * S - 8, rows), f32), gram_out] + [((rows, 128), bf16)] * 3,
        [VMEM] * 4,
        60000000,
        250000,
    )(prev_basis, *tiles)
    last, gram = call(
        lambda *refs: last_kernel(vecs, *refs),
        [((8, rows), f32), gram_out],
        [VMEM] * 14,
        80000000,
        900000,
    )(tile, *received, choose, aux, high, low, early, *parts, lines)
    total = float(length * rows)
    basis, factors = call(
        lambda *refs: finish_kernel(total, *refs),
        [((comps, S, rows), f32), ((comps, S, vecs + S), f32)],
        [VMEM] * 4,
        50000000,
        400000,
    )(summed(gram), prev_basis, lines, last)
    return basis, jnp.swapaxes(factors, 1, 2)


def solution(mesh):
    in_specs = (
        P("dom", None),
        P("dom", None),
        P("dom", None, None),
        P("dom", None),
        P(),
        P(None, None, "dom"),
        P(),
    )
    out_specs = (P(None, None, "dom"), P())
    return jax.shard_map(local, mesh=mesh, in_specs=in_specs, out_specs=out_specs, check_vma=False)
```

```python
import jax
import jax.numpy as jnp
from jax import lax
from jax.experimental import pallas as pl
from jax.experimental.pallas import tpu as pltpu
from jax.sharding import PartitionSpec as P

BLOCK = 64
S = 4
FAR = 8
COMPS = 3
DEAD = 1000.0
HIGHEST = lax.Precision.HIGHEST
NN = (((1,), (0,)), ((), ()))
NT = (((1,), (1,)), ((), ()))


def dot(a, b, dims=NN, precision=None):
    return lax.dot_general(a, b, dims, precision=precision, preferred_element_type=jnp.float32)


def iota(shape, axis):
    return lax.broadcasted_iota(jnp.int32, shape, axis)


PLACES = {(c, g): (g % 2, (0, 8, 0, 0)[g] + 32 * c) for c in range(COMPS) for g in range(4)}
PLACES.update({(0, 2): (0, 96), (1, 2): (0, 112), (2, 2): (1, 96)})


def own_lanes(rows, width):
    return iota((rows, width), 1) // BLOCK == iota((rows, width), 0) % 8


def fold(masked):
    total = masked[:, :128]
    for t in range(1, masked.shape[1] // 128):
        total = total + masked[:, t * 128 : (t + 1) * 128]
    return total + pltpu.roll(total, BLOCK, 1)


def lines_of(tile, width):
    wide = jnp.concatenate([tile] * (width // 128), axis=1)
    return joined(jnp.where(own_lanes(wide.shape[0], width), wide, 0.0))


def joined(wide):
    width = wide.shape[1]
    where = iota((8, width), 0)
    result = jnp.zeros((8, width), jnp.float32)
    for c in range(COMPS):
        line = jnp.sum(wide[c * 8 : (c + 1) * 8], axis=0, keepdims=True)
        result = jnp.where(where == c, jnp.broadcast_to(line, result.shape), result)
    return result


def split(x):
    parts = []
    for _ in range(3):
        parts.append(x.astype(jnp.bfloat16))
        x = x - parts[-1].astype(jnp.float32)
    return parts


def split_dot(x, parts):
    left = [part.astype(jnp.float32) for part in split(x)]
    left.append(jnp.zeros((-3 * x.shape[0] % 16, x.shape[1]), jnp.float32))
    left = jnp.concatenate([part for part in left if part.shape[0]], axis=0).astype(jnp.bfloat16)
    products = dot(left, parts[0]) + dot(left, parts[1]) + dot(left, parts[2])
    rows = x.shape[0]
    return products[:rows] + (products[rows : 2 * rows] + products[2 * rows : 3 * rows])


def fetch(pairs, sems):
    copies = [pltpu.make_async_copy(src, dst, sems.at[i]) for i, (src, dst) in enumerate(pairs)]
    for copy in copies:
        copy.start()
    return copies


def start_kernel(
    prev_in, mix_in, list_in, count_in, strips_in, out_ref, head_ref, prev_ref, mix_ref, list_ref, count_ref, sems
):
    copies = fetch(
        [
            (prev_in, prev_ref),
            (mix_in, mix_ref),
            (list_in, list_ref),
            (count_in, count_ref),
            (strips_in.at[pl.ds(0, head_ref.shape[0])], head_ref),
        ],
        sems,
    )
    for copy in copies[1:4]:
        copy.wait()
    comps, vecs, rows = prev_ref.shape
    eye = iota((vecs, vecs), 0) == iota((vecs, vecs), 1)
    weights = []
    for c in range(comps):
        line = jnp.broadcast_to(mix_ref[c : c + 1, :], eye.shape)
        weights.append(jnp.sum(jnp.where(eye, line, 0.0), axis=1, keepdims=True))
    order = list_ref[0].astype(jnp.float32)
    order = jnp.concatenate([order, jnp.zeros((4, 120), jnp.float32)], axis=1)
    meta = jnp.zeros((8, 128), jnp.float32)
    slot = iota((1, 128), 1)
    for link in range(4):
        live = slot < jnp.broadcast_to(count_ref[0:1, link : link + 1], slot.shape)
        line = jnp.where(live, order[link : link + 1], DEAD)
        line = pltpu.roll(jnp.broadcast_to(line, (8, 128)), 8 + 8 * link, 1)
        meta = jnp.where(iota((8, 128), 1) // 8 == link + 1, line, meta)
    out_ref[8 * comps :, :] = meta
    copies[0].wait()
    own = own_lanes(8, rows)
    for c in range(comps):
        start = jnp.sum(weights[c] * prev_ref[c], axis=0, keepdims=True)
        line = jnp.broadcast_to(start, own.shape)
        out_ref[c * 8 : (c + 1) * 8, :] = fold(jnp.where(own, line, 0.0))
    copies[4].wait()


def prepare_kernel(
    head, strips_in, columns_in, shifts_in, high_ref, low_ref, aux_ref, strips, columns, shifts, sems
):
    parts, depth = strips.shape[:2]
    first = head.shape[0]
    pairs = [(strips_in.at[pl.ds(first + p * depth, depth)], strips.at[p]) for p in range(parts)]
    copies = fetch([(columns_in, columns), (shifts_in, shifts)] + pairs, sems)

    def turn(block, at):
        turned = block.T
        high = turned.astype(jnp.bfloat16)
        columns = pl.ds(at, block.shape[0])
        high_ref[:, columns] = high
        low_ref[:, columns] = (turned - high.astype(jnp.float32)).astype(jnp.bfloat16)

    turn(head[...], 0)
    copies[0].wait()
    copies[1].wait()
    where = iota((8, 128), 1)
    table = jnp.zeros((8, 128), jnp.float32)
    eye = iota((8, 8), 0) == iota((8, 8), 1)
    for k in range(columns.shape[0]):
        line = jnp.broadcast_to(columns[k : k + 1, :].astype(jnp.float32), (8, 8))
        column = jnp.sum(jnp.where(eye, line, 0.0), axis=1, keepdims=True)
        table = jnp.where(where == k, column, table)
    for k in range(S):
        aux_ref[8 * k : 8 * k + 8, :] = jnp.full((8, 128), shifts[k], jnp.float32)
    aux_ref[8 * S :, :] = table
    for p in range(parts):
        copies[2 + p].wait()
        turn(strips[p], first + p * depth)


def selection(table, metas, place, length):
    even, even_far = lax.rem(place, 2) == 0, lax.rem(place // FAR, 2) == 0
    near, far_odd, far_even, across = metas
    moved = (place == 2) | (place == length - 3)
    across = jnp.where(moved, far_odd, across)
    circle = jnp.where(moved, 16.0, 32.0)
    slots = [
        (place >= 1, jnp.where(even, circle, 8.0), jnp.where(even, across, near)),
        (place < length - 1, jnp.where(even, 8.0, circle), jnp.where(even, near, across)),
        (place >= FAR, jnp.where(even_far, 16.0, 24.0), jnp.where(even_far, far_odd, far_even)),
        (place < length - FAR, jnp.where(even_far, 24.0, 16.0), jnp.where(even_far, far_even, far_odd)),
    ]
    lane = iota((1, 128), 1)
    target = lane.astype(jnp.float32)
    for link, (valid, base, order) in enumerate(slots):
        order = order + jnp.where(valid, base, DEAD)
        target = jnp.where(lane // 8 == link + 1, order, target)
    target = jnp.broadcast_to(target, (8, 128))
    lane = iota((8, 128), 1).astype(jnp.float32)
    at = [
        jnp.sum(jnp.where(lane == table[:, k : k + 1], target, 0.0), axis=1, keepdims=True)
        for k in range(1, 4)
    ]
    return jnp.concatenate([jnp.broadcast_to(x, (8, 128)) for x in at], axis=0).astype(jnp.int32)


def product(choose, pieces, high, low):
    rows = 8 * COMPS
    front = iota((8, 128), 1) < BLOCK
    picked = [[pieces[0][8 * c : 8 * c + 8] for c in range(COMPS)]]
    for k in range(3):
        code = choose[8 * k : 8 * k + 8]
        index, place = code & 7, code >> 3
        blocks = []
        for c in range(COMPS):
            block = jnp.zeros((8, 128), jnp.float32)
            for p, piece in enumerate(pieces):
                found = jnp.take_along_axis(piece[8 * c : 8 * c + 8], index, axis=0)
                block = jnp.where(place == p, found, block)
            blocks.append(block)
        picked.append(blocks)
    x = [
        jnp.concatenate(
            [jnp.where(front, picked[2 * t][c], picked[2 * t + 1][c]) for t in range(2)], axis=1
        )
        for c in range(COMPS)
    ]
    x = jnp.concatenate(x, axis=0)
    top = x.astype(jnp.bfloat16).astype(jnp.float32)
    left = jnp.concatenate([top, x - top], axis=0).astype(jnp.bfloat16)
    both = dot(left, high) + dot(left, low)
    image = both[:rows] + both[rows:]
    return jnp.where(own_lanes(rows, image.shape[1]), image, 0.0)


def multiply(choose, pieces, shift, high, low):
    image = fold(product(choose, pieces, high, low))
    return image - jnp.concatenate([shift] * COMPS, axis=0) * pieces[0]


def first_kernel(length, own, a, b, c, d, aux, high, low, tile_ref, choose_ref):
    rows = 8 * COMPS
    refs = (own, a, b, c, d)
    pieces = [ref[:rows, :] for ref in refs]
    metas = [ref[rows : rows + 1, :] for ref in refs[1:]]
    choose = selection(aux[8 * S :, :], metas, lax.axis_index("dom"), length)
    choose_ref[...] = choose
    tile_ref[...] = multiply(choose, pieces, aux[:8, :], high[...], low[...])


def middle_kernel(step, own, a, b, c, d, choose, aux, high, low, tile_ref):
    pieces = [ref[...] for ref in (own, a, b, c, d)]
    tile_ref[...] = multiply(choose[...], pieces, aux[8 * step : 8 * step + 8, :], high[...], low[...])


def collect(gram, width, vecs):
    lane, comp = iota(gram.shape, 1), iota(gram.shape, 0)
    mine = jnp.where(lane < width, lane // vecs, lane % 8) == comp
    return jnp.sum(jnp.where(mine, gram, 0.0), axis=0, keepdims=True)


def early_kernel(prev_ref, t0, t1, t2, lines_ref, gram_ref, *split_refs):
    comps, vecs, rows = prev_ref.shape
    width = comps * vecs
    lines = jnp.concatenate([lines_of(t[...], rows) for t in (t0, t1, t2)], axis=0)
    lines_ref[...] = lines
    prev = prev_ref[...].reshape(width, rows)
    full = dot(prev, prev, NT, HIGHEST)
    full = jnp.concatenate([full, jnp.zeros((width, 128 - width), jnp.float32)], axis=1)
    lane = iota((8, 128), 1)
    tiles = [jnp.zeros((8, 128), jnp.float32)] * 2
    for (c, g), (t, first) in PLACES.items():
        at = c * vecs + 8 * g
        piece = pltpu.roll(full[at : at + 8], (first - at) % 128, 1)
        tiles[t] = jnp.where((lane >= first) & (lane < first + vecs - 8 * g), piece, tiles[t])
    gram_ref[:16, :] = jnp.concatenate(tiles, axis=0)
    against = jnp.concatenate([prev, lines, jnp.zeros((8, rows), jnp.float32)], axis=0)
    for ref, part in zip(split_refs, split(against.T)):
        ref[...] = part
    gram = dot(lines, against, NT, HIGHEST)
    result = jnp.zeros((8, 128), jnp.float32)
    for k in range(S - 1):
        line = collect(gram[k * 8 : (k + 1) * 8], width, vecs)
        result = jnp.where(iota((8, 128), 0) == k, jnp.broadcast_to(line, result.shape), result)
    gram_ref[16:, :] = result


def last_kernel(
    vecs, own, a, b, c, d, choose, aux, high, low, early, t0, t1, t2, lines, line_ref, gram_ref
):
    pieces = [ref[...] for ref in (own, a, b, c, d)]
    image = joined(product(choose[...], pieces, high[...], low[...]))
    width = COMPS * vecs
    shift = aux[8 * S - 8 : 8 * S, :1]
    last = image - shift * lines[8 * S - 16 :, :]
    line_ref[...] = last
    gram = split_dot(last, (t0[...], t1[...], t2[...]))
    square = jnp.sum(last * last, axis=1, keepdims=True)
    gram = jnp.where(iota(gram.shape, 1) == width + 8 * (S - 1) + iota(gram.shape, 0), square, gram)
    line = collect(gram, width, vecs)
    gram_ref[:16, :] = early[:16, :]
    gram_ref[16:, :] = jnp.where(
        iota((8, 128), 0) == S - 1, jnp.broadcast_to(line, (8, 128)), early[16:, :]
    )


def finish_kernel(total, gram_in, prev_ref, lines, last, basis_ref, factors_ref):
    comps, vecs, rows = prev_ref.shape
    width = comps * vecs
    gram = gram_in[...] * (1.0 / total)
    small = gram[16:]
    lane, comp = iota((8, 128), 1), iota((8, 128), 0)
    in_prev = (lane < width) & (lane // vecs == comp)
    coef, cross = [], []
    for k in range(S):
        line = jnp.broadcast_to(small[k : k + 1], (8, 128))
        coef.append(jnp.where(in_prev, line, 0.0))
        cross.append([jnp.where(lane == width + 8 * l + comp, line, 0.0) for l in range(k + 1)])
    coefs = jnp.concatenate(coef, axis=0)
    pieces, turns = [], {}
    for c in range(comps):
        for g in range(vecs // 8):
            t, first = PLACES[c, g]
            at = c * vecs + 8 * g
            turn = t, (at - first) % 128
            if turn not in turns:
                piece = gram[8 * t : 8 * t + 8]
                turns[turn] = pltpu.roll(piece, turn[1], 1) if turn[1] else piece
            piece = turns[turn]
            piece = jnp.where(lane < at + 8, 0.5 * piece, piece)
            piece = jnp.where((lane >= at) & (lane < (c + 1) * vecs), piece, 0.0)
            pieces.append(piece - jnp.where(lane == at + comp, 1.0, 0.0))
    half = jnp.concatenate(pieces, axis=0)
    turned = dot(coefs[:, :width], half, precision=HIGHEST)
    prev = prev_ref[...].reshape(width, rows)
    basis = jnp.concatenate([lines[...], last[...]], axis=0)
    projected = basis - dot(coefs[:, :width], prev, precision=HIGHEST)
    unit, scale = {}, {}
    for l in range(S):
        for k in range(l, S):
            value = turned[k * 8 : (k + 1) * 8] * coef[l] + turned[l * 8 : (l + 1) * 8] * coef[k] + cross[k][l]
            value = jnp.sum(value, axis=1, keepdims=True)
            for m in range(l):
                value = value - (unit[k, m] * scale[m]) * unit[l, m]
            if k == l:
                scale[l] = value
            else:
                unit[k, l] = value / scale[l]
    roots = [jnp.sqrt(scale[k]) for k in range(S)]
    lower = {(k, l): unit[k, l] * roots[l] if l < k else roots[k] for k in range(S) for l in range(k + 1)}
    vectors = []
    for k in range(S):
        value = projected[k * 8 : (k + 1) * 8]
        for l in range(k):
            value = value - unit[k, l] * vectors[l]
        vectors.append(value)
        value = value * (1.0 / roots[k])
        for c in range(comps):
            basis_ref[c, k : k + 1, :] = value[c : c + 1]
    for c in range(comps):
        factors_ref[c, :, :vecs] = small[:S, c * vecs : (c + 1) * vecs]
    for k in range(S):
        line = jnp.zeros((8, 128), jnp.float32)
        for l in range(k + 1):
            line = jnp.where(lane == l, lower[k, l], line)
        for c in range(comps):
            factors_ref[c, k : k + 1, vecs:] = line[c : c + 1, :S]


VMEM = pl.BlockSpec(memory_space=pltpu.VMEM)
HBM = pl.BlockSpec(memory_space=pltpu.HBM)


def in_hbm(*arrays):
    return [pltpu.with_memory_space_constraint(x, pltpu.HBM) for x in arrays]


def call(kernel, outs, specs, flops, moved, scratch=()):
    shapes = [jax.ShapeDtypeStruct(shape, kind) for shape, kind in outs]
    return pl.pallas_call(
        kernel,
        out_shape=shapes if len(shapes) > 1 else shapes[0],
        in_specs=specs,
        out_specs=[VMEM] * len(shapes) if len(shapes) > 1 else VMEM,
        scratch_shapes=list(scratch),
        compiler_params=pltpu.CompilerParams(vmem_limit_bytes=24 * 1024 * 1024),
        cost_estimate=pl.CostEstimate(flops=flops, bytes_accessed=moved, transcendentals=0),
    )


def send(value, target):
    return lax.ppermute(value, "dom", [(d, target[d]) for d in range(lax.axis_size("dom"))])


def neighbours(length, step, odd):
    target = {}
    for d in range(length):
        other = d + step if (d // step) % 2 == odd else d - step
        target[d] = other if 0 <= other < length else None
    return target


def ghosts(tile):
    length = lax.axis_size("dom")
    last = length - 1
    near, across = neighbours(length, 1, 0), neighbours(length, 1, 1)
    far_even, far_odd = neighbours(length, FAR, 0), neighbours(length, FAR, 1)
    across.update({0: 2, 2: 1, 1: 0, last: last - 2, last - 2: last - 1, last - 1: last})
    for d in range(length):
        if far_odd[d] is None:
            far_odd[d] = d ^ 1
    far_odd.update({1: 2, 2: 3, 3: 0, 0: 1})
    far_odd.update({last - 1: last - 2, last - 2: last - 3, last - 3: last, last: last - 1})
    return [send(tile, target) for target in (near, far_odd, far_even, across)]


def summed(value):
    length = lax.axis_size("dom")

    def fetched(step):
        return send(value, {d: d ^ (step | 1) for d in range(length)})

    value = value + fetched(1)
    step = 2
    while step < length:
        if 2 * step < length:
            farthest = fetched(3 * step)
            first, second = fetched(step), fetched(2 * step)
            value = (value + first) + (second + farthest)
        else:
            value = value + fetched(step)
        step *= 4
    return value


def local(strips, columns, send_list, send_count, shifts, prev_basis, mix):
    comps, vecs, rows = prev_basis.shape
    blocks = columns.shape[0]
    width = strips.shape[1]
    f32, bf16, dma = jnp.float32, jnp.bfloat16, pltpu.SemaphoreType.DMA
    tile_out = ((comps * blocks, 128), f32)
    tile, head = call(
        start_kernel,
        [((comps * blocks + 8, 128), f32), ((rows // 2, width), f32)],
        [HBM] * 5,
        600000,
        250000,
        [
            pltpu.VMEM(prev_basis.shape, f32),
            pltpu.VMEM(mix.shape, f32),
            pltpu.VMEM(send_list.shape, jnp.int32),
            pltpu.VMEM(send_count.shape, jnp.int32),
            dma((5,)),
        ],
    )(*in_hbm(prev_basis, mix, send_list, send_count, strips))
    high, low, aux = call(
        prepare_kernel,
        [((width, rows), bf16), ((width, rows), bf16), ((8 * S + 8, 128), f32)],
        [VMEM] + [HBM] * 3,
        1000000,
        1000000,
        [
            pltpu.VMEM((2, rows // 4, width), f32),
            pltpu.VMEM(columns.shape[::-1], jnp.int32),
            pltpu.SMEM(shifts.shape, f32),
            dma((4,)),
        ],
    )(head, *in_hbm(strips, columns.T, shifts))
    tiles = []
    length = lax.axis_size("dom")
    tile, choose = call(
        lambda *refs: first_kernel(length, *refs),
        [tile_out, ((3 * blocks, 128), jnp.int32)],
        [VMEM] * 8,
        50000000,
        600000,
    )(tile, *ghosts(tile), aux, high, low)
    tiles.append(tile)
    for step in (1, 2):
        tile = call(
            lambda *refs, step=step: middle_kernel(step, *refs), [tile_out], [VMEM] * 9, 50000000, 600000
        )(tile, *ghosts(tile), choose, aux, high, low)
        tiles.append(tile)
    received = ghosts(tile)
    gram_out = ((24, 128), f32)
    lines, early, *parts = call(
        early_kernel,
        [((8 * S - 8, rows), f32), gram_out] + [((rows, 128), bf16)] * 3,
        [VMEM] * 4,
        60000000,
        250000,
    )(prev_basis, *tiles)
    last, gram = call(
        lambda *refs: last_kernel(vecs, *refs),
        [((8, rows), f32), gram_out],
        [VMEM] * 14,
        80000000,
        900000,
    )(tile, *received, choose, aux, high, low, early, *parts, lines)
    total = float(length * rows)
    basis, factors = call(
        lambda *refs: finish_kernel(total, *refs),
        [((comps, S, rows), f32), ((comps, S, vecs + S), f32)],
        [VMEM] * 4,
        50000000,
        400000,
    )(summed(gram), prev_basis, lines, last)
    return basis, jnp.swapaxes(factors, 1, 2)


def solution(mesh):
    in_specs = (
        P("dom", None),
        P("dom", None),
        P("dom", None, None),
        P("dom", None),
        P(),
        P(None, None, "dom"),
        P(),
    )
    out_specs = (P(None, None, "dom"), P())
    return jax.shard_map(local, mesh=mesh, in_specs=in_specs, out_specs=out_specs, check_vma=False)
```

```python
import jax
import jax.numpy as jnp
from jax import lax
from jax.experimental import pallas as pl
from jax.experimental.pallas import tpu as pltpu
from jax.sharding import PartitionSpec as P

BLOCK = 64
S = 4
FAR = 8
COMPS = 3
DEAD = 1000.0
HIGHEST = lax.Precision.HIGHEST
NN = (((1,), (0,)), ((), ()))
NT = (((1,), (1,)), ((), ()))


def dot(a, b, dims=NN, precision=None):
    return lax.dot_general(a, b, dims, precision=precision, preferred_element_type=jnp.float32)


def iota(shape, axis):
    return lax.broadcasted_iota(jnp.int32, shape, axis)


PLACES = {(c, g): (g % 2, (0, 8, 0, 0)[g] + 32 * c) for c in range(COMPS) for g in range(4)}
PLACES.update({(0, 2): (0, 96), (1, 2): (0, 112), (2, 2): (1, 96)})


def own_lanes(rows, width):
    return iota((rows, width), 1) // BLOCK == iota((rows, width), 0) % 8


def fold(masked):
    total = masked[:, :128]
    for t in range(1, masked.shape[1] // 128):
        total = total + masked[:, t * 128 : (t + 1) * 128]
    return total + pltpu.roll(total, BLOCK, 1)


def lines_of(tile, width):
    wide = jnp.concatenate([tile] * (width // 128), axis=1)
    return joined(jnp.where(own_lanes(wide.shape[0], width), wide, 0.0))


def joined(wide):
    width = wide.shape[1]
    where = iota((8, width), 0)
    result = jnp.zeros((8, width), jnp.float32)
    for c in range(COMPS):
        line = jnp.sum(wide[c * 8 : (c + 1) * 8], axis=0, keepdims=True)
        result = jnp.where(where == c, jnp.broadcast_to(line, result.shape), result)
    return result


def split(x):
    parts = []
    for _ in range(3):
        parts.append(x.astype(jnp.bfloat16))
        x = x - parts[-1].astype(jnp.float32)
    return parts


def split_dot(x, parts):
    left = [part.astype(jnp.float32) for part in split(x)]
    left.append(jnp.zeros((-3 * x.shape[0] % 16, x.shape[1]), jnp.float32))
    left = jnp.concatenate([part for part in left if part.shape[0]], axis=0).astype(jnp.bfloat16)
    products = dot(left, parts[0]) + dot(left, parts[1]) + dot(left, parts[2])
    rows = x.shape[0]
    return products[:rows] + (products[rows : 2 * rows] + products[2 * rows : 3 * rows])


def fetch(pairs, sems):
    copies = [pltpu.make_async_copy(src, dst, sems.at[i]) for i, (src, dst) in enumerate(pairs)]
    for copy in copies:
        copy.start()
    return copies


def start_kernel(prev_in, mix_in, list_in, count_in, out_ref, prev_ref, mix_ref, list_ref, count_ref, sems):
    copies = fetch(
        [(prev_in, prev_ref), (mix_in, mix_ref), (list_in, list_ref), (count_in, count_ref)], sems
    )
    for copy in copies[1:]:
        copy.wait()
    comps, vecs, rows = prev_ref.shape
    eye = iota((vecs, vecs), 0) == iota((vecs, vecs), 1)
    weights = []
    for c in range(comps):
        line = jnp.broadcast_to(mix_ref[c : c + 1, :], eye.shape)
        weights.append(jnp.sum(jnp.where(eye, line, 0.0), axis=1, keepdims=True))
    order = list_ref[0].astype(jnp.float32)
    order = jnp.concatenate([order, jnp.zeros((4, 120), jnp.float32)], axis=1)
    meta = jnp.zeros((8, 128), jnp.float32)
    slot = iota((1, 128), 1)
    for link in range(4):
        live = slot < jnp.broadcast_to(count_ref[0:1, link : link + 1], slot.shape)
        line = jnp.where(live, order[link : link + 1], DEAD)
        line = pltpu.roll(jnp.broadcast_to(line, (8, 128)), 8 + 8 * link, 1)
        meta = jnp.where(iota((8, 128), 1) // 8 == link + 1, line, meta)
    out_ref[8 * comps :, :] = meta
    copies[0].wait()
    own = own_lanes(8, rows)
    for c in range(comps):
        start = jnp.sum(weights[c] * prev_ref[c], axis=0, keepdims=True)
        line = jnp.broadcast_to(start, own.shape)
        out_ref[c * 8 : (c + 1) * 8, :] = fold(jnp.where(own, line, 0.0))


def prepare_kernel(strips_in, columns_in, shifts_in, high_ref, low_ref, aux_ref, strips, columns, shifts, sems):
    parts = strips.shape[0]
    depth = strips.shape[1]
    pairs = [(columns_in, columns), (shifts_in, shifts)]
    pairs += [(strips_in.at[pl.ds(p * depth, depth)], strips.at[p]) for p in range(parts)]
    copies = fetch(pairs, sems)
    copies[0].wait()
    copies[1].wait()
    eye = iota((8, 8), 0) == iota((8, 8), 1)
    for k in range(1, columns.shape[0]):
        line = jnp.broadcast_to(columns[k : k + 1, :].astype(jnp.float32), (8, 8))
        column = jnp.sum(jnp.where(eye, line, 0.0), axis=1, keepdims=True)
        at = 8 * S + 8 * (k - 1)
        aux_ref[at : at + 8, :] = jnp.broadcast_to(column, (8, 128))
    for k in range(S):
        aux_ref[8 * k : 8 * k + 8, :] = jnp.full((8, 128), shifts[k], jnp.float32)
    for p in range(parts):
        copies[2 + p].wait()
        turned = strips[p].T
        high = turned.astype(jnp.bfloat16)
        high_ref[:, p * depth : (p + 1) * depth] = high
        low_ref[:, p * depth : (p + 1) * depth] = (turned - high.astype(jnp.float32)).astype(jnp.bfloat16)


def selection(table, metas, place, length):
    even, even_far = lax.rem(place, 2) == 0, lax.rem(place // FAR, 2) == 0
    near, far_odd, far_even, across = metas
    moved = (place == 2) | (place == length - 3)
    across = jnp.where(moved, far_odd, across)
    circle = jnp.where(moved, 16.0, 32.0)
    slots = [
        (place >= 1, jnp.where(even, circle, 8.0), jnp.where(even, across, near)),
        (place < length - 1, jnp.where(even, 8.0, circle), jnp.where(even, near, across)),
        (place >= FAR, jnp.where(even_far, 16.0, 24.0), jnp.where(even_far, far_odd, far_even)),
        (place < length - FAR, jnp.where(even_far, 24.0, 16.0), jnp.where(even_far, far_even, far_odd)),
    ]
    lane = iota((1, 128), 1)
    target = lane.astype(jnp.float32)
    for link, (valid, base, order) in enumerate(slots):
        order = order + jnp.where(valid, base, DEAD)
        target = jnp.where(lane // 8 == link + 1, order, target)
    target = jnp.broadcast_to(target, (8, 128))
    index = table.astype(jnp.int32)
    at = [jnp.take_along_axis(target, index[8 * k : 8 * k + 8], axis=1) for k in range(3)]
    return jnp.concatenate(at, axis=0).astype(jnp.int32)


def product(choose, pieces, high, low):
    rows = 8 * COMPS
    front = iota((8, 128), 1) < BLOCK
    picked = [[pieces[0][8 * c : 8 * c + 8] for c in range(COMPS)]]
    for k in range(3):
        code = choose[8 * k : 8 * k + 8]
        index, place = code & 7, code >> 3
        blocks = []
        for c in range(COMPS):
            block = jnp.zeros((8, 128), jnp.float32)
            for p, piece in enumerate(pieces):
                found = jnp.take_along_axis(piece[8 * c : 8 * c + 8], index, axis=0)
                block = jnp.where(place == p, found, block)
            blocks.append(block)
        picked.append(blocks)
    x = [
        jnp.concatenate(
            [jnp.where(front, picked[2 * t][c], picked[2 * t + 1][c]) for t in range(2)], axis=1
        )
        for c in range(COMPS)
    ]
    x = jnp.concatenate(x, axis=0)
    top = x.astype(jnp.bfloat16).astype(jnp.float32)
    left = jnp.concatenate([top, x - top], axis=0).astype(jnp.bfloat16)
    both = dot(left, high) + dot(left, low)
    image = both[:rows] + both[rows:]
    return jnp.where(own_lanes(rows, image.shape[1]), image, 0.0)


def multiply(choose, pieces, shift, high, low):
    image = fold(product(choose, pieces, high, low))
    return image - jnp.concatenate([shift] * COMPS, axis=0) * pieces[0]


def first_kernel(length, own, a, b, c, d, aux, high, low, tile_ref, choose_ref):
    rows = 8 * COMPS
    refs = (own, a, b, c, d)
    pieces = [ref[:rows, :] for ref in refs]
    metas = [ref[rows : rows + 1, :] for ref in refs[1:]]
    choose = selection(aux[8 * S :, :], metas, lax.axis_index("dom"), length)
    choose_ref[...] = choose
    tile_ref[...] = multiply(choose, pieces, aux[:8, :], high[...], low[...])


def middle_kernel(step, own, a, b, c, d, choose, aux, high, low, tile_ref):
    pieces = [ref[...] for ref in (own, a, b, c, d)]
    tile_ref[...] = multiply(choose[...], pieces, aux[8 * step : 8 * step + 8, :], high[...], low[...])


def collect(gram, width, vecs):
    lane, comp = iota(gram.shape, 1), iota(gram.shape, 0)
    mine = jnp.where(lane < width, lane // vecs, lane % 8) == comp
    return jnp.sum(jnp.where(mine, gram, 0.0), axis=0, keepdims=True)


def early_kernel(prev_ref, t0, t1, t2, lines_ref, gram_ref, *split_refs):
    comps, vecs, rows = prev_ref.shape
    width = comps * vecs
    lines = jnp.concatenate([lines_of(t[...], rows) for t in (t0, t1, t2)], axis=0)
    lines_ref[...] = lines
    prev = prev_ref[...].reshape(width, rows)
    full = dot(prev, prev, NT, HIGHEST)
    full = jnp.concatenate([full, jnp.zeros((width, 128 - width), jnp.float32)], axis=1)
    lane = iota((8, 128), 1)
    tiles = [jnp.zeros((8, 128), jnp.float32)] * 2
    for (c, g), (t, first) in PLACES.items():
        at = c * vecs + 8 * g
        piece = pltpu.roll(full[at : at + 8], (first - at) % 128, 1)
        tiles[t] = jnp.where((lane >= first) & (lane < first + vecs - 8 * g), piece, tiles[t])
    gram_ref[:16, :] = jnp.concatenate(tiles, axis=0)
    against = jnp.concatenate([prev, lines, jnp.zeros((8, rows), jnp.float32)], axis=0)
    for ref, part in zip(split_refs, split(against.T)):
        ref[...] = part
    gram = dot(lines, against, NT, HIGHEST)
    result = jnp.zeros((8, 128), jnp.float32)
    for k in range(S - 1):
        line = collect(gram[k * 8 : (k + 1) * 8], width, vecs)
        result = jnp.where(iota((8, 128), 0) == k, jnp.broadcast_to(line, result.shape), result)
    gram_ref[16:, :] = result


def last_kernel(
    vecs, own, a, b, c, d, choose, aux, high, low, early, t0, t1, t2, lines, line_ref, gram_ref
):
    pieces = [ref[...] for ref in (own, a, b, c, d)]
    image = joined(product(choose[...], pieces, high[...], low[...]))
    width = COMPS * vecs
    shift = aux[8 * S - 8 : 8 * S, :1]
    last = image - shift * lines[8 * S - 16 :, :]
    line_ref[...] = last
    gram = split_dot(last, (t0[...], t1[...], t2[...]))
    square = jnp.sum(last * last, axis=1, keepdims=True)
    gram = jnp.where(iota(gram.shape, 1) == width + 8 * (S - 1) + iota(gram.shape, 0), square, gram)
    line = collect(gram, width, vecs)
    gram_ref[:16, :] = early[:16, :]
    gram_ref[16:, :] = jnp.where(
        iota((8, 128), 0) == S - 1, jnp.broadcast_to(line, (8, 128)), early[16:, :]
    )


def finish_kernel(total, gram_ins, prev_ref, lines, last, basis_ref, factors_ref):
    comps, vecs, rows = prev_ref.shape
    width = comps * vecs
    gram = added([ref[...] for ref in gram_ins]) * (1.0 / total)
    small = gram[16:]
    lane, comp = iota((8, 128), 1), iota((8, 128), 0)
    in_prev = (lane < width) & (lane // vecs == comp)
    coef, cross = [], []
    for k in range(S):
        line = jnp.broadcast_to(small[k : k + 1], (8, 128))
        coef.append(jnp.where(in_prev, line, 0.0))
        cross.append([jnp.where(lane == width + 8 * l + comp, line, 0.0) for l in range(k + 1)])
    coefs = jnp.concatenate(coef, axis=0)
    pieces, turns = [], {}
    for c in range(comps):
        for g in range(vecs // 8):
            t, first = PLACES[c, g]
            at = c * vecs + 8 * g
            turn = t, (at - first) % 128
            if turn not in turns:
                piece = gram[8 * t : 8 * t + 8]
                turns[turn] = pltpu.roll(piece, turn[1], 1) if turn[1] else piece
            piece = turns[turn]
            piece = jnp.where(lane < at + 8, 0.5 * piece, piece)
            piece = jnp.where((lane >= at) & (lane < (c + 1) * vecs), piece, 0.0)
            pieces.append(piece - jnp.where(lane == at + comp, 1.0, 0.0))
    half = jnp.concatenate(pieces, axis=0)
    turned = dot(coefs[:, :width], half, precision=HIGHEST)
    prev = prev_ref[...].reshape(width, rows)
    basis = jnp.concatenate([lines[...], last[...]], axis=0)
    projected = basis - dot(coefs[:, :width], prev, precision=HIGHEST)
    unit, scale = {}, {}
    for l in range(S):
        for k in range(l, S):
            value = turned[k * 8 : (k + 1) * 8] * coef[l] + turned[l * 8 : (l + 1) * 8] * coef[k] + cross[k][l]
            value = jnp.sum(value, axis=1, keepdims=True)
            for m in range(l):
                value = value - (unit[k, m] * scale[m]) * unit[l, m]
            if k == l:
                scale[l] = value
            else:
                unit[k, l] = value / scale[l]
    roots = [jnp.sqrt(scale[k]) for k in range(S)]
    lower = {(k, l): unit[k, l] * roots[l] if l < k else roots[k] for k in range(S) for l in range(k + 1)}
    vectors = []
    for k in range(S):
        value = projected[k * 8 : (k + 1) * 8]
        for l in range(k):
            value = value - unit[k, l] * vectors[l]
        vectors.append(value)
        value = value * (1.0 / roots[k])
        for c in range(comps):
            basis_ref[c, k : k + 1, :] = value[c : c + 1]
    for c in range(comps):
        factors_ref[c, :, :vecs] = small[:S, c * vecs : (c + 1) * vecs]
    for k in range(S):
        line = jnp.zeros((8, 128), jnp.float32)
        for l in range(k + 1):
            line = jnp.where(lane == l, lower[k, l], line)
        for c in range(comps):
            factors_ref[c, k : k + 1, vecs:] = line[c : c + 1, :S]


VMEM = pl.BlockSpec(memory_space=pltpu.VMEM)
HBM = pl.BlockSpec(memory_space=pltpu.HBM)


def in_hbm(*arrays):
    return [pltpu.with_memory_space_constraint(x, pltpu.HBM) for x in arrays]


def call(kernel, outs, specs, flops, moved, scratch=()):
    shapes = [jax.ShapeDtypeStruct(shape, kind) for shape, kind in outs]
    return pl.pallas_call(
        kernel,
        out_shape=shapes if len(shapes) > 1 else shapes[0],
        in_specs=specs,
        out_specs=[VMEM] * len(shapes) if len(shapes) > 1 else VMEM,
        scratch_shapes=list(scratch),
        compiler_params=pltpu.CompilerParams(vmem_limit_bytes=24 * 1024 * 1024),
        cost_estimate=pl.CostEstimate(flops=flops, bytes_accessed=moved, transcendentals=0),
    )


def send(value, target):
    return lax.ppermute(value, "dom", [(d, target[d]) for d in range(lax.axis_size("dom"))])


def neighbours(length, step, odd):
    target = {}
    for d in range(length):
        other = d + step if (d // step) % 2 == odd else d - step
        target[d] = other if 0 <= other < length else None
    return target


def ghosts(tile):
    length = lax.axis_size("dom")
    last = length - 1
    near, across = neighbours(length, 1, 0), neighbours(length, 1, 1)
    far_even, far_odd = neighbours(length, FAR, 0), neighbours(length, FAR, 1)
    across.update({0: 2, 2: 1, 1: 0, last: last - 2, last - 2: last - 1, last - 1: last})
    for d in range(length):
        if far_odd[d] is None:
            far_odd[d] = d ^ 1
    far_odd.update({1: 2, 2: 3, 3: 0, 0: 1})
    far_odd.update({last - 1: last - 2, last - 2: last - 3, last - 3: last, last: last - 1})
    return [send(tile, target) for target in (near, far_odd, far_even, across)]


def summed(value):
    length = lax.axis_size("dom")

    def fetched(step):
        return send(value, {d: d ^ (step | 1) for d in range(length)})

    parts = [value, fetched(1)]
    step = 2
    while step < length:
        value = added(parts)
        steps = (3 * step, step, 2 * step) if 2 * step < length else (step,)
        got = [fetched(s) for s in steps]
        parts = [value] + got[1:] + got[:1]
        step *= 4
    return parts


def added(parts):
    if len(parts) == 2:
        return parts[0] + parts[1]
    return (parts[0] + parts[1]) + (parts[2] + parts[3])


def local(strips, columns, send_list, send_count, shifts, prev_basis, mix):
    comps, vecs, rows = prev_basis.shape
    blocks = columns.shape[0]
    width = strips.shape[1]
    f32, bf16, dma = jnp.float32, jnp.bfloat16, pltpu.SemaphoreType.DMA
    tile_out = ((comps * blocks, 128), f32)
    tile = call(
        start_kernel,
        [((comps * blocks + 8, 128), f32)],
        [HBM] * 4,
        600000,
        250000,
        [
            pltpu.VMEM(prev_basis.shape, f32),
            pltpu.VMEM(mix.shape, f32),
            pltpu.VMEM(send_list.shape, jnp.int32),
            pltpu.VMEM(send_count.shape, jnp.int32),
            dma((4,)),
        ],
    )(*in_hbm(prev_basis, mix, send_list, send_count))
    high, low, aux = call(
        prepare_kernel,
        [((width, rows), bf16), ((width, rows), bf16), ((8 * S + 24, 128), f32)],
        [HBM] * 3,
        1000000,
        1000000,
        [
            pltpu.VMEM((4, rows // 4, width), f32),
            pltpu.VMEM(columns.shape[::-1], jnp.int32),
            pltpu.SMEM(shifts.shape, f32),
            dma((6,)),
        ],
    )(*in_hbm(strips, columns.T, shifts))
    tiles = []
    length = lax.axis_size("dom")
    tile, choose = call(
        lambda *refs: first_kernel(length, *refs),
        [tile_out, ((3 * blocks, 128), jnp.int32)],
        [VMEM] * 8,
        50000000,
        600000,
    )(tile, *ghosts(tile), aux, high, low)
    tiles.append(tile)
    for step in (1, 2):
        tile = call(
            lambda *refs, step=step: middle_kernel(step, *refs), [tile_out], [VMEM] * 9, 50000000, 600000
        )(tile, *ghosts(tile), choose, aux, high, low)
        tiles.append(tile)
    received = ghosts(tile)
    gram_out = ((24, 128), f32)
    lines, early, *parts = call(
        early_kernel,
        [((8 * S - 8, rows), f32), gram_out] + [((rows, 128), bf16)] * 3,
        [VMEM] * 4,
        60000000,
        250000,
    )(prev_basis, *tiles)
    last, gram = call(
        lambda *refs: last_kernel(vecs, *refs),
        [((8, rows), f32), gram_out],
        [VMEM] * 14,
        80000000,
        900000,
    )(tile, *received, choose, aux, high, low, early, *parts, lines)
    total = float(length * rows)
    parts = summed(gram)
    count = len(parts)
    basis, factors = call(
        lambda *refs: finish_kernel(total, refs[:count], *refs[count:]),
        [((comps, S, rows), f32), ((comps, S, vecs + S), f32)],
        [VMEM] * (count + 3),
        50000000,
        400000,
    )(*parts, prev_basis, lines, last)
    return basis, jnp.swapaxes(factors, 1, 2)


def solution(mesh):
    in_specs = (
        P("dom", None),
        P("dom", None),
        P("dom", None, None),
        P("dom", None),
        P(),
        P(None, None, "dom"),
        P(),
    )
    out_specs = (P(None, None, "dom"), P())
    return jax.shard_map(local, mesh=mesh, in_specs=in_specs, out_specs=out_specs, check_vma=False)
```

```python
import jax
import jax.numpy as jnp
from jax import lax
from jax.experimental import pallas as pl
from jax.experimental.pallas import tpu as pltpu
from jax.sharding import PartitionSpec as P

BLOCK = 64
S = 4
FAR = 8
COMPS = 3
DEAD = 1000.0
HIGHEST = lax.Precision.HIGHEST
NN = (((1,), (0,)), ((), ()))
NT = (((1,), (1,)), ((), ()))


def dot(a, b, dims=NN, precision=None):
    return lax.dot_general(a, b, dims, precision=precision, preferred_element_type=jnp.float32)


def iota(shape, axis):
    return lax.broadcasted_iota(jnp.int32, shape, axis)


PLACES = {(c, g): (g % 2, (0, 8, 0, 0)[g] + 32 * c) for c in range(COMPS) for g in range(4)}
PLACES.update({(0, 2): (0, 96), (1, 2): (0, 112), (2, 2): (1, 96)})


def own_lanes(rows, width):
    return iota((rows, width), 1) // BLOCK == iota((rows, width), 0) % 8


def fold(masked):
    total = masked[:, :128]
    for t in range(1, masked.shape[1] // 128):
        total = total + masked[:, t * 128 : (t + 1) * 128]
    return total + pltpu.roll(total, BLOCK, 1)


def lines_of(tile, width):
    wide = jnp.concatenate([tile] * (width // 128), axis=1)
    return joined(jnp.where(own_lanes(wide.shape[0], width), wide, 0.0))


def joined(wide):
    width = wide.shape[1]
    where = iota((8, width), 0)
    result = jnp.zeros((8, width), jnp.float32)
    for c in range(COMPS):
        line = jnp.sum(wide[c * 8 : (c + 1) * 8], axis=0, keepdims=True)
        result = jnp.where(where == c, jnp.broadcast_to(line, result.shape), result)
    return result


def split(x):
    parts = []
    for _ in range(3):
        parts.append(x.astype(jnp.bfloat16))
        x = x - parts[-1].astype(jnp.float32)
    return parts


def split_dot(x, parts):
    left = [part.astype(jnp.float32) for part in split(x)]
    left.append(jnp.zeros((-3 * x.shape[0] % 16, x.shape[1]), jnp.float32))
    left = jnp.concatenate([part for part in left if part.shape[0]], axis=0).astype(jnp.bfloat16)
    products = dot(left, parts[0]) + dot(left, parts[1]) + dot(left, parts[2])
    rows = x.shape[0]
    return products[:rows] + (products[rows : 2 * rows] + products[2 * rows : 3 * rows])


def fetch(pairs, sems):
    copies = [pltpu.make_async_copy(src, dst, sems.at[i]) for i, (src, dst) in enumerate(pairs)]
    for copy in copies:
        copy.start()
    return copies


def start_kernel(prev_in, mix_in, list_in, count_in, out_ref, prev_ref, mix_ref, list_ref, count_ref, sems):
    copies = fetch(
        [(prev_in, prev_ref), (mix_in, mix_ref), (list_in, list_ref), (count_in, count_ref)], sems
    )
    for copy in copies[1:]:
        copy.wait()
    comps, vecs, rows = prev_ref.shape
    eye = iota((vecs, vecs), 0) == iota((vecs, vecs), 1)
    weights = []
    for c in range(comps):
        line = jnp.broadcast_to(mix_ref[c : c + 1, :], eye.shape)
        weights.append(jnp.sum(jnp.where(eye, line, 0.0), axis=1, keepdims=True))
    order = list_ref[0].astype(jnp.float32)
    order = jnp.concatenate([order, jnp.zeros((4, 120), jnp.float32)], axis=1)
    meta = jnp.zeros((8, 128), jnp.float32)
    slot = iota((1, 128), 1)
    for link in range(4):
        live = slot < jnp.broadcast_to(count_ref[0:1, link : link + 1], slot.shape)
        line = jnp.where(live, order[link : link + 1], DEAD)
        line = pltpu.roll(jnp.broadcast_to(line, (8, 128)), 8 + 8 * link, 1)
        meta = jnp.where(iota((8, 128), 1) // 8 == link + 1, line, meta)
    out_ref[8 * comps :, :] = meta
    copies[0].wait()
    own = own_lanes(8, rows)
    for c in range(comps):
        start = jnp.sum(weights[c] * prev_ref[c], axis=0, keepdims=True)
        line = jnp.broadcast_to(start, own.shape)
        out_ref[c * 8 : (c + 1) * 8, :] = fold(jnp.where(own, line, 0.0))


def prepare_kernel(strips_in, columns_in, shifts_in, high_ref, low_ref, aux_ref, strips, columns, shifts, sems):
    parts = strips.shape[0]
    depth = strips.shape[1]
    pairs = [(columns_in, columns), (shifts_in, shifts)]
    pairs += [(strips_in.at[pl.ds(p * depth, depth)], strips.at[p]) for p in range(parts)]
    copies = fetch(pairs, sems)
    copies[0].wait()
    copies[1].wait()
    eye = iota((8, 8), 0) == iota((8, 8), 1)
    for k in range(1, columns.shape[0]):
        line = jnp.broadcast_to(columns[k : k + 1, :].astype(jnp.float32), (8, 8))
        column = jnp.sum(jnp.where(eye, line, 0.0), axis=1, keepdims=True)
        at = 8 * S + 8 * (k - 1)
        aux_ref[at : at + 8, :] = jnp.broadcast_to(column, (8, 128))
    for k in range(S):
        aux_ref[8 * k : 8 * k + 8, :] = jnp.full((8, 128), shifts[k], jnp.float32)
    for p in range(parts):
        copies[2 + p].wait()
        turned = strips[p].T
        high = turned.astype(jnp.bfloat16)
        high_ref[:, p * depth : (p + 1) * depth] = high
        low_ref[:, p * depth : (p + 1) * depth] = (turned - high.astype(jnp.float32)).astype(jnp.bfloat16)


def selection(table, metas, place, length):
    even, even_far = lax.rem(place, 2) == 0, lax.rem(place // FAR, 2) == 0
    near, far_odd, far_even, across = metas
    moved = (place == 2) | (place == length - 3)
    across = jnp.where(moved, far_odd, across)
    circle = jnp.where(moved, 16.0, 32.0)
    slots = [
        (place >= 1, jnp.where(even, circle, 8.0), jnp.where(even, across, near)),
        (place < length - 1, jnp.where(even, 8.0, circle), jnp.where(even, near, across)),
        (place >= FAR, jnp.where(even_far, 16.0, 24.0), jnp.where(even_far, far_odd, far_even)),
        (place < length - FAR, jnp.where(even_far, 24.0, 16.0), jnp.where(even_far, far_even, far_odd)),
    ]
    lane = iota((1, 128), 1)
    target = lane.astype(jnp.float32)
    for link, (valid, base, order) in enumerate(slots):
        order = order + jnp.where(valid, base, DEAD)
        target = jnp.where(lane // 8 == link + 1, order, target)
    target = jnp.broadcast_to(target, (8, 128))
    index = table.astype(jnp.int32)
    at = [jnp.take_along_axis(target, index[8 * k : 8 * k + 8], axis=1) for k in range(3)]
    return jnp.concatenate(at, axis=0).astype(jnp.int32)


def product(choose, pieces, high, low):
    rows = 8 * COMPS
    front = iota((8, 128), 1) < BLOCK
    picked = [[pieces[0][8 * c : 8 * c + 8] for c in range(COMPS)]]
    for k in range(3):
        code = choose[8 * k : 8 * k + 8]
        index, place = code & 7, code >> 3
        blocks = []
        for c in range(COMPS):
            block = jnp.zeros((8, 128), jnp.float32)
            for p, piece in enumerate(pieces):
                found = jnp.take_along_axis(piece[8 * c : 8 * c + 8], index, axis=0)
                block = jnp.where(place == p, found, block)
            blocks.append(block)
        picked.append(blocks)
    x = [
        jnp.concatenate(
            [jnp.where(front, picked[2 * t][c], picked[2 * t + 1][c]) for t in range(2)], axis=1
        )
        for c in range(COMPS)
    ]
    x = jnp.concatenate(x, axis=0)
    top = x.astype(jnp.bfloat16).astype(jnp.float32)
    left = jnp.concatenate([top, x - top], axis=0).astype(jnp.bfloat16)
    both = dot(left, high) + dot(left, low)
    image = both[:rows] + both[rows:]
    return jnp.where(own_lanes(rows, image.shape[1]), image, 0.0)


def multiply(choose, pieces, shift, high, low):
    image = fold(product(choose, pieces, high, low))
    return image - jnp.concatenate([shift] * COMPS, axis=0) * pieces[0]


def first_kernel(length, own, a, c, d, b, aux, high, low, tile_ref, choose_ref):
    rows = 8 * COMPS
    refs = (own, a, b, c, d)
    pieces = [ref[:rows, :] for ref in refs]
    metas = [ref[rows : rows + 1, :] for ref in refs[1:]]
    choose = selection(aux[8 * S :, :], metas, lax.axis_index("dom"), length)
    choose_ref[...] = choose
    tile_ref[...] = multiply(choose, pieces, aux[:8, :], high[...], low[...])


def middle_kernel(step, own, a, b, c, d, choose, aux, high, low, tile_ref):
    pieces = [ref[...] for ref in (own, a, b, c, d)]
    tile_ref[...] = multiply(choose[...], pieces, aux[8 * step : 8 * step + 8, :], high[...], low[...])


def collect(gram, width, vecs):
    lane, comp = iota(gram.shape, 1), iota(gram.shape, 0)
    mine = jnp.where(lane < width, lane // vecs, lane % 8) == comp
    return jnp.sum(jnp.where(mine, gram, 0.0), axis=0, keepdims=True)


def early_kernel(prev_ref, t0, t1, t2, lines_ref, gram_ref, *split_refs):
    comps, vecs, rows = prev_ref.shape
    width = comps * vecs
    lines = jnp.concatenate([lines_of(t[...], rows) for t in (t0, t1, t2)], axis=0)
    lines_ref[...] = lines
    prev = prev_ref[...].reshape(width, rows)
    full = dot(prev, prev, NT, HIGHEST)
    full = jnp.concatenate([full, jnp.zeros((width, 128 - width), jnp.float32)], axis=1)
    lane = iota((8, 128), 1)
    tiles = [jnp.zeros((8, 128), jnp.float32)] * 2
    for (c, g), (t, first) in PLACES.items():
        at = c * vecs + 8 * g
        piece = pltpu.roll(full[at : at + 8], (first - at) % 128, 1)
        tiles[t] = jnp.where((lane >= first) & (lane < first + vecs - 8 * g), piece, tiles[t])
    gram_ref[:16, :] = jnp.concatenate(tiles, axis=0)
    against = jnp.concatenate([prev, lines, jnp.zeros((8, rows), jnp.float32)], axis=0)
    for ref, part in zip(split_refs, split(against.T)):
        ref[...] = part
    gram = dot(lines, against, NT, HIGHEST)
    result = jnp.zeros((8, 128), jnp.float32)
    for k in range(S - 1):
        line = collect(gram[k * 8 : (k + 1) * 8], width, vecs)
        result = jnp.where(iota((8, 128), 0) == k, jnp.broadcast_to(line, result.shape), result)
    gram_ref[16:, :] = result


def last_kernel(
    vecs, own, a, b, c, d, choose, aux, high, low, early, t0, t1, t2, lines, line_ref, gram_ref
):
    pieces = [ref[...] for ref in (own, a, b, c, d)]
    image = joined(product(choose[...], pieces, high[...], low[...]))
    width = COMPS * vecs
    shift = aux[8 * S - 8 : 8 * S, :1]
    last = image - shift * lines[8 * S - 16 :, :]
    line_ref[...] = last
    gram = split_dot(last, (t0[...], t1[...], t2[...]))
    square = jnp.sum(last * last, axis=1, keepdims=True)
    gram = jnp.where(iota(gram.shape, 1) == width + 8 * (S - 1) + iota(gram.shape, 0), square, gram)
    line = collect(gram, width, vecs)
    gram_ref[:16, :] = early[:16, :]
    gram_ref[16:, :] = jnp.where(
        iota((8, 128), 0) == S - 1, jnp.broadcast_to(line, (8, 128)), early[16:, :]
    )


def finish_kernel(total, gram_ins, prev_ref, lines, last, basis_ref, factors_ref):
    comps, vecs, rows = prev_ref.shape
    width = comps * vecs
    gram = added([ref[...] for ref in gram_ins]) * (1.0 / total)
    small = gram[16:]
    lane, comp = iota((8, 128), 1), iota((8, 128), 0)
    in_prev = (lane < width) & (lane // vecs == comp)
    coef, cross = [], []
    for k in range(S):
        line = jnp.broadcast_to(small[k : k + 1], (8, 128))
        coef.append(jnp.where(in_prev, line, 0.0))
        cross.append([jnp.where(lane == width + 8 * l + comp, line, 0.0) for l in range(k + 1)])
    coefs = jnp.concatenate(coef, axis=0)
    pieces, turns = [], {}
    for c in range(comps):
        for g in range(vecs // 8):
            t, first = PLACES[c, g]
            at = c * vecs + 8 * g
            turn = t, (at - first) % 128
            if turn not in turns:
                piece = gram[8 * t : 8 * t + 8]
                turns[turn] = pltpu.roll(piece, turn[1], 1) if turn[1] else piece
            piece = turns[turn]
            piece = jnp.where(lane < at + 8, 0.5 * piece, piece)
            piece = jnp.where((lane >= at) & (lane < (c + 1) * vecs), piece, 0.0)
            pieces.append(piece - jnp.where(lane == at + comp, 1.0, 0.0))
    half = jnp.concatenate(pieces, axis=0)
    turned = dot(coefs[:, :width], half, precision=HIGHEST)
    prev = prev_ref[...].reshape(width, rows)
    basis = jnp.concatenate([lines[...], last[...]], axis=0)
    projected = basis - dot(coefs[:, :width], prev, precision=HIGHEST)
    unit, scale = {}, {}
    for l in range(S):
        for k in range(l, S):
            value = turned[k * 8 : (k + 1) * 8] * coef[l] + turned[l * 8 : (l + 1) * 8] * coef[k] + cross[k][l]
            value = jnp.sum(value, axis=1, keepdims=True)
            for m in range(l):
                value = value - (unit[k, m] * scale[m]) * unit[l, m]
            if k == l:
                scale[l] = value
            else:
                unit[k, l] = value / scale[l]
    roots = [jnp.sqrt(scale[k]) for k in range(S)]
    lower = {(k, l): unit[k, l] * roots[l] if l < k else roots[k] for k in range(S) for l in range(k + 1)}
    vectors = []
    for k in range(S):
        value = projected[k * 8 : (k + 1) * 8]
        for l in range(k):
            value = value - unit[k, l] * vectors[l]
        vectors.append(value)
        value = value * (1.0 / roots[k])
        for c in range(comps):
            basis_ref[c, k : k + 1, :] = value[c : c + 1]
    for c in range(comps):
        factors_ref[c, :, :vecs] = small[:S, c * vecs : (c + 1) * vecs]
    for k in range(S):
        line = jnp.zeros((8, 128), jnp.float32)
        for l in range(k + 1):
            line = jnp.where(lane == l, lower[k, l], line)
        for c in range(comps):
            factors_ref[c, k : k + 1, vecs:] = line[c : c + 1, :S]


VMEM = pl.BlockSpec(memory_space=pltpu.VMEM)
HBM = pl.BlockSpec(memory_space=pltpu.HBM)


def in_hbm(*arrays):
    return [pltpu.with_memory_space_constraint(x, pltpu.HBM) for x in arrays]


def call(kernel, outs, specs, flops, moved, scratch=()):
    shapes = [jax.ShapeDtypeStruct(shape, kind) for shape, kind in outs]
    return pl.pallas_call(
        kernel,
        out_shape=shapes if len(shapes) > 1 else shapes[0],
        in_specs=specs,
        out_specs=[VMEM] * len(shapes) if len(shapes) > 1 else VMEM,
        scratch_shapes=list(scratch),
        compiler_params=pltpu.CompilerParams(vmem_limit_bytes=24 * 1024 * 1024),
        cost_estimate=pl.CostEstimate(flops=flops, bytes_accessed=moved, transcendentals=0),
    )


def send(value, target):
    return lax.ppermute(value, "dom", [(d, target[d]) for d in range(lax.axis_size("dom"))])


def neighbours(length, step, odd):
    target = {}
    for d in range(length):
        other = d + step if (d // step) % 2 == odd else d - step
        target[d] = other if 0 <= other < length else None
    return target


def ghosts(tile):
    length = lax.axis_size("dom")
    last = length - 1
    near, across = neighbours(length, 1, 0), neighbours(length, 1, 1)
    far_even, far_odd = neighbours(length, FAR, 0), neighbours(length, FAR, 1)
    across.update({0: 2, 2: 1, 1: 0, last: last - 2, last - 2: last - 1, last - 1: last})
    for d in range(length):
        if far_odd[d] is None:
            far_odd[d] = d ^ 1
    far_odd.update({1: 2, 2: 3, 3: 0, 0: 1})
    far_odd.update({last - 1: last - 2, last - 2: last - 3, last - 3: last, last: last - 1})
    return [send(tile, target) for target in (near, far_odd, far_even, across)]


def summed(value):
    length = lax.axis_size("dom")

    def fetched(step):
        return send(value, {d: d ^ (step | 1) for d in range(length)})

    parts = [value, fetched(1)]
    step = 2
    while step < length:
        value = added(parts)
        steps = (3 * step, step, 2 * step) if 2 * step < length else (step,)
        got = [fetched(s) for s in steps]
        parts = [value] + got[1:] + got[:1]
        step *= 4
    return parts


def added(parts):
    if len(parts) == 2:
        return parts[0] + parts[1]
    return (parts[0] + parts[1]) + (parts[2] + parts[3])


def local(strips, columns, send_list, send_count, shifts, prev_basis, mix):
    comps, vecs, rows = prev_basis.shape
    blocks = columns.shape[0]
    width = strips.shape[1]
    f32, bf16, dma = jnp.float32, jnp.bfloat16, pltpu.SemaphoreType.DMA
    tile_out = ((comps * blocks, 128), f32)
    tile = call(
        start_kernel,
        [((comps * blocks + 8, 128), f32)],
        [HBM] * 4,
        600000,
        250000,
        [
            pltpu.VMEM(prev_basis.shape, f32),
            pltpu.VMEM(mix.shape, f32),
            pltpu.VMEM(send_list.shape, jnp.int32),
            pltpu.VMEM(send_count.shape, jnp.int32),
            dma((4,)),
        ],
    )(*in_hbm(prev_basis, mix, send_list, send_count))
    high, low, aux = call(
        prepare_kernel,
        [((width, rows), bf16), ((width, rows), bf16), ((8 * S + 24, 128), f32)],
        [HBM] * 3,
        1000000,
        1000000,
        [
            pltpu.VMEM((4, rows // 4, width), f32),
            pltpu.VMEM(columns.shape[::-1], jnp.int32),
            pltpu.SMEM(shifts.shape, f32),
            dma((6,)),
        ],
    )(*in_hbm(strips, columns.T, shifts))
    tiles = []
    length = lax.axis_size("dom")
    near, far_odd, far_even, across = ghosts(tile)
    tile, choose = call(
        lambda *refs: first_kernel(length, *refs),
        [tile_out, ((3 * blocks, 128), jnp.int32)],
        [VMEM] * 8,
        50000000,
        600000,
    )(tile, near, far_even, across, far_odd, aux, high, low)
    tiles.append(tile)
    for step in (1, 2):
        tile = call(
            lambda *refs, step=step: middle_kernel(step, *refs), [tile_out], [VMEM] * 9, 50000000, 600000
        )(tile, *ghosts(tile), choose, aux, high, low)
        tiles.append(tile)
    received = ghosts(tile)
    gram_out = ((24, 128), f32)
    lines, early, *parts = call(
        early_kernel,
        [((8 * S - 8, rows), f32), gram_out] + [((rows, 128), bf16)] * 3,
        [VMEM] * 4,
        60000000,
        250000,
    )(prev_basis, *tiles)
    last, gram = call(
        lambda *refs: last_kernel(vecs, *refs),
        [((8, rows), f32), gram_out],
        [VMEM] * 14,
        80000000,
        900000,
    )(tile, *received, choose, aux, high, low, early, *parts, lines)
    total = float(length * rows)
    parts = summed(gram)
    count = len(parts)
    basis, factors = call(
        lambda *refs: finish_kernel(total, refs[:count], *refs[count:]),
        [((comps, S, rows), f32), ((comps, S, vecs + S), f32)],
        [VMEM] * (count + 3),
        50000000,
        400000,
    )(*parts, prev_basis, lines, last)
    return basis, jnp.swapaxes(factors, 1, 2)


def solution(mesh):
    in_specs = (
        P("dom", None),
        P("dom", None),
        P("dom", None, None),
        P("dom", None),
        P(),
        P(None, None, "dom"),
        P(),
    )
    out_specs = (P(None, None, "dom"), P())
    return jax.shard_map(local, mesh=mesh, in_specs=in_specs, out_specs=out_specs, check_vma=False)
```

```python
import jax
import jax.numpy as jnp
from jax import lax
from jax.experimental import pallas as pl
from jax.experimental.pallas import tpu as pltpu
from jax.sharding import PartitionSpec as P

BLOCK = 64
S = 4
FAR = 8
COMPS = 3
DEAD = 1000.0
HIGHEST = lax.Precision.HIGHEST
NN = (((1,), (0,)), ((), ()))
NT = (((1,), (1,)), ((), ()))


def dot(a, b, dims=NN, precision=None):
    return lax.dot_general(a, b, dims, precision=precision, preferred_element_type=jnp.float32)


def iota(shape, axis):
    return lax.broadcasted_iota(jnp.int32, shape, axis)


PLACES = {(c, g): (g % 2, (0, 8, 0, 0)[g] + 32 * c) for c in range(COMPS) for g in range(4)}
PLACES.update({(0, 2): (0, 96), (1, 2): (0, 112), (2, 2): (1, 96)})


def own_lanes(rows, width):
    return iota((rows, width), 1) // BLOCK == iota((rows, width), 0) % 8


def fold(masked):
    total = masked[:, :128]
    for t in range(1, masked.shape[1] // 128):
        total = total + masked[:, t * 128 : (t + 1) * 128]
    return total + pltpu.roll(total, BLOCK, 1)


def lines_of(tile, width):
    wide = jnp.concatenate([tile] * (width // 128), axis=1)
    return joined(jnp.where(own_lanes(wide.shape[0], width), wide, 0.0))


def joined(wide):
    width = wide.shape[1]
    where = iota((8, width), 0)
    result = jnp.zeros((8, width), jnp.float32)
    for c in range(COMPS):
        line = jnp.sum(wide[c * 8 : (c + 1) * 8], axis=0, keepdims=True)
        result = jnp.where(where == c, jnp.broadcast_to(line, result.shape), result)
    return result


def split(x):
    parts = []
    for _ in range(3):
        parts.append(x.astype(jnp.bfloat16))
        x = x - parts[-1].astype(jnp.float32)
    return parts


def split_dot(x, parts):
    left = [part.astype(jnp.float32) for part in split(x)]
    left.append(jnp.zeros((-3 * x.shape[0] % 16, x.shape[1]), jnp.float32))
    left = jnp.concatenate([part for part in left if part.shape[0]], axis=0).astype(jnp.bfloat16)
    products = dot(left, parts[0]) + dot(left, parts[1]) + dot(left, parts[2])
    rows = x.shape[0]
    return products[:rows] + (products[rows : 2 * rows] + products[2 * rows : 3 * rows])


def fetch(pairs, sems):
    copies = [pltpu.make_async_copy(src, dst, sems.at[i]) for i, (src, dst) in enumerate(pairs)]
    for copy in copies:
        copy.start()
    return copies


def start_kernel(prev_in, mix_in, list_in, count_in, out_ref, prev_ref, mix_ref, list_ref, count_ref, sems):
    copies = fetch(
        [(prev_in, prev_ref), (mix_in, mix_ref), (list_in, list_ref), (count_in, count_ref)], sems
    )
    for copy in copies[1:]:
        copy.wait()
    comps, vecs, rows = prev_ref.shape
    eye = iota((vecs, vecs), 0) == iota((vecs, vecs), 1)
    weights = []
    for c in range(comps):
        line = jnp.broadcast_to(mix_ref[c : c + 1, :], eye.shape)
        weights.append(jnp.sum(jnp.where(eye, line, 0.0), axis=1, keepdims=True))
    order = list_ref[0].astype(jnp.float32)
    order = jnp.concatenate([order, jnp.zeros((4, 120), jnp.float32)], axis=1)
    meta = jnp.zeros((8, 128), jnp.float32)
    slot = iota((1, 128), 1)
    for link in range(4):
        live = slot < jnp.broadcast_to(count_ref[0:1, link : link + 1], slot.shape)
        line = jnp.where(live, order[link : link + 1], DEAD)
        line = pltpu.roll(jnp.broadcast_to(line, (8, 128)), 8 + 8 * link, 1)
        meta = jnp.where(iota((8, 128), 1) // 8 == link + 1, line, meta)
    out_ref[8 * comps :, :] = meta
    copies[0].wait()
    own = own_lanes(8, rows)
    for c in range(comps):
        start = jnp.sum(weights[c] * prev_ref[c], axis=0, keepdims=True)
        line = jnp.broadcast_to(start, own.shape)
        out_ref[c * 8 : (c + 1) * 8, :] = fold(jnp.where(own, line, 0.0))


def prepare_kernel(strips_in, columns_in, shifts_in, high_ref, low_ref, aux_ref, strips, columns, shifts, sems):
    parts = strips.shape[0]
    depth = strips.shape[1]
    pairs = [(columns_in, columns), (shifts_in, shifts)]
    pairs += [(strips_in.at[pl.ds(p * depth, depth)], strips.at[p]) for p in range(parts)]
    copies = fetch(pairs, sems)
    copies[0].wait()
    copies[1].wait()
    eye = iota((8, 8), 0) == iota((8, 8), 1)
    for k in range(1, columns.shape[0]):
        line = jnp.broadcast_to(columns[k : k + 1, :].astype(jnp.float32), (8, 8))
        column = jnp.sum(jnp.where(eye, line, 0.0), axis=1, keepdims=True)
        at = 8 * S + 8 * (k - 1)
        aux_ref[at : at + 8, :] = jnp.broadcast_to(column, (8, 128))
    for k in range(S):
        aux_ref[8 * k : 8 * k + 8, :] = jnp.full((8, 128), shifts[k], jnp.float32)
    for p in range(parts):
        copies[2 + p].wait()
        turned = strips[p].T
        high = turned.astype(jnp.bfloat16)
        high_ref[:, p * depth : (p + 1) * depth] = high
        low_ref[:, p * depth : (p + 1) * depth] = (turned - high.astype(jnp.float32)).astype(jnp.bfloat16)


def selection(table, metas, place, length):
    even, even_far = lax.rem(place, 2) == 0, lax.rem(place // FAR, 2) == 0
    near, far_odd, far_even, across = metas
    moved = (place == 2) | (place == length - 3)
    across = jnp.where(moved, far_odd, across)
    circle = jnp.where(moved, 16.0, 32.0)
    slots = [
        (place >= 1, jnp.where(even, circle, 8.0), jnp.where(even, across, near)),
        (place < length - 1, jnp.where(even, 8.0, circle), jnp.where(even, near, across)),
        (place >= FAR, jnp.where(even_far, 16.0, 24.0), jnp.where(even_far, far_odd, far_even)),
        (place < length - FAR, jnp.where(even_far, 24.0, 16.0), jnp.where(even_far, far_even, far_odd)),
    ]
    lane = iota((1, 128), 1)
    target = lane.astype(jnp.float32)
    for link, (valid, base, order) in enumerate(slots):
        order = order + jnp.where(valid, base, DEAD)
        target = jnp.where(lane // 8 == link + 1, order, target)
    target = jnp.broadcast_to(target, (8, 128))
    index = table.astype(jnp.int32)
    at = [jnp.take_along_axis(target, index[8 * k : 8 * k + 8], axis=1) for k in range(3)]
    return jnp.concatenate(at, axis=0).astype(jnp.int32)


def product(choose, pieces, high, low):
    rows = 8 * COMPS
    front = iota((8, 128), 1) < BLOCK
    picked = [[pieces[0][8 * c : 8 * c + 8] for c in range(COMPS)]]
    for k in range(3):
        code = choose[8 * k : 8 * k + 8]
        index, place = code & 7, code >> 3
        blocks = []
        for c in range(COMPS):
            block = jnp.zeros((8, 128), jnp.float32)
            for p, piece in enumerate(pieces):
                found = jnp.take_along_axis(piece[8 * c : 8 * c + 8], index, axis=0)
                block = jnp.where(place == p, found, block)
            blocks.append(block)
        picked.append(blocks)
    x = [
        jnp.concatenate(
            [jnp.where(front, picked[2 * t][c], picked[2 * t + 1][c]) for t in range(2)], axis=1
        )
        for c in range(COMPS)
    ]
    x = jnp.concatenate(x, axis=0)
    top = x.astype(jnp.bfloat16).astype(jnp.float32)
    left = jnp.concatenate([top, x - top], axis=0).astype(jnp.bfloat16)
    both = dot(left, high) + dot(left, low)
    image = both[:rows] + both[rows:]
    return jnp.where(own_lanes(rows, image.shape[1]), image, 0.0)


def multiply(choose, pieces, shift, high, low):
    image = fold(product(choose, pieces, high, low))
    return image - jnp.concatenate([shift] * COMPS, axis=0) * pieces[0]


def first_kernel(length, own, a, c, d, b, aux, high, low, tile_ref, choose_ref):
    rows = 8 * COMPS
    refs = (own, a, b, c, d)
    pieces = [ref[:rows, :] for ref in refs]
    metas = [ref[rows : rows + 1, :] for ref in refs[1:]]
    choose = selection(aux[8 * S :, :], metas, lax.axis_index("dom"), length)
    choose_ref[...] = choose
    tile_ref[...] = multiply(choose, pieces, aux[:8, :], high[...], low[...])


def middle_kernel(step, own, a, b, c, d, choose, aux, high, low, tile_ref):
    pieces = [ref[...] for ref in (own, a, b, c, d)]
    tile_ref[...] = multiply(choose[...], pieces, aux[8 * step : 8 * step + 8, :], high[...], low[...])


def collect(gram, width, vecs):
    lane, comp = iota(gram.shape, 1), iota(gram.shape, 0)
    mine = jnp.where(lane < width, lane // vecs, lane % 8) == comp
    return jnp.sum(jnp.where(mine, gram, 0.0), axis=0, keepdims=True)


def early_kernel(prev_ref, t0, t1, t2, lines_ref, gram_ref, *split_refs):
    comps, vecs, rows = prev_ref.shape
    width = comps * vecs
    lines = jnp.concatenate([lines_of(t[...], rows) for t in (t0, t1, t2)], axis=0)
    lines_ref[...] = lines
    prev = prev_ref[...].reshape(width, rows)
    full = dot(prev, prev, NT, HIGHEST)
    full = jnp.concatenate([full, jnp.zeros((width, 128 - width), jnp.float32)], axis=1)
    lane = iota((8, 128), 1)
    tiles = [jnp.zeros((8, 128), jnp.float32)] * 2
    for (c, g), (t, first) in PLACES.items():
        at = c * vecs + 8 * g
        piece = pltpu.roll(full[at : at + 8], (first - at) % 128, 1)
        tiles[t] = jnp.where((lane >= first) & (lane < first + vecs - 8 * g), piece, tiles[t])
    gram_ref[:16, :] = jnp.concatenate(tiles, axis=0)
    against = jnp.concatenate([prev, lines, jnp.zeros((8, rows), jnp.float32)], axis=0)
    for ref, part in zip(split_refs, split(against.T)):
        ref[...] = part
    gram = dot(lines, against, NT, HIGHEST)
    result = jnp.zeros((8, 128), jnp.float32)
    for k in range(S - 1):
        line = collect(gram[k * 8 : (k + 1) * 8], width, vecs)
        result = jnp.where(iota((8, 128), 0) == k, jnp.broadcast_to(line, result.shape), result)
    gram_ref[16:, :] = result


def last_kernel(
    vecs, own, a, b, c, d, choose, aux, high, low, early, t0, t1, t2, lines, line_ref, gram_ref
):
    pieces = [ref[...] for ref in (own, a, b, c, d)]
    image = joined(product(choose[...], pieces, high[...], low[...]))
    width = COMPS * vecs
    shift = aux[8 * S - 8 : 8 * S, :1]
    last = image - shift * lines[8 * S - 16 :, :]
    line_ref[...] = last
    gram = split_dot(last, (t0[...], t1[...], t2[...]))
    square = jnp.sum(last * last, axis=1, keepdims=True)
    gram = jnp.where(iota(gram.shape, 1) == width + 8 * (S - 1) + iota(gram.shape, 0), square, gram)
    line = collect(gram, width, vecs)
    gram_ref[:16, :] = early[:16, :]
    gram_ref[16:, :] = jnp.where(
        iota((8, 128), 0) == S - 1, jnp.broadcast_to(line, (8, 128)), early[16:, :]
    )


def finish_kernel(total, gram_ins, prev_ref, lines, last, basis_ref, factors_ref):
    comps, vecs, rows = prev_ref.shape
    width = comps * vecs
    gram = added([ref[...] for ref in gram_ins]) * (1.0 / total)
    small = gram[16:]
    lane, comp = iota((8, 128), 1), iota((8, 128), 0)
    in_prev = (lane < width) & (lane // vecs == comp)
    coef, cross = [], []
    for k in range(S):
        line = jnp.broadcast_to(small[k : k + 1], (8, 128))
        coef.append(jnp.where(in_prev, line, 0.0))
        cross.append([jnp.where(lane == width + 8 * l + comp, line, 0.0) for l in range(k + 1)])
    coefs = jnp.concatenate(coef, axis=0)
    pieces, turns = [], {}
    for c in range(comps):
        for g in range(vecs // 8):
            t, first = PLACES[c, g]
            at = c * vecs + 8 * g
            turn = t, (at - first) % 128
            if turn not in turns:
                piece = gram[8 * t : 8 * t + 8]
                turns[turn] = pltpu.roll(piece, turn[1], 1) if turn[1] else piece
            piece = turns[turn]
            piece = jnp.where(lane < at + 8, 0.5 * piece, piece)
            piece = jnp.where((lane >= at) & (lane < (c + 1) * vecs), piece, 0.0)
            pieces.append(piece - jnp.where(lane == at + comp, 1.0, 0.0))
    half = jnp.concatenate(pieces, axis=0)
    turned = dot(coefs[:, :width], half, precision=HIGHEST)
    prev = prev_ref[...].reshape(width, rows)
    basis = jnp.concatenate([lines[...], last[...]], axis=0)
    projected = basis - dot(coefs[:, :width], prev, precision=HIGHEST)
    unit, scale = {}, {}
    for l in range(S):
        for k in range(l, S):
            value = turned[k * 8 : (k + 1) * 8] * coef[l] + turned[l * 8 : (l + 1) * 8] * coef[k] + cross[k][l]
            value = jnp.sum(value, axis=1, keepdims=True)
            for m in range(l):
                value = value - (unit[k, m] * scale[m]) * unit[l, m]
            if k == l:
                scale[l] = value
            else:
                unit[k, l] = value / scale[l]
    roots = [jnp.sqrt(scale[k]) for k in range(S)]
    lower = {(k, l): unit[k, l] * roots[l] if l < k else roots[k] for k in range(S) for l in range(k + 1)}
    vectors = []
    for k in range(S):
        value = projected[k * 8 : (k + 1) * 8]
        for l in range(k):
            value = value - unit[k, l] * vectors[l]
        vectors.append(value)
        value = value * (1.0 / roots[k])
        for c in range(comps):
            basis_ref[c, k : k + 1, :] = value[c : c + 1]
    for c in range(comps):
        factors_ref[c, :, :vecs] = small[:S, c * vecs : (c + 1) * vecs]
    for k in range(S):
        line = jnp.zeros((8, 128), jnp.float32)
        for l in range(k + 1):
            line = jnp.where(lane == vecs + l, lower[k, l], line)
        for c in range(comps):
            factors_ref[c, k : k + 1, vecs:] = line[c : c + 1, vecs : vecs + S]


VMEM = pl.BlockSpec(memory_space=pltpu.VMEM)
HBM = pl.BlockSpec(memory_space=pltpu.HBM)


def in_hbm(*arrays):
    return [pltpu.with_memory_space_constraint(x, pltpu.HBM) for x in arrays]


def call(kernel, outs, specs, flops, moved, scratch=()):
    shapes = [jax.ShapeDtypeStruct(shape, kind) for shape, kind in outs]
    return pl.pallas_call(
        kernel,
        out_shape=shapes if len(shapes) > 1 else shapes[0],
        in_specs=specs,
        out_specs=[VMEM] * len(shapes) if len(shapes) > 1 else VMEM,
        scratch_shapes=list(scratch),
        compiler_params=pltpu.CompilerParams(vmem_limit_bytes=24 * 1024 * 1024),
        cost_estimate=pl.CostEstimate(flops=flops, bytes_accessed=moved, transcendentals=0),
    )


def send(value, target):
    return lax.ppermute(value, "dom", [(d, target[d]) for d in range(lax.axis_size("dom"))])


def neighbours(length, step, odd):
    target = {}
    for d in range(length):
        other = d + step if (d // step) % 2 == odd else d - step
        target[d] = other if 0 <= other < length else None
    return target


def ghosts(tile):
    length = lax.axis_size("dom")
    last = length - 1
    near, across = neighbours(length, 1, 0), neighbours(length, 1, 1)
    far_even, far_odd = neighbours(length, FAR, 0), neighbours(length, FAR, 1)
    across.update({0: 2, 2: 1, 1: 0, last: last - 2, last - 2: last - 1, last - 1: last})
    for d in range(length):
        if far_odd[d] is None:
            far_odd[d] = d ^ 1
    far_odd.update({1: 2, 2: 3, 3: 0, 0: 1})
    far_odd.update({last - 1: last - 2, last - 2: last - 3, last - 3: last, last: last - 1})
    return [send(tile, target) for target in (near, far_odd, far_even, across)]


def summed(value):
    length = lax.axis_size("dom")

    def fetched(step):
        return send(value, {d: d ^ (step | 1) for d in range(length)})

    parts = [value, fetched(1)]
    step = 2
    while step < length:
        value = added(parts)
        steps = (3 * step, step, 2 * step) if 2 * step < length else (step,)
        got = [fetched(s) for s in steps]
        parts = [value] + got[1:] + got[:1]
        step *= 4
    return parts


def added(parts):
    if len(parts) == 2:
        return parts[0] + parts[1]
    return (parts[0] + parts[1]) + (parts[2] + parts[3])


def local(strips, columns, send_list, send_count, shifts, prev_basis, mix):
    comps, vecs, rows = prev_basis.shape
    blocks = columns.shape[0]
    width = strips.shape[1]
    f32, bf16, dma = jnp.float32, jnp.bfloat16, pltpu.SemaphoreType.DMA
    tile_out = ((comps * blocks, 128), f32)
    tile = call(
        start_kernel,
        [((comps * blocks + 8, 128), f32)],
        [HBM] * 4,
        600000,
        250000,
        [
            pltpu.VMEM(prev_basis.shape, f32),
            pltpu.VMEM(mix.shape, f32),
            pltpu.VMEM(send_list.shape, jnp.int32),
            pltpu.VMEM(send_count.shape, jnp.int32),
            dma((4,)),
        ],
    )(*in_hbm(prev_basis, mix, send_list, send_count))
    high, low, aux = call(
        prepare_kernel,
        [((width, rows), bf16), ((width, rows), bf16), ((8 * S + 24, 128), f32)],
        [HBM] * 3,
        1000000,
        1000000,
        [
            pltpu.VMEM((2, rows // 2, width), f32),
            pltpu.VMEM(columns.shape[::-1], jnp.int32),
            pltpu.SMEM(shifts.shape, f32),
            dma((4,)),
        ],
    )(*in_hbm(strips, columns.T, shifts))
    tiles = []
    length = lax.axis_size("dom")
    near, far_odd, far_even, across = ghosts(tile)
    tile, choose = call(
        lambda *refs: first_kernel(length, *refs),
        [tile_out, ((3 * blocks, 128), jnp.int32)],
        [VMEM] * 8,
        50000000,
        600000,
    )(tile, near, far_even, across, far_odd, aux, high, low)
    tiles.append(tile)
    for step in (1, 2):
        tile = call(
            lambda *refs, step=step: middle_kernel(step, *refs), [tile_out], [VMEM] * 9, 50000000, 600000
        )(tile, *ghosts(tile), choose, aux, high, low)
        tiles.append(tile)
    received = ghosts(tile)
    gram_out = ((24, 128), f32)
    lines, early, *parts = call(
        early_kernel,
        [((8 * S - 8, rows), f32), gram_out] + [((rows, 128), bf16)] * 3,
        [VMEM] * 4,
        60000000,
        250000,
    )(prev_basis, *tiles)
    last, gram = call(
        lambda *refs: last_kernel(vecs, *refs),
        [((8, rows), f32), gram_out],
        [VMEM] * 14,
        80000000,
        900000,
    )(tile, *received, choose, aux, high, low, early, *parts, lines)
    total = float(length * rows)
    parts = summed(gram)
    count = len(parts)
    basis, factors = call(
        lambda *refs: finish_kernel(total, refs[:count], *refs[count:]),
        [((comps, S, rows), f32), ((comps, S, vecs + S), f32)],
        [VMEM] * (count + 3),
        50000000,
        400000,
    )(*parts, prev_basis, lines, last)
    return basis, jnp.swapaxes(factors, 1, 2)


def solution(mesh):
    in_specs = (
        P("dom", None),
        P("dom", None),
        P("dom", None, None),
        P("dom", None),
        P(),
        P(None, None, "dom"),
        P(),
    )
    out_specs = (P(None, None, "dom"), P())
    return jax.shard_map(local, mesh=mesh, in_specs=in_specs, out_specs=out_specs, check_vma=False)
```

```python
import jax
import jax.numpy as jnp
from jax import lax
from jax.experimental import pallas as pl
from jax.experimental.pallas import tpu as pltpu
from jax.sharding import PartitionSpec as P

BLOCK = 64
S = 4
FAR = 8
COMPS = 3
DEAD = 1000.0
HIGHEST = lax.Precision.HIGHEST
NN = (((1,), (0,)), ((), ()))
NT = (((1,), (1,)), ((), ()))


def dot(a, b, dims=NN, precision=None):
    return lax.dot_general(a, b, dims, precision=precision, preferred_element_type=jnp.float32)


def iota(shape, axis):
    return lax.broadcasted_iota(jnp.int32, shape, axis)


PLACES = {(c, g): (g % 2, (0, 8, 0, 0)[g] + 32 * c) for c in range(COMPS) for g in range(4)}
PLACES.update({(0, 2): (0, 96), (1, 2): (0, 112), (2, 2): (1, 96)})


def own_lanes(rows, width):
    return iota((rows, width), 1) // BLOCK == iota((rows, width), 0) % 8


def fold(masked):
    total = masked[:, :128]
    for t in range(1, masked.shape[1] // 128):
        total = total + masked[:, t * 128 : (t + 1) * 128]
    return total + pltpu.roll(total, BLOCK, 1)


def lines_of(tile, width):
    wide = jnp.concatenate([tile] * (width // 128), axis=1)
    return joined(jnp.where(own_lanes(wide.shape[0], width), wide, 0.0))


def joined(wide):
    width = wide.shape[1]
    where = iota((8, width), 0)
    result = jnp.zeros((8, width), jnp.float32)
    for c in range(COMPS):
        line = jnp.sum(wide[c * 8 : (c + 1) * 8], axis=0, keepdims=True)
        result = jnp.where(where == c, jnp.broadcast_to(line, result.shape), result)
    return result


def split(x):
    parts = []
    for _ in range(3):
        parts.append(x.astype(jnp.bfloat16))
        x = x - parts[-1].astype(jnp.float32)
    return parts


def split_dot(x, parts):
    left = [part.astype(jnp.float32) for part in split(x)]
    left.append(jnp.zeros((-3 * x.shape[0] % 16, x.shape[1]), jnp.float32))
    left = jnp.concatenate([part for part in left if part.shape[0]], axis=0).astype(jnp.bfloat16)
    products = dot(left, parts[0]) + dot(left, parts[1]) + dot(left, parts[2])
    rows = x.shape[0]
    return products[:rows] + (products[rows : 2 * rows] + products[2 * rows : 3 * rows])


def fetch(pairs, sems):
    copies = [pltpu.make_async_copy(src, dst, sems.at[i]) for i, (src, dst) in enumerate(pairs)]
    for copy in copies:
        copy.start()
    return copies


def start_kernel(prev_in, mix_in, list_in, count_in, out_ref, prev_ref, mix_ref, list_ref, count_ref, sems):
    copies = fetch(
        [(prev_in, prev_ref), (mix_in, mix_ref), (list_in, list_ref), (count_in, count_ref)], sems
    )
    for copy in copies[1:]:
        copy.wait()
    comps, vecs, rows = prev_ref.shape
    eye = iota((vecs, vecs), 0) == iota((vecs, vecs), 1)
    weights = []
    for c in range(comps):
        line = jnp.broadcast_to(mix_ref[c : c + 1, :], eye.shape)
        weights.append(jnp.sum(jnp.where(eye, line, 0.0), axis=1, keepdims=True))
    order = list_ref[0].astype(jnp.float32)
    order = jnp.concatenate([order, jnp.zeros((4, 120), jnp.float32)], axis=1)
    meta = jnp.zeros((8, 128), jnp.float32)
    slot = iota((1, 128), 1)
    for link in range(4):
        live = slot < jnp.broadcast_to(count_ref[0:1, link : link + 1], slot.shape)
        line = jnp.where(live, order[link : link + 1], DEAD)
        line = pltpu.roll(jnp.broadcast_to(line, (8, 128)), 8 + 8 * link, 1)
        meta = jnp.where(iota((8, 128), 1) // 8 == link + 1, line, meta)
    out_ref[8 * comps :, :] = meta
    copies[0].wait()
    own = own_lanes(8, rows)
    for c in range(comps):
        start = jnp.sum(weights[c] * prev_ref[c], axis=0, keepdims=True)
        line = jnp.broadcast_to(start, own.shape)
        out_ref[c * 8 : (c + 1) * 8, :] = fold(jnp.where(own, line, 0.0))


def prepare_kernel(strips_in, columns_in, shifts_in, high_ref, low_ref, aux_ref, strips, columns, shifts, sems):
    rows = strips.shape[0]
    cuts = [(0, rows * 3 // 4), (rows * 3 // 4, rows)]
    pairs = [(strips_in.at[pl.ds(a, b - a)], strips.at[pl.ds(a, b - a)]) for a, b in cuts]
    copies = fetch(pairs + [(columns_in, columns), (shifts_in, shifts)], sems)
    copies[2].wait()
    copies[3].wait()
    eye = iota((8, 8), 0) == iota((8, 8), 1)
    for k in range(1, columns.shape[0]):
        line = jnp.broadcast_to(columns[k : k + 1, :].astype(jnp.float32), (8, 8))
        column = jnp.sum(jnp.where(eye, line, 0.0), axis=1, keepdims=True)
        at = 8 * S + 8 * (k - 1)
        aux_ref[at : at + 8, :] = jnp.broadcast_to(column, (8, 128))
    for k in range(S):
        aux_ref[8 * k : 8 * k + 8, :] = jnp.full((8, 128), shifts[k], jnp.float32)
    for copy, (a, b) in zip(copies, cuts):
        copy.wait()
        turned = strips[a:b, :].T
        high = turned.astype(jnp.bfloat16)
        high_ref[:, a:b] = high
        low_ref[:, a:b] = (turned - high.astype(jnp.float32)).astype(jnp.bfloat16)


def selection(table, metas, place, length):
    even, even_far = lax.rem(place, 2) == 0, lax.rem(place // FAR, 2) == 0
    near, far_odd, far_even, across = metas
    moved = (place == 2) | (place == length - 3)
    across = jnp.where(moved, far_odd, across)
    circle = jnp.where(moved, 16.0, 32.0)
    slots = [
        (place >= 1, jnp.where(even, circle, 8.0), jnp.where(even, across, near)),
        (place < length - 1, jnp.where(even, 8.0, circle), jnp.where(even, near, across)),
        (place >= FAR, jnp.where(even_far, 16.0, 24.0), jnp.where(even_far, far_odd, far_even)),
        (place < length - FAR, jnp.where(even_far, 24.0, 16.0), jnp.where(even_far, far_even, far_odd)),
    ]
    lane = iota((1, 128), 1)
    target = lane.astype(jnp.float32)
    for link, (valid, base, order) in enumerate(slots):
        order = order + jnp.where(valid, base, DEAD)
        target = jnp.where(lane // 8 == link + 1, order, target)
    target = jnp.broadcast_to(target, (8, 128))
    index = table.astype(jnp.int32)
    at = [jnp.take_along_axis(target, index[8 * k : 8 * k + 8], axis=1) for k in range(3)]
    return jnp.concatenate(at, axis=0).astype(jnp.int32)


def product(choose, pieces, high, low):
    rows = 8 * COMPS
    front = iota((8, 128), 1) < BLOCK
    picked = [[pieces[0][8 * c : 8 * c + 8] for c in range(COMPS)]]
    for k in range(3):
        code = choose[8 * k : 8 * k + 8]
        index, place = code & 7, code >> 3
        blocks = []
        for c in range(COMPS):
            block = jnp.zeros((8, 128), jnp.float32)
            for p, piece in enumerate(pieces):
                found = jnp.take_along_axis(piece[8 * c : 8 * c + 8], index, axis=0)
                block = jnp.where(place == p, found, block)
            blocks.append(block)
        picked.append(blocks)
    x = [
        jnp.concatenate(
            [jnp.where(front, picked[2 * t][c], picked[2 * t + 1][c]) for t in range(2)], axis=1
        )
        for c in range(COMPS)
    ]
    x = jnp.concatenate(x, axis=0)
    top = x.astype(jnp.bfloat16).astype(jnp.float32)
    left = jnp.concatenate([top, x - top], axis=0).astype(jnp.bfloat16)
    both = dot(left, high) + dot(left, low)
    image = both[:rows] + both[rows:]
    return jnp.where(own_lanes(rows, image.shape[1]), image, 0.0)


def multiply(choose, pieces, shift, high, low):
    image = fold(product(choose, pieces, high, low))
    return image - jnp.concatenate([shift] * COMPS, axis=0) * pieces[0]


def first_kernel(length, own, a, c, d, b, aux, high, low, tile_ref, choose_ref):
    rows = 8 * COMPS
    refs = (own, a, b, c, d)
    pieces = [ref[:rows, :] for ref in refs]
    metas = [ref[rows : rows + 1, :] for ref in refs[1:]]
    choose = selection(aux[8 * S :, :], metas, lax.axis_index("dom"), length)
    choose_ref[...] = choose
    tile_ref[...] = multiply(choose, pieces, aux[:8, :], high[...], low[...])


def middle_kernel(step, own, a, b, c, d, choose, aux, high, low, tile_ref):
    pieces = [ref[...] for ref in (own, a, b, c, d)]
    tile_ref[...] = multiply(choose[...], pieces, aux[8 * step : 8 * step + 8, :], high[...], low[...])


def collect(gram, width, vecs):
    lane, comp = iota(gram.shape, 1), iota(gram.shape, 0)
    mine = jnp.where(lane < width, lane // vecs, lane % 8) == comp
    return jnp.sum(jnp.where(mine, gram, 0.0), axis=0, keepdims=True)


def early_kernel(prev_ref, t0, t1, t2, lines_ref, gram_ref, *split_refs):
    comps, vecs, rows = prev_ref.shape
    width = comps * vecs
    lines = jnp.concatenate([lines_of(t[...], rows) for t in (t0, t1, t2)], axis=0)
    lines_ref[...] = lines
    prev = prev_ref[...].reshape(width, rows)
    full = dot(prev, prev, NT, HIGHEST)
    full = jnp.concatenate([full, jnp.zeros((width, 128 - width), jnp.float32)], axis=1)
    lane = iota((8, 128), 1)
    tiles = [jnp.zeros((8, 128), jnp.float32)] * 2
    for (c, g), (t, first) in PLACES.items():
        at = c * vecs + 8 * g
        piece = pltpu.roll(full[at : at + 8], (first - at) % 128, 1)
        tiles[t] = jnp.where((lane >= first) & (lane < first + vecs - 8 * g), piece, tiles[t])
    gram_ref[:16, :] = jnp.concatenate(tiles, axis=0)
    against = jnp.concatenate([prev, lines, jnp.zeros((8, rows), jnp.float32)], axis=0)
    for ref, part in zip(split_refs, split(against.T)):
        ref[...] = part
    gram = dot(lines, against, NT, HIGHEST)
    result = jnp.zeros((8, 128), jnp.float32)
    for k in range(S - 1):
        line = collect(gram[k * 8 : (k + 1) * 8], width, vecs)
        result = jnp.where(iota((8, 128), 0) == k, jnp.broadcast_to(line, result.shape), result)
    gram_ref[16:, :] = result


def last_kernel(
    vecs, own, a, b, c, d, choose, aux, high, low, early, t0, t1, t2, lines, line_ref, gram_ref
):
    pieces = [ref[...] for ref in (own, a, b, c, d)]
    image = joined(product(choose[...], pieces, high[...], low[...]))
    width = COMPS * vecs
    shift = aux[8 * S - 8 : 8 * S, :1]
    last = image - shift * lines[8 * S - 16 :, :]
    line_ref[...] = last
    gram = split_dot(last, (t0[...], t1[...], t2[...]))
    square = jnp.sum(last * last, axis=1, keepdims=True)
    gram = jnp.where(iota(gram.shape, 1) == width + 8 * (S - 1) + iota(gram.shape, 0), square, gram)
    line = collect(gram, width, vecs)
    gram_ref[:16, :] = early[:16, :]
    gram_ref[16:, :] = jnp.where(
        iota((8, 128), 0) == S - 1, jnp.broadcast_to(line, (8, 128)), early[16:, :]
    )


def finish_kernel(total, gram_ins, prev_ref, lines, last, basis_ref, factors_ref):
    comps, vecs, rows = prev_ref.shape
    width = comps * vecs
    gram = added([ref[...] for ref in gram_ins]) * (1.0 / total)
    small = gram[16:]
    lane, comp = iota((8, 128), 1), iota((8, 128), 0)
    in_prev = (lane < width) & (lane // vecs == comp)
    coef, cross = [], []
    for k in range(S):
        line = jnp.broadcast_to(small[k : k + 1], (8, 128))
        coef.append(jnp.where(in_prev, line, 0.0))
        cross.append([jnp.where(lane == width + 8 * l + comp, line, 0.0) for l in range(k + 1)])
    coefs = jnp.concatenate(coef, axis=0)
    pieces, turns = [], {}
    for c in range(comps):
        for g in range(vecs // 8):
            t, first = PLACES[c, g]
            at = c * vecs + 8 * g
            turn = t, (at - first) % 128
            if turn not in turns:
                piece = gram[8 * t : 8 * t + 8]
                turns[turn] = pltpu.roll(piece, turn[1], 1) if turn[1] else piece
            piece = turns[turn]
            piece = jnp.where(lane < at + 8, 0.5 * piece, piece)
            piece = jnp.where((lane >= at) & (lane < (c + 1) * vecs), piece, 0.0)
            pieces.append(piece - jnp.where(lane == at + comp, 1.0, 0.0))
    half = jnp.concatenate(pieces, axis=0)
    turned = dot(coefs[:, :width], half, precision=HIGHEST)
    prev = prev_ref[...].reshape(width, rows)
    basis = jnp.concatenate([lines[...], last[...]], axis=0)
    projected = basis - dot(coefs[:, :width], prev, precision=HIGHEST)
    unit, scale = {}, {}
    for l in range(S):
        for k in range(l, S):
            value = turned[k * 8 : (k + 1) * 8] * coef[l] + turned[l * 8 : (l + 1) * 8] * coef[k] + cross[k][l]
            value = jnp.sum(value, axis=1, keepdims=True)
            for m in range(l):
                value = value - (unit[k, m] * scale[m]) * unit[l, m]
            if k == l:
                scale[l] = value
            else:
                unit[k, l] = value / scale[l]
    roots = [jnp.sqrt(scale[k]) for k in range(S)]
    lower = {(k, l): unit[k, l] * roots[l] if l < k else roots[k] for k in range(S) for l in range(k + 1)}
    vectors = []
    for k in range(S):
        value = projected[k * 8 : (k + 1) * 8]
        for l in range(k):
            value = value - unit[k, l] * vectors[l]
        vectors.append(value)
        value = value * (1.0 / roots[k])
        for c in range(comps):
            basis_ref[c, k : k + 1, :] = value[c : c + 1]
    for c in range(comps):
        factors_ref[c, :, :vecs] = small[:S, c * vecs : (c + 1) * vecs]
    for k in range(S):
        line = jnp.zeros((8, 128), jnp.float32)
        for l in range(k + 1):
            line = jnp.where(lane == vecs + l, lower[k, l], line)
        for c in range(comps):
            factors_ref[c, k : k + 1, vecs:] = line[c : c + 1, vecs : vecs + S]


VMEM = pl.BlockSpec(memory_space=pltpu.VMEM)
HBM = pl.BlockSpec(memory_space=pltpu.HBM)


def in_hbm(*arrays):
    return [pltpu.with_memory_space_constraint(x, pltpu.HBM) for x in arrays]


def call(kernel, outs, specs, flops, moved, scratch=()):
    shapes = [jax.ShapeDtypeStruct(shape, kind) for shape, kind in outs]
    return pl.pallas_call(
        kernel,
        out_shape=shapes if len(shapes) > 1 else shapes[0],
        in_specs=specs,
        out_specs=[VMEM] * len(shapes) if len(shapes) > 1 else VMEM,
        scratch_shapes=list(scratch),
        compiler_params=pltpu.CompilerParams(vmem_limit_bytes=24 * 1024 * 1024),
        cost_estimate=pl.CostEstimate(flops=flops, bytes_accessed=moved, transcendentals=0),
    )


def send(value, target):
    return lax.ppermute(value, "dom", [(d, target[d]) for d in range(lax.axis_size("dom"))])


def neighbours(length, step, odd):
    target = {}
    for d in range(length):
        other = d + step if (d // step) % 2 == odd else d - step
        target[d] = other if 0 <= other < length else None
    return target


def ghosts(tile):
    length = lax.axis_size("dom")
    last = length - 1
    near, across = neighbours(length, 1, 0), neighbours(length, 1, 1)
    far_even, far_odd = neighbours(length, FAR, 0), neighbours(length, FAR, 1)
    across.update({0: 2, 2: 1, 1: 0, last: last - 2, last - 2: last - 1, last - 1: last})
    for d in range(length):
        if far_odd[d] is None:
            far_odd[d] = d ^ 1
    far_odd.update({1: 2, 2: 3, 3: 0, 0: 1})
    far_odd.update({last - 1: last - 2, last - 2: last - 3, last - 3: last, last: last - 1})
    return [send(tile, target) for target in (near, far_odd, far_even, across)]


def summed(value):
    length = lax.axis_size("dom")

    def fetched(step):
        return send(value, {d: d ^ (step | 1) for d in range(length)})

    parts = [value, fetched(1)]
    step = 2
    while step < length:
        value = added(parts)
        steps = (3 * step, step, 2 * step) if 2 * step < length else (step,)
        got = [fetched(s) for s in steps]
        parts = [value] + got[1:] + got[:1]
        step *= 4
    return parts


def added(parts):
    if len(parts) == 2:
        return parts[0] + parts[1]
    return (parts[0] + parts[1]) + (parts[2] + parts[3])


def local(strips, columns, send_list, send_count, shifts, prev_basis, mix):
    comps, vecs, rows = prev_basis.shape
    blocks = columns.shape[0]
    width = strips.shape[1]
    f32, bf16, dma = jnp.float32, jnp.bfloat16, pltpu.SemaphoreType.DMA
    tile_out = ((comps * blocks, 128), f32)
    tile = call(
        start_kernel,
        [((comps * blocks + 8, 128), f32)],
        [HBM] * 4,
        600000,
        250000,
        [
            pltpu.VMEM(prev_basis.shape, f32),
            pltpu.VMEM(mix.shape, f32),
            pltpu.VMEM(send_list.shape, jnp.int32),
            pltpu.VMEM(send_count.shape, jnp.int32),
            dma((4,)),
        ],
    )(*in_hbm(prev_basis, mix, send_list, send_count))
    high, low, aux = call(
        prepare_kernel,
        [((width, rows), bf16), ((width, rows), bf16), ((8 * S + 24, 128), f32)],
        [HBM] * 3,
        1000000,
        1000000,
        [
            pltpu.VMEM((rows, width), f32),
            pltpu.VMEM(columns.shape[::-1], jnp.int32),
            pltpu.SMEM(shifts.shape, f32),
            dma((4,)),
        ],
    )(*in_hbm(strips, columns.T, shifts))
    tiles = []
    length = lax.axis_size("dom")
    near, far_odd, far_even, across = ghosts(tile)
    tile, choose = call(
        lambda *refs: first_kernel(length, *refs),
        [tile_out, ((3 * blocks, 128), jnp.int32)],
        [VMEM] * 8,
        50000000,
        600000,
    )(tile, near, far_even, across, far_odd, aux, high, low)
    tiles.append(tile)
    for step in (1, 2):
        tile = call(
            lambda *refs, step=step: middle_kernel(step, *refs), [tile_out], [VMEM] * 9, 50000000, 600000
        )(tile, *ghosts(tile), choose, aux, high, low)
        tiles.append(tile)
    received = ghosts(tile)
    gram_out = ((24, 128), f32)
    lines, early, *parts = call(
        early_kernel,
        [((8 * S - 8, rows), f32), gram_out] + [((rows, 128), bf16)] * 3,
        [VMEM] * 4,
        60000000,
        250000,
    )(prev_basis, *tiles)
    last, gram = call(
        lambda *refs: last_kernel(vecs, *refs),
        [((8, rows), f32), gram_out],
        [VMEM] * 14,
        80000000,
        900000,
    )(tile, *received, choose, aux, high, low, early, *parts, lines)
    total = float(length * rows)
    parts = summed(gram)
    count = len(parts)
    basis, factors = call(
        lambda *refs: finish_kernel(total, refs[:count], *refs[count:]),
        [((comps, S, rows), f32), ((comps, S, vecs + S), f32)],
        [VMEM] * (count + 3),
        50000000,
        400000,
    )(*parts, prev_basis, lines, last)
    return basis, jnp.swapaxes(factors, 1, 2)


def solution(mesh):
    in_specs = (
        P("dom", None),
        P("dom", None),
        P("dom", None, None),
        P("dom", None),
        P(),
        P(None, None, "dom"),
        P(),
    )
    out_specs = (P(None, None, "dom"), P())
    return jax.shard_map(local, mesh=mesh, in_specs=in_specs, out_specs=out_specs, check_vma=False)
```

```python
import jax
import jax.numpy as jnp
from jax import lax
from jax.experimental import pallas as pl
from jax.experimental.pallas import tpu as pltpu
from jax.sharding import PartitionSpec as P

BLOCK = 64
S = 4
FAR = 8
COMPS = 3
DEAD = 1000.0
HIGHEST = lax.Precision.HIGHEST
NN = (((1,), (0,)), ((), ()))
NT = (((1,), (1,)), ((), ()))


def dot(a, b, dims=NN, precision=None):
    return lax.dot_general(a, b, dims, precision=precision, preferred_element_type=jnp.float32)


def iota(shape, axis):
    return lax.broadcasted_iota(jnp.int32, shape, axis)


PLACES = {(c, g): (g % 2, (0, 8, 0, 0)[g] + 32 * c) for c in range(COMPS) for g in range(4)}
PLACES.update({(0, 2): (0, 96), (1, 2): (0, 112), (2, 2): (1, 96)})


def own_lanes(rows, width):
    return iota((rows, width), 1) // BLOCK == iota((rows, width), 0) % 8


def fold(masked):
    total = masked[:, :128]
    for t in range(1, masked.shape[1] // 128):
        total = total + masked[:, t * 128 : (t + 1) * 128]
    return total + pltpu.roll(total, BLOCK, 1)


def lines_of(tile, width):
    wide = jnp.concatenate([tile] * (width // 128), axis=1)
    return joined(jnp.where(own_lanes(wide.shape[0], width), wide, 0.0))


def joined(wide):
    width = wide.shape[1]
    where = iota((8, width), 0)
    result = jnp.zeros((8, width), jnp.float32)
    for c in range(COMPS):
        line = jnp.sum(wide[c * 8 : (c + 1) * 8], axis=0, keepdims=True)
        result = jnp.where(where == c, jnp.broadcast_to(line, result.shape), result)
    return result


def split(x):
    parts = []
    for _ in range(3):
        parts.append(x.astype(jnp.bfloat16))
        x = x - parts[-1].astype(jnp.float32)
    return parts


def split_dot(x, parts):
    left = [part.astype(jnp.float32) for part in split(x)]
    left.append(jnp.zeros((-3 * x.shape[0] % 16, x.shape[1]), jnp.float32))
    left = jnp.concatenate([part for part in left if part.shape[0]], axis=0).astype(jnp.bfloat16)
    products = dot(left, parts[0]) + dot(left, parts[1]) + dot(left, parts[2])
    rows = x.shape[0]
    return products[:rows] + (products[rows : 2 * rows] + products[2 * rows : 3 * rows])


def fetch(pairs, sems):
    copies = [pltpu.make_async_copy(src, dst, sems.at[i]) for i, (src, dst) in enumerate(pairs)]
    for copy in copies:
        copy.start()
    return copies


def start_kernel(prev_in, mix_in, list_in, count_in, out_ref, prev_ref, mix_ref, list_ref, count_ref, sems):
    copies = fetch(
        [(prev_in, prev_ref), (mix_in, mix_ref), (list_in, list_ref), (count_in, count_ref)], sems
    )
    for copy in copies[1:]:
        copy.wait()
    comps, vecs, rows = prev_ref.shape
    eye = iota((vecs, vecs), 0) == iota((vecs, vecs), 1)
    weights = []
    for c in range(comps):
        line = jnp.broadcast_to(mix_ref[c : c + 1, :], eye.shape)
        weights.append(jnp.sum(jnp.where(eye, line, 0.0), axis=1, keepdims=True))
    order = list_ref[0].astype(jnp.float32)
    order = jnp.concatenate([order, jnp.zeros((4, 120), jnp.float32)], axis=1)
    meta = jnp.zeros((8, 128), jnp.float32)
    slot = iota((1, 128), 1)
    for link in range(4):
        live = slot < jnp.broadcast_to(count_ref[0:1, link : link + 1], slot.shape)
        line = jnp.where(live, order[link : link + 1], DEAD)
        line = pltpu.roll(jnp.broadcast_to(line, (8, 128)), 8 + 8 * link, 1)
        meta = jnp.where(iota((8, 128), 1) // 8 == link + 1, line, meta)
    out_ref[8 * comps :, :] = meta
    copies[0].wait()
    own = own_lanes(8, rows)
    for c in range(comps):
        start = jnp.sum(weights[c] * prev_ref[c], axis=0, keepdims=True)
        line = jnp.broadcast_to(start, own.shape)
        out_ref[c * 8 : (c + 1) * 8, :] = fold(jnp.where(own, line, 0.0))


def prepare_kernel(strips_in, columns_in, shifts_in, high_ref, low_ref, aux_ref, strips, columns, shifts, sems):
    rows = strips.shape[0]
    cuts = [(0, rows // 2), (rows // 2, rows)]
    pairs = [(strips_in.at[pl.ds(a, b - a)], strips.at[pl.ds(a, b - a)]) for a, b in cuts]
    copies = fetch(pairs + [(columns_in, columns), (shifts_in, shifts)], sems)
    copies[2].wait()
    copies[3].wait()
    eye = iota((8, 8), 0) == iota((8, 8), 1)
    for k in range(1, columns.shape[0]):
        line = jnp.broadcast_to(columns[k : k + 1, :].astype(jnp.float32), (8, 8))
        column = jnp.sum(jnp.where(eye, line, 0.0), axis=1, keepdims=True)
        at = 8 * S + 8 * (k - 1)
        aux_ref[at : at + 8, :] = jnp.broadcast_to(column, (8, 128))
    for k in range(S):
        aux_ref[8 * k : 8 * k + 8, :] = jnp.full((8, 128), shifts[k], jnp.float32)
    for copy, (a, b) in zip(copies, cuts):
        copy.wait()
        turned = strips[a:b, :].T
        high = turned.astype(jnp.bfloat16)
        high_ref[:, a:b] = high
        low_ref[:, a:b] = (turned - high.astype(jnp.float32)).astype(jnp.bfloat16)


def selection(table, metas, place, length):
    even, even_far = lax.rem(place, 2) == 0, lax.rem(place // FAR, 2) == 0
    near, far_odd, far_even, across = metas
    moved = (place == 2) | (place == length - 3)
    across = jnp.where(moved, far_odd, across)
    circle = jnp.where(moved, 16.0, 32.0)
    slots = [
        (place >= 1, jnp.where(even, circle, 8.0), jnp.where(even, across, near)),
        (place < length - 1, jnp.where(even, 8.0, circle), jnp.where(even, near, across)),
        (place >= FAR, jnp.where(even_far, 16.0, 24.0), jnp.where(even_far, far_odd, far_even)),
        (place < length - FAR, jnp.where(even_far, 24.0, 16.0), jnp.where(even_far, far_even, far_odd)),
    ]
    lane = iota((1, 128), 1)
    target = lane.astype(jnp.float32)
    for link, (valid, base, order) in enumerate(slots):
        order = order + jnp.where(valid, base, DEAD)
        target = jnp.where(lane // 8 == link + 1, order, target)
    target = jnp.broadcast_to(target, (8, 128))
    index = table.astype(jnp.int32)
    at = [jnp.take_along_axis(target, index[8 * k : 8 * k + 8], axis=1) for k in range(3)]
    return jnp.concatenate(at, axis=0).astype(jnp.int32)


def product(choose, pieces, high, low):
    rows = 8 * COMPS
    front = iota((8, 128), 1) < BLOCK
    picked = [[pieces[0][8 * c : 8 * c + 8] for c in range(COMPS)]]
    for k in range(3):
        code = choose[8 * k : 8 * k + 8]
        index, place = code & 7, code >> 3
        blocks = []
        for c in range(COMPS):
            block = jnp.zeros((8, 128), jnp.float32)
            for p, piece in enumerate(pieces):
                found = jnp.take_along_axis(piece[8 * c : 8 * c + 8], index, axis=0)
                block = jnp.where(place == p, found, block)
            blocks.append(block)
        picked.append(blocks)
    x = [
        jnp.concatenate(
            [jnp.where(front, picked[2 * t][c], picked[2 * t + 1][c]) for t in range(2)], axis=1
        )
        for c in range(COMPS)
    ]
    x = jnp.concatenate(x, axis=0)
    top = x.astype(jnp.bfloat16).astype(jnp.float32)
    left = jnp.concatenate([top, x - top], axis=0).astype(jnp.bfloat16)
    both = dot(left, high) + dot(left, low)
    image = both[:rows] + both[rows:]
    return jnp.where(own_lanes(rows, image.shape[1]), image, 0.0)


def multiply(choose, pieces, shift, high, low):
    image = fold(product(choose, pieces, high, low))
    return image - jnp.concatenate([shift] * COMPS, axis=0) * pieces[0]


def first_kernel(length, own, a, c, d, b, aux, high, low, tile_ref, choose_ref):
    rows = 8 * COMPS
    refs = (own, a, b, c, d)
    pieces = [ref[:rows, :] for ref in refs]
    metas = [ref[rows : rows + 1, :] for ref in refs[1:]]
    choose = selection(aux[8 * S :, :], metas, lax.axis_index("dom"), length)
    choose_ref[...] = choose
    tile_ref[...] = multiply(choose, pieces, aux[:8, :], high[...], low[...])


def middle_kernel(step, own, a, b, c, d, choose, aux, high, low, tile_ref):
    pieces = [ref[...] for ref in (own, a, b, c, d)]
    tile_ref[...] = multiply(choose[...], pieces, aux[8 * step : 8 * step + 8, :], high[...], low[...])


def collect(gram, width, vecs):
    lane, comp = iota(gram.shape, 1), iota(gram.shape, 0)
    mine = jnp.where(lane < width, lane // vecs, lane % 8) == comp
    return jnp.sum(jnp.where(mine, gram, 0.0), axis=0, keepdims=True)


def early_kernel(prev_ref, t0, t1, t2, lines_ref, gram_ref, *split_refs):
    comps, vecs, rows = prev_ref.shape
    width = comps * vecs
    lines = jnp.concatenate([lines_of(t[...], rows) for t in (t0, t1, t2)], axis=0)
    lines_ref[...] = lines
    prev = prev_ref[...].reshape(width, rows)
    full = dot(prev, prev, NT, HIGHEST)
    full = jnp.concatenate([full, jnp.zeros((width, 128 - width), jnp.float32)], axis=1)
    lane = iota((8, 128), 1)
    tiles = [jnp.zeros((8, 128), jnp.float32)] * 2
    for (c, g), (t, first) in PLACES.items():
        at = c * vecs + 8 * g
        piece = pltpu.roll(full[at : at + 8], (first - at) % 128, 1)
        tiles[t] = jnp.where((lane >= first) & (lane < first + vecs - 8 * g), piece, tiles[t])
    gram_ref[:16, :] = jnp.concatenate(tiles, axis=0)
    against = jnp.concatenate([prev, lines, jnp.zeros((8, rows), jnp.float32)], axis=0)
    for ref, part in zip(split_refs, split(against.T)):
        ref[...] = part
    gram = dot(lines, against, NT, HIGHEST)
    result = jnp.zeros((8, 128), jnp.float32)
    for k in range(S - 1):
        line = collect(gram[k * 8 : (k + 1) * 8], width, vecs)
        result = jnp.where(iota((8, 128), 0) == k, jnp.broadcast_to(line, result.shape), result)
    gram_ref[16:, :] = result


def last_kernel(
    vecs, own, a, b, c, d, choose, aux, high, low, early, t0, t1, t2, lines, line_ref, gram_ref
):
    pieces = [ref[...] for ref in (own, a, b, c, d)]
    image = joined(product(choose[...], pieces, high[...], low[...]))
    width = COMPS * vecs
    shift = aux[8 * S - 8 : 8 * S, :1]
    last = image - shift * lines[8 * S - 16 :, :]
    line_ref[...] = last
    gram = split_dot(last, (t0[...], t1[...], t2[...]))
    square = jnp.sum(last * last, axis=1, keepdims=True)
    gram = jnp.where(iota(gram.shape, 1) == width + 8 * (S - 1) + iota(gram.shape, 0), square, gram)
    line = collect(gram, width, vecs)
    gram_ref[:16, :] = early[:16, :]
    gram_ref[16:, :] = jnp.where(
        iota((8, 128), 0) == S - 1, jnp.broadcast_to(line, (8, 128)), early[16:, :]
    )


def finish_kernel(total, gram_ins, prev_ref, lines, last, basis_ref, factors_ref):
    comps, vecs, rows = prev_ref.shape
    width = comps * vecs
    gram = added([ref[...] for ref in gram_ins]) * (1.0 / total)
    small = gram[16:]
    lane, comp = iota((8, 128), 1), iota((8, 128), 0)
    in_prev = (lane < width) & (lane // vecs == comp)
    coef, cross = [], []
    for k in range(S):
        line = jnp.broadcast_to(small[k : k + 1], (8, 128))
        coef.append(jnp.where(in_prev, line, 0.0))
        cross.append([jnp.where(lane == width + 8 * l + comp, line, 0.0) for l in range(k + 1)])
    coefs = jnp.concatenate(coef, axis=0)
    pieces, turns = [], {}
    for c in range(comps):
        for g in range(vecs // 8):
            t, first = PLACES[c, g]
            at = c * vecs + 8 * g
            turn = t, (at - first) % 128
            if turn not in turns:
                piece = gram[8 * t : 8 * t + 8]
                turns[turn] = pltpu.roll(piece, turn[1], 1) if turn[1] else piece
            piece = turns[turn]
            piece = jnp.where(lane < at + 8, 0.5 * piece, piece)
            piece = jnp.where((lane >= at) & (lane < (c + 1) * vecs), piece, 0.0)
            pieces.append(piece - jnp.where(lane == at + comp, 1.0, 0.0))
    half = jnp.concatenate(pieces, axis=0)
    turned = dot(coefs[:, :width], half, precision=HIGHEST)
    prev = prev_ref[...].reshape(width, rows)
    basis = jnp.concatenate([lines[...], last[...]], axis=0)
    projected = basis - dot(coefs[:, :width], prev, precision=HIGHEST)
    unit, scale = {}, {}
    for l in range(S):
        for k in range(l, S):
            value = turned[k * 8 : (k + 1) * 8] * coef[l] + turned[l * 8 : (l + 1) * 8] * coef[k] + cross[k][l]
            value = jnp.sum(value, axis=1, keepdims=True)
            for m in range(l):
                value = value - (unit[k, m] * scale[m]) * unit[l, m]
            if k == l:
                scale[l] = value
            else:
                unit[k, l] = value / scale[l]
    roots = [jnp.sqrt(scale[k]) for k in range(S)]
    lower = {(k, l): unit[k, l] * roots[l] if l < k else roots[k] for k in range(S) for l in range(k + 1)}
    vectors = []
    for k in range(S):
        value = projected[k * 8 : (k + 1) * 8]
        for l in range(k):
            value = value - unit[k, l] * vectors[l]
        vectors.append(value)
        value = value * (1.0 / roots[k])
        for c in range(comps):
            basis_ref[c, k : k + 1, :] = value[c : c + 1]
    for c in range(comps):
        factors_ref[c, :, :vecs] = small[:S, c * vecs : (c + 1) * vecs]
    for k in range(S):
        line = jnp.zeros((8, 128), jnp.float32)
        for l in range(k + 1):
            line = jnp.where(lane == vecs + l, lower[k, l], line)
        for c in range(comps):
            factors_ref[c, k : k + 1, vecs:] = line[c : c + 1, vecs : vecs + S]


VMEM = pl.BlockSpec(memory_space=pltpu.VMEM)
HBM = pl.BlockSpec(memory_space=pltpu.HBM)


def in_hbm(*arrays):
    return [pltpu.with_memory_space_constraint(x, pltpu.HBM) for x in arrays]


def call(kernel, outs, specs, flops, moved, scratch=()):
    shapes = [jax.ShapeDtypeStruct(shape, kind) for shape, kind in outs]
    return pl.pallas_call(
        kernel,
        out_shape=shapes if len(shapes) > 1 else shapes[0],
        in_specs=specs,
        out_specs=[VMEM] * len(shapes) if len(shapes) > 1 else VMEM,
        scratch_shapes=list(scratch),
        compiler_params=pltpu.CompilerParams(vmem_limit_bytes=24 * 1024 * 1024),
        cost_estimate=pl.CostEstimate(flops=flops, bytes_accessed=moved, transcendentals=0),
    )


def send(value, target):
    return lax.ppermute(value, "dom", [(d, target[d]) for d in range(lax.axis_size("dom"))])


def neighbours(length, step, odd):
    target = {}
    for d in range(length):
        other = d + step if (d // step) % 2 == odd else d - step
        target[d] = other if 0 <= other < length else None
    return target


def ghosts(tile):
    length = lax.axis_size("dom")
    last = length - 1
    near, across = neighbours(length, 1, 0), neighbours(length, 1, 1)
    far_even, far_odd = neighbours(length, FAR, 0), neighbours(length, FAR, 1)
    across.update({0: 2, 2: 1, 1: 0, last: last - 2, last - 2: last - 1, last - 1: last})
    for d in range(length):
        if far_odd[d] is None:
            far_odd[d] = d ^ 1
    far_odd.update({1: 2, 2: 3, 3: 0, 0: 1})
    far_odd.update({last - 1: last - 2, last - 2: last - 3, last - 3: last, last: last - 1})
    return [send(tile, target) for target in (near, far_odd, far_even, across)]


def summed(value):
    length = lax.axis_size("dom")

    def fetched(step):
        return send(value, {d: d ^ (step | 1) for d in range(length)})

    parts = [value, fetched(1)]
    step = 2
    while step < length:
        value = added(parts)
        steps = (3 * step, step, 2 * step) if 2 * step < length else (step,)
        got = [fetched(s) for s in steps]
        parts = [value] + got[1:] + got[:1]
        step *= 4
    return parts


def added(parts):
    if len(parts) == 2:
        return parts[0] + parts[1]
    return (parts[0] + parts[1]) + (parts[2] + parts[3])


def local(strips, columns, send_list, send_count, shifts, prev_basis, mix):
    comps, vecs, rows = prev_basis.shape
    blocks = columns.shape[0]
    width = strips.shape[1]
    f32, bf16, dma = jnp.float32, jnp.bfloat16, pltpu.SemaphoreType.DMA
    tile_out = ((comps * blocks, 128), f32)
    tile = call(
        start_kernel,
        [((comps * blocks + 8, 128), f32)],
        [HBM] * 4,
        600000,
        250000,
        [
            pltpu.VMEM(prev_basis.shape, f32),
            pltpu.VMEM(mix.shape, f32),
            pltpu.VMEM(send_list.shape, jnp.int32),
            pltpu.VMEM(send_count.shape, jnp.int32),
            dma((4,)),
        ],
    )(*in_hbm(prev_basis, mix, send_list, send_count))
    high, low, aux = call(
        prepare_kernel,
        [((width, rows), bf16), ((width, rows), bf16), ((8 * S + 24, 128), f32)],
        [HBM] * 3,
        1000000,
        1000000,
        [
            pltpu.VMEM((rows, width), f32),
            pltpu.VMEM(columns.shape[::-1], jnp.int32),
            pltpu.SMEM(shifts.shape, f32),
            dma((4,)),
        ],
    )(*in_hbm(strips, columns.T, shifts))
    tiles = []
    length = lax.axis_size("dom")
    near, far_odd, far_even, across = ghosts(tile)
    tile, choose = call(
        lambda *refs: first_kernel(length, *refs),
        [tile_out, ((3 * blocks, 128), jnp.int32)],
        [VMEM] * 8,
        50000000,
        600000,
    )(tile, near, far_even, across, far_odd, aux, high, low)
    tiles.append(tile)
    for step in (1, 2):
        tile = call(
            lambda *refs, step=step: middle_kernel(step, *refs), [tile_out], [VMEM] * 9, 50000000, 600000
        )(tile, *ghosts(tile), choose, aux, high, low)
        tiles.append(tile)
    received = ghosts(tile)
    gram_out = ((24, 128), f32)
    lines, early, *parts = call(
        early_kernel,
        [((8 * S - 8, rows), f32), gram_out] + [((rows, 128), bf16)] * 3,
        [VMEM] * 4,
        60000000,
        250000,
    )(prev_basis, *tiles)
    last, gram = call(
        lambda *refs: last_kernel(vecs, *refs),
        [((8, rows), f32), gram_out],
        [VMEM] * 14,
        80000000,
        900000,
    )(tile, *received, choose, aux, high, low, early, *parts, lines)
    total = float(length * rows)
    parts = summed(gram)
    count = len(parts)
    basis, factors = call(
        lambda *refs: finish_kernel(total, refs[:count], *refs[count:]),
        [((comps, S, rows), f32), ((comps, S, vecs + S), f32)],
        [VMEM] * (count + 3),
        50000000,
        400000,
    )(*parts, prev_basis, lines, last)
    return basis, jnp.swapaxes(factors, 1, 2)


def solution(mesh):
    in_specs = (
        P("dom", None),
        P("dom", None),
        P("dom", None, None),
        P("dom", None),
        P(),
        P(None, None, "dom"),
        P(),
    )
    out_specs = (P(None, None, "dom"), P())
    return jax.shard_map(local, mesh=mesh, in_specs=in_specs, out_specs=out_specs, check_vma=False)
```

```python
import jax
import jax.numpy as jnp
from jax import lax
from jax.experimental import pallas as pl
from jax.experimental.pallas import tpu as pltpu
from jax.sharding import PartitionSpec as P

BLOCK = 64
S = 4
FAR = 8
COMPS = 3
DEAD = 1000.0
HIGHEST = lax.Precision.HIGHEST
NN = (((1,), (0,)), ((), ()))
NT = (((1,), (1,)), ((), ()))


def dot(a, b, dims=NN, precision=None):
    return lax.dot_general(a, b, dims, precision=precision, preferred_element_type=jnp.float32)


def iota(shape, axis):
    return lax.broadcasted_iota(jnp.int32, shape, axis)


PLACES = {(c, g): (g % 2, (0, 8, 0, 0)[g] + 32 * c) for c in range(COMPS) for g in range(4)}
PLACES.update({(0, 2): (0, 96), (1, 2): (0, 112), (2, 2): (1, 96)})


def own_lanes(rows, width):
    return iota((rows, width), 1) // BLOCK == iota((rows, width), 0) % 8


def fold(masked):
    total = masked[:, :128]
    for t in range(1, masked.shape[1] // 128):
        total = total + masked[:, t * 128 : (t + 1) * 128]
    return total + pltpu.roll(total, BLOCK, 1)


def lines_of(tile, width):
    wide = jnp.concatenate([tile] * (width // 128), axis=1)
    return joined(jnp.where(own_lanes(wide.shape[0], width), wide, 0.0))


def joined(wide):
    width = wide.shape[1]
    where = iota((8, width), 0)
    result = jnp.zeros((8, width), jnp.float32)
    for c in range(COMPS):
        line = jnp.sum(wide[c * 8 : (c + 1) * 8], axis=0, keepdims=True)
        result = jnp.where(where == c, jnp.broadcast_to(line, result.shape), result)
    return result


def split(x):
    parts = []
    for _ in range(3):
        parts.append(x.astype(jnp.bfloat16))
        x = x - parts[-1].astype(jnp.float32)
    return parts


def split_dot(x, parts):
    left = [part.astype(jnp.float32) for part in split(x)]
    left.append(jnp.zeros((-3 * x.shape[0] % 16, x.shape[1]), jnp.float32))
    left = jnp.concatenate([part for part in left if part.shape[0]], axis=0).astype(jnp.bfloat16)
    products = dot(left, parts[0]) + dot(left, parts[1]) + dot(left, parts[2])
    rows = x.shape[0]
    return products[:rows] + (products[rows : 2 * rows] + products[2 * rows : 3 * rows])


def fetch(pairs, sems):
    copies = [pltpu.make_async_copy(src, dst, sems.at[i]) for i, (src, dst) in enumerate(pairs)]
    for copy in copies:
        copy.start()
    return copies


def start_kernel(prev_in, mix_in, list_in, count_in, out_ref, prev_ref, mix_ref, list_ref, count_ref, sems):
    copies = fetch(
        [(prev_in, prev_ref), (mix_in, mix_ref), (list_in, list_ref), (count_in, count_ref)], sems
    )
    for copy in copies[1:]:
        copy.wait()
    comps, vecs, rows = prev_ref.shape
    eye = iota((vecs, vecs), 0) == iota((vecs, vecs), 1)
    weights = []
    for c in range(comps):
        line = jnp.broadcast_to(mix_ref[c : c + 1, :], eye.shape)
        weights.append(jnp.sum(jnp.where(eye, line, 0.0), axis=1, keepdims=True))
    order = list_ref[0].astype(jnp.float32)
    order = jnp.concatenate([order, jnp.zeros((4, 120), jnp.float32)], axis=1)
    meta = jnp.zeros((8, 128), jnp.float32)
    slot = iota((1, 128), 1)
    for link in range(4):
        live = slot < jnp.broadcast_to(count_ref[0:1, link : link + 1], slot.shape)
        line = jnp.where(live, order[link : link + 1], DEAD)
        line = pltpu.roll(jnp.broadcast_to(line, (8, 128)), BLOCK + 8 + 8 * link, 1)
        meta = jnp.where(iota((8, 128), 1) // 8 == BLOCK // 8 + link + 1, line, meta)
    copies[0].wait()
    own = own_lanes(8, rows)
    for c in range(comps):
        start = jnp.sum(weights[c] * prev_ref[c], axis=0, keepdims=True)
        line = jnp.broadcast_to(start, own.shape)
        part = fold(jnp.where(own, line, 0.0))
        if c == comps - 1:
            part = jnp.where(iota((8, 128), 1) < BLOCK, part, meta)
        out_ref[c * 8 : (c + 1) * 8, :] = part


def prepare_kernel(strips_in, columns_in, shifts_in, high_ref, low_ref, aux_ref, strips, columns, shifts, sems):
    rows = strips.shape[0]
    cuts = [(0, rows // 2), (rows // 2, rows)]
    pairs = [(strips_in.at[pl.ds(a, b - a)], strips.at[pl.ds(a, b - a)]) for a, b in cuts]
    copies = fetch(pairs + [(columns_in, columns), (shifts_in, shifts)], sems)
    copies[2].wait()
    copies[3].wait()
    eye = iota((8, 8), 0) == iota((8, 8), 1)
    for k in range(1, columns.shape[0]):
        line = jnp.broadcast_to(columns[k : k + 1, :].astype(jnp.float32), (8, 8))
        column = jnp.sum(jnp.where(eye, line, 0.0), axis=1, keepdims=True)
        at = 8 * S + 8 * (k - 1)
        aux_ref[at : at + 8, :] = jnp.broadcast_to(column, (8, 128))
    for k in range(S):
        aux_ref[8 * k : 8 * k + 8, :] = jnp.full((8, 128), shifts[k], jnp.float32)
    for copy, (a, b) in zip(copies, cuts):
        copy.wait()
        turned = strips[a:b, :].T
        high = turned.astype(jnp.bfloat16)
        high_ref[:, a:b] = high
        low_ref[:, a:b] = (turned - high.astype(jnp.float32)).astype(jnp.bfloat16)


def selection(table, metas, place, length):
    even, even_far = lax.rem(place, 2) == 0, lax.rem(place // FAR, 2) == 0
    near, far_odd, far_even, across = metas
    moved = (place == 2) | (place == length - 3)
    across = jnp.where(moved, far_odd, across)
    circle = jnp.where(moved, 16.0, 32.0)
    slots = [
        (place >= 1, jnp.where(even, circle, 8.0), jnp.where(even, across, near)),
        (place < length - 1, jnp.where(even, 8.0, circle), jnp.where(even, near, across)),
        (place >= FAR, jnp.where(even_far, 16.0, 24.0), jnp.where(even_far, far_odd, far_even)),
        (place < length - FAR, jnp.where(even_far, 24.0, 16.0), jnp.where(even_far, far_even, far_odd)),
    ]
    lane = iota((1, 128), 1)
    target = lane.astype(jnp.float32)
    for link, (valid, base, order) in enumerate(slots):
        order = order + jnp.where(valid, base, DEAD)
        target = jnp.where(lane // 8 == link + 1, order, target)
    target = jnp.broadcast_to(target, (8, 128))
    index = table.astype(jnp.int32)
    at = [jnp.take_along_axis(target, index[8 * k : 8 * k + 8], axis=1) for k in range(3)]
    return jnp.concatenate(at, axis=0).astype(jnp.int32)


def product(choose, pieces, high, low):
    rows = 8 * COMPS
    front = iota((8, 128), 1) < BLOCK
    picked = [[pieces[0][8 * c : 8 * c + 8] for c in range(COMPS)]]
    for k in range(3):
        code = choose[8 * k : 8 * k + 8]
        index, place = code & 7, code >> 3
        blocks = []
        for c in range(COMPS):
            block = jnp.zeros((8, 128), jnp.float32)
            for p, piece in enumerate(pieces):
                found = jnp.take_along_axis(piece[8 * c : 8 * c + 8], index, axis=0)
                block = jnp.where(place == p, found, block)
            blocks.append(block)
        picked.append(blocks)
    x = [
        jnp.concatenate(
            [jnp.where(front, picked[2 * t][c], picked[2 * t + 1][c]) for t in range(2)], axis=1
        )
        for c in range(COMPS)
    ]
    x = jnp.concatenate(x, axis=0)
    top = x.astype(jnp.bfloat16).astype(jnp.float32)
    left = jnp.concatenate([top, x - top], axis=0).astype(jnp.bfloat16)
    both = dot(left, high) + dot(left, low)
    image = both[:rows] + both[rows:]
    return jnp.where(own_lanes(rows, image.shape[1]), image, 0.0)


def multiply(choose, pieces, shift, high, low):
    image = fold(product(choose, pieces, high, low))
    return image - jnp.concatenate([shift] * COMPS, axis=0) * pieces[0]


def first_kernel(length, own, a, c, d, b, aux, high, low, tile_ref, choose_ref):
    pieces, metas = [], []
    for ref in (own, a, b, c, d):
        last = ref[8 * COMPS - 8 :, :]
        turned = pltpu.roll(last, BLOCK, 1)
        last = jnp.where(iota((8, 128), 1) < BLOCK, last, turned)
        pieces.append(jnp.concatenate([ref[: 8 * COMPS - 8, :], last], axis=0))
        metas.append(turned[:1])
    metas = metas[1:]
    choose = selection(aux[8 * S :, :], metas, lax.axis_index("dom"), length)
    choose_ref[...] = choose
    tile_ref[...] = multiply(choose, pieces, aux[:8, :], high[...], low[...])


def middle_kernel(step, own, a, b, c, d, choose, aux, high, low, tile_ref):
    pieces = [ref[...] for ref in (own, a, b, c, d)]
    tile_ref[...] = multiply(choose[...], pieces, aux[8 * step : 8 * step + 8, :], high[...], low[...])


def collect(gram, width, vecs):
    lane, comp = iota(gram.shape, 1), iota(gram.shape, 0)
    mine = jnp.where(lane < width, lane // vecs, lane % 8) == comp
    return jnp.sum(jnp.where(mine, gram, 0.0), axis=0, keepdims=True)


def early_kernel(prev_ref, t0, t1, t2, lines_ref, gram_ref, *split_refs):
    comps, vecs, rows = prev_ref.shape
    width = comps * vecs
    lines = jnp.concatenate([lines_of(t[...], rows) for t in (t0, t1, t2)], axis=0)
    lines_ref[...] = lines
    prev = prev_ref[...].reshape(width, rows)
    full = dot(prev, prev, NT, HIGHEST)
    full = jnp.concatenate([full, jnp.zeros((width, 128 - width), jnp.float32)], axis=1)
    lane = iota((8, 128), 1)
    tiles = [jnp.zeros((8, 128), jnp.float32)] * 2
    for (c, g), (t, first) in PLACES.items():
        at = c * vecs + 8 * g
        piece = pltpu.roll(full[at : at + 8], (first - at) % 128, 1)
        tiles[t] = jnp.where((lane >= first) & (lane < first + vecs - 8 * g), piece, tiles[t])
    gram_ref[:16, :] = jnp.concatenate(tiles, axis=0)
    against = jnp.concatenate([prev, lines, jnp.zeros((8, rows), jnp.float32)], axis=0)
    for ref, part in zip(split_refs, split(against.T)):
        ref[...] = part
    gram = dot(lines, against, NT, HIGHEST)
    result = jnp.zeros((8, 128), jnp.float32)
    for k in range(S - 1):
        line = collect(gram[k * 8 : (k + 1) * 8], width, vecs)
        result = jnp.where(iota((8, 128), 0) == k, jnp.broadcast_to(line, result.shape), result)
    gram_ref[16:, :] = result


def last_kernel(
    vecs, own, a, b, c, d, choose, aux, high, low, early, t0, t1, t2, lines, line_ref, gram_ref
):
    pieces = [ref[...] for ref in (own, a, b, c, d)]
    image = joined(product(choose[...], pieces, high[...], low[...]))
    width = COMPS * vecs
    shift = aux[8 * S - 8 : 8 * S, :1]
    last = image - shift * lines[8 * S - 16 :, :]
    line_ref[...] = last
    gram = split_dot(last, (t0[...], t1[...], t2[...]))
    square = jnp.sum(last * last, axis=1, keepdims=True)
    gram = jnp.where(iota(gram.shape, 1) == width + 8 * (S - 1) + iota(gram.shape, 0), square, gram)
    line = collect(gram, width, vecs)
    gram_ref[:16, :] = early[:16, :]
    gram_ref[16:, :] = jnp.where(
        iota((8, 128), 0) == S - 1, jnp.broadcast_to(line, (8, 128)), early[16:, :]
    )


def finish_kernel(total, gram_ins, prev_ref, lines, last, basis_ref, factors_ref):
    comps, vecs, rows = prev_ref.shape
    width = comps * vecs
    gram = added([ref[...] for ref in gram_ins]) * (1.0 / total)
    small = gram[16:]
    lane, comp = iota((8, 128), 1), iota((8, 128), 0)
    in_prev = (lane < width) & (lane // vecs == comp)
    coef, cross = [], []
    for k in range(S):
        line = jnp.broadcast_to(small[k : k + 1], (8, 128))
        coef.append(jnp.where(in_prev, line, 0.0))
        cross.append([jnp.where(lane == width + 8 * l + comp, line, 0.0) for l in range(k + 1)])
    coefs = jnp.concatenate(coef, axis=0)
    pieces, turns = [], {}
    for c in range(comps):
        for g in range(vecs // 8):
            t, first = PLACES[c, g]
            at = c * vecs + 8 * g
            turn = t, (at - first) % 128
            if turn not in turns:
                piece = gram[8 * t : 8 * t + 8]
                turns[turn] = pltpu.roll(piece, turn[1], 1) if turn[1] else piece
            piece = turns[turn]
            piece = jnp.where(lane < at + 8, 0.5 * piece, piece)
            piece = jnp.where((lane >= at) & (lane < (c + 1) * vecs), piece, 0.0)
            pieces.append(piece - jnp.where(lane == at + comp, 1.0, 0.0))
    half = jnp.concatenate(pieces, axis=0)
    turned = dot(coefs[:, :width], half, precision=HIGHEST)
    prev = prev_ref[...].reshape(width, rows)
    basis = jnp.concatenate([lines[...], last[...]], axis=0)
    projected = basis - dot(coefs[:, :width], prev, precision=HIGHEST)
    unit, scale = {}, {}
    for l in range(S):
        for k in range(l, S):
            value = turned[k * 8 : (k + 1) * 8] * coef[l] + turned[l * 8 : (l + 1) * 8] * coef[k] + cross[k][l]
            value = jnp.sum(value, axis=1, keepdims=True)
            for m in range(l):
                value = value - (unit[k, m] * scale[m]) * unit[l, m]
            if k == l:
                scale[l] = value
            else:
                unit[k, l] = value / scale[l]
    roots = [jnp.sqrt(scale[k]) for k in range(S)]
    lower = {(k, l): unit[k, l] * roots[l] if l < k else roots[k] for k in range(S) for l in range(k + 1)}
    vectors = []
    for k in range(S):
        value = projected[k * 8 : (k + 1) * 8]
        for l in range(k):
            value = value - unit[k, l] * vectors[l]
        vectors.append(value)
        value = value * (1.0 / roots[k])
        for c in range(comps):
            basis_ref[c, k : k + 1, :] = value[c : c + 1]
    for c in range(comps):
        factors_ref[c, :, :vecs] = small[:S, c * vecs : (c + 1) * vecs]
    for k in range(S):
        line = jnp.zeros((8, 128), jnp.float32)
        for l in range(k + 1):
            line = jnp.where(lane == vecs + l, lower[k, l], line)
        for c in range(comps):
            factors_ref[c, k : k + 1, vecs:] = line[c : c + 1, vecs : vecs + S]


VMEM = pl.BlockSpec(memory_space=pltpu.VMEM)
HBM = pl.BlockSpec(memory_space=pltpu.HBM)


def in_hbm(*arrays):
    return [pltpu.with_memory_space_constraint(x, pltpu.HBM) for x in arrays]


def call(kernel, outs, specs, flops, moved, scratch=()):
    shapes = [jax.ShapeDtypeStruct(shape, kind) for shape, kind in outs]
    return pl.pallas_call(
        kernel,
        out_shape=shapes if len(shapes) > 1 else shapes[0],
        in_specs=specs,
        out_specs=[VMEM] * len(shapes) if len(shapes) > 1 else VMEM,
        scratch_shapes=list(scratch),
        compiler_params=pltpu.CompilerParams(vmem_limit_bytes=24 * 1024 * 1024),
        cost_estimate=pl.CostEstimate(flops=flops, bytes_accessed=moved, transcendentals=0),
    )


def send(value, target):
    return lax.ppermute(value, "dom", [(d, target[d]) for d in range(lax.axis_size("dom"))])


def neighbours(length, step, odd):
    target = {}
    for d in range(length):
        other = d + step if (d // step) % 2 == odd else d - step
        target[d] = other if 0 <= other < length else None
    return target


def ghosts(tile):
    length = lax.axis_size("dom")
    last = length - 1
    near, across = neighbours(length, 1, 0), neighbours(length, 1, 1)
    far_even, far_odd = neighbours(length, FAR, 0), neighbours(length, FAR, 1)
    across.update({0: 2, 2: 1, 1: 0, last: last - 2, last - 2: last - 1, last - 1: last})
    for d in range(length):
        if far_odd[d] is None:
            far_odd[d] = d ^ 1
    far_odd.update({1: 2, 2: 3, 3: 0, 0: 1})
    far_odd.update({last - 1: last - 2, last - 2: last - 3, last - 3: last, last: last - 1})
    return [send(tile, target) for target in (near, far_odd, far_even, across)]


def summed(value):
    length = lax.axis_size("dom")

    def fetched(step):
        return send(value, {d: d ^ (step | 1) for d in range(length)})

    parts = [value, fetched(1)]
    step = 2
    while step < length:
        value = added(parts)
        steps = (3 * step, step, 2 * step) if 2 * step < length else (step,)
        got = [fetched(s) for s in steps]
        parts = [value] + got[1:] + got[:1]
        step *= 4
    return parts


def added(parts):
    if len(parts) == 2:
        return parts[0] + parts[1]
    return (parts[0] + parts[1]) + (parts[2] + parts[3])


def local(strips, columns, send_list, send_count, shifts, prev_basis, mix):
    comps, vecs, rows = prev_basis.shape
    blocks = columns.shape[0]
    width = strips.shape[1]
    f32, bf16, dma = jnp.float32, jnp.bfloat16, pltpu.SemaphoreType.DMA
    tile_out = ((comps * blocks, 128), f32)
    tile = call(
        start_kernel,
        [tile_out],
        [HBM] * 4,
        600000,
        250000,
        [
            pltpu.VMEM(prev_basis.shape, f32),
            pltpu.VMEM(mix.shape, f32),
            pltpu.VMEM(send_list.shape, jnp.int32),
            pltpu.VMEM(send_count.shape, jnp.int32),
            dma((4,)),
        ],
    )(*in_hbm(prev_basis, mix, send_list, send_count))
    high, low, aux = call(
        prepare_kernel,
        [((width, rows), bf16), ((width, rows), bf16), ((8 * S + 24, 128), f32)],
        [HBM] * 3,
        1000000,
        1000000,
        [
            pltpu.VMEM((rows, width), f32),
            pltpu.VMEM(columns.shape[::-1], jnp.int32),
            pltpu.SMEM(shifts.shape, f32),
            dma((4,)),
        ],
    )(*in_hbm(strips, columns.T, shifts))
    tiles = []
    length = lax.axis_size("dom")
    near, far_odd, far_even, across = ghosts(tile)
    tile, choose = call(
        lambda *refs: first_kernel(length, *refs),
        [tile_out, ((3 * blocks, 128), jnp.int32)],
        [VMEM] * 8,
        50000000,
        600000,
    )(tile, near, far_even, across, far_odd, aux, high, low)
    tiles.append(tile)
    for step in (1, 2):
        tile = call(
            lambda *refs, step=step: middle_kernel(step, *refs), [tile_out], [VMEM] * 9, 50000000, 600000
        )(tile, *ghosts(tile), choose, aux, high, low)
        tiles.append(tile)
    received = ghosts(tile)
    gram_out = ((24, 128), f32)
    lines, early, *parts = call(
        early_kernel,
        [((8 * S - 8, rows), f32), gram_out] + [((rows, 128), bf16)] * 3,
        [VMEM] * 4,
        60000000,
        250000,
    )(prev_basis, *tiles)
    last, gram = call(
        lambda *refs: last_kernel(vecs, *refs),
        [((8, rows), f32), gram_out],
        [VMEM] * 14,
        80000000,
        900000,
    )(tile, *received, choose, aux, high, low, early, *parts, lines)
    total = float(length * rows)
    parts = summed(gram)
    count = len(parts)
    basis, factors = call(
        lambda *refs: finish_kernel(total, refs[:count], *refs[count:]),
        [((comps, S, rows), f32), ((comps, S, vecs + S), f32)],
        [VMEM] * (count + 3),
        50000000,
        400000,
    )(*parts, prev_basis, lines, last)
    return basis, jnp.swapaxes(factors, 1, 2)


def solution(mesh):
    in_specs = (
        P("dom", None),
        P("dom", None),
        P("dom", None, None),
        P("dom", None),
        P(),
        P(None, None, "dom"),
        P(),
    )
    out_specs = (P(None, None, "dom"), P())
    return jax.shard_map(local, mesh=mesh, in_specs=in_specs, out_specs=out_specs, check_vma=False)
```

```python
import jax
import jax.numpy as jnp
from jax import lax
from jax.experimental import pallas as pl
from jax.experimental.pallas import tpu as pltpu
from jax.sharding import PartitionSpec as P

BLOCK = 64
S = 4
FAR = 8
COMPS = 3
DEAD = 1000.0
HIGHEST = lax.Precision.HIGHEST
NN = (((1,), (0,)), ((), ()))
NT = (((1,), (1,)), ((), ()))


def dot(a, b, dims=NN, precision=None):
    return lax.dot_general(a, b, dims, precision=precision, preferred_element_type=jnp.float32)


def iota(shape, axis):
    return lax.broadcasted_iota(jnp.int32, shape, axis)


PLACES = {(c, g): (g % 2, (0, 8, 0, 0)[g] + 32 * c) for c in range(COMPS) for g in range(4)}
PLACES.update({(0, 2): (0, 96), (1, 2): (0, 112), (2, 2): (1, 96)})


def own_lanes(rows, width):
    return iota((rows, width), 1) // BLOCK == iota((rows, width), 0) % 8


def fold(masked):
    total = masked[:, :128]
    for t in range(1, masked.shape[1] // 128):
        total = total + masked[:, t * 128 : (t + 1) * 128]
    return total + pltpu.roll(total, BLOCK, 1)


def lines_of(tile, width):
    wide = jnp.concatenate([tile] * (width // 128), axis=1)
    return joined(jnp.where(own_lanes(wide.shape[0], width), wide, 0.0))


def joined(wide):
    width = wide.shape[1]
    where = iota((8, width), 0)
    result = jnp.zeros((8, width), jnp.float32)
    for c in range(COMPS):
        line = jnp.sum(wide[c * 8 : (c + 1) * 8], axis=0, keepdims=True)
        result = jnp.where(where == c, jnp.broadcast_to(line, result.shape), result)
    return result


def split(x):
    parts = []
    for _ in range(3):
        parts.append(x.astype(jnp.bfloat16))
        x = x - parts[-1].astype(jnp.float32)
    return parts


def split_dot(x, parts):
    left = [part.astype(jnp.float32) for part in split(x)]
    left.append(jnp.zeros((-3 * x.shape[0] % 16, x.shape[1]), jnp.float32))
    left = jnp.concatenate([part for part in left if part.shape[0]], axis=0).astype(jnp.bfloat16)
    products = dot(left, parts[0]) + dot(left, parts[1]) + dot(left, parts[2])
    rows = x.shape[0]
    return products[:rows] + (products[rows : 2 * rows] + products[2 * rows : 3 * rows])


def fetch(pairs, sems):
    copies = [pltpu.make_async_copy(src, dst, sems.at[i]) for i, (src, dst) in enumerate(pairs)]
    for copy in copies:
        copy.start()
    return copies


def start_kernel(prev_in, mix_in, list_in, count_in, out_ref, prev_ref, mix_ref, list_ref, count_ref, sems):
    comps = prev_ref.shape[0]
    cuts = [pl.ds(0, comps - 1), pl.ds(comps - 1, 1)]
    pairs = [(prev_in.at[cut], prev_ref.at[cut]) for cut in cuts]
    copies = fetch(pairs + [(mix_in, mix_ref), (list_in, list_ref), (count_in, count_ref)], sems)
    for copy in copies[2:]:
        copy.wait()
    comps, vecs, rows = prev_ref.shape
    eye = iota((vecs, vecs), 0) == iota((vecs, vecs), 1)
    weights = []
    for c in range(comps):
        line = jnp.broadcast_to(mix_ref[c : c + 1, :], eye.shape)
        weights.append(jnp.sum(jnp.where(eye, line, 0.0), axis=1, keepdims=True))
    order = list_ref[0].astype(jnp.float32)
    order = jnp.concatenate([order, jnp.zeros((4, 120), jnp.float32)], axis=1)
    meta = jnp.zeros((8, 128), jnp.float32)
    slot = iota((1, 128), 1)
    for link in range(4):
        live = slot < jnp.broadcast_to(count_ref[0:1, link : link + 1], slot.shape)
        line = jnp.where(live, order[link : link + 1], DEAD)
        line = pltpu.roll(jnp.broadcast_to(line, (8, 128)), 8 + 8 * link, 1)
        meta = jnp.where(iota((8, 128), 1) // 8 == link + 1, line, meta)
    out_ref[8 * comps :, :] = meta
    copies[0].wait()
    own = own_lanes(8, rows)
    for c in range(comps):
        if c == comps - 1:
            copies[1].wait()
        start = jnp.sum(weights[c] * prev_ref[c], axis=0, keepdims=True)
        line = jnp.broadcast_to(start, own.shape)
        out_ref[c * 8 : (c + 1) * 8, :] = fold(jnp.where(own, line, 0.0))


def prepare_kernel(strips_in, columns_in, shifts_in, high_ref, low_ref, aux_ref, strips, columns, shifts, sems):
    rows = strips.shape[0]
    cuts = [(0, rows // 2), (rows // 2, rows)]
    pairs = [(strips_in.at[pl.ds(a, b - a)], strips.at[pl.ds(a, b - a)]) for a, b in cuts]
    copies = fetch(pairs + [(columns_in, columns), (shifts_in, shifts)], sems)
    copies[2].wait()
    copies[3].wait()
    eye = iota((8, 8), 0) == iota((8, 8), 1)
    for k in range(1, columns.shape[0]):
        line = jnp.broadcast_to(columns[k : k + 1, :].astype(jnp.float32), (8, 8))
        column = jnp.sum(jnp.where(eye, line, 0.0), axis=1, keepdims=True)
        at = 8 * S + 8 * (k - 1)
        aux_ref[at : at + 8, :] = jnp.broadcast_to(column, (8, 128))
    for k in range(S):
        aux_ref[8 * k : 8 * k + 8, :] = jnp.full((8, 128), shifts[k], jnp.float32)
    for copy, (a, b) in zip(copies, cuts):
        copy.wait()
        turned = strips[a:b, :].T
        high = turned.astype(jnp.bfloat16)
        high_ref[:, a:b] = high
        low_ref[:, a:b] = (turned - high.astype(jnp.float32)).astype(jnp.bfloat16)


def selection(table, metas, place, length):
    even, even_far = lax.rem(place, 2) == 0, lax.rem(place // FAR, 2) == 0
    near, far_odd, far_even, across = metas
    moved = (place == 2) | (place == length - 3)
    across = jnp.where(moved, far_odd, across)
    circle = jnp.where(moved, 16.0, 32.0)
    slots = [
        (place >= 1, jnp.where(even, circle, 8.0), jnp.where(even, across, near)),
        (place < length - 1, jnp.where(even, 8.0, circle), jnp.where(even, near, across)),
        (place >= FAR, jnp.where(even_far, 16.0, 24.0), jnp.where(even_far, far_odd, far_even)),
        (place < length - FAR, jnp.where(even_far, 24.0, 16.0), jnp.where(even_far, far_even, far_odd)),
    ]
    lane = iota((1, 128), 1)
    target = lane.astype(jnp.float32)
    for link, (valid, base, order) in enumerate(slots):
        order = order + jnp.where(valid, base, DEAD)
        target = jnp.where(lane // 8 == link + 1, order, target)
    target = jnp.broadcast_to(target, (8, 128))
    index = table.astype(jnp.int32)
    at = [jnp.take_along_axis(target, index[8 * k : 8 * k + 8], axis=1) for k in range(3)]
    return jnp.concatenate(at, axis=0).astype(jnp.int32)


def product(choose, pieces, high, low):
    rows = 8 * COMPS
    front = iota((8, 128), 1) < BLOCK
    picked = [[pieces[0][8 * c : 8 * c + 8] for c in range(COMPS)]]
    for k in range(3):
        code = choose[8 * k : 8 * k + 8]
        index, place = code & 7, code >> 3
        blocks = []
        for c in range(COMPS):
            block = jnp.zeros((8, 128), jnp.float32)
            for p, piece in enumerate(pieces):
                found = jnp.take_along_axis(piece[8 * c : 8 * c + 8], index, axis=0)
                block = jnp.where(place == p, found, block)
            blocks.append(block)
        picked.append(blocks)
    x = [
        jnp.concatenate(
            [jnp.where(front, picked[2 * t][c], picked[2 * t + 1][c]) for t in range(2)], axis=1
        )
        for c in range(COMPS)
    ]
    x = jnp.concatenate(x, axis=0)
    top = x.astype(jnp.bfloat16).astype(jnp.float32)
    left = jnp.concatenate([top, x - top], axis=0).astype(jnp.bfloat16)
    both = dot(left, high) + dot(left, low)
    image = both[:rows] + both[rows:]
    return jnp.where(own_lanes(rows, image.shape[1]), image, 0.0)


def multiply(choose, pieces, shift, high, low):
    image = fold(product(choose, pieces, high, low))
    return image - jnp.concatenate([shift] * COMPS, axis=0) * pieces[0]


def first_kernel(length, own, a, c, d, b, aux, high, low, tile_ref, choose_ref):
    rows = 8 * COMPS
    refs = (own, a, b, c, d)
    pieces = [ref[:rows, :] for ref in refs]
    metas = [ref[rows : rows + 1, :] for ref in refs[1:]]
    choose = selection(aux[8 * S :, :], metas, lax.axis_index("dom"), length)
    choose_ref[...] = choose
    tile_ref[...] = multiply(choose, pieces, aux[:8, :], high[...], low[...])


def middle_kernel(step, own, a, b, c, d, choose, aux, high, low, tile_ref):
    pieces = [ref[...] for ref in (own, a, b, c, d)]
    tile_ref[...] = multiply(choose[...], pieces, aux[8 * step : 8 * step + 8, :], high[...], low[...])


def collect(gram, width, vecs):
    lane, comp = iota(gram.shape, 1), iota(gram.shape, 0)
    mine = jnp.where(lane < width, lane // vecs, lane % 8) == comp
    return jnp.sum(jnp.where(mine, gram, 0.0), axis=0, keepdims=True)


def early_kernel(prev_ref, t0, t1, t2, lines_ref, gram_ref, *split_refs):
    comps, vecs, rows = prev_ref.shape
    width = comps * vecs
    lines = jnp.concatenate([lines_of(t[...], rows) for t in (t0, t1, t2)], axis=0)
    lines_ref[...] = lines
    prev = prev_ref[...].reshape(width, rows)
    full = dot(prev, prev, NT, HIGHEST)
    full = jnp.concatenate([full, jnp.zeros((width, 128 - width), jnp.float32)], axis=1)
    lane = iota((8, 128), 1)
    tiles = [jnp.zeros((8, 128), jnp.float32)] * 2
    for (c, g), (t, first) in PLACES.items():
        at = c * vecs + 8 * g
        piece = pltpu.roll(full[at : at + 8], (first - at) % 128, 1)
        tiles[t] = jnp.where((lane >= first) & (lane < first + vecs - 8 * g), piece, tiles[t])
    gram_ref[:16, :] = jnp.concatenate(tiles, axis=0)
    against = jnp.concatenate([prev, lines, jnp.zeros((8, rows), jnp.float32)], axis=0)
    for ref, part in zip(split_refs, split(against.T)):
        ref[...] = part
    gram = dot(lines, against, NT, HIGHEST)
    result = jnp.zeros((8, 128), jnp.float32)
    for k in range(S - 1):
        line = collect(gram[k * 8 : (k + 1) * 8], width, vecs)
        result = jnp.where(iota((8, 128), 0) == k, jnp.broadcast_to(line, result.shape), result)
    gram_ref[16:, :] = result


def last_kernel(
    vecs, own, a, b, c, d, choose, aux, high, low, early, t0, t1, t2, lines, line_ref, gram_ref
):
    pieces = [ref[...] for ref in (own, a, b, c, d)]
    image = joined(product(choose[...], pieces, high[...], low[...]))
    width = COMPS * vecs
    shift = aux[8 * S - 8 : 8 * S, :1]
    last = image - shift * lines[8 * S - 16 :, :]
    line_ref[...] = last
    gram = split_dot(last, (t0[...], t1[...], t2[...]))
    square = jnp.sum(last * last, axis=1, keepdims=True)
    gram = jnp.where(iota(gram.shape, 1) == width + 8 * (S - 1) + iota(gram.shape, 0), square, gram)
    line = collect(gram, width, vecs)
    gram_ref[:16, :] = early[:16, :]
    gram_ref[16:, :] = jnp.where(
        iota((8, 128), 0) == S - 1, jnp.broadcast_to(line, (8, 128)), early[16:, :]
    )


def finish_kernel(total, gram_ins, prev_ref, lines, last, basis_ref, factors_ref):
    comps, vecs, rows = prev_ref.shape
    width = comps * vecs
    gram = added([ref[...] for ref in gram_ins]) * (1.0 / total)
    small = gram[16:]
    lane, comp = iota((8, 128), 1), iota((8, 128), 0)
    in_prev = (lane < width) & (lane // vecs == comp)
    coef, cross = [], []
    for k in range(S):
        line = jnp.broadcast_to(small[k : k + 1], (8, 128))
        coef.append(jnp.where(in_prev, line, 0.0))
        cross.append([jnp.where(lane == width + 8 * l + comp, line, 0.0) for l in range(k + 1)])
    coefs = jnp.concatenate(coef, axis=0)
    pieces, turns = [], {}
    for c in range(comps):
        for g in range(vecs // 8):
            t, first = PLACES[c, g]
            at = c * vecs + 8 * g
            turn = t, (at - first) % 128
            if turn not in turns:
                piece = gram[8 * t : 8 * t + 8]
                turns[turn] = pltpu.roll(piece, turn[1], 1) if turn[1] else piece
            piece = turns[turn]
            piece = jnp.where(lane < at + 8, 0.5 * piece, piece)
            piece = jnp.where((lane >= at) & (lane < (c + 1) * vecs), piece, 0.0)
            pieces.append(piece - jnp.where(lane == at + comp, 1.0, 0.0))
    half = jnp.concatenate(pieces, axis=0)
    turned = dot(coefs[:, :width], half, precision=HIGHEST)
    prev = prev_ref[...].reshape(width, rows)
    basis = jnp.concatenate([lines[...], last[...]], axis=0)
    projected = basis - dot(coefs[:, :width], prev, precision=HIGHEST)
    unit, scale = {}, {}
    for l in range(S):
        for k in range(l, S):
            value = turned[k * 8 : (k + 1) * 8] * coef[l] + turned[l * 8 : (l + 1) * 8] * coef[k] + cross[k][l]
            value = jnp.sum(value, axis=1, keepdims=True)
            for m in range(l):
                value = value - (unit[k, m] * scale[m]) * unit[l, m]
            if k == l:
                scale[l] = value
            else:
                unit[k, l] = value / scale[l]
    roots = [jnp.sqrt(scale[k]) for k in range(S)]
    lower = {(k, l): unit[k, l] * roots[l] if l < k else roots[k] for k in range(S) for l in range(k + 1)}
    vectors = []
    for k in range(S):
        value = projected[k * 8 : (k + 1) * 8]
        for l in range(k):
            value = value - unit[k, l] * vectors[l]
        vectors.append(value)
        value = value * (1.0 / roots[k])
        for c in range(comps):
            basis_ref[c, k : k + 1, :] = value[c : c + 1]
    for c in range(comps):
        factors_ref[c, :, :vecs] = small[:S, c * vecs : (c + 1) * vecs]
    for k in range(S):
        line = jnp.zeros((8, 128), jnp.float32)
        for l in range(k + 1):
            line = jnp.where(lane == vecs + l, lower[k, l], line)
        for c in range(comps):
            factors_ref[c, k : k + 1, vecs:] = line[c : c + 1, vecs : vecs + S]


VMEM = pl.BlockSpec(memory_space=pltpu.VMEM)
HBM = pl.BlockSpec(memory_space=pltpu.HBM)


def in_hbm(*arrays):
    return [pltpu.with_memory_space_constraint(x, pltpu.HBM) for x in arrays]


def call(kernel, outs, specs, flops, moved, scratch=()):
    shapes = [jax.ShapeDtypeStruct(shape, kind) for shape, kind in outs]
    return pl.pallas_call(
        kernel,
        out_shape=shapes if len(shapes) > 1 else shapes[0],
        in_specs=specs,
        out_specs=[VMEM] * len(shapes) if len(shapes) > 1 else VMEM,
        scratch_shapes=list(scratch),
        compiler_params=pltpu.CompilerParams(vmem_limit_bytes=24 * 1024 * 1024),
        cost_estimate=pl.CostEstimate(flops=flops, bytes_accessed=moved, transcendentals=0),
    )


def send(value, target):
    return lax.ppermute(value, "dom", [(d, target[d]) for d in range(lax.axis_size("dom"))])


def neighbours(length, step, odd):
    target = {}
    for d in range(length):
        other = d + step if (d // step) % 2 == odd else d - step
        target[d] = other if 0 <= other < length else None
    return target


def ghosts(tile):
    length = lax.axis_size("dom")
    last = length - 1
    near, across = neighbours(length, 1, 0), neighbours(length, 1, 1)
    far_even, far_odd = neighbours(length, FAR, 0), neighbours(length, FAR, 1)
    across.update({0: 2, 2: 1, 1: 0, last: last - 2, last - 2: last - 1, last - 1: last})
    for d in range(length):
        if far_odd[d] is None:
            far_odd[d] = d ^ 1
    far_odd.update({1: 2, 2: 3, 3: 0, 0: 1})
    far_odd.update({last - 1: last - 2, last - 2: last - 3, last - 3: last, last: last - 1})
    return [send(tile, target) for target in (near, far_odd, far_even, across)]


def summed(value):
    length = lax.axis_size("dom")

    def fetched(step):
        return send(value, {d: d ^ (step | 1) for d in range(length)})

    parts = [value, fetched(1)]
    step = 2
    while step < length:
        value = added(parts)
        steps = (3 * step, step, 2 * step) if 2 * step < length else (step,)
        got = [fetched(s) for s in steps]
        parts = [value] + got[1:] + got[:1]
        step *= 4
    return parts


def added(parts):
    if len(parts) == 2:
        return parts[0] + parts[1]
    return (parts[0] + parts[1]) + (parts[2] + parts[3])


def local(strips, columns, send_list, send_count, shifts, prev_basis, mix):
    comps, vecs, rows = prev_basis.shape
    blocks = columns.shape[0]
    width = strips.shape[1]
    f32, bf16, dma = jnp.float32, jnp.bfloat16, pltpu.SemaphoreType.DMA
    tile_out = ((comps * blocks, 128), f32)
    tile = call(
        start_kernel,
        [((comps * blocks + 8, 128), f32)],
        [HBM] * 4,
        600000,
        250000,
        [
            pltpu.VMEM(prev_basis.shape, f32),
            pltpu.VMEM(mix.shape, f32),
            pltpu.VMEM(send_list.shape, jnp.int32),
            pltpu.VMEM(send_count.shape, jnp.int32),
            dma((5,)),
        ],
    )(*in_hbm(prev_basis, mix, send_list, send_count))
    high, low, aux = call(
        prepare_kernel,
        [((width, rows), bf16), ((width, rows), bf16), ((8 * S + 24, 128), f32)],
        [HBM] * 3,
        1000000,
        1000000,
        [
            pltpu.VMEM((rows, width), f32),
            pltpu.VMEM(columns.shape[::-1], jnp.int32),
            pltpu.SMEM(shifts.shape, f32),
            dma((4,)),
        ],
    )(*in_hbm(strips, columns.T, shifts))
    tiles = []
    length = lax.axis_size("dom")
    near, far_odd, far_even, across = ghosts(tile)
    tile, choose = call(
        lambda *refs: first_kernel(length, *refs),
        [tile_out, ((3 * blocks, 128), jnp.int32)],
        [VMEM] * 8,
        50000000,
        600000,
    )(tile, near, far_even, across, far_odd, aux, high, low)
    tiles.append(tile)
    for step in (1, 2):
        tile = call(
            lambda *refs, step=step: middle_kernel(step, *refs), [tile_out], [VMEM] * 9, 50000000, 600000
        )(tile, *ghosts(tile), choose, aux, high, low)
        tiles.append(tile)
    received = ghosts(tile)
    gram_out = ((24, 128), f32)
    lines, early, *parts = call(
        early_kernel,
        [((8 * S - 8, rows), f32), gram_out] + [((rows, 128), bf16)] * 3,
        [VMEM] * 4,
        60000000,
        250000,
    )(prev_basis, *tiles)
    last, gram = call(
        lambda *refs: last_kernel(vecs, *refs),
        [((8, rows), f32), gram_out],
        [VMEM] * 14,
        80000000,
        900000,
    )(tile, *received, choose, aux, high, low, early, *parts, lines)
    total = float(length * rows)
    parts = summed(gram)
    count = len(parts)
    basis, factors = call(
        lambda *refs: finish_kernel(total, refs[:count], *refs[count:]),
        [((comps, S, rows), f32), ((comps, S, vecs + S), f32)],
        [VMEM] * (count + 3),
        50000000,
        400000,
    )(*parts, prev_basis, lines, last)
    return basis, jnp.swapaxes(factors, 1, 2)


def solution(mesh):
    in_specs = (
        P("dom", None),
        P("dom", None),
        P("dom", None, None),
        P("dom", None),
        P(),
        P(None, None, "dom"),
        P(),
    )
    out_specs = (P(None, None, "dom"), P())
    return jax.shard_map(local, mesh=mesh, in_specs=in_specs, out_specs=out_specs, check_vma=False)
```

```python
import jax
import jax.numpy as jnp
from jax import lax
from jax.experimental import pallas as pl
from jax.experimental.pallas import tpu as pltpu
from jax.sharding import PartitionSpec as P

BLOCK = 64
S = 4
FAR = 8
COMPS = 3
DEAD = 1000.0
HIGHEST = lax.Precision.HIGHEST
NN = (((1,), (0,)), ((), ()))
NT = (((1,), (1,)), ((), ()))


def dot(a, b, dims=NN, precision=None):
    return lax.dot_general(a, b, dims, precision=precision, preferred_element_type=jnp.float32)


def iota(shape, axis):
    return lax.broadcasted_iota(jnp.int32, shape, axis)


PLACES = {(c, g): (g % 2, (0, 8, 0, 0)[g] + 32 * c) for c in range(COMPS) for g in range(4)}
PLACES.update({(0, 2): (0, 96), (1, 2): (0, 112), (2, 2): (1, 96)})


def own_lanes(rows, width):
    return iota((rows, width), 1) // BLOCK == iota((rows, width), 0) % 8


def fold(masked):
    total = masked[:, :128]
    for t in range(1, masked.shape[1] // 128):
        total = total + masked[:, t * 128 : (t + 1) * 128]
    return total + pltpu.roll(total, BLOCK, 1)


def lines_of(tile, width):
    wide = jnp.concatenate([tile] * (width // 128), axis=1)
    return joined(jnp.where(own_lanes(wide.shape[0], width), wide, 0.0))


def joined(wide):
    width = wide.shape[1]
    where = iota((8, width), 0)
    result = jnp.zeros((8, width), jnp.float32)
    for c in range(COMPS):
        line = jnp.sum(wide[c * 8 : (c + 1) * 8], axis=0, keepdims=True)
        result = jnp.where(where == c, jnp.broadcast_to(line, result.shape), result)
    return result


def split(x):
    parts = []
    for _ in range(3):
        parts.append(x.astype(jnp.bfloat16))
        x = x - parts[-1].astype(jnp.float32)
    return parts


def split_dot(x, parts):
    left = [part.astype(jnp.float32) for part in split(x)]
    left.append(jnp.zeros((-3 * x.shape[0] % 16, x.shape[1]), jnp.float32))
    left = jnp.concatenate([part for part in left if part.shape[0]], axis=0).astype(jnp.bfloat16)
    products = dot(left, parts[0]) + dot(left, parts[1]) + dot(left, parts[2])
    rows = x.shape[0]
    return products[:rows] + (products[rows : 2 * rows] + products[2 * rows : 3 * rows])


def fetch(pairs, sems):
    copies = [pltpu.make_async_copy(src, dst, sems.at[i]) for i, (src, dst) in enumerate(pairs)]
    for copy in copies:
        copy.start()
    return copies


def start_kernel(prev_in, mix_in, list_in, count_in, out_ref, prev_ref, mix_ref, list_ref, count_ref, sems):
    copies = fetch(
        [(prev_in, prev_ref), (mix_in, mix_ref), (list_in, list_ref), (count_in, count_ref)], sems
    )
    for copy in copies[1:]:
        copy.wait()
    comps, vecs, rows = prev_ref.shape
    eye = iota((vecs, vecs), 0) == iota((vecs, vecs), 1)
    weights = []
    for c in range(comps):
        line = jnp.broadcast_to(mix_ref[c : c + 1, :], eye.shape)
        weights.append(jnp.sum(jnp.where(eye, line, 0.0), axis=1, keepdims=True))
    order = list_ref[0].astype(jnp.float32)
    order = jnp.concatenate([order, jnp.zeros((4, 120), jnp.float32)], axis=1)
    meta = jnp.zeros((8, 128), jnp.float32)
    slot = iota((1, 128), 1)
    for link in range(4):
        live = slot < jnp.broadcast_to(count_ref[0:1, link : link + 1], slot.shape)
        line = jnp.where(live, order[link : link + 1], DEAD)
        line = pltpu.roll(jnp.broadcast_to(line, (8, 128)), 8 + 8 * link, 1)
        meta = jnp.where(iota((8, 128), 1) // 8 == link + 1, line, meta)
    out_ref[8 * comps :, :] = meta
    copies[0].wait()
    own = own_lanes(8, rows)
    for c in range(comps):
        start = jnp.sum(weights[c] * prev_ref[c], axis=0, keepdims=True)
        line = jnp.broadcast_to(start, own.shape)
        out_ref[c * 8 : (c + 1) * 8, :] = fold(jnp.where(own, line, 0.0))


def prepare_kernel(strips_in, columns_in, shifts_in, high_ref, low_ref, aux_ref, strips, columns, shifts, sems):
    rows = strips.shape[0]
    cuts = [(0, rows * 3 // 4), (rows * 3 // 4, rows)]
    pairs = [(strips_in.at[pl.ds(a, b - a)], strips.at[pl.ds(a, b - a)]) for a, b in cuts]
    copies = fetch(pairs + [(columns_in, columns), (shifts_in, shifts)], sems)
    copies[2].wait()
    copies[3].wait()
    eye = iota((8, 8), 0) == iota((8, 8), 1)
    for k in range(1, columns.shape[0]):
        line = jnp.broadcast_to(columns[k : k + 1, :].astype(jnp.float32), (8, 8))
        column = jnp.sum(jnp.where(eye, line, 0.0), axis=1, keepdims=True)
        at = 8 * S + 8 * (k - 1)
        aux_ref[at : at + 8, :] = jnp.broadcast_to(column, (8, 128))
    for k in range(S):
        aux_ref[8 * k : 8 * k + 8, :] = jnp.full((8, 128), shifts[k], jnp.float32)
    for copy, (a, b) in zip(copies, cuts):
        copy.wait()
        turned = strips[a:b, :].T
        high = turned.astype(jnp.bfloat16)
        high_ref[:, a:b] = high
        low_ref[:, a:b] = (turned - high.astype(jnp.float32)).astype(jnp.bfloat16)


def selection(table, metas, place, length):
    even, even_far = lax.rem(place, 2) == 0, lax.rem(place // FAR, 2) == 0
    near, far_odd, far_even, across = metas
    moved = (place == 2) | (place == length - 3)
    across = jnp.where(moved, far_odd, across)
    circle = jnp.where(moved, 16.0, 32.0)
    slots = [
        (place >= 1, jnp.where(even, circle, 8.0), jnp.where(even, across, near)),
        (place < length - 1, jnp.where(even, 8.0, circle), jnp.where(even, near, across)),
        (place >= FAR, jnp.where(even_far, 16.0, 24.0), jnp.where(even_far, far_odd, far_even)),
        (place < length - FAR, jnp.where(even_far, 24.0, 16.0), jnp.where(even_far, far_even, far_odd)),
    ]
    lane = iota((1, 128), 1)
    target = lane.astype(jnp.float32)
    for link, (valid, base, order) in enumerate(slots):
        order = order + jnp.where(valid, base, DEAD)
        target = jnp.where(lane // 8 == link + 1, order, target)
    target = jnp.broadcast_to(target, (8, 128))
    index = table.astype(jnp.int32)
    at = [jnp.take_along_axis(target, index[8 * k : 8 * k + 8], axis=1) for k in range(3)]
    return jnp.concatenate(at, axis=0).astype(jnp.int32)


def product(choose, pieces, high, low):
    rows = 8 * COMPS
    front = iota((8, 128), 1) < BLOCK
    picked = [[pieces[0][8 * c : 8 * c + 8] for c in range(COMPS)]]
    for k in range(3):
        code = choose[8 * k : 8 * k + 8]
        index, place = code & 7, code >> 3
        blocks = []
        for c in range(COMPS):
            block = jnp.zeros((8, 128), jnp.float32)
            for p, piece in enumerate(pieces):
                found = jnp.take_along_axis(piece[8 * c : 8 * c + 8], index, axis=0)
                block = jnp.where(place == p, found, block)
            blocks.append(block)
        picked.append(blocks)
    x = [
        jnp.concatenate(
            [jnp.where(front, picked[2 * t][c], picked[2 * t + 1][c]) for t in range(2)], axis=1
        )
        for c in range(COMPS)
    ]
    x = jnp.concatenate(x, axis=0)
    top = x.astype(jnp.bfloat16).astype(jnp.float32)
    left = jnp.concatenate([top, x - top], axis=0).astype(jnp.bfloat16)
    both = dot(left, high) + dot(left, low)
    image = both[:rows] + both[rows:]
    return jnp.where(own_lanes(rows, image.shape[1]), image, 0.0)


def multiply(choose, pieces, shift, high, low):
    image = fold(product(choose, pieces, high, low))
    return image - jnp.concatenate([shift] * COMPS, axis=0) * pieces[0]


def first_kernel(length, own, a, c, d, b, aux, high, low, tile_ref, choose_ref):
    rows = 8 * COMPS
    refs = (own, a, b, c, d)
    pieces = [ref[:rows, :] for ref in refs]
    metas = [ref[rows : rows + 1, :] for ref in refs[1:]]
    choose = selection(aux[8 * S :, :], metas, lax.axis_index("dom"), length)
    choose_ref[...] = choose
    tile_ref[...] = multiply(choose, pieces, aux[:8, :], high[...], low[...])


def middle_kernel(step, own, a, b, c, d, choose, aux, high, low, tile_ref):
    pieces = [ref[...] for ref in (own, a, b, c, d)]
    tile_ref[...] = multiply(choose[...], pieces, aux[8 * step : 8 * step + 8, :], high[...], low[...])


def collect(gram, width, vecs):
    lane, comp = iota(gram.shape, 1), iota(gram.shape, 0)
    mine = jnp.where(lane < width, lane // vecs, lane % 8) == comp
    return jnp.sum(jnp.where(mine, gram, 0.0), axis=0, keepdims=True)


def early_kernel(prev_ref, t0, t1, t2, lines_ref, gram_ref, *split_refs):
    comps, vecs, rows = prev_ref.shape
    width = comps * vecs
    lines = jnp.concatenate([lines_of(t[...], rows) for t in (t0, t1, t2)], axis=0)
    lines_ref[...] = lines
    prev = prev_ref[...].reshape(width, rows)
    full = dot(prev, prev, NT, HIGHEST)
    full = jnp.concatenate([full, jnp.zeros((width, 128 - width), jnp.float32)], axis=1)
    lane = iota((8, 128), 1)
    tiles = [jnp.zeros((8, 128), jnp.float32)] * 2
    for (c, g), (t, first) in PLACES.items():
        at = c * vecs + 8 * g
        piece = pltpu.roll(full[at : at + 8], (first - at) % 128, 1)
        tiles[t] = jnp.where((lane >= first) & (lane < first + vecs - 8 * g), piece, tiles[t])
    gram_ref[:16, :] = jnp.concatenate(tiles, axis=0)
    against = jnp.concatenate([prev, lines, jnp.zeros((8, rows), jnp.float32)], axis=0)
    for ref, part in zip(split_refs, split(against.T)):
        ref[...] = part
    gram = dot(lines, against, NT, HIGHEST)
    result = jnp.zeros((8, 128), jnp.float32)
    for k in range(S - 1):
        line = collect(gram[k * 8 : (k + 1) * 8], width, vecs)
        result = jnp.where(iota((8, 128), 0) == k, jnp.broadcast_to(line, result.shape), result)
    gram_ref[16:, :] = result


def last_kernel(
    vecs, own, a, b, c, d, choose, aux, high, low, early, t0, t1, t2, lines, line_ref, gram_ref
):
    pieces = [ref[...] for ref in (own, a, b, c, d)]
    image = joined(product(choose[...], pieces, high[...], low[...]))
    width = COMPS * vecs
    shift = aux[8 * S - 8 : 8 * S, :1]
    last = image - shift * lines[8 * S - 16 :, :]
    line_ref[...] = last
    gram = split_dot(last, (t0[...], t1[...], t2[...]))
    square = jnp.sum(last * last, axis=1, keepdims=True)
    gram = jnp.where(iota(gram.shape, 1) == width + 8 * (S - 1) + iota(gram.shape, 0), square, gram)
    line = collect(gram, width, vecs)
    gram_ref[:16, :] = early[:16, :]
    gram_ref[16:, :] = jnp.where(
        iota((8, 128), 0) == S - 1, jnp.broadcast_to(line, (8, 128)), early[16:, :]
    )


def finish_kernel(total, gram_ins, prev_ref, lines, last, basis_ref, factors_ref):
    comps, vecs, rows = prev_ref.shape
    width = comps * vecs
    gram = added([ref[...] for ref in gram_ins]) * (1.0 / total)
    small = gram[16:]
    lane, comp = iota((8, 128), 1), iota((8, 128), 0)
    in_prev = (lane < width) & (lane // vecs == comp)
    coef, cross = [], []
    for k in range(S):
        line = jnp.broadcast_to(small[k : k + 1], (8, 128))
        coef.append(jnp.where(in_prev, line, 0.0))
        cross.append([jnp.where(lane == width + 8 * l + comp, line, 0.0) for l in range(k + 1)])
    coefs = jnp.concatenate(coef, axis=0)
    pieces, turns = [], {}
    for c in range(comps):
        for g in range(vecs // 8):
            t, first = PLACES[c, g]
            at = c * vecs + 8 * g
            turn = t, (at - first) % 128
            if turn not in turns:
                piece = gram[8 * t : 8 * t + 8]
                turns[turn] = pltpu.roll(piece, turn[1], 1) if turn[1] else piece
            piece = turns[turn]
            piece = jnp.where(lane < at + 8, 0.5 * piece, piece)
            piece = jnp.where((lane >= at) & (lane < (c + 1) * vecs), piece, 0.0)
            pieces.append(piece - jnp.where(lane == at + comp, 1.0, 0.0))
    half = jnp.concatenate(pieces, axis=0)
    turned = dot(coefs[:, :width], half, precision=HIGHEST)
    prev = prev_ref[...].reshape(width, rows)
    basis = jnp.concatenate([lines[...], last[...]], axis=0)
    projected = basis - dot(coefs[:, :width], prev, precision=HIGHEST)
    unit, scale = {}, {}
    for l in range(S):
        for k in range(l, S):
            value = turned[k * 8 : (k + 1) * 8] * coef[l] + turned[l * 8 : (l + 1) * 8] * coef[k] + cross[k][l]
            value = jnp.sum(value, axis=1, keepdims=True)
            for m in range(l):
                value = value - (unit[k, m] * scale[m]) * unit[l, m]
            if k == l:
                scale[l] = value
            else:
                unit[k, l] = value / scale[l]
    roots = [jnp.sqrt(scale[k]) for k in range(S)]
    lower = {(k, l): unit[k, l] * roots[l] if l < k else roots[k] for k in range(S) for l in range(k + 1)}
    vectors, results = [], []
    for k in range(S):
        value = projected[k * 8 : (k + 1) * 8]
        for l in range(k):
            value = value - unit[k, l] * vectors[l]
        vectors.append(value)
        results.append(value * (1.0 / roots[k]))
    for c in range(comps):
        basis_ref[c] = jnp.concatenate([value[c : c + 1] for value in results], axis=0)
    for c in range(comps):
        factors_ref[c, :, :vecs] = small[:S, c * vecs : (c + 1) * vecs]
    for k in range(S):
        line = jnp.zeros((8, 128), jnp.float32)
        for l in range(k + 1):
            line = jnp.where(lane == vecs + l, lower[k, l], line)
        for c in range(comps):
            factors_ref[c, k : k + 1, vecs:] = line[c : c + 1, vecs : vecs + S]


VMEM = pl.BlockSpec(memory_space=pltpu.VMEM)
HBM = pl.BlockSpec(memory_space=pltpu.HBM)


def in_hbm(*arrays):
    return [pltpu.with_memory_space_constraint(x, pltpu.HBM) for x in arrays]


def call(kernel, outs, specs, flops, moved, scratch=()):
    shapes = [jax.ShapeDtypeStruct(shape, kind) for shape, kind in outs]
    return pl.pallas_call(
        kernel,
        out_shape=shapes if len(shapes) > 1 else shapes[0],
        in_specs=specs,
        out_specs=[VMEM] * len(shapes) if len(shapes) > 1 else VMEM,
        scratch_shapes=list(scratch),
        compiler_params=pltpu.CompilerParams(vmem_limit_bytes=24 * 1024 * 1024),
        cost_estimate=pl.CostEstimate(flops=flops, bytes_accessed=moved, transcendentals=0),
    )


def send(value, target):
    return lax.ppermute(value, "dom", [(d, target[d]) for d in range(lax.axis_size("dom"))])


def neighbours(length, step, odd):
    target = {}
    for d in range(length):
        other = d + step if (d // step) % 2 == odd else d - step
        target[d] = other if 0 <= other < length else None
    return target


def ghosts(tile):
    length = lax.axis_size("dom")
    last = length - 1
    near, across = neighbours(length, 1, 0), neighbours(length, 1, 1)
    far_even, far_odd = neighbours(length, FAR, 0), neighbours(length, FAR, 1)
    across.update({0: 2, 2: 1, 1: 0, last: last - 2, last - 2: last - 1, last - 1: last})
    for d in range(length):
        if far_odd[d] is None:
            far_odd[d] = d ^ 1
    far_odd.update({1: 2, 2: 3, 3: 0, 0: 1})
    far_odd.update({last - 1: last - 2, last - 2: last - 3, last - 3: last, last: last - 1})
    return [send(tile, target) for target in (near, far_odd, far_even, across)]


def summed(value):
    length = lax.axis_size("dom")

    def fetched(step):
        return send(value, {d: d ^ (step | 1) for d in range(length)})

    parts = [value, fetched(1)]
    step = 2
    while step < length:
        value = added(parts)
        steps = (3 * step, step, 2 * step) if 2 * step < length else (step,)
        got = [fetched(s) for s in steps]
        parts = [value] + got[1:] + got[:1]
        step *= 4
    return parts


def added(parts):
    if len(parts) == 2:
        return parts[0] + parts[1]
    return (parts[0] + parts[1]) + (parts[2] + parts[3])


def local(strips, columns, send_list, send_count, shifts, prev_basis, mix):
    comps, vecs, rows = prev_basis.shape
    blocks = columns.shape[0]
    width = strips.shape[1]
    f32, bf16, dma = jnp.float32, jnp.bfloat16, pltpu.SemaphoreType.DMA
    tile_out = ((comps * blocks, 128), f32)
    tile = call(
        start_kernel,
        [((comps * blocks + 8, 128), f32)],
        [HBM] * 4,
        600000,
        250000,
        [
            pltpu.VMEM(prev_basis.shape, f32),
            pltpu.VMEM(mix.shape, f32),
            pltpu.VMEM(send_list.shape, jnp.int32),
            pltpu.VMEM(send_count.shape, jnp.int32),
            dma((4,)),
        ],
    )(*in_hbm(prev_basis, mix, send_list, send_count))
    high, low, aux = call(
        prepare_kernel,
        [((width, rows), bf16), ((width, rows), bf16), ((8 * S + 24, 128), f32)],
        [HBM] * 3,
        1000000,
        1000000,
        [
            pltpu.VMEM((rows, width), f32),
            pltpu.VMEM(columns.shape[::-1], jnp.int32),
            pltpu.SMEM(shifts.shape, f32),
            dma((4,)),
        ],
    )(*in_hbm(strips, columns.T, shifts))
    tiles = []
    length = lax.axis_size("dom")
    near, far_odd, far_even, across = ghosts(tile)
    tile, choose = call(
        lambda *refs: first_kernel(length, *refs),
        [tile_out, ((3 * blocks, 128), jnp.int32)],
        [VMEM] * 8,
        50000000,
        600000,
    )(tile, near, far_even, across, far_odd, aux, high, low)
    tiles.append(tile)
    for step in (1, 2):
        tile = call(
            lambda *refs, step=step: middle_kernel(step, *refs), [tile_out], [VMEM] * 9, 50000000, 600000
        )(tile, *ghosts(tile), choose, aux, high, low)
        tiles.append(tile)
    received = ghosts(tile)
    gram_out = ((24, 128), f32)
    lines, early, *parts = call(
        early_kernel,
        [((8 * S - 8, rows), f32), gram_out] + [((rows, 128), bf16)] * 3,
        [VMEM] * 4,
        60000000,
        250000,
    )(prev_basis, *tiles)
    last, gram = call(
        lambda *refs: last_kernel(vecs, *refs),
        [((8, rows), f32), gram_out],
        [VMEM] * 14,
        80000000,
        900000,
    )(tile, *received, choose, aux, high, low, early, *parts, lines)
    total = float(length * rows)
    parts = summed(gram)
    count = len(parts)
    basis, factors = call(
        lambda *refs: finish_kernel(total, refs[:count], *refs[count:]),
        [((comps, S, rows), f32), ((comps, S, vecs + S), f32)],
        [VMEM] * (count + 3),
        50000000,
        400000,
    )(*parts, prev_basis, lines, last)
    return basis, jnp.swapaxes(factors, 1, 2)


def solution(mesh):
    in_specs = (
        P("dom", None),
        P("dom", None),
        P("dom", None, None),
        P("dom", None),
        P(),
        P(None, None, "dom"),
        P(),
    )
    out_specs = (P(None, None, "dom"), P())
    return jax.shard_map(local, mesh=mesh, in_specs=in_specs, out_specs=out_specs, check_vma=False)
```

```python
import jax
import jax.numpy as jnp
from jax import lax
from jax.experimental import pallas as pl
from jax.experimental.pallas import tpu as pltpu
from jax.sharding import PartitionSpec as P

BLOCK = 64
S = 4
FAR = 8
COMPS = 3
DEAD = 1000.0
HIGHEST = lax.Precision.HIGHEST
NN = (((1,), (0,)), ((), ()))
NT = (((1,), (1,)), ((), ()))


def dot(a, b, dims=NN, precision=None):
    return lax.dot_general(a, b, dims, precision=precision, preferred_element_type=jnp.float32)


def iota(shape, axis):
    return lax.broadcasted_iota(jnp.int32, shape, axis)


PLACES = {(c, g): (g % 2, (0, 8, 0, 0)[g] + 32 * c) for c in range(COMPS) for g in range(4)}
PLACES.update({(0, 2): (0, 96), (1, 2): (0, 112), (2, 2): (1, 96)})


def own_lanes(rows, width):
    return iota((rows, width), 1) // BLOCK == iota((rows, width), 0) % 8


def fold(masked):
    total = masked[:, :128]
    for t in range(1, masked.shape[1] // 128):
        total = total + masked[:, t * 128 : (t + 1) * 128]
    return total + pltpu.roll(total, BLOCK, 1)


def lines_of(tile, width):
    wide = jnp.concatenate([tile] * (width // 128), axis=1)
    return joined(jnp.where(own_lanes(wide.shape[0], width), wide, 0.0))


def joined(wide):
    width = wide.shape[1]
    where = iota((8, width), 0)
    result = jnp.zeros((8, width), jnp.float32)
    for c in range(COMPS):
        line = jnp.sum(wide[c * 8 : (c + 1) * 8], axis=0, keepdims=True)
        result = jnp.where(where == c, jnp.broadcast_to(line, result.shape), result)
    return result


def split(x):
    parts = []
    for _ in range(3):
        parts.append(x.astype(jnp.bfloat16))
        x = x - parts[-1].astype(jnp.float32)
    return parts


def split_dot(x, parts):
    left = [part.astype(jnp.float32) for part in split(x)]
    left = jnp.concatenate(left, axis=0).astype(jnp.bfloat16)
    products = dot(left, parts[0]) + dot(left, parts[1]) + dot(left, parts[2])
    rows = x.shape[0]
    return products[:rows] + (products[rows : 2 * rows] + products[2 * rows : 3 * rows])


def fetch(pairs, sems):
    copies = [pltpu.make_async_copy(src, dst, sems.at[i]) for i, (src, dst) in enumerate(pairs)]
    for copy in copies:
        copy.start()
    return copies


def start_kernel(prev_in, mix_in, list_in, count_in, out_ref, prev_ref, mix_ref, list_ref, count_ref, sems):
    copies = fetch(
        [(prev_in, prev_ref), (mix_in, mix_ref), (list_in, list_ref), (count_in, count_ref)], sems
    )
    for copy in copies[1:]:
        copy.wait()
    comps, vecs, rows = prev_ref.shape
    eye = iota((vecs, vecs), 0) == iota((vecs, vecs), 1)
    weights = []
    for c in range(comps):
        line = jnp.broadcast_to(mix_ref[c : c + 1, :], eye.shape)
        weights.append(jnp.sum(jnp.where(eye, line, 0.0), axis=1, keepdims=True))
    order = list_ref[0].astype(jnp.float32)
    order = jnp.concatenate([order, jnp.zeros((4, 120), jnp.float32)], axis=1)
    meta = jnp.zeros((8, 128), jnp.float32)
    slot = iota((1, 128), 1)
    for link in range(4):
        live = slot < jnp.broadcast_to(count_ref[0:1, link : link + 1], slot.shape)
        line = jnp.where(live, order[link : link + 1], DEAD)
        line = pltpu.roll(jnp.broadcast_to(line, (8, 128)), 8 + 8 * link, 1)
        meta = jnp.where(iota((8, 128), 1) // 8 == link + 1, line, meta)
    out_ref[8 * comps :, :] = meta
    copies[0].wait()
    own = own_lanes(8, rows)
    for c in range(comps):
        start = jnp.sum(weights[c] * prev_ref[c], axis=0, keepdims=True)
        line = jnp.broadcast_to(start, own.shape)
        out_ref[c * 8 : (c + 1) * 8, :] = fold(jnp.where(own, line, 0.0))


def prepare_kernel(strips_in, columns_in, shifts_in, high_ref, low_ref, aux_ref, strips, columns, shifts, sems):
    rows = strips.shape[0]
    cuts = [(0, rows * 3 // 4), (rows * 3 // 4, rows)]
    pairs = [(strips_in.at[pl.ds(a, b - a)], strips.at[pl.ds(a, b - a)]) for a, b in cuts]
    copies = fetch(pairs + [(columns_in, columns), (shifts_in, shifts)], sems)
    copies[2].wait()
    copies[3].wait()
    eye = iota((8, 8), 0) == iota((8, 8), 1)
    for k in range(1, columns.shape[0]):
        line = jnp.broadcast_to(columns[k : k + 1, :].astype(jnp.float32), (8, 8))
        column = jnp.sum(jnp.where(eye, line, 0.0), axis=1, keepdims=True)
        at = 8 * S + 8 * (k - 1)
        aux_ref[at : at + 8, :] = jnp.broadcast_to(column, (8, 128))
    for k in range(S):
        aux_ref[8 * k : 8 * k + 8, :] = jnp.full((8, 128), shifts[k], jnp.float32)
    for copy, (a, b) in zip(copies, cuts):
        copy.wait()
        turned = strips[a:b, :].T
        high = turned.astype(jnp.bfloat16)
        high_ref[:, a:b] = high
        low_ref[:, a:b] = (turned - high.astype(jnp.float32)).astype(jnp.bfloat16)


def selection(table, metas, place, length):
    even, even_far = lax.rem(place, 2) == 0, lax.rem(place // FAR, 2) == 0
    near, far_odd, far_even, across = metas
    moved = (place == 2) | (place == length - 3)
    across = jnp.where(moved, far_odd, across)
    circle = jnp.where(moved, 16.0, 32.0)
    slots = [
        (place >= 1, jnp.where(even, circle, 8.0), jnp.where(even, across, near)),
        (place < length - 1, jnp.where(even, 8.0, circle), jnp.where(even, near, across)),
        (place >= FAR, jnp.where(even_far, 16.0, 24.0), jnp.where(even_far, far_odd, far_even)),
        (place < length - FAR, jnp.where(even_far, 24.0, 16.0), jnp.where(even_far, far_even, far_odd)),
    ]
    lane = iota((1, 128), 1)
    target = lane.astype(jnp.float32)
    for link, (valid, base, order) in enumerate(slots):
        order = order + jnp.where(valid, base, DEAD)
        target = jnp.where(lane // 8 == link + 1, order, target)
    target = jnp.broadcast_to(target, (8, 128))
    index = table.astype(jnp.int32)
    at = [jnp.take_along_axis(target, index[8 * k : 8 * k + 8], axis=1) for k in range(3)]
    return jnp.concatenate(at, axis=0).astype(jnp.int32)


def product(choose, pieces, high, low):
    rows = 8 * COMPS
    front = iota((8, 128), 1) < BLOCK
    picked = [[pieces[0][8 * c : 8 * c + 8] for c in range(COMPS)]]
    for k in range(3):
        code = choose[8 * k : 8 * k + 8]
        index, place = code & 7, code >> 3
        blocks = []
        for c in range(COMPS):
            block = jnp.zeros((8, 128), jnp.float32)
            for p, piece in enumerate(pieces):
                found = jnp.take_along_axis(piece[8 * c : 8 * c + 8], index, axis=0)
                block = jnp.where(place == p, found, block)
            blocks.append(block)
        picked.append(blocks)
    x = [
        jnp.concatenate(
            [jnp.where(front, picked[2 * t][c], picked[2 * t + 1][c]) for t in range(2)], axis=1
        )
        for c in range(COMPS)
    ]
    x = jnp.concatenate(x, axis=0)
    top = x.astype(jnp.bfloat16).astype(jnp.float32)
    left = jnp.concatenate([top, x - top], axis=0).astype(jnp.bfloat16)
    both = dot(left, high) + dot(left, low)
    image = both[:rows] + both[rows:]
    return jnp.where(own_lanes(rows, image.shape[1]), image, 0.0)


def multiply(choose, pieces, shift, high, low):
    image = fold(product(choose, pieces, high, low))
    return image - jnp.concatenate([shift] * COMPS, axis=0) * pieces[0]


def first_kernel(length, own, a, c, d, b, aux, high, low, tile_ref, choose_ref):
    rows = 8 * COMPS
    refs = (own, a, b, c, d)
    pieces = [ref[:rows, :] for ref in refs]
    metas = [ref[rows : rows + 1, :] for ref in refs[1:]]
    choose = selection(aux[8 * S :, :], metas, lax.axis_index("dom"), length)
    choose_ref[...] = choose
    tile_ref[...] = multiply(choose, pieces, aux[:8, :], high[...], low[...])


def middle_kernel(step, own, a, b, c, d, choose, aux, high, low, tile_ref):
    pieces = [ref[...] for ref in (own, a, b, c, d)]
    tile_ref[...] = multiply(choose[...], pieces, aux[8 * step : 8 * step + 8, :], high[...], low[...])


def collect(gram, width, vecs):
    lane, comp = iota(gram.shape, 1), iota(gram.shape, 0)
    mine = jnp.where(lane < width, lane // vecs, lane % 8) == comp
    return jnp.sum(jnp.where(mine, gram, 0.0), axis=0, keepdims=True)


def early_kernel(prev_ref, t0, t1, t2, lines_ref, gram_ref, *split_refs):
    comps, vecs, rows = prev_ref.shape
    width = comps * vecs
    lines = jnp.concatenate([lines_of(t[...], rows) for t in (t0, t1, t2)], axis=0)
    lines_ref[...] = lines
    prev = prev_ref[...].reshape(width, rows)
    full = dot(prev, prev, NT, HIGHEST)
    full = jnp.concatenate([full, jnp.zeros((width, 128 - width), jnp.float32)], axis=1)
    lane = iota((8, 128), 1)
    tiles = [jnp.zeros((8, 128), jnp.float32)] * 2
    for (c, g), (t, first) in PLACES.items():
        at = c * vecs + 8 * g
        piece = pltpu.roll(full[at : at + 8], (first - at) % 128, 1)
        tiles[t] = jnp.where((lane >= first) & (lane < first + vecs - 8 * g), piece, tiles[t])
    gram_ref[:16, :] = jnp.concatenate(tiles, axis=0)
    against = jnp.concatenate([prev, lines, jnp.zeros((8, rows), jnp.float32)], axis=0)
    for ref, part in zip(split_refs, split(against.T)):
        ref[...] = part
    gram = dot(lines, against, NT, HIGHEST)
    result = jnp.zeros((8, 128), jnp.float32)
    for k in range(S - 1):
        line = collect(gram[k * 8 : (k + 1) * 8], width, vecs)
        result = jnp.where(iota((8, 128), 0) == k, jnp.broadcast_to(line, result.shape), result)
    gram_ref[16:, :] = result


def last_kernel(
    vecs, own, a, b, c, d, choose, aux, high, low, early, t0, t1, t2, lines, line_ref, gram_ref
):
    pieces = [ref[...] for ref in (own, a, b, c, d)]
    image = joined(product(choose[...], pieces, high[...], low[...]))
    width = COMPS * vecs
    shift = aux[8 * S - 8 : 8 * S, :1]
    last = image - shift * lines[8 * S - 16 :, :]
    line_ref[...] = last
    gram = split_dot(last, (t0[...], t1[...], t2[...]))
    square = jnp.sum(last * last, axis=1, keepdims=True)
    gram = jnp.where(iota(gram.shape, 1) == width + 8 * (S - 1) + iota(gram.shape, 0), square, gram)
    line = collect(gram, width, vecs)
    gram_ref[:16, :] = early[:16, :]
    gram_ref[16:, :] = jnp.where(
        iota((8, 128), 0) == S - 1, jnp.broadcast_to(line, (8, 128)), early[16:, :]
    )


def finish_kernel(total, gram_ins, prev_ref, lines, last, basis_ref, factors_ref):
    comps, vecs, rows = prev_ref.shape
    width = comps * vecs
    gram = added([ref[...] for ref in gram_ins]) * (1.0 / total)
    small = gram[16:]
    lane, comp = iota((8, 128), 1), iota((8, 128), 0)
    in_prev = (lane < width) & (lane // vecs == comp)
    coef, cross = [], []
    for k in range(S):
        line = jnp.broadcast_to(small[k : k + 1], (8, 128))
        coef.append(jnp.where(in_prev, line, 0.0))
        cross.append([jnp.where(lane == width + 8 * l + comp, line, 0.0) for l in range(k + 1)])
    coefs = jnp.concatenate(coef, axis=0)
    pieces, turns = [], {}
    for c in range(comps):
        for g in range(vecs // 8):
            t, first = PLACES[c, g]
            at = c * vecs + 8 * g
            turn = t, (at - first) % 128
            if turn not in turns:
                piece = gram[8 * t : 8 * t + 8]
                turns[turn] = pltpu.roll(piece, turn[1], 1) if turn[1] else piece
            piece = turns[turn]
            piece = jnp.where(lane < at + 8, 0.5 * piece, piece)
            piece = jnp.where((lane >= at) & (lane < (c + 1) * vecs), piece, 0.0)
            pieces.append(piece - jnp.where(lane == at + comp, 1.0, 0.0))
    half = jnp.concatenate(pieces, axis=0)
    turned = dot(coefs[:, :width], half, precision=HIGHEST)
    prev = prev_ref[...].reshape(width, rows)
    basis = jnp.concatenate([lines[...], last[...]], axis=0)
    projected = basis - dot(coefs[:, :width], prev, precision=HIGHEST)
    unit, scale = {}, {}
    for l in range(S):
        for k in range(l, S):
            value = turned[k * 8 : (k + 1) * 8] * coef[l] + turned[l * 8 : (l + 1) * 8] * coef[k] + cross[k][l]
            value = jnp.sum(value, axis=1, keepdims=True)
            for m in range(l):
                value = value - (unit[k, m] * scale[m]) * unit[l, m]
            if k == l:
                scale[l] = value
            else:
                unit[k, l] = value / scale[l]
    roots = [jnp.sqrt(scale[k]) for k in range(S)]
    lower = {(k, l): unit[k, l] * roots[l] if l < k else roots[k] for k in range(S) for l in range(k + 1)}
    vectors = []
    for k in range(S):
        value = projected[k * 8 : (k + 1) * 8]
        for l in range(k):
            value = value - unit[k, l] * vectors[l]
        vectors.append(value)
        value = value * (1.0 / roots[k])
        for c in range(comps):
            basis_ref[c, k : k + 1, :] = value[c : c + 1]
    for c in range(comps):
        factors_ref[c, :, :vecs] = small[:S, c * vecs : (c + 1) * vecs]
    for k in range(S):
        line = jnp.zeros((8, 128), jnp.float32)
        for l in range(k + 1):
            line = jnp.where(lane == vecs + l, lower[k, l], line)
        for c in range(comps):
            factors_ref[c, k : k + 1, vecs:] = line[c : c + 1, vecs : vecs + S]


VMEM = pl.BlockSpec(memory_space=pltpu.VMEM)
HBM = pl.BlockSpec(memory_space=pltpu.HBM)


def in_hbm(*arrays):
    return [pltpu.with_memory_space_constraint(x, pltpu.HBM) for x in arrays]


def call(kernel, outs, specs, flops, moved, scratch=()):
    shapes = [jax.ShapeDtypeStruct(shape, kind) for shape, kind in outs]
    return pl.pallas_call(
        kernel,
        out_shape=shapes if len(shapes) > 1 else shapes[0],
        in_specs=specs,
        out_specs=[VMEM] * len(shapes) if len(shapes) > 1 else VMEM,
        scratch_shapes=list(scratch),
        compiler_params=pltpu.CompilerParams(vmem_limit_bytes=24 * 1024 * 1024),
        cost_estimate=pl.CostEstimate(flops=flops, bytes_accessed=moved, transcendentals=0),
    )


def send(value, target):
    return lax.ppermute(value, "dom", [(d, target[d]) for d in range(lax.axis_size("dom"))])


def neighbours(length, step, odd):
    target = {}
    for d in range(length):
        other = d + step if (d // step) % 2 == odd else d - step
        target[d] = other if 0 <= other < length else None
    return target


def ghosts(tile):
    length = lax.axis_size("dom")
    last = length - 1
    near, across = neighbours(length, 1, 0), neighbours(length, 1, 1)
    far_even, far_odd = neighbours(length, FAR, 0), neighbours(length, FAR, 1)
    across.update({0: 2, 2: 1, 1: 0, last: last - 2, last - 2: last - 1, last - 1: last})
    for d in range(length):
        if far_odd[d] is None:
            far_odd[d] = d ^ 1
    far_odd.update({1: 2, 2: 3, 3: 0, 0: 1})
    far_odd.update({last - 1: last - 2, last - 2: last - 3, last - 3: last, last: last - 1})
    return [send(tile, target) for target in (near, far_odd, far_even, across)]


def summed(value):
    length = lax.axis_size("dom")

    def fetched(step):
        return send(value, {d: d ^ (step | 1) for d in range(length)})

    parts = [value, fetched(1)]
    step = 2
    while step < length:
        value = added(parts)
        steps = (3 * step, step, 2 * step) if 2 * step < length else (step,)
        got = [fetched(s) for s in steps]
        parts = [value] + got[1:] + got[:1]
        step *= 4
    return parts


def added(parts):
    if len(parts) == 2:
        return parts[0] + parts[1]
    return (parts[0] + parts[1]) + (parts[2] + parts[3])


def local(strips, columns, send_list, send_count, shifts, prev_basis, mix):
    comps, vecs, rows = prev_basis.shape
    blocks = columns.shape[0]
    width = strips.shape[1]
    f32, bf16, dma = jnp.float32, jnp.bfloat16, pltpu.SemaphoreType.DMA
    tile_out = ((comps * blocks, 128), f32)
    tile = call(
        start_kernel,
        [((comps * blocks + 8, 128), f32)],
        [HBM] * 4,
        600000,
        250000,
        [
            pltpu.VMEM(prev_basis.shape, f32),
            pltpu.VMEM(mix.shape, f32),
            pltpu.VMEM(send_list.shape, jnp.int32),
            pltpu.VMEM(send_count.shape, jnp.int32),
            dma((4,)),
        ],
    )(*in_hbm(prev_basis, mix, send_list, send_count))
    high, low, aux = call(
        prepare_kernel,
        [((width, rows), bf16), ((width, rows), bf16), ((8 * S + 24, 128), f32)],
        [HBM] * 3,
        1000000,
        1000000,
        [
            pltpu.VMEM((rows, width), f32),
            pltpu.VMEM(columns.shape[::-1], jnp.int32),
            pltpu.SMEM(shifts.shape, f32),
            dma((4,)),
        ],
    )(*in_hbm(strips, columns.T, shifts))
    tiles = []
    length = lax.axis_size("dom")
    near, far_odd, far_even, across = ghosts(tile)
    tile, choose = call(
        lambda *refs: first_kernel(length, *refs),
        [tile_out, ((3 * blocks, 128), jnp.int32)],
        [VMEM] * 8,
        50000000,
        600000,
    )(tile, near, far_even, across, far_odd, aux, high, low)
    tiles.append(tile)
    for step in (1, 2):
        tile = call(
            lambda *refs, step=step: middle_kernel(step, *refs), [tile_out], [VMEM] * 9, 50000000, 600000
        )(tile, *ghosts(tile), choose, aux, high, low)
        tiles.append(tile)
    received = ghosts(tile)
    gram_out = ((24, 128), f32)
    lines, early, *parts = call(
        early_kernel,
        [((8 * S - 8, rows), f32), gram_out] + [((rows, 128), bf16)] * 3,
        [VMEM] * 4,
        60000000,
        250000,
    )(prev_basis, *tiles)
    last, gram = call(
        lambda *refs: last_kernel(vecs, *refs),
        [((8, rows), f32), gram_out],
        [VMEM] * 14,
        80000000,
        900000,
    )(tile, *received, choose, aux, high, low, early, *parts, lines)
    total = float(length * rows)
    parts = summed(gram)
    count = len(parts)
    basis, factors = call(
        lambda *refs: finish_kernel(total, refs[:count], *refs[count:]),
        [((comps, S, rows), f32), ((comps, S, vecs + S), f32)],
        [VMEM] * (count + 3),
        50000000,
        400000,
    )(*parts, prev_basis, lines, last)
    return basis, jnp.swapaxes(factors, 1, 2)


def solution(mesh):
    in_specs = (
        P("dom", None),
        P("dom", None),
        P("dom", None, None),
        P("dom", None),
        P(),
        P(None, None, "dom"),
        P(),
    )
    out_specs = (P(None, None, "dom"), P())
    return jax.shard_map(local, mesh=mesh, in_specs=in_specs, out_specs=out_specs, check_vma=False)
```

```python
import jax
import jax.numpy as jnp
from jax import lax
from jax.experimental import pallas as pl
from jax.experimental.pallas import tpu as pltpu
from jax.sharding import PartitionSpec as P

BLOCK = 64
S = 4
FAR = 8
COMPS = 3
DEAD = 1000.0
HIGHEST = lax.Precision.HIGHEST
NN = (((1,), (0,)), ((), ()))
NT = (((1,), (1,)), ((), ()))


def dot(a, b, dims=NN, precision=None):
    return lax.dot_general(a, b, dims, precision=precision, preferred_element_type=jnp.float32)


def iota(shape, axis):
    return lax.broadcasted_iota(jnp.int32, shape, axis)


PLACES = {(c, g): (g % 2, (0, 8, 0, 0)[g] + 32 * c) for c in range(COMPS) for g in range(4)}
PLACES.update({(0, 2): (0, 96), (1, 2): (0, 112), (2, 2): (1, 96)})


def own_lanes(rows, width):
    return iota((rows, width), 1) // BLOCK == iota((rows, width), 0) % 8


def fold(masked):
    total = masked[:, :128]
    for t in range(1, masked.shape[1] // 128):
        total = total + masked[:, t * 128 : (t + 1) * 128]
    return total + pltpu.roll(total, BLOCK, 1)


def lines_of(tile, width):
    wide = jnp.concatenate([tile] * (width // 128), axis=1)
    return joined(jnp.where(own_lanes(wide.shape[0], width), wide, 0.0))


def joined(wide):
    width = wide.shape[1]
    where = iota((8, width), 0)
    result = jnp.zeros((8, width), jnp.float32)
    for c in range(COMPS):
        line = jnp.sum(wide[c * 8 : (c + 1) * 8], axis=0, keepdims=True)
        result = jnp.where(where == c, jnp.broadcast_to(line, result.shape), result)
    return result


def split(x):
    parts = []
    for _ in range(3):
        parts.append(x.astype(jnp.bfloat16))
        x = x - parts[-1].astype(jnp.float32)
    return parts


def split_dot(x, parts):
    left = [part.astype(jnp.float32) for part in split(x)]
    left.append(jnp.zeros((-3 * x.shape[0] % 16, x.shape[1]), jnp.float32))
    left = jnp.concatenate([part for part in left if part.shape[0]], axis=0).astype(jnp.bfloat16)
    products = dot(left, parts[0]) + dot(left, parts[1]) + dot(left, parts[2])
    rows = x.shape[0]
    return products[:rows] + (products[rows : 2 * rows] + products[2 * rows : 3 * rows])


def fetch(pairs, sems):
    copies = [pltpu.make_async_copy(src, dst, sems.at[i]) for i, (src, dst) in enumerate(pairs)]
    for copy in copies:
        copy.start()
    return copies


def start_kernel(prev_in, mix_in, list_in, count_in, out_ref, prev_ref, mix_ref, list_ref, count_ref, sems):
    copies = fetch(
        [(prev_in, prev_ref), (mix_in, mix_ref), (list_in, list_ref), (count_in, count_ref)], sems
    )
    for copy in copies[1:]:
        copy.wait()
    comps, vecs, rows = prev_ref.shape
    eye = iota((vecs, vecs), 0) == iota((vecs, vecs), 1)
    weights = []
    for c in range(comps):
        line = jnp.broadcast_to(mix_ref[c : c + 1, :], eye.shape)
        weights.append(jnp.sum(jnp.where(eye, line, 0.0), axis=1, keepdims=True))
    order = list_ref[0].astype(jnp.float32)
    order = jnp.concatenate([order, jnp.zeros((4, 120), jnp.float32)], axis=1)
    meta = jnp.zeros((8, 128), jnp.float32)
    slot = iota((1, 128), 1)
    for link in range(4):
        live = slot < jnp.broadcast_to(count_ref[0:1, link : link + 1], slot.shape)
        line = jnp.where(live, order[link : link + 1], DEAD)
        line = pltpu.roll(jnp.broadcast_to(line, (8, 128)), 8 + 8 * link, 1)
        meta = jnp.where(iota((8, 128), 1) // 8 == link + 1, line, meta)
    out_ref[8 * comps :, :] = meta
    copies[0].wait()
    own = own_lanes(8, rows)
    for c in range(comps):
        start = jnp.sum(weights[c] * prev_ref[c], axis=0, keepdims=True)
        line = jnp.broadcast_to(start, own.shape)
        out_ref[c * 8 : (c + 1) * 8, :] = fold(jnp.where(own, line, 0.0))


def prepare_kernel(strips_in, columns_in, shifts_in, high_ref, low_ref, aux_ref, strips, columns, shifts, sems):
    rows = strips.shape[0]
    cuts = [(0, rows * 3 // 4), (rows * 3 // 4, rows)]
    pairs = [(strips_in.at[pl.ds(a, b - a)], strips.at[pl.ds(a, b - a)]) for a, b in cuts]
    copies = fetch(pairs + [(columns_in, columns), (shifts_in, shifts)], sems)
    copies[2].wait()
    copies[3].wait()
    eye = iota((8, 8), 0) == iota((8, 8), 1)
    for k in range(1, columns.shape[0]):
        line = jnp.broadcast_to(columns[k : k + 1, :].astype(jnp.float32), (8, 8))
        column = jnp.sum(jnp.where(eye, line, 0.0), axis=1, keepdims=True)
        at = 8 * S + 8 * (k - 1)
        aux_ref[at : at + 8, :] = jnp.broadcast_to(column, (8, 128))
    for k in range(S):
        aux_ref[8 * k : 8 * k + 8, :] = jnp.full((8, 128), shifts[k], jnp.float32)
    for copy, (a, b) in zip(copies, cuts):
        copy.wait()
        turned = strips[a:b, :].T
        high = turned.astype(jnp.bfloat16)
        high_ref[:, a:b] = high
        low_ref[:, a:b] = (turned - high.astype(jnp.float32)).astype(jnp.bfloat16)


def selection(table, metas, place, length):
    even, even_far = lax.rem(place, 2) == 0, lax.rem(place // FAR, 2) == 0
    near, far_odd, far_even, across = metas
    moved = (place == 2) | (place == length - 3)
    across = jnp.where(moved, far_odd, across)
    circle = jnp.where(moved, 16.0, 32.0)
    slots = [
        (place >= 1, jnp.where(even, circle, 8.0), jnp.where(even, across, near)),
        (place < length - 1, jnp.where(even, 8.0, circle), jnp.where(even, near, across)),
        (place >= FAR, jnp.where(even_far, 16.0, 24.0), jnp.where(even_far, far_odd, far_even)),
        (place < length - FAR, jnp.where(even_far, 24.0, 16.0), jnp.where(even_far, far_even, far_odd)),
    ]
    lane = iota((1, 128), 1)
    target = lane.astype(jnp.float32)
    for link, (valid, base, order) in enumerate(slots):
        order = order + jnp.where(valid, base, DEAD)
        target = jnp.where(lane // 8 == link + 1, order, target)
    target = jnp.broadcast_to(target, (8, 128))
    index = table.astype(jnp.int32)
    at = [jnp.take_along_axis(target, index[8 * k : 8 * k + 8], axis=1) for k in range(3)]
    return jnp.concatenate(at, axis=0).astype(jnp.int32)


def product(choose, pieces, high, low):
    rows = 8 * COMPS
    front = iota((8, 128), 1) < BLOCK
    picked = [[pieces[0][8 * c : 8 * c + 8] for c in range(COMPS)]]
    for k in range(3):
        code = choose[8 * k : 8 * k + 8]
        index, place = code & 7, code >> 3
        blocks = []
        for c in range(COMPS):
            block = jnp.zeros((8, 128), jnp.float32)
            for p, piece in enumerate(pieces):
                found = jnp.take_along_axis(piece[8 * c : 8 * c + 8], index, axis=0)
                block = jnp.where(place == p, found, block)
            blocks.append(block)
        picked.append(blocks)
    x = [
        jnp.concatenate(
            [jnp.where(front, picked[2 * t][c], picked[2 * t + 1][c]) for t in range(2)], axis=1
        )
        for c in range(COMPS)
    ]
    x = jnp.concatenate(x, axis=0)
    top = x.astype(jnp.bfloat16).astype(jnp.float32)
    left = jnp.concatenate([top, x - top], axis=0).astype(jnp.bfloat16)
    both = dot(left, high) + dot(left, low)
    image = both[:rows] + both[rows:]
    return jnp.where(own_lanes(rows, image.shape[1]), image, 0.0)


def multiply(choose, pieces, shift, high, low):
    image = fold(product(choose, pieces, high, low))
    return image - jnp.concatenate([shift] * COMPS, axis=0) * pieces[0]


def first_kernel(length, own, a, c, d, b, aux, high, low, tile_ref, choose_ref):
    rows = 8 * COMPS
    refs = (own, a, b, c, d)
    pieces = [ref[:rows, :] for ref in refs]
    metas = [ref[rows : rows + 1, :] for ref in refs[1:]]
    choose = selection(aux[8 * S :, :], metas, lax.axis_index("dom"), length)
    choose_ref[...] = choose
    tile_ref[...] = multiply(choose, pieces, aux[:8, :], high[...], low[...])


def middle_kernel(step, own, a, b, c, d, choose, aux, high, low, tile_ref):
    pieces = [ref[...] for ref in (own, a, b, c, d)]
    tile_ref[...] = multiply(choose[...], pieces, aux[8 * step : 8 * step + 8, :], high[...], low[...])


def collect(gram, width, vecs):
    lane, comp = iota(gram.shape, 1), iota(gram.shape, 0)
    mine = jnp.where(lane < width, lane // vecs, lane % 8) == comp
    return jnp.sum(jnp.where(mine, gram, 0.0), axis=0, keepdims=True)


def early_kernel(prev_ref, t0, t1, t2, lines_ref, gram_ref, *split_refs):
    comps, vecs, rows = prev_ref.shape
    width = comps * vecs
    lines = jnp.concatenate([lines_of(t[...], rows) for t in (t0, t1, t2)], axis=0)
    lines_ref[...] = lines
    prev = prev_ref[...].reshape(width, rows)
    full = dot(prev, prev, NT, HIGHEST)
    full = jnp.concatenate([full, jnp.zeros((width, 128 - width), jnp.float32)], axis=1)
    lane = iota((8, 128), 1)
    tiles = [jnp.zeros((8, 128), jnp.float32)] * 2
    for (c, g), (t, first) in PLACES.items():
        at = c * vecs + 8 * g
        piece = pltpu.roll(full[at : at + 8], (first - at) % 128, 1)
        tiles[t] = jnp.where((lane >= first) & (lane < first + vecs - 8 * g), piece, tiles[t])
    gram_ref[:16, :] = jnp.concatenate(tiles, axis=0)
    against = jnp.concatenate([prev, lines, jnp.zeros((8, rows), jnp.float32)], axis=0)
    for ref, part in zip(split_refs, split(against.T)):
        ref[...] = part
    gram = dot(lines, against, NT, HIGHEST)
    result = jnp.zeros((8, 128), jnp.float32)
    for k in range(S - 1):
        line = collect(gram[k * 8 : (k + 1) * 8], width, vecs)
        result = jnp.where(iota((8, 128), 0) == k, jnp.broadcast_to(line, result.shape), result)
    gram_ref[16:, :] = result


def last_kernel(
    vecs, own, a, b, c, d, choose, aux, high, low, early, t0, t1, t2, lines, line_ref, gram_ref
):
    pieces = [ref[...] for ref in (own, a, b, c, d)]
    image = joined(product(choose[...], pieces, high[...], low[...]))
    width = COMPS * vecs
    shift = aux[8 * S - 8 : 8 * S, :1]
    last = image - shift * lines[8 * S - 16 :, :]
    line_ref[...] = last
    gram = split_dot(last, (t0[...], t1[...], t2[...]))
    square = jnp.sum(last * last, axis=1, keepdims=True)
    gram = jnp.where(iota(gram.shape, 1) == width + 8 * (S - 1) + iota(gram.shape, 0), square, gram)
    line = collect(gram, width, vecs)
    gram_ref[:16, :] = early[:16, :]
    gram_ref[16:, :] = jnp.where(
        iota((8, 128), 0) == S - 1, jnp.broadcast_to(line, (8, 128)), early[16:, :]
    )


def finish_kernel(total, gram_ins, prev_ref, lines, last, basis_ref, factors_ref):
    comps, vecs, rows = prev_ref.shape
    width = comps * vecs
    gram = added([ref[...] for ref in gram_ins]) * (1.0 / total)
    small = gram[16:]
    lane, comp = iota((8, 128), 1), iota((8, 128), 0)
    in_prev = (lane < width) & (lane // vecs == comp)
    coef, cross = [], []
    for k in range(S):
        line = jnp.broadcast_to(small[k : k + 1], (8, 128))
        coef.append(jnp.where(in_prev, line, 0.0))
        cross.append([jnp.where(lane == width + 8 * l + comp, line, 0.0) for l in range(k + 1)])
    coefs = jnp.concatenate(coef, axis=0)
    pieces, turns = [], {}
    for c in range(comps):
        for g in range(vecs // 8):
            t, first = PLACES[c, g]
            at = c * vecs + 8 * g
            turn = t, (at - first) % 128
            if turn not in turns:
                piece = gram[8 * t : 8 * t + 8]
                turns[turn] = pltpu.roll(piece, turn[1], 1) if turn[1] else piece
            piece = turns[turn]
            piece = jnp.where(lane < at + 8, 0.5 * piece, piece)
            piece = jnp.where((lane >= at) & (lane < (c + 1) * vecs), piece, 0.0)
            pieces.append(piece - jnp.where(lane == at + comp, 1.0, 0.0))
    half = jnp.concatenate(pieces, axis=0)
    turned = dot(coefs[:, :width], half, precision=HIGHEST)
    prev = prev_ref[...].reshape(width, rows)
    basis = jnp.concatenate([lines[...], last[...]], axis=0)
    projected = basis - dot(coefs[:, :width], prev, precision=HIGHEST)
    unit, scale, entry = {}, {}, {}
    for l in range(S):
        for k in range(l, S):
            value = turned[k * 8 : (k + 1) * 8] * coef[l] + turned[l * 8 : (l + 1) * 8] * coef[k] + cross[k][l]
            value = jnp.sum(value, axis=1, keepdims=True)
            for m in range(l):
                value = value - entry[k, m] * unit[l, m]
            if k == l:
                scale[l] = entry[l, l] = value
            else:
                entry[k, l], unit[k, l] = value, value / scale[l]
    roots = [jnp.sqrt(scale[k]) for k in range(S)]
    lower = {(k, l): unit[k, l] * roots[l] if l < k else roots[k] for k in range(S) for l in range(k + 1)}
    vectors = []
    for k in range(S):
        value = projected[k * 8 : (k + 1) * 8]
        for l in range(k):
            value = value - unit[k, l] * vectors[l]
        vectors.append(value)
        value = value * (1.0 / roots[k])
        for c in range(comps):
            basis_ref[c, k : k + 1, :] = value[c : c + 1]
    for c in range(comps):
        factors_ref[c, :, :vecs] = small[:S, c * vecs : (c + 1) * vecs]
    for k in range(S):
        line = jnp.zeros((8, 128), jnp.float32)
        for l in range(k + 1):
            line = jnp.where(lane == vecs + l, lower[k, l], line)
        for c in range(comps):
            factors_ref[c, k : k + 1, vecs:] = line[c : c + 1, vecs : vecs + S]


VMEM = pl.BlockSpec(memory_space=pltpu.VMEM)
HBM = pl.BlockSpec(memory_space=pltpu.HBM)


def in_hbm(*arrays):
    return [pltpu.with_memory_space_constraint(x, pltpu.HBM) for x in arrays]


def call(kernel, outs, specs, flops, moved, scratch=()):
    shapes = [jax.ShapeDtypeStruct(shape, kind) for shape, kind in outs]
    return pl.pallas_call(
        kernel,
        out_shape=shapes if len(shapes) > 1 else shapes[0],
        in_specs=specs,
        out_specs=[VMEM] * len(shapes) if len(shapes) > 1 else VMEM,
        scratch_shapes=list(scratch),
        compiler_params=pltpu.CompilerParams(vmem_limit_bytes=24 * 1024 * 1024),
        cost_estimate=pl.CostEstimate(flops=flops, bytes_accessed=moved, transcendentals=0),
    )


def send(value, target):
    return lax.ppermute(value, "dom", [(d, target[d]) for d in range(lax.axis_size("dom"))])


def neighbours(length, step, odd):
    target = {}
    for d in range(length):
        other = d + step if (d // step) % 2 == odd else d - step
        target[d] = other if 0 <= other < length else None
    return target


def ghosts(tile):
    length = lax.axis_size("dom")
    last = length - 1
    near, across = neighbours(length, 1, 0), neighbours(length, 1, 1)
    far_even, far_odd = neighbours(length, FAR, 0), neighbours(length, FAR, 1)
    across.update({0: 2, 2: 1, 1: 0, last: last - 2, last - 2: last - 1, last - 1: last})
    for d in range(length):
        if far_odd[d] is None:
            far_odd[d] = d ^ 1
    far_odd.update({1: 2, 2: 3, 3: 0, 0: 1})
    far_odd.update({last - 1: last - 2, last - 2: last - 3, last - 3: last, last: last - 1})
    return [send(tile, target) for target in (near, far_odd, far_even, across)]


def summed(value):
    length = lax.axis_size("dom")

    def fetched(step):
        return send(value, {d: d ^ (step | 1) for d in range(length)})

    parts = [value, fetched(1)]
    step = 2
    while step < length:
        value = added(parts)
        steps = (3 * step, step, 2 * step) if 2 * step < length else (step,)
        got = [fetched(s) for s in steps]
        parts = [value] + got[1:] + got[:1]
        step *= 4
    return parts


def added(parts):
    if len(parts) == 2:
        return parts[0] + parts[1]
    return (parts[0] + parts[1]) + (parts[2] + parts[3])


def local(strips, columns, send_list, send_count, shifts, prev_basis, mix):
    comps, vecs, rows = prev_basis.shape
    blocks = columns.shape[0]
    width = strips.shape[1]
    f32, bf16, dma = jnp.float32, jnp.bfloat16, pltpu.SemaphoreType.DMA
    tile_out = ((comps * blocks, 128), f32)
    tile = call(
        start_kernel,
        [((comps * blocks + 8, 128), f32)],
        [HBM] * 4,
        600000,
        250000,
        [
            pltpu.VMEM(prev_basis.shape, f32),
            pltpu.VMEM(mix.shape, f32),
            pltpu.VMEM(send_list.shape, jnp.int32),
            pltpu.VMEM(send_count.shape, jnp.int32),
            dma((4,)),
        ],
    )(*in_hbm(prev_basis, mix, send_list, send_count))
    high, low, aux = call(
        prepare_kernel,
        [((width, rows), bf16), ((width, rows), bf16), ((8 * S + 24, 128), f32)],
        [HBM] * 3,
        1000000,
        1000000,
        [
            pltpu.VMEM((rows, width), f32),
            pltpu.VMEM(columns.shape[::-1], jnp.int32),
            pltpu.SMEM(shifts.shape, f32),
            dma((4,)),
        ],
    )(*in_hbm(strips, columns.T, shifts))
    tiles = []
    length = lax.axis_size("dom")
    near, far_odd, far_even, across = ghosts(tile)
    tile, choose = call(
        lambda *refs: first_kernel(length, *refs),
        [tile_out, ((3 * blocks, 128), jnp.int32)],
        [VMEM] * 8,
        50000000,
        600000,
    )(tile, near, far_even, across, far_odd, aux, high, low)
    tiles.append(tile)
    for step in (1, 2):
        tile = call(
            lambda *refs, step=step: middle_kernel(step, *refs), [tile_out], [VMEM] * 9, 50000000, 600000
        )(tile, *ghosts(tile), choose, aux, high, low)
        tiles.append(tile)
    received = ghosts(tile)
    gram_out = ((24, 128), f32)
    lines, early, *parts = call(
        early_kernel,
        [((8 * S - 8, rows), f32), gram_out] + [((rows, 128), bf16)] * 3,
        [VMEM] * 4,
        60000000,
        250000,
    )(prev_basis, *tiles)
    last, gram = call(
        lambda *refs: last_kernel(vecs, *refs),
        [((8, rows), f32), gram_out],
        [VMEM] * 14,
        80000000,
        900000,
    )(tile, *received, choose, aux, high, low, early, *parts, lines)
    total = float(length * rows)
    parts = summed(gram)
    count = len(parts)
    basis, factors = call(
        lambda *refs: finish_kernel(total, refs[:count], *refs[count:]),
        [((comps, S, rows), f32), ((comps, S, vecs + S), f32)],
        [VMEM] * (count + 3),
        50000000,
        400000,
    )(*parts, prev_basis, lines, last)
    return basis, jnp.swapaxes(factors, 1, 2)


def solution(mesh):
    in_specs = (
        P("dom", None),
        P("dom", None),
        P("dom", None, None),
        P("dom", None),
        P(),
        P(None, None, "dom"),
        P(),
    )
    out_specs = (P(None, None, "dom"), P())
    return jax.shard_map(local, mesh=mesh, in_specs=in_specs, out_specs=out_specs, check_vma=False)
```
